32 devices in a mesh: cuts: 2 (over core), fsdp: 4 (over y, x), tp: 4 (over z).
Axes of the slice: x: 2, y: 2, z: 4, core: 2. Of those that a mesh axis runs over, the one named last changes fastest.
Arguments:
- tokens: bfloat16 [8192, 2048], P(('cuts', 'fsdp')), may hold values from -6 to 6
- cotangent: bfloat16 [8192, 2048], P(('cuts', 'fsdp')), may hold values from -6 to 6
- gate_frozen_matrix: bfloat16 [2048, 4096], P(('cuts', 'fsdp'), 'tp'), may hold values from -0.125 to 0.125
- up_frozen_matrix: bfloat16 [2048, 4096], P(('cuts', 'fsdp'), 'tp'), may hold values from -0.125 to 0.125
- down_frozen_matrix: bfloat16 [4096, 2048], P('tp', ('cuts', 'fsdp')), may hold values from -0.09375 to 0.09375
- gate_adapter_input_factor: bfloat16 [2048, 64], replicated, may hold values from -0.125 to 0.125
- up_adapter_input_factor: bfloat16 [2048, 64], replicated, may hold values from -0.125 to 0.125
- gate_adapter_output_factor: bfloat16 [64, 4096], P(None, 'tp'), may hold values from -0.75 to 0.75
- up_adapter_output_factor: bfloat16 [64, 4096], P(None, 'tp'), may hold values from -0.75 to 0.75
- down_adapter_input_factor: bfloat16 [4096, 64], P('tp'), may hold values from -0.09375 to 0.09375
- down_leave: bfloat16 [2048, 64], replicated, may hold values from -0.75 to 0.75
Outputs:
- token_input_gradient: bfloat16 [8192, 2048], P(('cuts', 'fsdp'), 'tp')
- wide_grads: float32 [2048, 192], P(('cuts', 'fsdp', 'tp'))
- narrow_grads: float32 [4096, 192], P('tp')
The draws below stay inside these ranges and needn't reach their ends.
All inputs are finite; a program needn't handle non-finite values.
Results may differ from the reference program's by a relative error of at most 0.0055.
Values may be sent and summed in bfloat16 or wider, within the bound.
No kernel may reach another device: no remote copies, remote signals or barrier semaphores. Data moves between devices by JAX's collectives and lax.ppermute only.
A program may use at most 128 MiB of HBM per device.

```python
import math
import jax
import jax.numpy as jnp

D = 2048
RANK = 64
HIDDEN_SIZE = 4096
TOKEN_COUNT = 8192


def spiked(drawn, own_key, source, target, shards_of, factor):
    owner, partner = [(jnp.arange(drawn.shape[axis_at]) // (drawn.shape[axis_at] // shards_of)).reshape([-1 if axis == axis_at else 1 for axis in range(drawn.ndim)]) for axis_at in (source, target)]
    chosen = jax.random.permutation(own_key, shards_of)[partner]
    strong = (owner == chosen) | (owner == (partner + shards_of // 2) % shards_of)
    return jnp.where(strong, factor * drawn, drawn)


def steps_of(stream_key, extent, shards, smallest, largest):
    level, own = 1.0, jax.random.fold_in(stream_key, 6)
    for position, shards_of in shards:
        steps = jnp.exp(jax.random.uniform(jax.random.fold_in(own, position), (shards_of,), jnp.float32, smallest / len(shards), largest / len(shards)))
        level = level * jnp.repeat(steps, extent[position] // shards_of).reshape([-1 if axis == position else 1 for axis in range(len(extent))])
    return level


def centred(stream_key, extent, width, reach, pieces=(), kind=jnp.bfloat16):
    drawn = jax.random.normal(stream_key, extent, jnp.float32) * width
    if len(pieces) > 0:
        drawn = steps_of(stream_key, extent, pieces, -0.22, 0.18) * drawn
    return jnp.clip(drawn, min=-reach, max=reach).astype(kind)


def noise_with(stream_key, dims, scale, most, split, heavy, held_as=jnp.bfloat16):
    entries = scale * jax.random.normal(stream_key, dims, jnp.float32)
    if split:
        entries = entries * steps_of(stream_key, dims, split, -0.22, 0.18)
    return jnp.clip(spiked(entries, jax.random.fold_in(stream_key, 3), *heavy), -most, most).astype(held_as)


def setup_inputs(seed: int = 0) -> dict:
    seeds = jax.random.split(jax.random.key(seed), 12)
    tokens = noise_with(seeds[0], (TOKEN_COUNT, D), 1.0, 6.0, ((0, 8),), (0, 1, 8, 2.0))
    cotangent = noise_with(seeds[1], (TOKEN_COUNT, D), 1.0, 6.0, ((0, 8),), (0, 1, 8, 2.0))
    gate_frozen_matrix = centred(seeds[2], (D, HIDDEN_SIZE), D ** -0.5, 0.125, ((0, 8), (1, 4)))
    up_frozen_matrix = centred(seeds[3], (D, HIDDEN_SIZE), D ** -0.5, 0.125, ((0, 8), (1, 4)))
    down_frozen_matrix = centred(seeds[4], (HIDDEN_SIZE, D), HIDDEN_SIZE ** -0.5, 0.09375, ((0, 4), (1, 8)))
    gate_adapter_input_factor = centred(seeds[5], (D, RANK), D ** -0.5, 0.125)
    up_adapter_input_factor = centred(seeds[6], (D, RANK), D ** -0.5, 0.125)
    gate_adapter_output_factor = centred(seeds[7], (RANK, HIDDEN_SIZE), RANK ** -0.5, 0.75, ((1, 4),))
    up_adapter_output_factor = centred(seeds[8], (RANK, HIDDEN_SIZE), RANK ** -0.5, 0.75, ((1, 4),))
    down_adapter_input_factor = centred(seeds[9], (HIDDEN_SIZE, RANK), HIDDEN_SIZE ** -0.5, 0.09375, ((0, 4),))
    down_leave = centred(seeds[10], (D, RANK), RANK ** -0.5, 0.75)
    return dict(tokens=tokens, cotangent=cotangent, gate_frozen_matrix=gate_frozen_matrix, up_frozen_matrix=up_frozen_matrix, down_frozen_matrix=down_frozen_matrix, gate_adapter_input_factor=gate_adapter_input_factor, up_adapter_input_factor=up_adapter_input_factor, gate_adapter_output_factor=gate_adapter_output_factor, up_adapter_output_factor=up_adapter_output_factor, down_adapter_input_factor=down_adapter_input_factor, down_leave=down_leave)


adapter_scaling = 0.5

def matrix_product(left, right):
    return jnp.dot(left, right, preferred_element_type=jnp.float32)

def reference(tokens, cotangent, gate_frozen_matrix, up_frozen_matrix, down_frozen_matrix, gate_adapter_input_factor, up_adapter_input_factor, gate_adapter_output_factor, up_adapter_output_factor, down_adapter_input_factor, down_leave):
    gate_adapter_hidden = matrix_product(tokens, gate_adapter_input_factor).astype(jnp.bfloat16)
    up_adapter_hidden = matrix_product(tokens, up_adapter_input_factor).astype(jnp.bfloat16)
    gate_preactivation = matrix_product(tokens, gate_frozen_matrix) + adapter_scaling * matrix_product(gate_adapter_hidden, gate_adapter_output_factor)
    up_preactivation = matrix_product(tokens, up_frozen_matrix) + adapter_scaling * matrix_product(up_adapter_hidden, up_adapter_output_factor)
    sig = jax.nn.sigmoid(gate_preactivation)
    hidden = (gate_preactivation * sig * up_preactivation).astype(jnp.bfloat16)
    down_low = matrix_product(hidden, down_adapter_input_factor).astype(jnp.bfloat16)
    backward_adapter_input = matrix_product(cotangent, down_leave).astype(jnp.bfloat16)
    hidden_state_gradient = matrix_product(cotangent, down_frozen_matrix.T) + adapter_scaling * matrix_product(backward_adapter_input, down_adapter_input_factor.T)
    gate_output_gradient = (hidden_state_gradient * up_preactivation * sig * (1.0 + gate_preactivation * (1.0 - sig))).astype(jnp.bfloat16)
    up_output_gradient = (hidden_state_gradient * gate_preactivation * sig).astype(jnp.bfloat16)
    gate_backward_adapter = matrix_product(gate_output_gradient, gate_adapter_output_factor.T).astype(jnp.bfloat16)
    up_backward_adapter = matrix_product(up_output_gradient, up_adapter_output_factor.T).astype(jnp.bfloat16)
    token_input_gradient = (matrix_product(gate_output_gradient, gate_frozen_matrix.T) + matrix_product(up_output_gradient, up_frozen_matrix.T) + adapter_scaling * (matrix_product(gate_backward_adapter, gate_adapter_input_factor.T) + matrix_product(up_backward_adapter, up_adapter_input_factor.T))).astype(jnp.bfloat16)
    gradient_scaling = adapter_scaling / math.sqrt(TOKEN_COUNT)
    wide_grads = gradient_scaling * jnp.concatenate([matrix_product(tokens.T, gate_backward_adapter), matrix_product(tokens.T, up_backward_adapter), matrix_product(cotangent.T, down_low)], axis=1)
    narrow_grads = gradient_scaling * jnp.concatenate([matrix_product(hidden.T, backward_adapter_input), matrix_product(gate_output_gradient.T, gate_adapter_hidden), matrix_product(up_output_gradient.T, up_adapter_hidden)], axis=1)
    return (token_input_gradient, wide_grads, narrow_grads)
```

```python
import functools
import math

import jax
import jax.numpy as jnp
from jax import lax
from jax.experimental import pallas as pl
from jax.experimental.pallas import tpu as pltpu
from jax.sharding import PartitionSpec as P

adapter_scaling = 0.5
VMEM_LIMIT = 56 * 1024 * 1024
ROW_TILE = 256
PIECES = 4
HALVES = 2
QUARTER_ORDER = ((3, 2, 1, 0), (0, 3, 2, 1), (3, 0, 1, 2), (0, 1, 2, 3))


def matrix_product(left, right):
    return jnp.dot(left, right, preferred_element_type=jnp.float32)


def contract_trailing_axis(left, right):
    return lax.dot_general(
        left, right, (((1,), (1,)), ((), ())), preferred_element_type=jnp.float32
    )


def contract_first(left, right):
    return lax.dot_general(
        left, right, (((0,), (0,)), ((), ())), preferred_element_type=jnp.float32
    )


def flip(array, axis, bit):
    size = lax.axis_size(axis)
    return lax.ppermute(array, axis, [(i, i ^ bit) for i in range(size)])


def forward_kernel(n_alias, layout, piece, position_ref, *refs):
    (tokens_ref, cotangent_ref, gate_low_ref, up_low_ref, back_low_ref) = refs[:5]
    (gate_out_ref, up_out_ref, down_in_ref) = refs[5:8]
    refs = refs[8:]
    blocks, refs = refs[: len(layout)], refs[len(layout) :]
    low_before_ref = refs[n_alias - 1] if n_alias else None
    refs = refs[n_alias:]
    (hidden_ref, gate_grad_ref, up_grad_ref, gate_full_ref, up_full_ref, low_ref) = refs[:6]
    weights, sems, out_sems = refs[6:]
    step = pl.program_id(0)
    columns = weights.shape[2]
    rows = blocks[0].shape[1]

    def block_copies():
        copies = []
        for number, (mask, offset) in enumerate(layout):
            block = blocks[number]
            place = pl.multiple_of(
                lax.bitwise_xor(position_ref[0], jnp.int32(mask)) * rows + offset, block.shape[1]
            )
            copies.append(
                pltpu.make_async_copy(
                    block, weights.at[:, pl.ds(place, block.shape[1]), :], sems.at[number]
                )
            )
        return copies

    def full_copies():
        return [
            pltpu.make_async_copy(
                weights.at[which],
                full.at[:, pl.ds(piece * columns, columns)],
                out_sems.at[which],
            )
            for which, full in enumerate((gate_full_ref, up_full_ref))
        ]

    @pl.when(step == 0)
    def _():
        for copy in block_copies():
            copy.start()
        for copy in block_copies():
            copy.wait()
        for copy in full_copies():
            copy.start()

    tokens = tokens_ref[...]
    gate = matrix_product(tokens, weights[0]) + adapter_scaling * matrix_product(
        gate_low_ref[...], gate_out_ref[...]
    )
    up = matrix_product(tokens, weights[1]) + adapter_scaling * matrix_product(
        up_low_ref[...], up_out_ref[...]
    )
    hidden_grad = matrix_product(
        cotangent_ref[...], weights[2]
    ) + adapter_scaling * contract_trailing_axis(back_low_ref[...], down_in_ref[...])
    sig = 1.0 / (1.0 + jnp.exp(-gate))
    gated = gate * sig
    hidden_ref[...] = (gated * up).astype(jnp.bfloat16)
    gate_grad = (hidden_grad * up * sig * (1.0 + gate * (1.0 - sig))).astype(jnp.bfloat16)
    up_grad = (hidden_grad * gated).astype(jnp.bfloat16)
    gate_grad_ref[...] = gate_grad
    up_grad_ref[...] = up_grad
    low = jnp.concatenate(
        [
            contract_trailing_axis(gate_grad, gate_out_ref[...]),
            contract_trailing_axis(up_grad, up_out_ref[...]),
        ],
        axis=1,
    )
    if low_before_ref is not None:
        low = low + low_before_ref[...]
    low_ref[...] = low

    @pl.when(step == pl.num_programs(0) - 1)
    def _():
        for copy in full_copies():
            copy.wait()


def forward_piece(
    piece, columns, position, tokens, cotangent, lows, factors, blocks, layout, before
):
    rows, width = tokens.shape
    rank = lows[0].shape[1]
    hidden_size = factors[0].shape[1]
    tile = min(ROW_TILE, rows)
    row_block = lambda last: pl.BlockSpec((tile, last), lambda i: (i, 0))
    anywhere = pl.BlockSpec(memory_space=pl.ANY)
    piece_block = pl.BlockSpec((tile, columns), lambda i: (i, piece))
    in_specs = (
        [pl.BlockSpec(memory_space=pltpu.SMEM)]
        + [row_block(width)] * 2
        + [row_block(rank)] * 3
        + [pl.BlockSpec((rank, columns), lambda i: (0, piece))] * 2
        + [pl.BlockSpec((columns, rank), lambda i: (piece, 0))]
        + [anywhere] * len(blocks)
    )
    args = [position, tokens, cotangent, *lows, *factors, *blocks]
    aliases = {}
    if before:
        for number, array in enumerate(before):
            aliases[len(args)] = number
            args.append(array)
            in_specs.append(anywhere if number < 5 else row_block(2 * rank))
    out_shape = (
        [jax.ShapeDtypeStruct((rows, hidden_size), jnp.bfloat16)] * 3
        + [jax.ShapeDtypeStruct((width, hidden_size), jnp.bfloat16)] * 2
        + [jax.ShapeDtypeStruct((rows, 2 * rank), jnp.float32)]
    )
    out_specs = [piece_block] * 3 + [anywhere] * 2 + [row_block(2 * rank)]
    return pl.pallas_call(
        functools.partial(forward_kernel, len(before), layout, piece),
        grid=(rows // tile,),
        in_specs=in_specs,
        out_specs=out_specs,
        out_shape=out_shape,
        scratch_shapes=[
            pltpu.VMEM((3, width, columns), jnp.bfloat16),
            pltpu.SemaphoreType.DMA((len(blocks),)),
            pltpu.SemaphoreType.DMA((2,)),
        ],
        input_output_aliases=aliases,
        compiler_params=pltpu.CompilerParams(vmem_limit_bytes=VMEM_LIMIT),
        cost_estimate=pl.CostEstimate(
            flops=6 * rows * width * columns,
            bytes_accessed=4 * rows * width + 10 * width * columns + 6 * rows * columns,
            transcendentals=rows * columns,
        ),
        name="forward_piece",
    )(*args)


def token_grad_kernel(quarter_ref, gate_grad_ref, up_grad_ref, gate_ref, up_ref, low_ref, factor_ref, out_ref):
    total = contract_trailing_axis(gate_grad_ref[...], gate_ref[...])
    total += contract_trailing_axis(up_grad_ref[...], up_ref[...])
    low = (adapter_scaling * low_ref[...]).astype(jnp.bfloat16)
    total += contract_trailing_axis(low, factor_ref[...])
    out_ref[...] = total.astype(out_ref.dtype)


def token_grad(quarter, half, kind, gate_grad, up_grad, gate, up, low, factor, columns):
    rows, hidden_size = gate_grad.shape
    part = rows // HALVES
    tile = min(ROW_TILE, part)
    steps = part // tile
    row_block = lambda last: pl.BlockSpec((tile, last), lambda i, q: (half * steps + i, 0))
    quarter_block = lambda last: pl.BlockSpec((columns, last), lambda i, q: (q[0], 0))
    return pl.pallas_call(
        token_grad_kernel,
        grid_spec=pltpu.PrefetchScalarGridSpec(
            num_scalar_prefetch=1,
            grid=(steps,),
            in_specs=[
                row_block(hidden_size),
                row_block(hidden_size),
                quarter_block(hidden_size),
                quarter_block(hidden_size),
                row_block(low.shape[1]),
                quarter_block(low.shape[1]),
            ],
            out_specs=pl.BlockSpec((tile, columns), lambda i, q: (i, 0)),
        ),
        out_shape=jax.ShapeDtypeStruct((part, columns), kind),
        compiler_params=pltpu.CompilerParams(vmem_limit_bytes=VMEM_LIMIT),
        cost_estimate=pl.CostEstimate(
            flops=4 * part * columns * hidden_size,
            bytes_accessed=4 * (part + columns) * hidden_size + 2 * part * columns,
            transcendentals=0,
        ),
        name="token_grad",
    )(quarter, gate_grad, up_grad, gate, up, low, factor)


def gather_blocks(own):
    size = lax.axis_size("fsdp")
    rows = own.shape[1]
    half = rows // 2
    whole = {0: own}
    upper, lower = {}, {}
    bits = [1 << number for number in range(size.bit_length() - 1)]
    for bit in bits:
        whole[bit] = flip(own, "fsdp", bit)
    for mask, block in whole.items():
        upper[mask], lower[mask] = block[:, :half], block[:, half:]
    for mask in range(size):
        if mask not in whole:
            high = 1 << (mask.bit_length() - 1)
            upper[mask] = flip(upper[mask ^ high], "fsdp", high)
    for mask in sorted(range(size), key=lambda m: bin(m).count("1")):
        if mask not in whole:
            low = mask & -mask
            lower[mask] = flip(lower[mask ^ low], "fsdp", low)
    blocks, layout = [], []
    for mask in range(size):
        if mask in whole:
            blocks.append(whole[mask])
            layout.append((mask, 0))
        else:
            blocks += [upper[mask], lower[mask]]
            layout += [(mask, 0), (mask, half)]
    other = [flip(block, "cuts", 1) for block in blocks]
    layout = layout + [(mask | size, offset) for mask, offset in layout]
    return blocks + other, tuple(layout)


def sum_over_plane(parts, cut, place):
    half = parts.shape[0] // 2
    parts = parts.reshape(2, half, *parts.shape[1:])
    mine = lax.dynamic_index_in_dim(parts, cut, 0, keepdims=False)
    parts = mine + flip(lax.dynamic_index_in_dim(parts, 1 - cut, 0, keepdims=False), "cuts", 1)
    bit = half // 2
    while bit:
        parts = parts.reshape(2, bit, *parts.shape[1:])
        up = (place // bit) % 2
        mine = lax.dynamic_index_in_dim(parts, up, 0, keepdims=False)
        parts = mine + flip(lax.dynamic_index_in_dim(parts, 1 - up, 0, keepdims=False), "fsdp", bit)
        bit //= 2
    return parts[0]


def copy_over_plane(rows, cut, place):
    bit = 1
    while bit < lax.axis_size("fsdp"):
        other = flip(rows, "fsdp", bit)
        up = (place // bit) % 2
        rows = jnp.where(
            up == 0, jnp.concatenate([rows, other]), jnp.concatenate([other, rows])
        )
        bit *= 2
    other = flip(rows, "cuts", 1)
    return jnp.where(cut == 0, jnp.concatenate([rows, other]), jnp.concatenate([other, rows]))


def sum_over_line(slots, place):
    first, second, third, last = slots
    shift = lambda array, pairs: lax.ppermute(array, "tp", pairs)
    plus = lambda a, b: (a.astype(jnp.float32) + b.astype(jnp.float32)).astype(jnp.bfloat16)
    came = shift(first, [(0, 1), (3, 2)])
    onward = plus(second, came)
    from_left = shift(onward, [(0, 1), (1, 2)])
    from_right = shift(onward, [(3, 2), (2, 1)])
    to_right = plus(jnp.where(place == 2, first, third), from_left)
    to_left = plus(jnp.where(place == 1, first, third), from_right)
    from_left = shift(to_right, [(0, 1), (1, 2), (2, 3)])
    from_right = shift(to_left, [(3, 2), (2, 1), (1, 0)])
    return (last + from_left.astype(jnp.float32) + from_right.astype(jnp.float32)).astype(
        jnp.bfloat16
    )


def per_device(
    tokens,
    cotangent,
    gate_frozen_matrix,
    up_frozen_matrix,
    down_frozen_matrix,
    gate_adapter_input_factor,
    up_adapter_input_factor,
    gate_adapter_output_factor,
    up_adapter_output_factor,
    down_adapter_input_factor,
    down_leave,
):
    groups = lax.axis_size(("cuts", "fsdp"))
    quarters = lax.axis_size("tp")
    cut = lax.axis_index("cuts")
    place = lax.axis_index("fsdp")
    quarter = lax.axis_index("tp")
    rows, width = tokens.shape
    hidden_size = gate_frozen_matrix.shape[1]
    rank = down_leave.shape[1]
    gradient_scaling = adapter_scaling / math.sqrt(rows * groups)
    position = lax.axis_index(("cuts", "fsdp")).astype(jnp.int32).reshape(1)

    columns = hidden_size // PIECES
    gathered = []
    for piece in range(PIECES):
        span = slice(piece * columns, (piece + 1) * columns)
        own = jnp.stack(
            [
                gate_frozen_matrix[:, span],
                up_frozen_matrix[:, span],
                down_frozen_matrix[span].T,
            ]
        )
        gathered.append(gather_blocks(own))

    lows = [
        matrix_product(tokens, gate_adapter_input_factor).astype(jnp.bfloat16),
        matrix_product(tokens, up_adapter_input_factor).astype(jnp.bfloat16),
        matrix_product(cotangent, down_leave).astype(jnp.bfloat16),
    ]
    factors = [gate_adapter_output_factor, up_adapter_output_factor, down_adapter_input_factor]
    state = ()
    for piece in range(PIECES):
        blocks, layout = gathered[piece]
        state = forward_piece(
            piece, columns, position, tokens, cotangent, lows, factors, blocks, layout, state
        )
    hidden, gate_grad, up_grad, gate_full, up_full, low = state

    input_factor = jnp.concatenate([gate_adapter_input_factor, up_adapter_input_factor], axis=1)
    order = jnp.asarray(QUARTER_ORDER, jnp.int32)[quarter]
    results = []
    for half in range(HALVES):
        slots = [
            token_grad(
                order[k : k + 1],
                half,
                jnp.float32 if k == quarters - 1 else jnp.bfloat16,
                gate_grad,
                up_grad,
                gate_full,
                up_full,
                low,
                input_factor,
                width // quarters,
            )
            for k in range(quarters)
        ]
        results.append(sum_over_line(slots, quarter))
    token_input_gradient = jnp.concatenate(results)

    down_low = matrix_product(hidden, down_adapter_input_factor).astype(jnp.bfloat16)
    narrow = gradient_scaling * jnp.concatenate(
        [
            contract_first(hidden, lows[2]),
            contract_first(gate_grad, lows[0]),
            contract_first(up_grad, lows[1]),
        ],
        axis=1,
    )
    wide = gradient_scaling * jnp.concatenate(
        [contract_first(tokens, low.astype(jnp.bfloat16)), contract_first(cotangent, down_low)],
        axis=1,
    )
    wide_rows = width // groups
    narrow_rows = hidden_size // groups
    both = jnp.concatenate(
        [
            wide.reshape(groups, wide_rows, 3 * rank),
            narrow.reshape(groups, narrow_rows, 3 * rank),
        ],
        axis=1,
    )
    both = sum_over_plane(both, cut, place)
    narrow_grads = copy_over_plane(both[wide_rows:], cut, place)
    wide_grads = both[:wide_rows]
    bit = quarters // 2
    while bit:
        parts = wide_grads.reshape(2, -1, 3 * rank)
        up = (quarter // bit) % 2
        mine = lax.dynamic_index_in_dim(parts, up, 0, keepdims=False)
        wide_grads = mine + flip(
            lax.dynamic_index_in_dim(parts, 1 - up, 0, keepdims=False), "tp", bit
        )
        bit //= 2
    return (token_input_gradient, wide_grads, narrow_grads)


def solution(mesh):
    in_specs = (
        P(("cuts", "fsdp"), None),
        P(("cuts", "fsdp"), None),
        P(("cuts", "fsdp"), "tp"),
        P(("cuts", "fsdp"), "tp"),
        P("tp", ("cuts", "fsdp")),
        P(),
        P(),
        P(None, "tp"),
        P(None, "tp"),
        P("tp", None),
        P(),
    )
    out_specs = (P(("cuts", "fsdp"), "tp"), P(("cuts", "fsdp", "tp"), None), P("tp", None))
    return jax.shard_map(
        per_device, mesh=mesh, in_specs=in_specs, out_specs=out_specs, check_vma=False
    )
```

```python
import functools
import math

import jax
import jax.numpy as jnp
from jax import lax
from jax.experimental import pallas as pl
from jax.experimental.pallas import tpu as pltpu
from jax.sharding import PartitionSpec as P

adapter_scaling = 0.5
VMEM_LIMIT = 56 * 1024 * 1024
ROW_TILE = 512
PIECES = 4
HALVES = 2
QUARTER_ORDER = ((3, 2, 1, 0), (0, 3, 2, 1), (3, 0, 1, 2), (0, 1, 2, 3))


def matrix_product(left, right):
    return jnp.dot(left, right, preferred_element_type=jnp.float32)


def contract_trailing_axis(left, right):
    return lax.dot_general(
        left, right, (((1,), (1,)), ((), ())), preferred_element_type=jnp.float32
    )


def contract_first(left, right):
    return lax.dot_general(
        left, right, (((0,), (0,)), ((), ())), preferred_element_type=jnp.float32
    )


def flip(array, axis, bit):
    size = lax.axis_size(axis)
    return lax.ppermute(array, axis, [(i, i ^ bit) for i in range(size)])


def forward_kernel(n_alias, layout, piece, position_ref, *refs):
    (tokens_ref, cotangent_ref, gate_low_ref, up_low_ref, back_low_ref) = refs[:5]
    (gate_out_ref, up_out_ref, down_in_ref) = refs[5:8]
    refs = refs[8:]
    blocks, refs = refs[: len(layout)], refs[len(layout) :]
    low_before_ref = refs[n_alias - 1] if n_alias else None
    refs = refs[n_alias:]
    (hidden_ref, gate_grad_ref, up_grad_ref, gate_full_ref, up_full_ref, low_ref) = refs[:6]
    weights, sems, out_sems = refs[6:]
    step = pl.program_id(0)
    columns = weights.shape[2]
    rows = blocks[0].shape[1]

    def block_copies():
        copies = []
        for number, group in enumerate(layout):
            block = blocks[number]
            size = block.shape[1]
            for index, (mask, offset) in enumerate(group):
                place = pl.multiple_of(
                    lax.bitwise_xor(position_ref[0], jnp.int32(mask)) * rows + offset, size
                )
                copies.append(
                    pltpu.make_async_copy(
                        block.at[pl.ds(3 * index, 3)],
                        weights.at[:, pl.ds(place, size), :],
                        sems.at[len(copies)],
                    )
                )
        return copies

    def full_copies():
        return [
            pltpu.make_async_copy(
                weights.at[which],
                full.at[:, pl.ds(piece * columns, columns)],
                out_sems.at[which],
            )
            for which, full in enumerate((gate_full_ref, up_full_ref))
        ]

    @pl.when(step == 0)
    def _():
        for copy in block_copies():
            copy.start()
        for copy in block_copies():
            copy.wait()
        for copy in full_copies():
            copy.start()

    tokens = tokens_ref[...]
    gate = matrix_product(tokens, weights[0]) + adapter_scaling * matrix_product(
        gate_low_ref[...], gate_out_ref[...]
    )
    up = matrix_product(tokens, weights[1]) + adapter_scaling * matrix_product(
        up_low_ref[...], up_out_ref[...]
    )
    hidden_grad = matrix_product(
        cotangent_ref[...], weights[2]
    ) + adapter_scaling * contract_trailing_axis(back_low_ref[...], down_in_ref[...])
    sig = 1.0 / (1.0 + jnp.exp(-gate))
    gated = gate * sig
    hidden_ref[...] = (gated * up).astype(jnp.bfloat16)
    gate_grad = (hidden_grad * up * sig * (1.0 + gate * (1.0 - sig))).astype(jnp.bfloat16)
    up_grad = (hidden_grad * gated).astype(jnp.bfloat16)
    gate_grad_ref[...] = gate_grad
    up_grad_ref[...] = up_grad
    low = jnp.concatenate(
        [
            contract_trailing_axis(gate_grad, gate_out_ref[...]),
            contract_trailing_axis(up_grad, up_out_ref[...]),
        ],
        axis=1,
    )
    if low_before_ref is not None:
        low = low + low_before_ref[...]
    low_ref[...] = low

    @pl.when(step == pl.num_programs(0) - 1)
    def _():
        for copy in full_copies():
            copy.wait()


def forward_piece(
    piece, columns, position, tokens, cotangent, lows, factors, blocks, layout, before
):
    rows, width = tokens.shape
    rank = lows[0].shape[1]
    hidden_size = factors[0].shape[1]
    tile = min(ROW_TILE, rows)
    row_block = lambda last: pl.BlockSpec((tile, last), lambda i: (i, 0))
    anywhere = pl.BlockSpec(memory_space=pl.ANY)
    piece_block = pl.BlockSpec((tile, columns), lambda i: (i, piece))
    in_specs = (
        [pl.BlockSpec(memory_space=pltpu.SMEM)]
        + [row_block(width)] * 2
        + [row_block(rank)] * 3
        + [pl.BlockSpec((rank, columns), lambda i: (0, piece))] * 2
        + [pl.BlockSpec((columns, rank), lambda i: (piece, 0))]
        + [anywhere] * len(blocks)
    )
    args = [position, tokens, cotangent, *lows, *factors, *blocks]
    aliases = {}
    if before:
        for number, array in enumerate(before):
            aliases[len(args)] = number
            args.append(array)
            in_specs.append(anywhere if number < 5 else row_block(2 * rank))
    out_shape = (
        [jax.ShapeDtypeStruct((rows, hidden_size), jnp.bfloat16)] * 3
        + [jax.ShapeDtypeStruct((width, hidden_size), jnp.bfloat16)] * 2
        + [jax.ShapeDtypeStruct((rows, 2 * rank), jnp.float32)]
    )
    out_specs = [piece_block] * 3 + [anywhere] * 2 + [row_block(2 * rank)]
    return pl.pallas_call(
        functools.partial(forward_kernel, len(before), layout, piece),
        grid=(rows // tile,),
        in_specs=in_specs,
        out_specs=out_specs,
        out_shape=out_shape,
        scratch_shapes=[
            pltpu.VMEM((3, width, columns), jnp.bfloat16),
            pltpu.SemaphoreType.DMA((sum(map(len, layout)),)),
            pltpu.SemaphoreType.DMA((2,)),
        ],
        input_output_aliases=aliases,
        compiler_params=pltpu.CompilerParams(vmem_limit_bytes=VMEM_LIMIT),
        cost_estimate=pl.CostEstimate(
            flops=6 * rows * width * columns,
            bytes_accessed=4 * rows * width + 10 * width * columns + 6 * rows * columns,
            transcendentals=rows * columns,
        ),
        name="forward_piece",
    )(*args)


def token_grad_kernel(quarter_ref, gate_grad_ref, up_grad_ref, gate_ref, up_ref, low_ref, factor_ref, out_ref):
    total = contract_trailing_axis(gate_grad_ref[...], gate_ref[...])
    total += contract_trailing_axis(up_grad_ref[...], up_ref[...])
    low = (adapter_scaling * low_ref[...]).astype(jnp.bfloat16)
    total += contract_trailing_axis(low, factor_ref[...])
    out_ref[...] = total.astype(out_ref.dtype)


def token_grad(quarter, half, kind, gate_grad, up_grad, gate, up, low, factor, columns):
    rows, hidden_size = gate_grad.shape
    part = rows // HALVES
    tile = min(ROW_TILE, part)
    steps = part // tile
    row_block = lambda last: pl.BlockSpec((tile, last), lambda i, q: (half * steps + i, 0))
    quarter_block = lambda last: pl.BlockSpec((columns, last), lambda i, q: (q[0], 0))
    return pl.pallas_call(
        token_grad_kernel,
        grid_spec=pltpu.PrefetchScalarGridSpec(
            num_scalar_prefetch=1,
            grid=(steps,),
            in_specs=[
                row_block(hidden_size),
                row_block(hidden_size),
                quarter_block(hidden_size),
                quarter_block(hidden_size),
                row_block(low.shape[1]),
                quarter_block(low.shape[1]),
            ],
            out_specs=pl.BlockSpec((tile, columns), lambda i, q: (i, 0)),
        ),
        out_shape=jax.ShapeDtypeStruct((part, columns), kind),
        compiler_params=pltpu.CompilerParams(vmem_limit_bytes=VMEM_LIMIT),
        cost_estimate=pl.CostEstimate(
            flops=4 * part * columns * hidden_size,
            bytes_accessed=4 * (part + columns) * hidden_size + 2 * part * columns,
            transcendentals=0,
        ),
        name="token_grad",
    )(quarter, gate_grad, up_grad, gate, up, low, factor)


def move_kernel(n_in, plan, *refs):
    ins, outs, sems = refs[:n_in], refs[n_in:-1], refs[-1]
    copies = []
    for number, (source, rows, target, place) in enumerate(plan):
        block = ins[source]
        if rows is not None:
            block = block.at[:, pl.ds(*rows), :]
        copies.append(
            pltpu.make_async_copy(
                block, outs[target].at[pl.ds(place, block.shape[0])], sems.at[number]
            )
        )
    for copy in copies:
        copy.start()
    for copy in copies:
        copy.wait()


def move(arrays, shapes, plan, ahead=()):
    anywhere = pl.BlockSpec(memory_space=pl.ANY)
    return pl.pallas_call(
        functools.partial(move_kernel, len(arrays) + len(ahead), plan),
        in_specs=[anywhere] * (len(arrays) + len(ahead)),
        out_specs=[anywhere] * len(shapes),
        out_shape=[jax.ShapeDtypeStruct(shape, arrays[0].dtype) for shape in shapes],
        scratch_shapes=[pltpu.SemaphoreType.DMA((len(plan),))],
        name="move",
    )(*arrays, *ahead)


def nothing_kernel(*refs):
    pass


def hold(arrays, ahead):
    anywhere = pl.BlockSpec(memory_space=pl.ANY)
    return pl.pallas_call(
        nothing_kernel,
        in_specs=[anywhere] * (len(arrays) + len(ahead)),
        out_specs=[anywhere] * len(arrays),
        out_shape=[jax.ShapeDtypeStruct(array.shape, array.dtype) for array in arrays],
        input_output_aliases={number: number for number in range(len(arrays))},
        name="hold",
    )(*arrays, *ahead)


def gather_square(own, came, ahead_first, ahead_second):
    mats, rows, columns = own.shape
    half = rows // 2
    near, far = came[1], came[2]
    first, upper, lower = move(
        [own, near, far],
        [(3 * mats, rows, columns), (mats, half, columns), (mats, half, columns)],
        (
            (1, (0, half), 1, 0),
            (2, (half, half), 2, 0),
            (0, None, 0, 0),
            (1, None, 0, mats),
            (2, None, 0, 2 * mats),
        ),
        ahead_first,
    )
    upper = flip(upper, "fsdp", 2)
    lower = flip(lower, "fsdp", 1)
    first_other = flip(first, "cuts", 1)
    (second,) = move(
        [upper, lower],
        [(2 * mats, half, columns)],
        ((0, None, 0, 0), (1, None, 0, mats)),
        ahead_second,
    )
    blocks = [first, second, first_other, flip(second, "cuts", 1)]
    layout = [[(0, 0), (1, 0), (2, 0)], [(3, 0), (3, half)]]
    layout += [[(mask | 4, offset) for mask, offset in group] for group in layout]
    return blocks, tuple(map(tuple, layout)), first


def single_flips(own):
    size = lax.axis_size("fsdp")
    return {1 << n: flip(own, "fsdp", 1 << n) for n in range(size.bit_length() - 1)}


def gather_rest(own, came):
    size = lax.axis_size("fsdp")
    half = own.shape[1] // 2
    whole = {0: own, **came}
    upper, lower = {}, {}
    for mask, block in whole.items():
        upper[mask], lower[mask] = block[:, :half], block[:, half:]
    for mask in range(size):
        if mask not in whole:
            high = 1 << (mask.bit_length() - 1)
            upper[mask] = flip(upper[mask ^ high], "fsdp", high)
    for mask in sorted(range(size), key=lambda m: bin(m).count("1")):
        if mask not in whole:
            low = mask & -mask
            lower[mask] = flip(lower[mask ^ low], "fsdp", low)
    first = jnp.concatenate(list(whole.values()))
    rest = [mask for mask in range(size) if mask not in whole]
    second = jnp.concatenate([part[mask] for mask in rest for part in (upper, lower)])
    layout = [[(mask, 0) for mask in whole]]
    layout.append([(mask, offset) for mask in rest for offset in (0, half)])
    blocks = [first, second, flip(first, "cuts", 1), flip(second, "cuts", 1)]
    layout += [[(mask | size, offset) for mask, offset in group] for group in layout]
    return blocks, tuple(map(tuple, layout))


def sum_over_plane(parts, cut, place):
    half = parts.shape[0] // 2
    parts = parts.reshape(2, half, *parts.shape[1:])
    mine = lax.dynamic_index_in_dim(parts, cut, 0, keepdims=False)
    parts = mine + flip(lax.dynamic_index_in_dim(parts, 1 - cut, 0, keepdims=False), "cuts", 1)
    bit = half // 2
    while bit:
        parts = parts.reshape(2, bit, *parts.shape[1:])
        up = (place // bit) % 2
        mine = lax.dynamic_index_in_dim(parts, up, 0, keepdims=False)
        parts = mine + flip(lax.dynamic_index_in_dim(parts, 1 - up, 0, keepdims=False), "fsdp", bit)
        bit //= 2
    return parts[0]


def copy_over_plane(rows, cut, place):
    bit = 1
    while bit < lax.axis_size("fsdp"):
        other = flip(rows, "fsdp", bit)
        up = (place // bit) % 2
        rows = jnp.where(
            up == 0, jnp.concatenate([rows, other]), jnp.concatenate([other, rows])
        )
        bit *= 2
    other = flip(rows, "cuts", 1)
    return jnp.where(cut == 0, jnp.concatenate([rows, other]), jnp.concatenate([other, rows]))


def per_device(
    tokens,
    cotangent,
    gate_frozen_matrix,
    up_frozen_matrix,
    down_frozen_matrix,
    gate_adapter_input_factor,
    up_adapter_input_factor,
    gate_adapter_output_factor,
    up_adapter_output_factor,
    down_adapter_input_factor,
    down_leave,
):
    groups = lax.axis_size(("cuts", "fsdp"))
    quarters = lax.axis_size("tp")
    cut = lax.axis_index("cuts")
    place = lax.axis_index("fsdp")
    quarter = lax.axis_index("tp")
    rows, width = tokens.shape
    hidden_size = gate_frozen_matrix.shape[1]
    rank = down_leave.shape[1]
    gradient_scaling = adapter_scaling / math.sqrt(rows * groups)
    position = lax.axis_index(("cuts", "fsdp")).astype(jnp.int32).reshape(1)

    lows = [
        matrix_product(tokens, gate_adapter_input_factor).astype(jnp.bfloat16),
        matrix_product(tokens, up_adapter_input_factor).astype(jnp.bfloat16),
        matrix_product(cotangent, down_leave).astype(jnp.bfloat16),
    ]
    factors = [gate_adapter_output_factor, up_adapter_output_factor, down_adapter_input_factor]
    columns = hidden_size // PIECES
    state = ()
    came, states, firsts = [], [], []
    for piece in range(PIECES):
        span = slice(piece * columns, (piece + 1) * columns)
        own = jnp.stack(
            [
                gate_frozen_matrix[:, span],
                up_frozen_matrix[:, span],
                down_frozen_matrix[span].T,
            ]
        )
        square = lax.axis_size("fsdp") == 4
        if square and piece == 2:
            (own,) = hold([own], [firsts[0]])
        if square and piece > 2:
            (own,) = hold([own], [states[piece - 3][-1]])
        came.append(single_flips(own))
        if square:
            blocks, layout, first = gather_square(
                own,
                came[piece],
                [states[piece - 2][-1]] if piece >= 2 else [],
                [states[piece - 1][-1]] if piece >= 1 else [],
            )
            firsts.append(first)
        else:
            blocks, layout = gather_rest(own, came[piece])
        state = forward_piece(
            piece, columns, position, tokens, cotangent, lows, factors, blocks, layout, state
        )
        states.append(state)
    hidden, gate_grad, up_grad, gate_full, up_full, low = state

    input_factor = jnp.concatenate([gate_adapter_input_factor, up_adapter_input_factor], axis=1)
    order = jnp.asarray(QUARTER_ORDER, jnp.int32)[quarter]
    share = lambda k, half: token_grad(
        order[k : k + 1],
        half,
        jnp.float32 if k == quarters - 1 else jnp.bfloat16,
        gate_grad,
        up_grad,
        gate_full,
        up_full,
        low,
        input_factor,
        width // quarters,
    )
    shift = lambda array, pairs: lax.ppermute(array, "tp", pairs)
    plus = lambda a, b: (a.astype(jnp.float32) + b.astype(jnp.float32)).astype(jnp.bfloat16)
    first = [share(0, half) for half in range(HALVES)]
    came = [shift(part, [(0, 1), (3, 2)]) for part in first]
    second = [share(1, half) for half in range(HALVES)]
    sums = [plus(second[half], came[half]) for half in range(HALVES)]
    from_left = [shift(part, [(0, 1), (1, 2)]) for part in sums]
    from_right = [shift(part, [(3, 2), (2, 1)]) for part in sums]
    gate_grad, up_grad, hidden = hold([gate_grad, up_grad, hidden], sums)
    third = [share(2, half) for half in range(HALVES)]
    last = [share(3, half) for half in range(HALVES)]
    hidden, gate_grad, up_grad = hold(
        [hidden, gate_grad, up_grad], third + last + [from_left[0], from_right[0]]
    )
    to_right = [
        plus(jnp.where(quarter == 2, first[half], third[half]), from_left[half])
        for half in range(HALVES)
    ]
    to_left = [
        plus(jnp.where(quarter == 1, first[half], third[half]), from_right[half])
        for half in range(HALVES)
    ]
    from_left = [shift(part, [(0, 1), (1, 2), (2, 3)]) for part in to_right]
    from_right = [shift(part, [(3, 2), (2, 1), (1, 0)]) for part in to_left]
    token_input_gradient = jnp.concatenate(
        [
            (
                last[half]
                + from_left[half].astype(jnp.float32)
                + from_right[half].astype(jnp.float32)
            ).astype(jnp.bfloat16)
            for half in range(HALVES)
        ]
    )
    down_low = matrix_product(hidden, down_adapter_input_factor).astype(jnp.bfloat16)
    narrow = gradient_scaling * jnp.concatenate(
        [
            contract_first(hidden, lows[2]),
            contract_first(gate_grad, lows[0]),
            contract_first(up_grad, lows[1]),
        ],
        axis=1,
    )
    wide = gradient_scaling * jnp.concatenate(
        [contract_first(tokens, low.astype(jnp.bfloat16)), contract_first(cotangent, down_low)],
        axis=1,
    )
    wide_rows = width // groups
    narrow_rows = hidden_size // groups
    both = jnp.concatenate(
        [
            wide.reshape(groups, wide_rows, 3 * rank),
            narrow.reshape(groups, narrow_rows, 3 * rank),
        ],
        axis=1,
    )
    both = sum_over_plane(both, cut, place)
    narrow_grads = copy_over_plane(both[wide_rows:], cut, place)
    wide_grads = both[:wide_rows]
    bit = quarters // 2
    while bit:
        parts = wide_grads.reshape(2, -1, 3 * rank)
        up = (quarter // bit) % 2
        mine = lax.dynamic_index_in_dim(parts, up, 0, keepdims=False)
        wide_grads = mine + flip(
            lax.dynamic_index_in_dim(parts, 1 - up, 0, keepdims=False), "tp", bit
        )
        bit //= 2
    return (token_input_gradient, wide_grads, narrow_grads)


def solution(mesh):
    in_specs = (
        P(("cuts", "fsdp"), None),
        P(("cuts", "fsdp"), None),
        P(("cuts", "fsdp"), "tp"),
        P(("cuts", "fsdp"), "tp"),
        P("tp", ("cuts", "fsdp")),
        P(),
        P(),
        P(None, "tp"),
        P(None, "tp"),
        P("tp", None),
        P(),
    )
    out_specs = (P(("cuts", "fsdp"), "tp"), P(("cuts", "fsdp", "tp"), None), P("tp", None))
    return jax.shard_map(
        per_device, mesh=mesh, in_specs=in_specs, out_specs=out_specs, check_vma=False
    )
```

```python
import functools
import math

import jax
import jax.numpy as jnp
from jax import lax
from jax.experimental import pallas as pl
from jax.experimental.pallas import tpu as pltpu
from jax.sharding import PartitionSpec as P

adapter_scaling = 0.5
VMEM_LIMIT = 20 * 1024 * 1024
ROW_TILE = 512
PIECES = (384, 384, 256)
HALVES = 2
QUARTER_ORDER = ((3, 2, 1, 0), (0, 3, 2, 1), (3, 0, 1, 2), (0, 1, 2, 3))


def matrix_product(left, right):
    return jnp.dot(left, right, preferred_element_type=jnp.float32)


def contract_trailing_axis(left, right):
    return lax.dot_general(
        left, right, (((1,), (1,)), ((), ())), preferred_element_type=jnp.float32
    )


def contract_first(left, right):
    return lax.dot_general(
        left, right, (((0,), (0,)), ((), ())), preferred_element_type=jnp.float32
    )


def flip(array, axis, bit):
    size = lax.axis_size(axis)
    return lax.ppermute(array, axis, [(i, i ^ bit) for i in range(size)])


def in_vmem(array):
    return pltpu.with_memory_space_constraint(array, pltpu.VMEM)


def vmem_call(kernel, scalars, arrays, ahead, results, aliases, scratch, flops, name):
    vmem = pl.BlockSpec(memory_space=pltpu.VMEM)
    first = len(scalars)
    return pl.pallas_call(
        kernel,
        in_specs=[pl.BlockSpec(memory_space=pltpu.SMEM)] * first
        + [vmem] * len(arrays)
        + [pl.BlockSpec(memory_space=pl.ANY)] * len(ahead),
        out_specs=[vmem] * len(results),
        out_shape=[pltpu.VMEM(shape, kind) for shape, kind in results],
        scratch_shapes=scratch,
        input_output_aliases={first + source: target for source, target in aliases.items()},
        compiler_params=pltpu.CompilerParams(vmem_limit_bytes=VMEM_LIMIT),
        cost_estimate=pl.CostEstimate(flops=flops, bytes_accessed=0, transcendentals=0),
        name=name,
    )(*scalars, *map(in_vmem, arrays), *ahead)


def lows_kernel(tokens, cotangent, gate_in, up_in, leave, gate_low, up_low, back_low, turned):
    for number, (left, right, out) in enumerate(
        ((tokens, gate_in, gate_low), (tokens, up_in, up_low), (cotangent, leave, back_low))
    ):
        value = matrix_product(left[...], right[...]).astype(jnp.bfloat16)
        out[...] = value
        rank = value.shape[1]
        turned[number * rank : (number + 1) * rank, :] = value.astype(jnp.float32).T.astype(
            jnp.bfloat16
        )


def low_rank_values(tokens, cotangent, gate_in, up_in, leave):
    rows, width = tokens.shape
    rank = leave.shape[1]
    return vmem_call(
        lows_kernel,
        [],
        [tokens, cotangent, gate_in, up_in, leave],
        [],
        [((rows, rank), jnp.bfloat16)] * 3 + [((3 * rank, rows), jnp.bfloat16)],
        {},
        [],
        6 * rows * width * rank,
        "low_rank_values",
    )


def forward_kernel(layout, has_before, start, position, *refs):
    (tokens, cotangent, gate_low, up_low, back_low, gate_out, up_out, down_in) = refs[:8]
    blocks = refs[8 : 8 + len(layout)]
    low_before = refs[8 + len(layout) + 5] if has_before else None
    hidden_out, gate_grad_out, up_grad_out, gate_full, up_full, low_out, down_full = refs[-7:]
    columns = blocks[0].shape[2]
    rows = max(block.shape[1] for block in blocks)
    span = slice(start, start + columns)
    for block, (mask, offset) in zip(blocks, layout):
        size = block.shape[1]
        place = pl.multiple_of(
            lax.bitwise_xor(position[0], jnp.int32(mask)) * rows + offset, size
        )
        gate_full[pl.ds(place, size), span] = block[0]
        up_full[pl.ds(place, size), span] = block[1]
        down_full[pl.ds(place, size), :] = block[2]
    tile = min(ROW_TILE, tokens.shape[0])
    for row in range(0, tokens.shape[0], tile):
        part = slice(row, row + tile)
        gate = matrix_product(tokens[part, :], gate_full[:, span])
        gate += adapter_scaling * matrix_product(gate_low[part, :], gate_out[:, span])
        up = matrix_product(tokens[part, :], up_full[:, span])
        up += adapter_scaling * matrix_product(up_low[part, :], up_out[:, span])
        hidden_grad = matrix_product(cotangent[part, :], down_full[...])
        hidden_grad += adapter_scaling * contract_trailing_axis(back_low[part, :], down_in[span, :])
        sig = 1.0 / (1.0 + jnp.exp(-gate))
        gated = gate * sig
        hidden_out[part, span] = (gated * up).astype(jnp.bfloat16)
        gate_grad = (hidden_grad * up * sig * (1.0 + gate * (1.0 - sig))).astype(jnp.bfloat16)
        up_grad = (hidden_grad * gated).astype(jnp.bfloat16)
        gate_grad_out[part, span] = gate_grad
        up_grad_out[part, span] = up_grad
        low = jnp.concatenate(
            [
                contract_trailing_axis(gate_grad, gate_out[:, span]),
                contract_trailing_axis(up_grad, up_out[:, span]),
            ],
            axis=1,
        )
        if has_before:
            low = low + low_before[part, :]
        low_out[part, :] = low


def forward_piece(start, position, tokens, cotangent, lows, factors, blocks, layout, before):
    rows, width = tokens.shape
    rank = lows[0].shape[1]
    hidden_size = factors[0].shape[1]
    columns = blocks[0].shape[2]
    arrays = [tokens, cotangent, *lows, *factors, *blocks, *before]
    return vmem_call(
        functools.partial(forward_kernel, layout, bool(before), start),
        [position],
        arrays,
        [],
        [((rows, hidden_size), jnp.bfloat16)] * 3
        + [((width, hidden_size), jnp.bfloat16)] * 2
        + [((rows, 2 * rank), jnp.float32)],
        {len(arrays) - len(before) + number: number for number in range(len(before))},
        [pltpu.VMEM((width, columns), jnp.bfloat16)],
        6 * rows * width * columns,
        "forward_piece",
    )


def token_grad_kernel(half, quarter, gate_grad, up_grad, gate, up, low, factor, *refs):
    out = refs[-1]
    rows, columns = out.shape
    part = slice(half * rows, (half + 1) * rows)
    span = pl.ds(pl.multiple_of(quarter[0] * columns, columns), columns)
    total = contract_trailing_axis(gate_grad[part, :], gate[span, :])
    total += contract_trailing_axis(up_grad[part, :], up[span, :])
    total += contract_trailing_axis(
        (adapter_scaling * low[part, :]).astype(jnp.bfloat16), factor[span, :]
    )
    out[...] = total.astype(out.dtype)


def token_grad(quarter, half, kind, arrays, columns, ahead):
    rows, hidden_size = arrays[0].shape
    return vmem_call(
        functools.partial(token_grad_kernel, half),
        [quarter],
        arrays,
        ahead,
        [((rows // HALVES, columns), kind)],
        {},
        [],
        4 * rows // HALVES * columns * hidden_size,
        "token_grad",
    )[0]


def adapter_kernel(
    scaling, tokens, cotangent, hidden, gate_grad, up_grad, low, turned, down_turned, *refs
):
    wide, narrow = refs[-2:]
    rank = down_turned.shape[0]
    back = low[...].T.astype(jnp.bfloat16)
    down_low = contract_trailing_axis(down_turned[...], hidden[...]).astype(jnp.bfloat16)
    wide[: 2 * rank, :] = scaling * matrix_product(back, tokens[...])
    wide[2 * rank :, :] = scaling * matrix_product(down_low, cotangent[...])
    narrow[:rank, :] = scaling * matrix_product(turned[2 * rank :, :], hidden[...])
    narrow[rank : 2 * rank, :] = scaling * matrix_product(turned[:rank, :], gate_grad[...])
    narrow[2 * rank :, :] = scaling * matrix_product(turned[rank : 2 * rank, :], up_grad[...])


def adapter_grads(scaling, arrays, ahead):
    rows, width = arrays[0].shape
    hidden_size = arrays[2].shape[1]
    rank = arrays[-1].shape[0]
    return vmem_call(
        functools.partial(adapter_kernel, scaling),
        [],
        arrays,
        ahead,
        [((3 * rank, width), jnp.float32), ((3 * rank, hidden_size), jnp.float32)],
        {},
        [],
        6 * rank * rows * (width + hidden_size),
        "adapter_grads",
    )


def nothing_kernel(*refs):
    pass


def hold(arrays, ahead):
    anywhere = pl.BlockSpec(memory_space=pl.ANY)
    return pl.pallas_call(
        nothing_kernel,
        in_specs=[anywhere] * (len(arrays) + len(ahead)),
        out_specs=[anywhere] * len(arrays),
        out_shape=[jax.ShapeDtypeStruct(array.shape, array.dtype) for array in arrays],
        input_output_aliases={number: number for number in range(len(arrays))},
        name="hold",
    )(*arrays, *ahead)


def single_flips(own):
    size = lax.axis_size("fsdp")
    return {1 << n: flip(own, "fsdp", 1 << n) for n in range(size.bit_length() - 1)}


def gather_blocks(own, came, ahead_first, ahead_second):
    size = lax.axis_size("fsdp")
    half = own.shape[1] // 2
    whole = {0: own, **came}
    upper, lower = {}, {}
    for mask, block in whole.items():
        upper[mask], lower[mask] = block[:, :half], block[:, half:]
    if ahead_first:
        for mask, parts in ((1, upper), (2, lower)):
            (parts[mask],) = hold([parts[mask]], ahead_first)
    for mask in range(size):
        if mask not in whole:
            high = 1 << (mask.bit_length() - 1)
            upper[mask] = flip(upper[mask ^ high], "fsdp", high)
    for mask in sorted(range(size), key=lambda m: bin(m).count("1")):
        if mask not in whole:
            low = mask & -mask
            lower[mask] = flip(lower[mask ^ low], "fsdp", low)
    blocks, layout, held = [], [], []
    for mask in range(size):
        if mask in whole:
            blocks.append(whole[mask])
            layout.append((mask, 0))
        else:
            for part, offset in ((upper[mask], 0), (lower[mask], half)):
                if ahead_second:
                    (part,) = hold([part], ahead_second)
                blocks.append(part)
                layout.append((mask, offset))
    other = [flip(block, "cuts", 1) for block in blocks]
    layout += [(mask | size, offset) for mask, offset in layout]
    return blocks + other, tuple(layout)


def sum_over_plane(parts, cut, place):
    def step(parts, up, send):
        halves = [part.shape[1] // 2 for part in parts]
        take = lambda which: [
            lax.dynamic_slice_in_dim(part, which * half, half, 1)
            for part, half in zip(parts, halves)
        ]
        came = send(jnp.concatenate(take(1 - up), axis=1))
        starts = [sum(halves[:number]) for number in range(len(halves))]
        return [
            part + came[:, start : start + half]
            for part, start, half in zip(take(up), starts, halves)
        ]

    parts = step(parts, cut, lambda array: flip(array, "cuts", 1))
    bit = lax.axis_size("fsdp") // 2
    while bit:
        parts = step(parts, (place // bit) % 2, lambda array: flip(array, "fsdp", bit))
        bit //= 2
    return parts


def copy_over_plane(rows, cut, place):
    bit = 1
    while bit < lax.axis_size("fsdp"):
        other = flip(rows, "fsdp", bit)
        up = (place // bit) % 2
        rows = jnp.where(
            up == 0, jnp.concatenate([rows, other]), jnp.concatenate([other, rows])
        )
        bit *= 2
    other = flip(rows, "cuts", 1)
    return jnp.where(cut == 0, jnp.concatenate([rows, other]), jnp.concatenate([other, rows]))


def per_device(
    tokens,
    cotangent,
    gate_frozen_matrix,
    up_frozen_matrix,
    down_frozen_matrix,
    gate_adapter_input_factor,
    up_adapter_input_factor,
    gate_adapter_output_factor,
    up_adapter_output_factor,
    down_adapter_input_factor,
    down_leave,
):
    groups = lax.axis_size(("cuts", "fsdp"))
    quarters = lax.axis_size("tp")
    cut = lax.axis_index("cuts")
    place = lax.axis_index("fsdp")
    quarter = lax.axis_index("tp")
    rows, width = tokens.shape
    hidden_size = gate_frozen_matrix.shape[1]
    rank = down_leave.shape[1]
    gradient_scaling = adapter_scaling / math.sqrt(rows * groups)
    position = lax.axis_index(("cuts", "fsdp")).astype(jnp.int32).reshape(1)

    *lows, turned = low_rank_values(
        tokens, cotangent, gate_adapter_input_factor, up_adapter_input_factor, down_leave
    )
    factors = [gate_adapter_output_factor, up_adapter_output_factor, down_adapter_input_factor]
    state = ()
    came, states = [], []
    square = lax.axis_size("fsdp") == 4
    for piece, columns in enumerate(PIECES):
        start = sum(PIECES[:piece])
        span = slice(start, start + columns)
        own = jnp.stack(
            [
                gate_frozen_matrix[:, span],
                up_frozen_matrix[:, span],
                down_frozen_matrix[span].T,
            ]
        )
        if square and piece >= 2:
            (own,) = hold([own], list(came[piece - 2].values()))
        came.append(single_flips(own))
        blocks, layout = gather_blocks(
            own,
            came[piece],
            [states[piece - 2][-1]] if square and piece >= 2 else [],
            [states[piece - 1][-1]] if square and piece >= 1 else [],
        )
        state = forward_piece(
            start, position, tokens, cotangent, lows, factors, blocks, layout, state
        )
        states.append(state)
    hidden, gate_grad, up_grad, gate_full, up_full, low = state

    input_factor = jnp.concatenate([gate_adapter_input_factor, up_adapter_input_factor], axis=1)
    order = jnp.asarray(QUARTER_ORDER, jnp.int32)[quarter]
    share = lambda k, half, *ahead: token_grad(
        order[k : k + 1],
        half,
        jnp.float32 if k == quarters - 1 else jnp.bfloat16,
        [gate_grad, up_grad, gate_full, up_full, low, input_factor],
        width // quarters,
        list(ahead),
    )
    shift = lambda array, pairs: lax.ppermute(array, "tp", pairs)
    plus = lambda a, b: (a.astype(jnp.float32) + b.astype(jnp.float32)).astype(jnp.bfloat16)
    both = range(HALVES)
    first = [share(0, half) for half in both]
    came = [shift(part, [(0, 1), (3, 2)]) for part in first]
    second = [share(1, half, *first) for half in both]
    sums = [plus(second[half], came[half]) for half in both]
    from_left = [shift(part, [(0, 1), (1, 2)]) for part in sums]
    from_right = [shift(part, [(3, 2), (2, 1)]) for part in sums]
    third = [share(2, half, *sums) for half in both]
    last = [share(3, half, *third) for half in both]
    wide, narrow = adapter_grads(
        gradient_scaling,
        [
            tokens,
            cotangent,
            hidden,
            gate_grad,
            up_grad,
            low,
            turned,
            down_adapter_input_factor.T,
        ],
        [*last, from_left[0], from_right[0]],
    )
    to_right = [
        plus(jnp.where(quarter == 2, first[half], third[half]), from_left[half]) for half in both
    ]
    to_left = [
        plus(jnp.where(quarter == 1, first[half], third[half]), from_right[half]) for half in both
    ]
    from_left = [shift(part, [(0, 1), (1, 2), (2, 3)]) for part in to_right]
    from_right = [shift(part, [(3, 2), (2, 1), (1, 0)]) for part in to_left]
    token_input_gradient = jnp.concatenate(
        [
            (
                last[half]
                + from_left[half].astype(jnp.float32)
                + from_right[half].astype(jnp.float32)
            ).astype(jnp.bfloat16)
            for half in both
        ]
    )

    wide, narrow = sum_over_plane([wide, narrow], cut, place)
    narrow_grads = copy_over_plane(narrow.T, cut, place)
    bit = quarters // 2
    while bit:
        part = wide.shape[1] // 2
        up = (quarter // bit) % 2
        mine = lax.dynamic_slice_in_dim(wide, up * part, part, 1)
        wide = mine + flip(lax.dynamic_slice_in_dim(wide, (1 - up) * part, part, 1), "tp", bit)
        bit //= 2
    return (token_input_gradient, wide.T, narrow_grads)


def solution(mesh):
    in_specs = (
        P(("cuts", "fsdp"), None),
        P(("cuts", "fsdp"), None),
        P(("cuts", "fsdp"), "tp"),
        P(("cuts", "fsdp"), "tp"),
        P("tp", ("cuts", "fsdp")),
        P(),
        P(),
        P(None, "tp"),
        P(None, "tp"),
        P("tp", None),
        P(),
    )
    out_specs = (P(("cuts", "fsdp"), "tp"), P(("cuts", "fsdp", "tp"), None), P("tp", None))
    return jax.shard_map(
        per_device, mesh=mesh, in_specs=in_specs, out_specs=out_specs, check_vma=False
    )
```

```python
import functools
import math

import jax
import jax.numpy as jnp
from jax import lax
from jax.experimental import pallas as pl
from jax.experimental.pallas import tpu as pltpu
from jax.sharding import PartitionSpec as P

adapter_scaling = 0.5
MEBIBYTE = 1024 * 1024
COST = 20
HALVES = 2
TILE = 512
STRIP = 256
QUARTER_ORDER = ((3, 2, 1, 0), (0, 3, 2, 1), (3, 0, 1, 2), (0, 1, 2, 3))


def matrix_product(left, right):
    return jnp.dot(left, right, preferred_element_type=jnp.float32)


def contract_trailing_axis(left, right):
    return lax.dot_general(
        left, right, (((1,), (1,)), ((), ())), preferred_element_type=jnp.float32
    )


def contract_first(left, right):
    return lax.dot_general(
        left, right, (((0,), (0,)), ((), ())), preferred_element_type=jnp.float32
    )


def any_plane(
    tokens,
    cotangent,
    gate_frozen_matrix,
    up_frozen_matrix,
    down_frozen_matrix,
    gate_adapter_input_factor,
    up_adapter_input_factor,
    gate_adapter_output_factor,
    up_adapter_output_factor,
    down_adapter_input_factor,
    down_leave,
):
    token_groups = lax.axis_size(("cuts", "fsdp"))
    quarters = lax.axis_size("tp")
    tp_index = lax.axis_index("tp")
    token_rows = tokens.shape[0]
    width = tokens.shape[1]
    gradient_scaling = adapter_scaling / math.sqrt(token_rows * token_groups)
    gate_adapter_hidden = matrix_product(tokens, gate_adapter_input_factor).astype(jnp.bfloat16)
    up_adapter_hidden = matrix_product(tokens, up_adapter_input_factor).astype(jnp.bfloat16)
    pieces = (
        lax.all_gather(gate_frozen_matrix, ("cuts", "fsdp"), axis=0, tiled=True),
        lax.all_gather(up_frozen_matrix, ("cuts", "fsdp"), axis=0, tiled=True),
    )
    columns = tokens
    gate_frozen_output = matrix_product(columns, pieces[0])
    up_frozen_output = matrix_product(columns, pieces[1])
    gate_preactivation = gate_frozen_output + adapter_scaling * matrix_product(
        gate_adapter_hidden, gate_adapter_output_factor
    )
    up_preactivation = up_frozen_output + adapter_scaling * matrix_product(
        up_adapter_hidden, up_adapter_output_factor
    )
    sig = jax.nn.sigmoid(gate_preactivation)
    hidden = (gate_preactivation * sig * up_preactivation).astype(jnp.bfloat16)
    down_part = matrix_product(hidden, down_adapter_input_factor)
    down_low = lax.psum(down_part.astype(jnp.bfloat16), "tp")
    backward_adapter_input = matrix_product(cotangent, down_leave).astype(jnp.bfloat16)
    columns = cotangent
    hidden_state_gradient = contract_trailing_axis(
        columns, lax.all_gather(down_frozen_matrix, ("cuts", "fsdp"), axis=1, tiled=True)
    )
    hidden_state_gradient = hidden_state_gradient + adapter_scaling * contract_trailing_axis(
        backward_adapter_input, down_adapter_input_factor
    )
    gate_output_gradient = (
        hidden_state_gradient * up_preactivation * sig * (1.0 + gate_preactivation * (1.0 - sig))
    ).astype(jnp.bfloat16)
    up_output_gradient = (hidden_state_gradient * gate_preactivation * sig).astype(jnp.bfloat16)
    gate_part = contract_trailing_axis(gate_output_gradient, gate_adapter_output_factor)
    up_part = contract_trailing_axis(up_output_gradient, up_adapter_output_factor)
    gate_sum, up_sum = lax.psum((gate_part, up_part), "tp")
    gate_backward_adapter = gate_sum.astype(jnp.bfloat16)
    up_backward_adapter = up_sum.astype(jnp.bfloat16)
    pieces = lax.all_gather(
        (gate_frozen_matrix, up_frozen_matrix), ("cuts", "fsdp"), axis=0, tiled=True
    )
    partial_value = contract_trailing_axis(
        gate_output_gradient, pieces[0]
    ) + contract_trailing_axis(up_output_gradient, pieces[1])
    frozen_path_gradient = lax.psum_scatter(partial_value, "tp", scatter_dimension=1, tiled=True)
    slice_width = width // quarters
    gate_slice = lax.dynamic_slice_in_dim(
        gate_adapter_input_factor, tp_index * slice_width, slice_width, 0
    )
    up_slice = lax.dynamic_slice_in_dim(
        up_adapter_input_factor, tp_index * slice_width, slice_width, 0
    )
    adapter_hidden_gradient = contract_trailing_axis(
        gate_backward_adapter, gate_slice
    ) + contract_trailing_axis(up_backward_adapter, up_slice)
    token_input_gradient = (
        frozen_path_gradient + adapter_scaling * adapter_hidden_gradient
    ).astype(jnp.bfloat16)
    narrow_part = gradient_scaling * jnp.concatenate(
        [
            contract_first(hidden, backward_adapter_input),
            contract_first(gate_output_gradient, gate_adapter_hidden),
            contract_first(up_output_gradient, up_adapter_hidden),
        ],
        axis=1,
    )
    narrow_grads = lax.psum(narrow_part, ("cuts", "fsdp"))
    token_side = jnp.concatenate([gate_backward_adapter, up_backward_adapter], axis=1)
    group_rows = lax.psum_scatter(
        gradient_scaling
        * jnp.concatenate(
            [contract_first(tokens, token_side), contract_first(cotangent, down_low)], axis=1
        ),
        ("cuts", "fsdp"),
        scatter_dimension=0,
        tiled=True,
    )
    fine_rows = width // (token_groups * quarters)
    wide_grads = lax.dynamic_slice_in_dim(group_rows, tp_index * fine_rows, fine_rows, 0)
    return (token_input_gradient, wide_grads, narrow_grads)


def flip(array, axis, bit):
    size = lax.axis_size(axis)
    return lax.ppermute(array, axis, [(i, i ^ bit) for i in range(size)])


def vmem_call(kernel, scalars, arrays, ahead, results, aliases, scratch, limit, flops, name):
    vmem = pl.BlockSpec(memory_space=pltpu.VMEM)
    first = len(scalars)
    return pl.pallas_call(
        kernel,
        in_specs=[pl.BlockSpec(memory_space=pltpu.SMEM)] * first
        + [vmem] * len(arrays)
        + [pl.BlockSpec(memory_space=pl.ANY)] * len(ahead),
        out_specs=[vmem] * len(results),
        out_shape=[pltpu.VMEM(shape, kind) for shape, kind in results],
        scratch_shapes=scratch,
        input_output_aliases={first + source: target for source, target in aliases.items()},
        compiler_params=pltpu.CompilerParams(vmem_limit_bytes=limit * MEBIBYTE),
        cost_estimate=pl.CostEstimate(flops=COST * flops, bytes_accessed=0, transcendentals=0),
        name=name,
    )(
        *scalars,
        *[pltpu.with_memory_space_constraint(array, pltpu.VMEM) for array in arrays],
        *ahead,
    )


def lows_kernel(tokens, cotangent, gate_in, up_in, leave, gate_low, up_low, back_low, turned):
    for number, (left, right, out) in enumerate(
        ((tokens, gate_in, gate_low), (tokens, up_in, up_low), (cotangent, leave, back_low))
    ):
        value = matrix_product(left[...], right[...]).astype(jnp.bfloat16)
        out[...] = value
        rank = value.shape[1]
        turned[number * rank : (number + 1) * rank, :] = value.astype(jnp.float32).T.astype(
            jnp.bfloat16
        )


def low_rank_values(tokens, cotangent, gate_in, up_in, leave):
    rows, width = tokens.shape
    rank = leave.shape[1]
    return vmem_call(
        lows_kernel,
        [],
        [tokens, cotangent, gate_in, up_in, leave],
        [],
        [((rows, rank), jnp.bfloat16)] * 3 + [((3 * rank, rows), jnp.bfloat16)],
        {},
        [],
        16,
        24 * rows * width * rank,
        "low_rank_values",
    )


def width_part(ref, part, position, masks, rows):
    return jnp.concatenate(
        [
            ref[part, pl.ds(pl.multiple_of(lax.bitwise_xor(position[0], mask) * rows, rows), rows)]
            for mask in masks
        ],
        axis=1,
    )


def stacked(units, which, span):
    return jnp.concatenate([unit[which, :, span] for unit in units], axis=0)


def first_kernel(masks, n_units, position, *refs):
    tokens, cotangent, gate_low, up_low, back_low, gate_out, up_out, down_in = refs[:8]
    units = refs[8 : 8 + n_units]
    sums = refs[-3:]
    rows = 2 * units[0].shape[1]
    hidden = units[0].shape[2]
    for row in range(0, tokens.shape[0], TILE):
        part = slice(row, row + TILE)
        left = width_part(tokens, part, position, masks, rows)
        back = width_part(cotangent, part, position, masks, rows)
        for column in range(0, hidden, TILE):
            span = slice(column, column + TILE)
            sums[0][part, span] = matrix_product(
                left, stacked(units, 0, span)
            ) + adapter_scaling * matrix_product(gate_low[part, :], gate_out[:, span])
            sums[1][part, span] = matrix_product(
                left, stacked(units, 1, span)
            ) + adapter_scaling * matrix_product(up_low[part, :], up_out[:, span])
            sums[2][part, span] = matrix_product(
                back, stacked(units, 2, span)
            ) + adapter_scaling * contract_trailing_axis(back_low[part, :], down_in[span, :])


def next_kernel(masks, n_units, position, *refs):
    tokens, cotangent = refs[:2]
    units = refs[2 : 2 + n_units]
    before = refs[2 + n_units : 5 + n_units]
    sums = refs[-3:]
    rows = 2 * units[0].shape[1]
    hidden = units[0].shape[2]
    for row in range(0, tokens.shape[0], TILE):
        part = slice(row, row + TILE)
        left = width_part(tokens, part, position, masks, rows)
        back = width_part(cotangent, part, position, masks, rows)
        for column in range(0, hidden, TILE):
            span = slice(column, column + TILE)
            for which in range(3):
                sums[which][part, span] = before[which][part, span] + matrix_product(
                    back if which == 2 else left, stacked(units, which, span)
                )


def last_kernel(masks, n_units, half, position, *refs):
    tokens, cotangent, gate_out, up_out = refs[:4]
    units = refs[4 : 4 + n_units]
    sums = refs[4 + n_units : 7 + n_units]
    hidden_out, gate_grad_out, up_grad_out, low_out = refs[-4:]
    rows = 2 * units[0].shape[1]
    count, hidden = hidden_out.shape
    part = slice(half * count, (half + 1) * count)
    left = width_part(tokens, part, position, masks, rows)
    back = width_part(cotangent, part, position, masks, rows)
    gate_low = up_low = 0.0
    for column in range(0, hidden, STRIP):
        span = slice(column, column + STRIP)
        gate = sums[0][part, span] + matrix_product(left, stacked(units, 0, span))
        up = sums[1][part, span] + matrix_product(left, stacked(units, 1, span))
        hidden_grad = sums[2][part, span] + matrix_product(back, stacked(units, 2, span))
        sig = 1.0 / (1.0 + jnp.exp(-gate))
        gated = gate * sig
        hidden_out[:, span] = (gated * up).astype(jnp.bfloat16)
        gate_grad = (hidden_grad * up * sig * (1.0 + gate * (1.0 - sig))).astype(jnp.bfloat16)
        up_grad = (hidden_grad * gated).astype(jnp.bfloat16)
        gate_grad_out[:, span] = gate_grad
        up_grad_out[:, span] = up_grad
        gate_low += contract_trailing_axis(gate_grad, gate_out[:, span])
        up_low += contract_trailing_axis(up_grad, up_out[:, span])
    low_out[...] = jnp.concatenate([gate_low, up_low], axis=1)


def first_sums(position, tokens, cotangent, lows, factors, masks, units):
    rows, _ = tokens.shape
    hidden = units[0].shape[2]
    return vmem_call(
        functools.partial(first_kernel, masks, len(units)),
        [position],
        [tokens, cotangent, *lows, *factors, *units],
        [],
        [((rows, hidden), jnp.float32)] * 3,
        {},
        [],
        20,
        12 * rows * hidden * units[0].shape[1] * len(units),
        "first_sums",
    )


def next_sums(position, tokens, cotangent, masks, units, before):
    rows, _ = tokens.shape
    hidden = units[0].shape[2]
    return vmem_call(
        functools.partial(next_kernel, masks, len(units)),
        [position],
        [tokens, cotangent, *units, *before],
        [],
        [((rows, hidden), jnp.float32)] * 3,
        {2 + len(units) + number: number for number in range(3)},
        [],
        20,
        12 * rows * hidden * units[0].shape[1] * len(units),
        "next_sums",
    )


def hidden_and_grads(half, position, tokens, cotangent, factors, masks, units, sums, ahead):
    rows = tokens.shape[0] // HALVES
    rank, hidden = factors[0].shape
    return vmem_call(
        functools.partial(last_kernel, masks, len(units), half),
        [position],
        [tokens, cotangent, *factors[:2], *units, *sums],
        ahead,
        [((rows, hidden), jnp.bfloat16)] * 3 + [((rows, 2 * rank), jnp.float32)],
        {},
        [],
        20,
        24 * rows * hidden * units[0].shape[1] * len(units),
        "hidden_and_grads",
    )


def token_grad_kernel(mode, n_units, quarter, place, position, gate_grad, up_grad, low, factor, *refs):
    units = refs[:n_units]
    came = refs[n_units : n_units + {"first": 0, "sum": 1, "both": 3, "last": 2}[mode]]
    gate, up = refs[-2:]
    outs = refs[-4:-2] if mode == "both" else refs[-3:-2]
    columns = outs[0].shape[1]
    half = units[0].shape[1]
    per_quarter = columns // (2 * half)
    for number, unit in enumerate(units):
        block = lax.bitwise_xor(position[0], number // 2)

        @pl.when(lax.div(block, per_quarter) == quarter[0])
        def _():
            row = lax.rem(block, per_quarter) * (2 * half) + (number % 2) * half
            row = pl.ds(pl.multiple_of(row, half), half)
            gate[row, :] = unit[0]
            up[row, :] = unit[1]

    total = contract_trailing_axis(gate_grad[...], gate[...])
    total += contract_trailing_axis(up_grad[...], up[...])
    low = (adapter_scaling * low[...]).astype(jnp.bfloat16)
    span = pl.ds(pl.multiple_of(quarter[0] * columns, columns), columns)
    total += contract_trailing_axis(low, factor[span, :])
    came = [ref[...].astype(jnp.float32) for ref in came]
    if mode == "both":
        first, left, right = came
        outs[0][...] = (jnp.where(place[0] == 2, first, total) + left).astype(jnp.bfloat16)
        outs[1][...] = (jnp.where(place[0] == 1, first, total) + right).astype(jnp.bfloat16)
    else:
        outs[0][...] = sum(came, total).astype(jnp.bfloat16)


def token_grad(mode, scalars, arrays, units, columns, came, ahead):
    rows, hidden = arrays[0].shape
    outs = vmem_call(
        functools.partial(token_grad_kernel, mode, len(units)),
        scalars,
        [*arrays, *units, *came],
        ahead,
        [((rows, columns), jnp.bfloat16)] * (2 if mode == "both" else 1),
        {},
        [pltpu.VMEM((columns, hidden), jnp.bfloat16)] * 2,
        16,
        8 * rows * columns * hidden,
        "token_grad",
    )
    return outs if mode == "both" else outs[0]


def adapter_kernel(scaling, *refs):
    hidden, gate_grad, up_grad, low = (
        refs[number * HALVES : (number + 1) * HALVES] for number in range(4)
    )
    tokens, cotangent, turned, down_turned = refs[4 * HALVES : 4 * HALVES + 4]
    wide, narrow = refs[-2:]
    rank = down_turned.shape[0]
    rows = hidden[0].shape[0]
    parts = [slice(half * rows, (half + 1) * rows) for half in range(HALVES)]
    wide[: 2 * rank, :] = scaling * sum(
        matrix_product(low[half][...].T.astype(jnp.bfloat16), tokens[part, :])
        for half, part in enumerate(parts)
    )
    wide[2 * rank :, :] = scaling * sum(
        matrix_product(
            contract_trailing_axis(down_turned[...], hidden[half][...]).astype(jnp.bfloat16),
            cotangent[part, :],
        )
        for half, part in enumerate(parts)
    )
    for number, arrays in enumerate((hidden, gate_grad, up_grad)):
        source = (2, 0, 1)[number]
        narrow[number * rank : (number + 1) * rank, :] = scaling * sum(
            matrix_product(turned[source * rank : (source + 1) * rank, part], arrays[half][...])
            for half, part in enumerate(parts)
        )


def adapter_grads(scaling, arrays, ahead):
    rows, width = arrays[-4].shape
    rank, hidden = arrays[-1].shape
    return vmem_call(
        functools.partial(adapter_kernel, scaling),
        [],
        arrays,
        ahead,
        [((3 * rank, width), jnp.float32), ((3 * rank, hidden), jnp.float32)],
        {},
        [],
        20,
        24 * rank * rows * (width + hidden),
        "adapter_grads",
    )


def sum_over_plane(parts, cut, place):
    def step(parts, up, send):
        halves = [part.shape[1] // 2 for part in parts]
        take = lambda which: [
            lax.dynamic_slice_in_dim(part, which * half, half, 1)
            for part, half in zip(parts, halves)
        ]
        came = send(jnp.concatenate(take(1 - up), axis=1))
        starts = [sum(halves[:number]) for number in range(len(halves))]
        return [
            part + came[:, start : start + half]
            for part, start, half in zip(take(up), starts, halves)
        ]

    parts = step(parts, cut, lambda array: flip(array, "cuts", 1))
    bit = lax.axis_size("fsdp") // 2
    while bit:
        parts = step(parts, (place // bit) % 2, lambda array: flip(array, "fsdp", bit))
        bit //= 2
    return parts


def copy_over_plane(rows, cut, place):
    bit = 1
    while bit < lax.axis_size("fsdp"):
        other = flip(rows, "fsdp", bit)
        up = (place // bit) % 2
        rows = jnp.where(
            up == 0, jnp.concatenate([rows, other]), jnp.concatenate([other, rows])
        )
        bit *= 2
    other = flip(rows, "cuts", 1)
    return jnp.where(cut == 0, jnp.concatenate([rows, other]), jnp.concatenate([other, rows]))


def square_plane(
    tokens,
    cotangent,
    gate_frozen_matrix,
    up_frozen_matrix,
    down_frozen_matrix,
    gate_adapter_input_factor,
    up_adapter_input_factor,
    gate_adapter_output_factor,
    up_adapter_output_factor,
    down_adapter_input_factor,
    down_leave,
):
    groups = lax.axis_size(("cuts", "fsdp"))
    quarters = lax.axis_size("tp")
    cut = lax.axis_index("cuts")
    place = lax.axis_index("fsdp")
    quarter = lax.axis_index("tp")
    rows, width = tokens.shape
    gradient_scaling = adapter_scaling / math.sqrt(rows * groups)
    position = lax.axis_index(("cuts", "fsdp")).astype(jnp.int32).reshape(1)
    factors = [gate_adapter_output_factor, up_adapter_output_factor, down_adapter_input_factor]
    half_rows = gate_frozen_matrix.shape[0] // 2

    units = {}
    for half in range(2):
        span = slice(half * half_rows, (half + 1) * half_rows)
        units[0, half] = jnp.stack(
            [gate_frozen_matrix[span], up_frozen_matrix[span], down_frozen_matrix[:, span].T]
        )
    units[1, 0] = flip(units[0, 0], "fsdp", 1)
    units[2, 1] = flip(units[0, 1], "fsdp", 2)
    units[1, 1] = flip(units[0, 1], "fsdp", 1)
    units[2, 0] = flip(units[0, 0], "fsdp", 2)
    units[3, 0] = flip(units[1, 0], "fsdp", 2)
    units[3, 1] = flip(units[2, 1], "fsdp", 1)
    for mask in range(4):
        for half in range(2):
            units[mask | 4, half] = flip(units[mask, half], "cuts", 1)
    pick = lambda masks: [units[mask, half] for mask in masks for half in range(2)]

    *lows, turned = low_rank_values(
        tokens, cotangent, gate_adapter_input_factor, up_adapter_input_factor, down_leave
    )
    sums = first_sums(position, tokens, cotangent, lows, factors, (0, 4), pick((0, 4)))
    sums = next_sums(position, tokens, cotangent, (1, 2, 5, 6), pick((1, 2, 5, 6)), sums)

    input_factor = jnp.concatenate([gate_adapter_input_factor, up_adapter_input_factor], axis=1)
    order = jnp.asarray(QUARTER_ORDER, jnp.int32)[quarter]
    shift = lambda array, pairs: lax.ppermute(array, "tp", pairs)
    states, first = [], []
    share = lambda k, half, mode, came=(), ahead=(): token_grad(
        mode,
        [order[k : k + 1], quarter.astype(jnp.int32).reshape(1), position],
        [states[half][1], states[half][2], states[half][3], input_factor],
        pick(range(8)),
        width // quarters,
        came,
        ahead,
    )
    both = range(HALVES)
    for half in both:
        states.append(
            hidden_and_grads(
                half,
                position,
                tokens,
                cotangent,
                factors,
                (3, 7),
                pick((3, 7)),
                sums,
                first[:],
            )
        )
        first.append(share(0, half, "first"))
    came = [shift(part, [(0, 1), (3, 2)]) for part in first]
    partial = [share(1, half, "sum", [came[half]], first[1:]) for half in both]
    from_left = [shift(part, [(0, 1), (1, 2)]) for part in partial]
    from_right = [shift(part, [(3, 2), (2, 1)]) for part in partial]
    partial = [
        share(2, half, "both", [first[half], from_left[half], from_right[half]], partial[1:])
        for half in both
    ]
    from_left = [shift(part[0], [(0, 1), (1, 2), (2, 3)]) for part in partial]
    from_right = [shift(part[1], [(3, 2), (2, 1), (1, 0)]) for part in partial]

    hidden, gate_grad, up_grad, low = zip(*states)
    wide, narrow = adapter_grads(
        gradient_scaling,
        [
            *hidden,
            *gate_grad,
            *up_grad,
            *low,
            tokens,
            cotangent,
            turned,
            down_adapter_input_factor.T,
        ],
        [came[1], *first],
    )
    wide, narrow = sum_over_plane([wide, narrow], cut, place)
    narrow_grads = copy_over_plane(narrow.T, cut, place)
    bit = quarters // 2
    while bit:
        part = wide.shape[1] // 2
        up = (quarter // bit) % 2
        mine = lax.dynamic_slice_in_dim(wide, up * part, part, 1)
        wide = mine + flip(lax.dynamic_slice_in_dim(wide, (1 - up) * part, part, 1), "tp", bit)
        bit //= 2
    wide_grads = wide.T

    token_input_gradient = jnp.concatenate(
        [
            share(
                3,
                half,
                "last",
                [from_left[half], from_right[half]],
                [*partial[1], wide_grads, narrow_grads] if half else partial[1],
            )
            for half in both
        ]
    )
    return (token_input_gradient, wide_grads, narrow_grads)


def per_device(*arrays):
    sizes = [lax.axis_size(axis) for axis in ("cuts", "fsdp", "tp")]
    return (square_plane if sizes == [2, 4, 4] else any_plane)(*arrays)


def solution(mesh):
    in_specs = (
        P(("cuts", "fsdp"), None),
        P(("cuts", "fsdp"), None),
        P(("cuts", "fsdp"), "tp"),
        P(("cuts", "fsdp"), "tp"),
        P("tp", ("cuts", "fsdp")),
        P(),
        P(),
        P(None, "tp"),
        P(None, "tp"),
        P("tp", None),
        P(),
    )
    out_specs = (P(("cuts", "fsdp"), "tp"), P(("cuts", "fsdp", "tp"), None), P("tp", None))
    return jax.shard_map(
        per_device, mesh=mesh, in_specs=in_specs, out_specs=out_specs, check_vma=False
    )
```

```python
import functools
import math

import jax
import jax.numpy as jnp
from jax import lax
from jax.experimental import pallas as pl
from jax.experimental.pallas import tpu as pltpu
from jax.sharding import PartitionSpec as P

adapter_scaling = 0.5
MEBIBYTE = 1024 * 1024
COST = 20
HALVES = 2
LIMITS = {"first": 14, "next": 10, "last": 18, "token": 8, "adapter": 12, "small": 4}
TILE = 512
STRIP = 256
QUARTER_ORDER = ((3, 2, 1, 0), (0, 3, 2, 1), (3, 0, 1, 2), (0, 1, 2, 3))


def matrix_product(left, right):
    return jnp.dot(left, right, preferred_element_type=jnp.float32)


def contract_trailing_axis(left, right):
    return lax.dot_general(
        left, right, (((1,), (1,)), ((), ())), preferred_element_type=jnp.float32
    )


def contract_first(left, right):
    return lax.dot_general(
        left, right, (((0,), (0,)), ((), ())), preferred_element_type=jnp.float32
    )


def any_plane(
    tokens,
    cotangent,
    gate_frozen_matrix,
    up_frozen_matrix,
    down_frozen_matrix,
    gate_adapter_input_factor,
    up_adapter_input_factor,
    gate_adapter_output_factor,
    up_adapter_output_factor,
    down_adapter_input_factor,
    down_leave,
):
    token_groups = lax.axis_size(("cuts", "fsdp"))
    quarters = lax.axis_size("tp")
    tp_index = lax.axis_index("tp")
    token_rows = tokens.shape[0]
    width = tokens.shape[1]
    gradient_scaling = adapter_scaling / math.sqrt(token_rows * token_groups)
    gate_adapter_hidden = matrix_product(tokens, gate_adapter_input_factor).astype(jnp.bfloat16)
    up_adapter_hidden = matrix_product(tokens, up_adapter_input_factor).astype(jnp.bfloat16)
    pieces = (
        lax.all_gather(gate_frozen_matrix, ("cuts", "fsdp"), axis=0, tiled=True),
        lax.all_gather(up_frozen_matrix, ("cuts", "fsdp"), axis=0, tiled=True),
    )
    columns = tokens
    gate_frozen_output = matrix_product(columns, pieces[0])
    up_frozen_output = matrix_product(columns, pieces[1])
    gate_preactivation = gate_frozen_output + adapter_scaling * matrix_product(
        gate_adapter_hidden, gate_adapter_output_factor
    )
    up_preactivation = up_frozen_output + adapter_scaling * matrix_product(
        up_adapter_hidden, up_adapter_output_factor
    )
    sig = jax.nn.sigmoid(gate_preactivation)
    hidden = (gate_preactivation * sig * up_preactivation).astype(jnp.bfloat16)
    down_part = matrix_product(hidden, down_adapter_input_factor)
    down_low = lax.psum(down_part.astype(jnp.bfloat16), "tp")
    backward_adapter_input = matrix_product(cotangent, down_leave).astype(jnp.bfloat16)
    columns = cotangent
    hidden_state_gradient = contract_trailing_axis(
        columns, lax.all_gather(down_frozen_matrix, ("cuts", "fsdp"), axis=1, tiled=True)
    )
    hidden_state_gradient = hidden_state_gradient + adapter_scaling * contract_trailing_axis(
        backward_adapter_input, down_adapter_input_factor
    )
    gate_output_gradient = (
        hidden_state_gradient * up_preactivation * sig * (1.0 + gate_preactivation * (1.0 - sig))
    ).astype(jnp.bfloat16)
    up_output_gradient = (hidden_state_gradient * gate_preactivation * sig).astype(jnp.bfloat16)
    gate_part = contract_trailing_axis(gate_output_gradient, gate_adapter_output_factor)
    up_part = contract_trailing_axis(up_output_gradient, up_adapter_output_factor)
    gate_sum, up_sum = lax.psum((gate_part, up_part), "tp")
    gate_backward_adapter = gate_sum.astype(jnp.bfloat16)
    up_backward_adapter = up_sum.astype(jnp.bfloat16)
    pieces = lax.all_gather(
        (gate_frozen_matrix, up_frozen_matrix), ("cuts", "fsdp"), axis=0, tiled=True
    )
    partial_value = contract_trailing_axis(
        gate_output_gradient, pieces[0]
    ) + contract_trailing_axis(up_output_gradient, pieces[1])
    frozen_path_gradient = lax.psum_scatter(partial_value, "tp", scatter_dimension=1, tiled=True)
    slice_width = width // quarters
    gate_slice = lax.dynamic_slice_in_dim(
        gate_adapter_input_factor, tp_index * slice_width, slice_width, 0
    )
    up_slice = lax.dynamic_slice_in_dim(
        up_adapter_input_factor, tp_index * slice_width, slice_width, 0
    )
    adapter_hidden_gradient = contract_trailing_axis(
        gate_backward_adapter, gate_slice
    ) + contract_trailing_axis(up_backward_adapter, up_slice)
    token_input_gradient = (
        frozen_path_gradient + adapter_scaling * adapter_hidden_gradient
    ).astype(jnp.bfloat16)
    narrow_part = gradient_scaling * jnp.concatenate(
        [
            contract_first(hidden, backward_adapter_input),
            contract_first(gate_output_gradient, gate_adapter_hidden),
            contract_first(up_output_gradient, up_adapter_hidden),
        ],
        axis=1,
    )
    narrow_grads = lax.psum(narrow_part, ("cuts", "fsdp"))
    token_side = jnp.concatenate([gate_backward_adapter, up_backward_adapter], axis=1)
    group_rows = lax.psum_scatter(
        gradient_scaling
        * jnp.concatenate(
            [contract_first(tokens, token_side), contract_first(cotangent, down_low)], axis=1
        ),
        ("cuts", "fsdp"),
        scatter_dimension=0,
        tiled=True,
    )
    fine_rows = width // (token_groups * quarters)
    wide_grads = lax.dynamic_slice_in_dim(group_rows, tp_index * fine_rows, fine_rows, 0)
    return (token_input_gradient, wide_grads, narrow_grads)


def flip(array, axis, bit):
    size = lax.axis_size(axis)
    return lax.ppermute(array, axis, [(i, i ^ bit) for i in range(size)])


def vmem_call(kernel, scalars, arrays, ahead, results, aliases, scratch, limit, flops, name):
    vmem = pl.BlockSpec(memory_space=pltpu.VMEM)
    first = len(scalars)
    return pl.pallas_call(
        kernel,
        in_specs=[pl.BlockSpec(memory_space=pltpu.SMEM)] * first
        + [vmem] * len(arrays)
        + [pl.BlockSpec(memory_space=pl.ANY)] * len(ahead),
        out_specs=[vmem] * len(results),
        out_shape=[pltpu.VMEM(shape, kind) for shape, kind in results],
        scratch_shapes=scratch,
        input_output_aliases={first + source: target for source, target in aliases.items()},
        compiler_params=pltpu.CompilerParams(vmem_limit_bytes=limit * MEBIBYTE),
        cost_estimate=pl.CostEstimate(flops=COST * flops, bytes_accessed=0, transcendentals=0),
        name=name,
    )(
        *scalars,
        *[pltpu.with_memory_space_constraint(array, pltpu.VMEM) for array in arrays],
        *ahead,
    )


def width_part(ref, part, here, masks, rows):
    return jnp.concatenate(
        [
            ref[part, pl.ds(pl.multiple_of(lax.bitwise_xor(here[0], mask) * rows, rows), rows)]
            for mask in masks
        ],
        axis=1,
    )


def stacked(units, which, span):
    return jnp.concatenate([unit[which, :, span] for unit in units], axis=0)


def put_in_place(units, here, masks, gate_full, up_full):
    half = units[0].shape[1]
    for number, unit in enumerate(units):
        block = lax.bitwise_xor(here[0], masks[number // 2])
        row = pl.ds(pl.multiple_of((2 * block + number % 2) * half, half), half)
        gate_full[row, :] = unit[0]
        up_full[row, :] = unit[1]


def first_kernel(masks, n_units, here, *refs):
    tokens, cotangent, gate_in, up_in, leave, gate_out, up_out, down_in = refs[:8]
    units = refs[8 : 8 + n_units]
    sums, (turned, gate_full, up_full) = refs[-9:-3], refs[-3:]
    rows = 2 * units[0].shape[1]
    hidden = units[0].shape[2]
    rank = leave.shape[0]
    put_in_place(units, here, masks, gate_full, up_full)
    tile = tokens.shape[0] // HALVES
    for half in range(HALVES):
        part = slice(half * tile, (half + 1) * tile)
        lows = []
        for number, (ref, factor) in enumerate(
            ((tokens, gate_in), (tokens, up_in), (cotangent, leave))
        ):
            low = contract_trailing_axis(ref[part, :], factor[...]).astype(jnp.bfloat16)
            turned[number * rank : (number + 1) * rank, part] = low.astype(jnp.float32).T.astype(
                jnp.bfloat16
            )
            lows.append(low)
        left = width_part(tokens, part, here, masks, rows)
        back = width_part(cotangent, part, here, masks, rows)
        for column in range(0, hidden, TILE):
            span = slice(column, column + TILE)
            for which, factor in enumerate((gate_out, up_out, down_in)):
                sums[3 * half + which][:, span] = matrix_product(
                    back if which == 2 else left, stacked(units, which, span)
                ) + adapter_scaling * matrix_product(lows[which], factor[:, span])


def next_kernel(masks, n_units, here, *refs):
    tokens, cotangent = refs[:2]
    units = refs[2 : 2 + n_units]
    before = refs[2 + n_units : 8 + n_units]
    sums, (gate_full, up_full) = refs[-8:-2], refs[-2:]
    rows = 2 * units[0].shape[1]
    hidden = units[0].shape[2]
    put_in_place(units, here, masks, gate_full, up_full)
    tile = tokens.shape[0] // HALVES
    for half in range(HALVES):
        part = slice(half * tile, (half + 1) * tile)
        left = width_part(tokens, part, here, masks, rows)
        back = width_part(cotangent, part, here, masks, rows)
        for column in range(0, hidden, TILE):
            span = slice(column, column + TILE)
            for which in range(3):
                number = 3 * half + which
                sums[number][:, span] = before[number][:, span] + matrix_product(
                    back if which == 2 else left, stacked(units, which, span)
                )


def last_kernel(masks, n_units, half, n_full, here, *refs):
    tokens, cotangent, gate_out, up_out = refs[:4]
    units = refs[4 : 4 + n_units]
    sums = refs[4 + n_units : 7 + n_units]
    hidden_out, gate_grad_out, up_grad_out, low_out = refs[len(refs) - 4 - n_full :][:4]
    if n_full:
        put_in_place(units, here, masks, *refs[-2:])
    rows = 2 * units[0].shape[1]
    count, hidden = hidden_out.shape
    part = slice(half * count, (half + 1) * count)
    left = width_part(tokens, part, here, masks, rows)
    back = width_part(cotangent, part, here, masks, rows)
    gate_low = up_low = 0.0
    for column in range(0, hidden, STRIP):
        span = slice(column, column + STRIP)
        gate = sums[0][:, span] + matrix_product(left, stacked(units, 0, span))
        up = sums[1][:, span] + matrix_product(left, stacked(units, 1, span))
        hidden_grad = sums[2][:, span] + matrix_product(back, stacked(units, 2, span))
        sig = 1.0 / (1.0 + jnp.exp(-gate))
        gated = gate * sig
        hidden_out[:, span] = (gated * up).astype(jnp.bfloat16)
        gate_grad = (hidden_grad * up * sig * (1.0 + gate * (1.0 - sig))).astype(jnp.bfloat16)
        up_grad = (hidden_grad * gated).astype(jnp.bfloat16)
        gate_grad_out[:, span] = gate_grad
        up_grad_out[:, span] = up_grad
        gate_low += contract_trailing_axis(gate_grad, gate_out[:, span])
        up_low += contract_trailing_axis(up_grad, up_out[:, span])
    low_out[...] = jnp.concatenate([gate_low, up_low], axis=1)


def sums_and_full(rows, width, hidden):
    return [((rows // HALVES, hidden), jnp.float32)] * (3 * HALVES), [
        ((width, hidden), jnp.bfloat16)
    ] * 2


def first_sums(here, tokens, cotangent, factors, masks, units):
    rows, width = tokens.shape
    hidden = units[0].shape[2]
    sums, full = sums_and_full(rows, width, hidden)
    rank = factors[0].shape[0]
    outs = vmem_call(
        functools.partial(first_kernel, masks, len(units)),
        [here],
        [tokens, cotangent, *factors, *units],
        [],
        [*sums, ((3 * rank, rows), jnp.bfloat16), *full],
        {},
        [],
        LIMITS["first"],
        12 * rows * hidden * units[0].shape[1] * len(units),
        "first_sums",
    )
    return outs[: len(sums)], outs[len(sums)], outs[len(sums) + 1 :]


def next_sums(here, tokens, cotangent, masks, units, before, full):
    rows, width = tokens.shape
    hidden = units[0].shape[2]
    sums, shapes = sums_and_full(rows, width, hidden)
    first = 2 + len(units)
    outs = vmem_call(
        functools.partial(next_kernel, masks, len(units)),
        [here],
        [tokens, cotangent, *units, *before, *full],
        [],
        [*sums, *shapes],
        {first + number: number for number in range(len(sums) + 2)},
        [],
        LIMITS["next"],
        12 * rows * hidden * units[0].shape[1] * len(units),
        "next_sums",
    )
    return outs[: len(sums)], outs[len(sums) :]


def hidden_and_grads(half, here, tokens, cotangent, factors, masks, units, sums, full, ahead):
    rows = tokens.shape[0] // HALVES
    rank, hidden = factors[0].shape
    arrays = [tokens, cotangent, *factors, *units, *sums[3 * half : 3 * half + 3]]
    outs = vmem_call(
        functools.partial(last_kernel, masks, len(units), half, len(full)),
        [here],
        [*arrays, *full],
        ahead,
        [((rows, hidden), jnp.bfloat16)] * 3
        + [((rows, 2 * rank), jnp.float32)]
        + [(array.shape, array.dtype) for array in full],
        {len(arrays) + number: 4 + number for number in range(len(full))},
        [],
        LIMITS["last"],
        24 * rows * hidden * units[0].shape[1] * len(units),
        "hidden_and_grads",
    )
    return outs[:4], outs[4:]


def token_grad_kernel(mode, step, here, gate_grad, up_grad, low, factor, gate, up, *refs):
    came = refs[: {"first": 0, "sum": 1, "both": 3, "last": 2}[mode]]
    outs = refs[-2:] if mode == "both" else refs[-1:]
    columns = outs[0].shape[1]
    quarter = sum(
        jnp.where(here[1] == place, order[step], 0) for place, order in enumerate(QUARTER_ORDER)
    )
    span = pl.ds(pl.multiple_of(quarter * columns, columns), columns)
    total = contract_trailing_axis(gate_grad[...], gate[span, :])
    total += contract_trailing_axis(up_grad[...], up[span, :])
    total += matrix_product((adapter_scaling * low[...]).astype(jnp.bfloat16), factor[:, span])
    came = [ref[...].astype(jnp.float32) for ref in came]
    if mode == "both":
        first, left, right = came
        outs[0][...] = (jnp.where(here[1] == 2, first, total) + left).astype(jnp.bfloat16)
        outs[1][...] = (jnp.where(here[1] == 1, first, total) + right).astype(jnp.bfloat16)
    else:
        outs[0][...] = sum(came, total).astype(jnp.bfloat16)


def token_grad(mode, step, here, arrays, columns, came, ahead):
    rows, hidden = arrays[0].shape
    outs = vmem_call(
        functools.partial(token_grad_kernel, mode, step),
        [here],
        [*arrays, *came],
        ahead,
        [((rows, columns), jnp.bfloat16)] * (2 if mode == "both" else 1),
        {},
        [],
        LIMITS["token"],
        8 * rows * columns * hidden,
        "token_grad",
    )
    return outs if mode == "both" else outs[0]


def adapter_kernel(scaling, here, *refs):
    hidden, gate_grad, up_grad, low = (
        refs[number * HALVES : (number + 1) * HALVES] for number in range(4)
    )
    tokens, cotangent, turned, down_in = refs[4 * HALVES : 4 * HALVES + 4]
    keep, send, wide, narrow = refs[-4:]
    rank = down_in.shape[0]
    rows = hidden[0].shape[0]
    parts = [slice(half * rows, (half + 1) * rows) for half in range(HALVES)]
    wide[: 2 * rank, :] = scaling * sum(
        matrix_product(low[half][...].T.astype(jnp.bfloat16), tokens[part, :])
        for half, part in enumerate(parts)
    )
    wide[2 * rank :, :] = scaling * sum(
        matrix_product(
            contract_trailing_axis(down_in[...], hidden[half][...]).astype(jnp.bfloat16),
            cotangent[part, :],
        )
        for half, part in enumerate(parts)
    )
    for number, arrays in enumerate((hidden, gate_grad, up_grad)):
        source = (2, 0, 1)[number]
        narrow[number * rank : (number + 1) * rank, :] = scaling * sum(
            matrix_product(turned[source * rank : (source + 1) * rank, part], arrays[half][...])
            for half, part in enumerate(parts)
        )
    groups = 2 * keep.shape[0]
    wide_columns, narrow_columns = wide.shape[1] // groups, narrow.shape[1] // groups
    for mask in range(groups):
        out = (keep if mask < groups // 2 else send).at[mask % (groups // 2)]
        block = lax.bitwise_xor(here[0], mask)
        out[:, :wide_columns] = wide[
            :, pl.ds(pl.multiple_of(block * wide_columns, wide_columns), wide_columns)
        ]
        out[:, wide_columns:] = narrow[
            :, pl.ds(pl.multiple_of(block * narrow_columns, narrow_columns), narrow_columns)
        ]


def adapter_grads(scaling, here, groups, arrays, ahead):
    rows, width = arrays[-4].shape
    rank, hidden = arrays[-1].shape
    return vmem_call(
        functools.partial(adapter_kernel, scaling),
        [here],
        arrays,
        ahead,
        [((groups // 2, 3 * rank, (width + hidden) // groups), jnp.float32)] * 2,
        {},
        [pltpu.VMEM((3 * rank, width), jnp.float32), pltpu.VMEM((3 * rank, hidden), jnp.float32)],
        LIMITS["adapter"],
        24 * rank * rows * (width + hidden),
        "adapter_grads",
    )


def halve_kernel(here, keep, came, *outs):
    count = keep.shape[0] // len(outs)
    for number, out in enumerate(outs):
        span = slice(number * count, (number + 1) * count)
        out[...] = keep[span] + came[span]


def halve(here, keep, came, parts=2):
    return vmem_call(
        halve_kernel,
        [here],
        [keep, came],
        [],
        [((keep.shape[0] // parts, *keep.shape[1:]), keep.dtype)] * parts,
        {},
        [],
        LIMITS["small"],
        500 * MEBIBYTE,
        "halve",
    )


def turn_kernel(wide_columns, here, kept, came, narrow, keep, send, wide):
    total = kept[0] + came[0]
    narrow[...] = total[:, wide_columns:].T
    wide[...] = total[:, :wide_columns].T
    rows = keep.shape[1]
    for mask in range(4):
        block = pl.ds(pl.multiple_of(lax.bitwise_xor(here[1], mask) * rows, rows), rows)
        (keep if mask < 2 else send)[mask % 2] = wide[block, :]


def turn(here, keep, came, wide_columns):
    _, rows, columns = keep.shape
    return vmem_call(
        functools.partial(turn_kernel, wide_columns),
        [here],
        [keep, came],
        [],
        [((columns - wide_columns, rows), keep.dtype)]
        + [((2, wide_columns // 4, rows), keep.dtype)] * 2,
        {},
        [pltpu.VMEM((wide_columns, rows), keep.dtype)],
        LIMITS["small"],
        500 * MEBIBYTE,
        "turn",
    )


def whole_kernel(here, near, far, out):
    rows = near.shape[1]
    for number in range(2 * near.shape[0]):
        ref = near if number < near.shape[0] else far
        block = lax.bitwise_xor(here[0], number) * rows
        out[pl.ds(pl.multiple_of(block, rows), rows), :] = ref[number % near.shape[0]]


def whole(here, near, far):
    count, rows, columns = near.shape
    return vmem_call(
        whole_kernel,
        [here],
        [near, far],
        [],
        [((2 * count * rows, columns), near.dtype)],
        {},
        [],
        LIMITS["small"],
        500 * MEBIBYTE,
        "whole",
    )[0]


def square_plane(
    tokens,
    cotangent,
    gate_frozen_matrix,
    up_frozen_matrix,
    down_frozen_matrix,
    gate_adapter_input_factor,
    up_adapter_input_factor,
    gate_adapter_output_factor,
    up_adapter_output_factor,
    down_adapter_input_factor,
    down_leave,
):
    groups = lax.axis_size(("cuts", "fsdp"))
    quarters = lax.axis_size("tp")
    rows, width = tokens.shape
    gradient_scaling = adapter_scaling / math.sqrt(rows * groups)
    here = jnp.stack([lax.axis_index(("cuts", "fsdp")), lax.axis_index("tp")]).astype(jnp.int32)
    gate_in, up_in, leave, down_in = (
        array.T
        for array in (
            gate_adapter_input_factor,
            up_adapter_input_factor,
            down_leave,
            down_adapter_input_factor,
        )
    )
    gate_out, up_out = gate_adapter_output_factor, up_adapter_output_factor
    half_rows = gate_frozen_matrix.shape[0] // 2

    units = {}
    for half in range(2):
        span = slice(half * half_rows, (half + 1) * half_rows)
        units[0, half] = jnp.stack(
            [gate_frozen_matrix[span], up_frozen_matrix[span], down_frozen_matrix[:, span].T]
        )
    units[1, 0] = flip(units[0, 0], "fsdp", 1)
    units[2, 1] = flip(units[0, 1], "fsdp", 2)
    units[1, 1] = flip(units[0, 1], "fsdp", 1)
    units[2, 0] = flip(units[0, 0], "fsdp", 2)
    units[3, 0] = flip(units[1, 0], "fsdp", 2)
    units[3, 1] = flip(units[2, 1], "fsdp", 1)
    for mask in range(4):
        for half in range(2):
            units[mask | 4, half] = flip(units[mask, half], "cuts", 1)
    pick = lambda masks: [units[mask, half] for mask in masks for half in range(2)]

    sums, turned, full = first_sums(
        here,
        tokens,
        cotangent,
        [gate_in, up_in, leave, gate_out, up_out, down_in],
        (0, 4),
        pick((0, 4)),
    )
    masks = (1, 2, 5, 6)
    sums, full = next_sums(here, tokens, cotangent, masks, pick(masks), sums, full)

    factor = jnp.concatenate([gate_in, up_in])
    shift = lambda array, pairs: lax.ppermute(array, "tp", pairs)
    states, first = [], []
    share = lambda step, half, mode, came=(), ahead=(): token_grad(
        mode,
        step,
        here,
        [*states[half][1:], factor, *full],
        width // quarters,
        came,
        ahead,
    )
    both = range(HALVES)
    for half in both:
        state, placed = hidden_and_grads(
            half,
            here,
            tokens,
            cotangent,
            [gate_out, up_out],
            (3, 7),
            pick((3, 7)),
            sums,
            [] if half else full,
            first[:],
        )
        full = placed or full
        states.append(state)
        first.append(share(0, half, "first"))
    came = [shift(part, [(0, 1), (3, 2)]) for part in first]
    partial = [share(1, half, "sum", [came[half]], first[1:]) for half in both]
    from_left = [shift(part, [(0, 1), (1, 2)]) for part in partial]
    from_right = [shift(part, [(3, 2), (2, 1)]) for part in partial]
    partial = [
        share(2, half, "both", [first[half], from_left[half], from_right[half]], partial[1:])
        for half in both
    ]
    from_left = [shift(part[0], [(0, 1), (1, 2), (2, 3)]) for part in partial]
    from_right = [shift(part[1], [(3, 2), (2, 1), (1, 0)]) for part in partial]

    keep, send = adapter_grads(
        gradient_scaling,
        here,
        groups,
        [
            *[state[number] for number in range(4) for state in states],
            tokens,
            cotangent,
            turned,
            down_in,
        ],
        [came[1], *first],
    )
    keep, send = halve(here, keep, flip(send, "cuts", 1))
    keep, send = halve(here, keep, flip(send, "fsdp", 2))
    narrow, keep, send = turn(here, keep, flip(send, "fsdp", 1), width // groups)
    keep, send = halve(here, keep, flip(send, "tp", 2))
    wide_grads = halve(here, keep, flip(send, "tp", 1), 1)[0][0]
    near = jnp.stack([narrow, flip(narrow, "fsdp", 1)])
    near = jnp.concatenate([near, flip(near, "fsdp", 2)])
    narrow_grads = whole(here, near, flip(near, "cuts", 1))

    token_input_gradient = jnp.concatenate(
        [
            share(
                3,
                half,
                "last",
                [from_left[half], from_right[half]],
                [*partial[1], wide_grads, narrow_grads] if half else partial[1],
            )
            for half in both
        ]
    )
    return (token_input_gradient, wide_grads, narrow_grads)


def per_device(*arrays):
    sizes = [lax.axis_size(axis) for axis in ("cuts", "fsdp", "tp")]
    return (square_plane if sizes == [2, 4, 4] else any_plane)(*arrays)


def solution(mesh):
    in_specs = (
        P(("cuts", "fsdp"), None),
        P(("cuts", "fsdp"), None),
        P(("cuts", "fsdp"), "tp"),
        P(("cuts", "fsdp"), "tp"),
        P("tp", ("cuts", "fsdp")),
        P(),
        P(),
        P(None, "tp"),
        P(None, "tp"),
        P("tp", None),
        P(),
    )
    out_specs = (P(("cuts", "fsdp"), "tp"), P(("cuts", "fsdp", "tp"), None), P("tp", None))
    return jax.shard_map(
        per_device, mesh=mesh, in_specs=in_specs, out_specs=out_specs, check_vma=False
    )
```

```python
import functools
import math

import jax
import jax.numpy as jnp
from jax import lax
from jax.experimental import pallas as pl
from jax.experimental.pallas import tpu as pltpu
from jax.sharding import PartitionSpec as P

adapter_scaling = 0.5
MEBIBYTE = 1024 * 1024
COST = 20
HALVES = 2
COSTS = {"sums": 1, "pair": 1}
LIMITS = {"low": 6, "sums": 12, "last": 14, "token": 8, "adapter": 12, "small": 4}
TILE = 512
STRIP = 256
QUARTER_ORDER = ((3, 2, 1, 0), (0, 3, 2, 1), (3, 0, 1, 2), (0, 1, 2, 3))


def matrix_product(left, right):
    return jnp.dot(left, right, preferred_element_type=jnp.float32)


def contract_trailing_axis(left, right):
    return lax.dot_general(
        left, right, (((1,), (1,)), ((), ())), preferred_element_type=jnp.float32
    )


def contract_first(left, right):
    return lax.dot_general(
        left, right, (((0,), (0,)), ((), ())), preferred_element_type=jnp.float32
    )


def any_plane(
    tokens,
    cotangent,
    gate_frozen_matrix,
    up_frozen_matrix,
    down_frozen_matrix,
    gate_adapter_input_factor,
    up_adapter_input_factor,
    gate_adapter_output_factor,
    up_adapter_output_factor,
    down_adapter_input_factor,
    down_leave,
):
    token_groups = lax.axis_size(("cuts", "fsdp"))
    quarters = lax.axis_size("tp")
    tp_index = lax.axis_index("tp")
    token_rows = tokens.shape[0]
    width = tokens.shape[1]
    gradient_scaling = adapter_scaling / math.sqrt(token_rows * token_groups)
    gate_adapter_hidden = matrix_product(tokens, gate_adapter_input_factor).astype(jnp.bfloat16)
    up_adapter_hidden = matrix_product(tokens, up_adapter_input_factor).astype(jnp.bfloat16)
    pieces = (
        lax.all_gather(gate_frozen_matrix, ("cuts", "fsdp"), axis=0, tiled=True),
        lax.all_gather(up_frozen_matrix, ("cuts", "fsdp"), axis=0, tiled=True),
    )
    columns = tokens
    gate_frozen_output = matrix_product(columns, pieces[0])
    up_frozen_output = matrix_product(columns, pieces[1])
    gate_preactivation = gate_frozen_output + adapter_scaling * matrix_product(
        gate_adapter_hidden, gate_adapter_output_factor
    )
    up_preactivation = up_frozen_output + adapter_scaling * matrix_product(
        up_adapter_hidden, up_adapter_output_factor
    )
    sig = jax.nn.sigmoid(gate_preactivation)
    hidden = (gate_preactivation * sig * up_preactivation).astype(jnp.bfloat16)
    down_part = matrix_product(hidden, down_adapter_input_factor)
    down_low = lax.psum(down_part.astype(jnp.bfloat16), "tp")
    backward_adapter_input = matrix_product(cotangent, down_leave).astype(jnp.bfloat16)
    columns = cotangent
    hidden_state_gradient = contract_trailing_axis(
        columns, lax.all_gather(down_frozen_matrix, ("cuts", "fsdp"), axis=1, tiled=True)
    )
    hidden_state_gradient = hidden_state_gradient + adapter_scaling * contract_trailing_axis(
        backward_adapter_input, down_adapter_input_factor
    )
    gate_output_gradient = (
        hidden_state_gradient * up_preactivation * sig * (1.0 + gate_preactivation * (1.0 - sig))
    ).astype(jnp.bfloat16)
    up_output_gradient = (hidden_state_gradient * gate_preactivation * sig).astype(jnp.bfloat16)
    gate_part = contract_trailing_axis(gate_output_gradient, gate_adapter_output_factor)
    up_part = contract_trailing_axis(up_output_gradient, up_adapter_output_factor)
    gate_sum, up_sum = lax.psum((gate_part, up_part), "tp")
    gate_backward_adapter = gate_sum.astype(jnp.bfloat16)
    up_backward_adapter = up_sum.astype(jnp.bfloat16)
    pieces = lax.all_gather(
        (gate_frozen_matrix, up_frozen_matrix), ("cuts", "fsdp"), axis=0, tiled=True
    )
    partial_value = contract_trailing_axis(
        gate_output_gradient, pieces[0]
    ) + contract_trailing_axis(up_output_gradient, pieces[1])
    frozen_path_gradient = lax.psum_scatter(partial_value, "tp", scatter_dimension=1, tiled=True)
    slice_width = width // quarters
    gate_slice = lax.dynamic_slice_in_dim(
        gate_adapter_input_factor, tp_index * slice_width, slice_width, 0
    )
    up_slice = lax.dynamic_slice_in_dim(
        up_adapter_input_factor, tp_index * slice_width, slice_width, 0
    )
    adapter_hidden_gradient = contract_trailing_axis(
        gate_backward_adapter, gate_slice
    ) + contract_trailing_axis(up_backward_adapter, up_slice)
    token_input_gradient = (
        frozen_path_gradient + adapter_scaling * adapter_hidden_gradient
    ).astype(jnp.bfloat16)
    narrow_part = gradient_scaling * jnp.concatenate(
        [
            contract_first(hidden, backward_adapter_input),
            contract_first(gate_output_gradient, gate_adapter_hidden),
            contract_first(up_output_gradient, up_adapter_hidden),
        ],
        axis=1,
    )
    narrow_grads = lax.psum(narrow_part, ("cuts", "fsdp"))
    token_side = jnp.concatenate([gate_backward_adapter, up_backward_adapter], axis=1)
    group_rows = lax.psum_scatter(
        gradient_scaling
        * jnp.concatenate(
            [contract_first(tokens, token_side), contract_first(cotangent, down_low)], axis=1
        ),
        ("cuts", "fsdp"),
        scatter_dimension=0,
        tiled=True,
    )
    fine_rows = width // (token_groups * quarters)
    wide_grads = lax.dynamic_slice_in_dim(group_rows, tp_index * fine_rows, fine_rows, 0)
    return (token_input_gradient, wide_grads, narrow_grads)


def flip(array, axis, bit):
    size = lax.axis_size(axis)
    return lax.ppermute(array, axis, [(i, i ^ bit) for i in range(size)])


def vmem_call(
    kernel, scalars, arrays, ahead, results, aliases, scratch, limit, flops, name, final=False
):
    vmem = pl.BlockSpec(memory_space=pltpu.VMEM)
    first = len(scalars)
    return pl.pallas_call(
        kernel,
        in_specs=[pl.BlockSpec(memory_space=pltpu.SMEM)] * first
        + [vmem] * len(arrays)
        + [pl.BlockSpec(memory_space=pl.ANY)] * len(ahead),
        out_specs=[vmem] * len(results),
        out_shape=[
            jax.ShapeDtypeStruct(shape, kind) if final else pltpu.VMEM(shape, kind)
            for shape, kind in results
        ],
        scratch_shapes=scratch,
        input_output_aliases={first + source: target for source, target in aliases.items()},
        compiler_params=pltpu.CompilerParams(vmem_limit_bytes=limit * MEBIBYTE),
        cost_estimate=pl.CostEstimate(flops=COST * flops, bytes_accessed=0, transcendentals=0),
        name=name,
    )(
        *scalars,
        *[pltpu.with_memory_space_constraint(array, pltpu.VMEM) for array in arrays],
        *ahead,
    )


def width_part(ref, part, here, masks, rows):
    return jnp.concatenate(
        [
            ref[part, pl.ds(pl.multiple_of(lax.bitwise_xor(here[0], mask) * rows, rows), rows)]
            for mask in masks
        ],
        axis=1,
    )


def stacked(units, which, span):
    return jnp.concatenate([unit[which, :, span] for unit in units], axis=0)


def put_in_place(units, here, gate_full, up_full):
    half = units[0].shape[1]
    for number, unit in enumerate(units):
        block = lax.bitwise_xor(here[0], number // 2)
        row = pl.ds(pl.multiple_of((2 * block + number % 2) * half, half), half)
        gate_full[row, :] = unit[0]
        up_full[row, :] = unit[1]


def lows_kernel(tokens, cotangent, gate_in, up_in, leave, *refs):
    gate_low, up_low, back_low, turned = refs[-4:]
    rank = leave.shape[0]
    for number, (ref, factor, out) in enumerate(
        ((tokens, gate_in, gate_low), (tokens, up_in, up_low), (cotangent, leave, back_low))
    ):
        low = contract_trailing_axis(ref[...], factor[...]).astype(jnp.bfloat16)
        out[...] = low
        turned[number * rank : (number + 1) * rank, :] = low.astype(jnp.float32).T.astype(
            jnp.bfloat16
        )


def low_rank_values(tokens, cotangent, factors, ahead):
    rows, width = tokens.shape
    rank = factors[0].shape[0]
    return vmem_call(
        lows_kernel,
        [],
        [tokens, cotangent, *factors],
        ahead,
        [((rows, rank), jnp.bfloat16)] * 3 + [((3 * rank, rows), jnp.bfloat16)],
        {},
        [],
        LIMITS["low"],
        24 * rows * width * rank,
        "low_rank_values",
    )


def pair_kernel(first, second, *refs):
    refs[-1][0] = first[...]
    refs[-1][1] = second[...]


def pair(first, second, ahead):
    return vmem_call(
        pair_kernel,
        [],
        [first, second],
        ahead,
        [((2, *first.shape), first.dtype)],
        {},
        [],
        LIMITS["small"],
        COSTS["pair"],
        "pair",
    )[0]


def single_units(refs):
    return [
        part
        for ref in refs
        for part in ([ref] if len(ref.shape) == 3 else [ref.at[0], ref.at[1]])
    ]


def sums_kernel(masks, order, n_arrays, last, here, *refs):
    tokens, cotangent, gate_low, up_low, back_low, gate_out, up_out, down_in = refs[:8]
    units = single_units(refs[8 : 8 + n_arrays])
    units = [units[number] for number in order]
    sums, rest = refs[-8:-2], refs[-2:]
    rows = 2 * units[0].shape[1]
    hidden = units[0].shape[2]
    tile = tokens.shape[0] // HALVES
    for half in range(HALVES):
        part = slice(half * tile, (half + 1) * tile)
        left = width_part(tokens, part, here, masks, rows)
        back = width_part(cotangent, part, here, masks, rows)
        for ref, out in zip((tokens, cotangent), rest):
            out[part, :] = width_part(ref, part, here, last, rows)
        for column in range(0, hidden, TILE):
            span = slice(column, column + TILE)
            for which, (low, factor) in enumerate(
                ((gate_low, gate_out), (up_low, up_out), (back_low, down_in))
            ):
                sums[3 * half + which][:, span] = matrix_product(
                    back if which == 2 else left, stacked(units, which, span)
                ) + adapter_scaling * matrix_product(low[part, :], factor[:, span])


def width_sums(here, tokens, cotangent, lows, factors, masks, order, arrays, last):
    rows, width = tokens.shape
    _, half, hidden = arrays[0].shape[-3:]
    outs = vmem_call(
        functools.partial(sums_kernel, masks, order, len(arrays), last),
        [here],
        [tokens, cotangent, *lows, *factors, *arrays],
        [],
        [((rows // HALVES, hidden), jnp.float32)] * (3 * HALVES)
        + [((rows, 2 * half * len(last)), jnp.bfloat16)] * 2,
        {},
        [],
        LIMITS["sums"],
        COSTS["sums"],
        "width_sums",
    )
    return outs[:-2], outs[-2:]


def last_kernel(half, n_arrays, order, count, here, *refs):
    left, back, gate_out, up_out = refs[:4]
    units = single_units(refs[4 : 4 + n_arrays])
    units = [units[number] for number in order]
    sums = refs[4 + n_arrays : 7 + n_arrays]
    outs = refs[-6:] if len(units) > count else refs[-4:]
    hidden_out, gate_grad_out, up_grad_out, low_out = outs[:4]
    if len(units) > count:
        put_in_place(units, here, *outs[4:])
        units = units[6:8] + units[14:16]
    rows, hidden = hidden_out.shape
    part = slice(half * rows, (half + 1) * rows)
    gate_low = up_low = 0.0
    for column in range(0, hidden, STRIP):
        span = slice(column, column + STRIP)
        gate = sums[0][:, span] + matrix_product(left[part, :], stacked(units, 0, span))
        up = sums[1][:, span] + matrix_product(left[part, :], stacked(units, 1, span))
        hidden_grad = sums[2][:, span] + matrix_product(back[part, :], stacked(units, 2, span))
        sig = 1.0 / (1.0 + jnp.exp(-gate))
        gated = gate * sig
        hidden_out[:, span] = (gated * up).astype(jnp.bfloat16)
        gate_grad = (hidden_grad * up * sig * (1.0 + gate * (1.0 - sig))).astype(jnp.bfloat16)
        up_grad = (hidden_grad * gated).astype(jnp.bfloat16)
        gate_grad_out[:, span] = gate_grad
        up_grad_out[:, span] = up_grad
        gate_low += contract_trailing_axis(gate_grad, gate_out[:, span])
        up_low += contract_trailing_axis(up_grad, up_out[:, span])
    low_out[...] = jnp.concatenate([gate_low, up_low], axis=1)


def hidden_and_grads(half, here, parts, factors, order, count, arrays, sums, width, ahead):
    rows = parts[0].shape[0] // HALVES
    rank, hidden = factors[0].shape
    arrays = [*parts, *factors, *arrays, *sums[3 * half : 3 * half + 3]]
    full = [((width, hidden), jnp.bfloat16)] * 2 if len(order) > count else []
    outs = vmem_call(
        functools.partial(last_kernel, half, len(arrays) - 7, order, count),
        [here],
        arrays,
        ahead,
        [((rows, hidden), jnp.bfloat16)] * 3 + [((rows, 2 * rank), jnp.float32)] + full,
        {},
        [],
        LIMITS["last"],
        24 * rows * hidden * parts[0].shape[1],
        "hidden_and_grads",
    )
    return outs[:4], outs[4:]


def token_grad_kernel(mode, step, here, gate_grad, up_grad, low, factor, gate, up, *refs):
    came = refs[: {"first": 0, "sum": 1, "both": 3, "last": 2}[mode]]
    outs = refs[-2:] if mode == "both" else refs[-1:]
    columns = outs[0].shape[1]
    quarter = sum(
        jnp.where(here[1] == place, order[step], 0) for place, order in enumerate(QUARTER_ORDER)
    )
    span = pl.ds(pl.multiple_of(quarter * columns, columns), columns)
    total = contract_trailing_axis(gate_grad[...], gate[span, :])
    total += contract_trailing_axis(up_grad[...], up[span, :])
    total += matrix_product((adapter_scaling * low[...]).astype(jnp.bfloat16), factor[:, span])
    came = [ref[...].astype(jnp.float32) for ref in came]
    if mode == "both":
        first, left, right = came
        outs[0][...] = (jnp.where(here[1] == 2, first, total) + left).astype(jnp.bfloat16)
        outs[1][...] = (jnp.where(here[1] == 1, first, total) + right).astype(jnp.bfloat16)
    else:
        outs[0][...] = sum(came, total).astype(jnp.bfloat16)


def token_grad(mode, step, here, arrays, columns, came, ahead):
    rows, hidden = arrays[0].shape
    outs = vmem_call(
        functools.partial(token_grad_kernel, mode, step),
        [here],
        [*arrays, *came],
        ahead,
        [((rows, columns), jnp.bfloat16)] * (2 if mode == "both" else 1),
        {},
        [],
        LIMITS["token"],
        8 * rows * columns * hidden,
        "token_grad",
        mode == "last",
    )
    return outs if mode == "both" else outs[0]


def adapter_kernel(scaling, here, *refs):
    hidden, gate_grad, up_grad, low = (
        refs[number * HALVES : (number + 1) * HALVES] for number in range(4)
    )
    tokens, cotangent, turned, down_in = refs[4 * HALVES : 4 * HALVES + 4]
    keep, send, wide, narrow = refs[-4:]
    rank = down_in.shape[0]
    rows = hidden[0].shape[0]
    parts = [slice(half * rows, (half + 1) * rows) for half in range(HALVES)]
    wide[: 2 * rank, :] = scaling * sum(
        matrix_product(low[half][...].T.astype(jnp.bfloat16), tokens[part, :])
        for half, part in enumerate(parts)
    )
    wide[2 * rank :, :] = scaling * sum(
        matrix_product(
            contract_trailing_axis(down_in[...], hidden[half][...]).astype(jnp.bfloat16),
            cotangent[part, :],
        )
        for half, part in enumerate(parts)
    )
    for number, arrays in enumerate((hidden, gate_grad, up_grad)):
        source = (2, 0, 1)[number]
        narrow[number * rank : (number + 1) * rank, :] = scaling * sum(
            matrix_product(turned[source * rank : (source + 1) * rank, part], arrays[half][...])
            for half, part in enumerate(parts)
        )
    groups = 2 * keep.shape[0]
    wide_columns, narrow_columns = wide.shape[1] // groups, narrow.shape[1] // groups
    for mask in range(groups):
        out = (keep if mask < groups // 2 else send).at[mask % (groups // 2)]
        block = lax.bitwise_xor(here[0], mask)
        out[:, :wide_columns] = wide[
            :, pl.ds(pl.multiple_of(block * wide_columns, wide_columns), wide_columns)
        ]
        out[:, wide_columns:] = narrow[
            :, pl.ds(pl.multiple_of(block * narrow_columns, narrow_columns), narrow_columns)
        ]


def adapter_grads(scaling, here, groups, arrays, ahead):
    rows, width = arrays[-4].shape
    rank, hidden = arrays[-1].shape
    return vmem_call(
        functools.partial(adapter_kernel, scaling),
        [here],
        arrays,
        ahead,
        [((groups // 2, 3 * rank, (width + hidden) // groups), jnp.float32)] * 2,
        {},
        [pltpu.VMEM((3 * rank, width), jnp.float32), pltpu.VMEM((3 * rank, hidden), jnp.float32)],
        LIMITS["adapter"],
        24 * rank * rows * (width + hidden),
        "adapter_grads",
    )


def halve_kernel(here, keep, came, kept, send):
    count = kept.shape[0]
    kept[...] = keep[:count] + came[:count].astype(jnp.float32)
    send[...] = (keep[count:] + came[count:].astype(jnp.float32)).astype(send.dtype)


def halve(here, keep, came):
    shape = (keep.shape[0] // 2, *keep.shape[1:])
    return vmem_call(
        halve_kernel,
        [here],
        [keep, came],
        [],
        [(shape, jnp.float32), (shape, jnp.bfloat16)],
        {},
        [],
        LIMITS["small"],
        500 * MEBIBYTE,
        "halve",
    )


def sum_kernel(here, keep, came, out):
    out[...] = keep[0] + came[0].astype(jnp.float32)


def last_sum(here, keep, came):
    return vmem_call(
        sum_kernel,
        [here],
        [keep, came],
        [],
        [(keep.shape[1:], jnp.float32)],
        {},
        [],
        LIMITS["small"],
        500 * MEBIBYTE,
        "last_sum",
        True,
    )[0]


def turn_kernel(wide_columns, here, kept, came, narrow, keep, send, wide):
    total = kept[0] + came[0].astype(jnp.float32)
    narrow[...] = total[:, wide_columns:].T
    wide[...] = total[:, :wide_columns].T
    rows = keep.shape[1]
    for mask in range(4):
        block = pl.ds(pl.multiple_of(lax.bitwise_xor(here[1], mask) * rows, rows), rows)
        (keep if mask < 2 else send)[mask % 2] = wide[block, :].astype((keep if mask < 2 else send).dtype)


def turn(here, keep, came, wide_columns):
    _, rows, columns = keep.shape
    return vmem_call(
        functools.partial(turn_kernel, wide_columns),
        [here],
        [keep, came],
        [],
        [((columns - wide_columns, rows), keep.dtype)]
        + [((2, wide_columns // 4, rows), kind) for kind in (jnp.float32, jnp.bfloat16)],
        {},
        [pltpu.VMEM((wide_columns, rows), keep.dtype)],
        LIMITS["small"],
        500 * MEBIBYTE,
        "turn",
    )


def whole_kernel(here, near, far, out):
    rows = near.shape[1]
    for number in range(2 * near.shape[0]):
        ref = near if number < near.shape[0] else far
        block = lax.bitwise_xor(here[0], number) * rows
        out[pl.ds(pl.multiple_of(block, rows), rows), :] = ref[number % near.shape[0]]


def whole(here, near, far):
    count, rows, columns = near.shape
    return vmem_call(
        whole_kernel,
        [here],
        [near, far],
        [],
        [((2 * count * rows, columns), near.dtype)],
        {},
        [],
        LIMITS["small"],
        500 * MEBIBYTE,
        "whole",
        True,
    )[0]


def square_plane(
    tokens,
    cotangent,
    gate_frozen_matrix,
    up_frozen_matrix,
    down_frozen_matrix,
    gate_adapter_input_factor,
    up_adapter_input_factor,
    gate_adapter_output_factor,
    up_adapter_output_factor,
    down_adapter_input_factor,
    down_leave,
):
    groups = lax.axis_size(("cuts", "fsdp"))
    quarters = lax.axis_size("tp")
    rows, width = tokens.shape
    gradient_scaling = adapter_scaling / math.sqrt(rows * groups)
    here = jnp.stack([lax.axis_index(("cuts", "fsdp")), lax.axis_index("tp")]).astype(jnp.int32)
    gate_in, up_in, leave, down_in = (
        array.T
        for array in (
            gate_adapter_input_factor,
            up_adapter_input_factor,
            down_leave,
            down_adapter_input_factor,
        )
    )
    gate_out, up_out = gate_adapter_output_factor, up_adapter_output_factor
    half_rows = gate_frozen_matrix.shape[0] // 2

    units = {}
    for half in range(2):
        span = slice(half * half_rows, (half + 1) * half_rows)
        units[0, half] = jnp.stack(
            [gate_frozen_matrix[span], up_frozen_matrix[span], down_frozen_matrix[:, span].T]
        )
    units[1, 0] = flip(units[0, 0], "fsdp", 1)
    units[2, 1] = flip(units[0, 1], "fsdp", 2)
    units[1, 1] = flip(units[0, 1], "fsdp", 1)
    units[2, 0] = flip(units[0, 0], "fsdp", 2)
    units[3, 0] = flip(units[1, 0], "fsdp", 2)
    units[3, 1] = flip(units[2, 1], "fsdp", 1)
    for half in range(2):
        units[4, half] = flip(units[0, half], "cuts", 1)
    *lows, turned = low_rank_values(
        tokens, cotangent, [gate_in, up_in, leave], [units[1, 0], units[2, 1]]
    )
    pairs = {}
    for number, (one, two, ahead) in enumerate(
        (((1, 0), (2, 1), [turned]), ((1, 1), (2, 0), [turned]))
    ):
        pairs[number] = flip(pair(units[one], units[two], ahead), "cuts", 1)
    keys = [(0, 0), (0, 1), (1, 0), (1, 1), (2, 0), (2, 1), (4, 0), (4, 1)]
    placed = keys + [(5, 0), (6, 1), (5, 1), (6, 0)]
    arrays = [units[key] for key in keys] + [pairs[0], pairs[1]]
    masks = (0, 1, 2, 4, 5, 6)
    order = [placed.index((mask, half)) for mask in masks for half in range(2)]
    sums, parts = width_sums(
        here, tokens, cotangent, lows, [gate_out, up_out, down_in], masks, order, arrays, (3, 7)
    )
    tail = [units[3, 0], units[3, 1]]
    tail.append(flip(pair(*tail, [sums[0]]), "cuts", 1))
    placed = [(3, 0), (3, 1), (7, 0), (7, 1), *placed]
    order = [placed.index((mask, half)) for mask in range(8) for half in range(2)]

    factor = jnp.concatenate([gate_in, up_in])
    shift = lambda array, pairs: lax.ppermute(array, "tp", pairs)
    states, first, full = [], [], []
    share = lambda step, half, mode, came=(), ahead=(): token_grad(
        mode,
        step,
        here,
        [*states[half][1:], factor, *full],
        width // quarters,
        came,
        ahead,
    )
    both = range(HALVES)
    for half in both:
        state, placed = hidden_and_grads(
            half,
            here,
            parts,
            [gate_out, up_out],
            range(4) if half else order,
            4,
            tail if half else tail + arrays,
            sums,
            width,
            first[:],
        )
        full = placed or full
        states.append(state)
        first.append(share(0, half, "first"))
    came = [shift(part, [(0, 1), (3, 2)]) for part in first]
    partial = [share(1, half, "sum", [came[half]], first[1:]) for half in both]
    from_left = [shift(part, [(0, 1), (1, 2)]) for part in partial]
    from_right = [shift(part, [(3, 2), (2, 1)]) for part in partial]
    partial = [
        share(2, half, "both", [first[half], from_left[half], from_right[half]], partial[1:])
        for half in both
    ]
    from_left = [shift(part[0], [(0, 1), (1, 2), (2, 3)]) for part in partial]
    from_right = [shift(part[1], [(3, 2), (2, 1), (1, 0)]) for part in partial]

    keep, send = adapter_grads(
        gradient_scaling,
        here,
        groups,
        [
            *[state[number] for number in range(4) for state in states],
            tokens,
            cotangent,
            turned,
            down_in,
        ],
        first,
    )
    keep, send = halve(here, keep, flip(send, "cuts", 1))
    keep, send = halve(here, keep, flip(send, "fsdp", 2))
    narrow, keep, send = turn(here, keep, flip(send, "fsdp", 1), width // groups)
    keep, send = halve(here, keep, flip(send, "tp", 2))
    wide_grads = last_sum(here, keep, flip(send, "tp", 1))
    near = jnp.stack([narrow, flip(narrow, "fsdp", 1)])
    near = jnp.concatenate([near, flip(near, "fsdp", 2)])
    narrow_grads = whole(here, near, flip(near, "cuts", 1))

    token_input_gradient = jnp.concatenate(
        [
            share(
                3,
                half,
                "last",
                [from_left[half], from_right[half]],
                [*partial[1], wide_grads, narrow_grads] if half else partial[1],
            )
            for half in both
        ]
    )
    return (token_input_gradient, wide_grads, narrow_grads)


def per_device(*arrays):
    sizes = [lax.axis_size(axis) for axis in ("cuts", "fsdp", "tp")]
    return (square_plane if sizes == [2, 4, 4] else any_plane)(*arrays)


def solution(mesh):
    in_specs = (
        P(("cuts", "fsdp"), None),
        P(("cuts", "fsdp"), None),
        P(("cuts", "fsdp"), "tp"),
        P(("cuts", "fsdp"), "tp"),
        P("tp", ("cuts", "fsdp")),
        P(),
        P(),
        P(None, "tp"),
        P(None, "tp"),
        P("tp", None),
        P(),
    )
    out_specs = (P(("cuts", "fsdp"), "tp"), P(("cuts", "fsdp", "tp"), None), P("tp", None))
    return jax.shard_map(
        per_device, mesh=mesh, in_specs=in_specs, out_specs=out_specs, check_vma=False
    )
```

```python
import functools
import math

import jax
import jax.numpy as jnp
from jax import lax
from jax.experimental import pallas as pl
from jax.experimental.pallas import tpu as pltpu
from jax.sharding import PartitionSpec as P

adapter_scaling = 0.5
MEBIBYTE = 1024 * 1024
COST = 20
HALVES = 2
COSTS = {"sums": 1, "pair": 1}
LIMITS = {"low": 6, "sums": 12, "last": 14, "token": 8, "adapter": 12, "small": 4}
TILE = 512
STRIP = 256
QUARTER_ORDER = ((3, 2, 1, 0), (0, 3, 2, 1), (3, 0, 1, 2), (0, 1, 2, 3))


def matrix_product(left, right):
    return jnp.dot(left, right, preferred_element_type=jnp.float32)


def contract_trailing_axis(left, right):
    return lax.dot_general(
        left, right, (((1,), (1,)), ((), ())), preferred_element_type=jnp.float32
    )


def contract_first(left, right):
    return lax.dot_general(
        left, right, (((0,), (0,)), ((), ())), preferred_element_type=jnp.float32
    )


def any_plane(
    tokens,
    cotangent,
    gate_frozen_matrix,
    up_frozen_matrix,
    down_frozen_matrix,
    gate_adapter_input_factor,
    up_adapter_input_factor,
    gate_adapter_output_factor,
    up_adapter_output_factor,
    down_adapter_input_factor,
    down_leave,
):
    token_groups = lax.axis_size(("cuts", "fsdp"))
    quarters = lax.axis_size("tp")
    tp_index = lax.axis_index("tp")
    token_rows = tokens.shape[0]
    width = tokens.shape[1]
    gradient_scaling = adapter_scaling / math.sqrt(token_rows * token_groups)
    gate_adapter_hidden = matrix_product(tokens, gate_adapter_input_factor).astype(jnp.bfloat16)
    up_adapter_hidden = matrix_product(tokens, up_adapter_input_factor).astype(jnp.bfloat16)
    pieces = (
        lax.all_gather(gate_frozen_matrix, ("cuts", "fsdp"), axis=0, tiled=True),
        lax.all_gather(up_frozen_matrix, ("cuts", "fsdp"), axis=0, tiled=True),
    )
    columns = tokens
    gate_frozen_output = matrix_product(columns, pieces[0])
    up_frozen_output = matrix_product(columns, pieces[1])
    gate_preactivation = gate_frozen_output + adapter_scaling * matrix_product(
        gate_adapter_hidden, gate_adapter_output_factor
    )
    up_preactivation = up_frozen_output + adapter_scaling * matrix_product(
        up_adapter_hidden, up_adapter_output_factor
    )
    sig = jax.nn.sigmoid(gate_preactivation)
    hidden = (gate_preactivation * sig * up_preactivation).astype(jnp.bfloat16)
    down_part = matrix_product(hidden, down_adapter_input_factor)
    down_low = lax.psum(down_part.astype(jnp.bfloat16), "tp")
    backward_adapter_input = matrix_product(cotangent, down_leave).astype(jnp.bfloat16)
    columns = cotangent
    hidden_state_gradient = contract_trailing_axis(
        columns, lax.all_gather(down_frozen_matrix, ("cuts", "fsdp"), axis=1, tiled=True)
    )
    hidden_state_gradient = hidden_state_gradient + adapter_scaling * contract_trailing_axis(
        backward_adapter_input, down_adapter_input_factor
    )
    gate_output_gradient = (
        hidden_state_gradient * up_preactivation * sig * (1.0 + gate_preactivation * (1.0 - sig))
    ).astype(jnp.bfloat16)
    up_output_gradient = (hidden_state_gradient * gate_preactivation * sig).astype(jnp.bfloat16)
    gate_part = contract_trailing_axis(gate_output_gradient, gate_adapter_output_factor)
    up_part = contract_trailing_axis(up_output_gradient, up_adapter_output_factor)
    gate_sum, up_sum = lax.psum((gate_part, up_part), "tp")
    gate_backward_adapter = gate_sum.astype(jnp.bfloat16)
    up_backward_adapter = up_sum.astype(jnp.bfloat16)
    pieces = lax.all_gather(
        (gate_frozen_matrix, up_frozen_matrix), ("cuts", "fsdp"), axis=0, tiled=True
    )
    partial_value = contract_trailing_axis(
        gate_output_gradient, pieces[0]
    ) + contract_trailing_axis(up_output_gradient, pieces[1])
    frozen_path_gradient = lax.psum_scatter(partial_value, "tp", scatter_dimension=1, tiled=True)
    slice_width = width // quarters
    gate_slice = lax.dynamic_slice_in_dim(
        gate_adapter_input_factor, tp_index * slice_width, slice_width, 0
    )
    up_slice = lax.dynamic_slice_in_dim(
        up_adapter_input_factor, tp_index * slice_width, slice_width, 0
    )
    adapter_hidden_gradient = contract_trailing_axis(
        gate_backward_adapter, gate_slice
    ) + contract_trailing_axis(up_backward_adapter, up_slice)
    token_input_gradient = (
        frozen_path_gradient + adapter_scaling * adapter_hidden_gradient
    ).astype(jnp.bfloat16)
    narrow_part = gradient_scaling * jnp.concatenate(
        [
            contract_first(hidden, backward_adapter_input),
            contract_first(gate_output_gradient, gate_adapter_hidden),
            contract_first(up_output_gradient, up_adapter_hidden),
        ],
        axis=1,
    )
    narrow_grads = lax.psum(narrow_part, ("cuts", "fsdp"))
    token_side = jnp.concatenate([gate_backward_adapter, up_backward_adapter], axis=1)
    group_rows = lax.psum_scatter(
        gradient_scaling
        * jnp.concatenate(
            [contract_first(tokens, token_side), contract_first(cotangent, down_low)], axis=1
        ),
        ("cuts", "fsdp"),
        scatter_dimension=0,
        tiled=True,
    )
    fine_rows = width // (token_groups * quarters)
    wide_grads = lax.dynamic_slice_in_dim(group_rows, tp_index * fine_rows, fine_rows, 0)
    return (token_input_gradient, wide_grads, narrow_grads)


def flip(array, axis, bit):
    size = lax.axis_size(axis)
    return lax.ppermute(array, axis, [(i, i ^ bit) for i in range(size)])


def vmem_call(
    kernel, scalars, arrays, ahead, results, aliases, scratch, limit, flops, name, final=False
):
    vmem = pl.BlockSpec(memory_space=pltpu.VMEM)
    first = len(scalars)
    return pl.pallas_call(
        kernel,
        in_specs=[pl.BlockSpec(memory_space=pltpu.SMEM)] * first
        + [vmem] * len(arrays)
        + [pl.BlockSpec(memory_space=pl.ANY)] * len(ahead),
        out_specs=[vmem] * len(results),
        out_shape=[
            jax.ShapeDtypeStruct(shape, kind) if final else pltpu.VMEM(shape, kind)
            for shape, kind in results
        ],
        scratch_shapes=scratch,
        input_output_aliases={first + source: target for source, target in aliases.items()},
        compiler_params=pltpu.CompilerParams(vmem_limit_bytes=limit * MEBIBYTE),
        cost_estimate=pl.CostEstimate(flops=COST * flops, bytes_accessed=0, transcendentals=0),
        name=name,
    )(
        *scalars,
        *[pltpu.with_memory_space_constraint(array, pltpu.VMEM) for array in arrays],
        *ahead,
    )


def width_part(ref, part, here, masks, rows):
    return jnp.concatenate(
        [
            ref[part, pl.ds(pl.multiple_of(lax.bitwise_xor(here[0], mask) * rows, rows), rows)]
            for mask in masks
        ],
        axis=1,
    )


def stacked(units, which, span):
    return jnp.concatenate([unit[which, :, span] for unit in units], axis=0)


def put_in_place(units, here, gate_full, up_full):
    half = units[0].shape[1]
    for number, unit in enumerate(units):
        block = lax.bitwise_xor(here[0], number // 2)
        row = pl.ds(pl.multiple_of((2 * block + number % 2) * half, half), half)
        gate_full[row, :] = unit[0]
        up_full[row, :] = unit[1]


def lows_kernel(tokens, cotangent, gate_in, up_in, leave, *refs):
    gate_low, up_low, back_low, turned = refs[-4:]
    rank = leave.shape[0]
    for number, (ref, factor, out) in enumerate(
        ((tokens, gate_in, gate_low), (tokens, up_in, up_low), (cotangent, leave, back_low))
    ):
        low = contract_trailing_axis(ref[...], factor[...]).astype(jnp.bfloat16)
        out[...] = low
        turned[number * rank : (number + 1) * rank, :] = low.astype(jnp.float32).T.astype(
            jnp.bfloat16
        )


def low_rank_values(tokens, cotangent, factors, ahead):
    rows, width = tokens.shape
    rank = factors[0].shape[0]
    tile = rows // 4
    by_rows = lambda columns: pl.BlockSpec((tile, columns), lambda i: (i, 0))
    return pl.pallas_call(
        lows_kernel,
        grid=(rows // tile,),
        in_specs=[by_rows(width)] * 2
        + [pl.BlockSpec((rank, width), lambda i: (0, 0))] * 3
        + [pl.BlockSpec(memory_space=pl.ANY)] * len(ahead),
        out_specs=[by_rows(rank)] * 3 + [pl.BlockSpec((3 * rank, tile), lambda i: (0, i))],
        out_shape=[jax.ShapeDtypeStruct((rows, rank), jnp.bfloat16)] * 3
        + [jax.ShapeDtypeStruct((3 * rank, rows), jnp.bfloat16)],
        compiler_params=pltpu.CompilerParams(vmem_limit_bytes=LIMITS["low"] * MEBIBYTE),
        cost_estimate=pl.CostEstimate(
            flops=24 * COST * rows * width * rank, bytes_accessed=0, transcendentals=0
        ),
        name="low_rank_values",
    )(tokens, cotangent, *factors, *ahead)


def own_kernel(gate, up, down, *units):
    for half, unit in enumerate(units):
        rows = unit.shape[1]
        part = slice(half * rows, (half + 1) * rows)
        unit[0] = gate[part, :]
        unit[1] = up[part, :]
        unit[2] = down[:, part].astype(jnp.float32).T.astype(jnp.bfloat16)


def own_units(gate, up, down):
    rows, hidden = gate.shape
    vmem = pl.BlockSpec(memory_space=pltpu.VMEM)
    return pl.pallas_call(
        own_kernel,
        in_specs=[vmem] * 3,
        out_specs=[vmem] * 2,
        out_shape=[pltpu.VMEM((3, rows // 2, hidden), jnp.bfloat16)] * 2,
        compiler_params=pltpu.CompilerParams(vmem_limit_bytes=LIMITS["low"] * MEBIBYTE),
        cost_estimate=pl.CostEstimate(flops=MEBIBYTE, bytes_accessed=0, transcendentals=0),
        name="own_units",
    )(gate, up, down)


def pair_kernel(first, second, *refs):
    refs[-1][0] = first[...]
    refs[-1][1] = second[...]


def pair(first, second, ahead):
    return vmem_call(
        pair_kernel,
        [],
        [first, second],
        ahead,
        [((2, *first.shape), first.dtype)],
        {},
        [],
        LIMITS["small"],
        COSTS["pair"],
        "pair",
    )[0]


def single_units(refs):
    return [
        part
        for ref in refs
        for part in ([ref] if len(ref.shape) == 3 else [ref.at[0], ref.at[1]])
    ]


def sums_kernel(masks, order, n_arrays, last, here, *refs):
    tokens, cotangent, gate_low, up_low, back_low, gate_out, up_out, down_in = refs[:8]
    units = single_units(refs[8 : 8 + n_arrays])
    units = [units[number] for number in order]
    sums, rest = refs[-8:-2], refs[-2:]
    rows = 2 * units[0].shape[1]
    hidden = units[0].shape[2]
    tile = tokens.shape[0] // HALVES
    for half in range(HALVES):
        part = slice(half * tile, (half + 1) * tile)
        left = width_part(tokens, part, here, masks, rows)
        back = width_part(cotangent, part, here, masks, rows)
        for ref, out in zip((tokens, cotangent), rest):
            out[part, :] = width_part(ref, part, here, last, rows)
        for column in range(0, hidden, TILE):
            span = slice(column, column + TILE)
            for which, (low, factor) in enumerate(
                ((gate_low, gate_out), (up_low, up_out), (back_low, down_in))
            ):
                sums[3 * half + which][:, span] = matrix_product(
                    back if which == 2 else left, stacked(units, which, span)
                ) + adapter_scaling * matrix_product(low[part, :], factor[:, span])


def width_sums(here, tokens, cotangent, lows, factors, masks, order, arrays, last):
    rows, width = tokens.shape
    _, half, hidden = arrays[0].shape[-3:]
    outs = vmem_call(
        functools.partial(sums_kernel, masks, order, len(arrays), last),
        [here],
        [tokens, cotangent, *lows, *factors, *arrays],
        [],
        [((rows // HALVES, hidden), jnp.float32)] * (3 * HALVES)
        + [((rows, 2 * half * len(last)), jnp.bfloat16)] * 2,
        {},
        [],
        LIMITS["sums"],
        COSTS["sums"],
        "width_sums",
    )
    return outs[:-2], outs[-2:]


def last_kernel(half, n_arrays, order, count, here, *refs):
    left, back, gate_out, up_out = refs[:4]
    units = single_units(refs[4 : 4 + n_arrays])
    units = [units[number] for number in order]
    sums = refs[4 + n_arrays : 7 + n_arrays]
    outs = refs[-6:] if len(units) > count else refs[-4:]
    hidden_out, gate_grad_out, up_grad_out, low_out = outs[:4]
    if len(units) > count:
        put_in_place(units, here, *outs[4:])
        units = units[6:8] + units[14:16]
    rows, hidden = hidden_out.shape
    part = slice(half * rows, (half + 1) * rows)
    gate_low = up_low = 0.0
    for column in range(0, hidden, STRIP):
        span = slice(column, column + STRIP)
        gate = sums[0][:, span] + matrix_product(left[part, :], stacked(units, 0, span))
        up = sums[1][:, span] + matrix_product(left[part, :], stacked(units, 1, span))
        hidden_grad = sums[2][:, span] + matrix_product(back[part, :], stacked(units, 2, span))
        sig = 1.0 / (1.0 + jnp.exp(-gate))
        gated = gate * sig
        hidden_out[:, span] = (gated * up).astype(jnp.bfloat16)
        gate_grad = (hidden_grad * up * sig * (1.0 + gate * (1.0 - sig))).astype(jnp.bfloat16)
        up_grad = (hidden_grad * gated).astype(jnp.bfloat16)
        gate_grad_out[:, span] = gate_grad
        up_grad_out[:, span] = up_grad
        gate_low += contract_trailing_axis(gate_grad, gate_out[:, span])
        up_low += contract_trailing_axis(up_grad, up_out[:, span])
    low_out[...] = jnp.concatenate([gate_low, up_low], axis=1)


def hidden_and_grads(half, here, parts, factors, order, count, arrays, sums, width, ahead):
    rows = parts[0].shape[0] // HALVES
    rank, hidden = factors[0].shape
    arrays = [*parts, *factors, *arrays, *sums[3 * half : 3 * half + 3]]
    full = [((width, hidden), jnp.bfloat16)] * 2 if len(order) > count else []
    outs = vmem_call(
        functools.partial(last_kernel, half, len(arrays) - 7, order, count),
        [here],
        arrays,
        ahead,
        [((rows, hidden), jnp.bfloat16)] * 3 + [((rows, 2 * rank), jnp.float32)] + full,
        {},
        [],
        LIMITS["last"],
        24 * rows * hidden * parts[0].shape[1],
        "hidden_and_grads",
    )
    return outs[:4], outs[4:]


def token_grad_kernel(mode, step, here, gate_grad, up_grad, low, factor, gate, up, *refs):
    came = refs[: {"first": 0, "sum": 1, "both": 3, "last": 2}[mode]]
    outs = refs[-2:] if mode == "both" else refs[-1:]
    columns = outs[0].shape[1]
    quarter = sum(
        jnp.where(here[1] == place, order[step], 0) for place, order in enumerate(QUARTER_ORDER)
    )
    span = pl.ds(pl.multiple_of(quarter * columns, columns), columns)
    total = contract_trailing_axis(gate_grad[...], gate[span, :])
    total += contract_trailing_axis(up_grad[...], up[span, :])
    total += matrix_product((adapter_scaling * low[...]).astype(jnp.bfloat16), factor[:, span])
    came = [ref[...].astype(jnp.float32) for ref in came]
    if mode == "both":
        first, left, right = came
        outs[0][...] = (jnp.where(here[1] == 2, first, total) + left).astype(jnp.bfloat16)
        outs[1][...] = (jnp.where(here[1] == 1, first, total) + right).astype(jnp.bfloat16)
    else:
        outs[0][...] = sum(came, total).astype(jnp.bfloat16)


def token_grad(mode, step, here, arrays, columns, came, ahead):
    rows, hidden = arrays[0].shape
    outs = vmem_call(
        functools.partial(token_grad_kernel, mode, step),
        [here],
        [*arrays, *came],
        ahead,
        [((rows, columns), jnp.bfloat16)] * (2 if mode == "both" else 1),
        {},
        [],
        LIMITS["token"],
        8 * rows * columns * hidden,
        "token_grad",
    )
    return outs if mode == "both" else outs[0]


def last_token_grad(step, half, here, arrays, columns, came, ahead, before):
    rows, hidden = arrays[0].shape
    arrays = [*arrays, *came]
    return pl.pallas_call(
        functools.partial(token_grad_kernel, "last", step),
        grid=(1,),
        in_specs=[pl.BlockSpec(memory_space=pltpu.SMEM)]
        + [pl.BlockSpec(memory_space=pltpu.VMEM)] * len(arrays)
        + [pl.BlockSpec(memory_space=pl.ANY)] * (len(before) + len(ahead)),
        out_specs=pl.BlockSpec((rows, columns), lambda i: (half, 0)),
        out_shape=jax.ShapeDtypeStruct((HALVES * rows, columns), jnp.bfloat16),
        input_output_aliases={1 + len(arrays): 0} if before else {},
        compiler_params=pltpu.CompilerParams(vmem_limit_bytes=LIMITS["token"] * MEBIBYTE),
        cost_estimate=pl.CostEstimate(
            flops=8 * COST * rows * columns * hidden, bytes_accessed=0, transcendentals=0
        ),
        name="last_token_grad",
    )(
        here,
        *[pltpu.with_memory_space_constraint(array, pltpu.VMEM) for array in arrays],
        *before,
        *ahead,
    )


def adapter_kernel(scaling, here, *refs):
    hidden, gate_grad, up_grad, low = (
        refs[number * HALVES : (number + 1) * HALVES] for number in range(4)
    )
    tokens, cotangent, turned, down_in = refs[4 * HALVES : 4 * HALVES + 4]
    keep, send, wide, narrow = refs[-4:]
    rank = down_in.shape[0]
    rows = hidden[0].shape[0]
    parts = [slice(half * rows, (half + 1) * rows) for half in range(HALVES)]
    wide[: 2 * rank, :] = scaling * sum(
        matrix_product(low[half][...].T.astype(jnp.bfloat16), tokens[part, :])
        for half, part in enumerate(parts)
    )
    wide[2 * rank :, :] = scaling * sum(
        matrix_product(
            contract_trailing_axis(down_in[...], hidden[half][...]).astype(jnp.bfloat16),
            cotangent[part, :],
        )
        for half, part in enumerate(parts)
    )
    for number, arrays in enumerate((hidden, gate_grad, up_grad)):
        source = (2, 0, 1)[number]
        narrow[number * rank : (number + 1) * rank, :] = scaling * sum(
            matrix_product(turned[source * rank : (source + 1) * rank, part], arrays[half][...])
            for half, part in enumerate(parts)
        )
    groups = 2 * keep.shape[0]
    wide_columns, narrow_columns = wide.shape[1] // groups, narrow.shape[1] // groups
    for mask in range(groups):
        out = (keep if mask < groups // 2 else send).at[mask % (groups // 2)]
        block = lax.bitwise_xor(here[0], mask)
        out[:, :wide_columns] = wide[
            :, pl.ds(pl.multiple_of(block * wide_columns, wide_columns), wide_columns)
        ]
        out[:, wide_columns:] = narrow[
            :, pl.ds(pl.multiple_of(block * narrow_columns, narrow_columns), narrow_columns)
        ]


def adapter_grads(scaling, here, groups, arrays, ahead):
    rows, width = arrays[-4].shape
    rank, hidden = arrays[-1].shape
    return vmem_call(
        functools.partial(adapter_kernel, scaling),
        [here],
        arrays,
        ahead,
        [((groups // 2, 3 * rank, (width + hidden) // groups), jnp.float32)] * 2,
        {},
        [pltpu.VMEM((3 * rank, width), jnp.float32), pltpu.VMEM((3 * rank, hidden), jnp.float32)],
        LIMITS["adapter"],
        24 * rank * rows * (width + hidden),
        "adapter_grads",
    )


def halve_kernel(here, keep, came, kept, send):
    count = kept.shape[0]
    kept[...] = keep[:count] + came[:count].astype(jnp.float32)
    send[...] = (keep[count:] + came[count:].astype(jnp.float32)).astype(send.dtype)


def halve(here, keep, came):
    shape = (keep.shape[0] // 2, *keep.shape[1:])
    return vmem_call(
        halve_kernel,
        [here],
        [keep, came],
        [],
        [(shape, jnp.float32), (shape, jnp.bfloat16)],
        {},
        [],
        LIMITS["small"],
        20 * MEBIBYTE,
        "halve",
    )


def sum_kernel(here, keep, came, out):
    out[...] = keep[0] + came[0].astype(jnp.float32)


def last_sum(here, keep, came):
    return vmem_call(
        sum_kernel,
        [here],
        [keep, came],
        [],
        [(keep.shape[1:], jnp.float32)],
        {},
        [],
        LIMITS["small"],
        20 * MEBIBYTE,
        "last_sum",
        True,
    )[0]


def turn_kernel(wide_columns, here, kept, came, narrow, keep, send, wide):
    total = kept[0] + came[0].astype(jnp.float32)
    narrow[...] = total[:, wide_columns:]
    wide[...] = total[:, :wide_columns].T
    rows = keep.shape[1]
    for mask in range(4):
        block = pl.ds(pl.multiple_of(lax.bitwise_xor(here[1], mask) * rows, rows), rows)
        (keep if mask < 2 else send)[mask % 2] = wide[block, :].astype((keep if mask < 2 else send).dtype)


def turn(here, keep, came, wide_columns):
    _, rows, columns = keep.shape
    return vmem_call(
        functools.partial(turn_kernel, wide_columns),
        [here],
        [keep, came],
        [],
        [((rows, columns - wide_columns), keep.dtype)]
        + [((2, wide_columns // 4, rows), kind) for kind in (jnp.float32, jnp.bfloat16)],
        {},
        [pltpu.VMEM((wide_columns, rows), keep.dtype)],
        LIMITS["small"],
        20 * MEBIBYTE,
        "turn",
    )


def whole_kernel(here, near, far, out):
    columns = near.shape[2]
    for number in range(2 * near.shape[0]):
        ref = near if number < near.shape[0] else far
        block = lax.bitwise_xor(here[0], number) * columns
        out[:, pl.ds(pl.multiple_of(block, columns), columns)] = ref[number % near.shape[0]]


def whole(here, near, far):
    count, rows, columns = near.shape
    return vmem_call(
        whole_kernel,
        [here],
        [near, far],
        [],
        [((rows, 2 * count * columns), near.dtype)],
        {},
        [],
        LIMITS["small"],
        20 * MEBIBYTE,
        "whole",
        True,
    )[0]


def square_plane(
    tokens,
    cotangent,
    gate_frozen_matrix,
    up_frozen_matrix,
    down_frozen_matrix,
    gate_adapter_input_factor,
    up_adapter_input_factor,
    gate_adapter_output_factor,
    up_adapter_output_factor,
    down_adapter_input_factor,
    down_leave,
):
    groups = lax.axis_size(("cuts", "fsdp"))
    quarters = lax.axis_size("tp")
    rows, width = tokens.shape
    gradient_scaling = adapter_scaling / math.sqrt(rows * groups)
    here = jnp.stack([lax.axis_index(("cuts", "fsdp")), lax.axis_index("tp")]).astype(jnp.int32)
    gate_in, up_in, leave, down_in = (
        array.T
        for array in (
            gate_adapter_input_factor,
            up_adapter_input_factor,
            down_leave,
            down_adapter_input_factor,
        )
    )
    gate_out, up_out = gate_adapter_output_factor, up_adapter_output_factor

    units = {}
    units[0, 0], units[0, 1] = own_units(
        gate_frozen_matrix, up_frozen_matrix, down_frozen_matrix
    )
    units[1, 0] = flip(units[0, 0], "fsdp", 1)
    units[2, 1] = flip(units[0, 1], "fsdp", 2)
    units[1, 1] = flip(units[0, 1], "fsdp", 1)
    units[2, 0] = flip(units[0, 0], "fsdp", 2)
    units[3, 0] = flip(units[1, 0], "fsdp", 2)
    units[3, 1] = flip(units[2, 1], "fsdp", 1)
    for half in range(2):
        units[4, half] = flip(units[0, half], "cuts", 1)
    *lows, turned = low_rank_values(
        tokens, cotangent, [gate_in, up_in, leave], [units[1, 0], units[2, 1]]
    )
    pairs = {}
    for number, (one, two, ahead) in enumerate(
        (((1, 0), (2, 1), [turned]), ((1, 1), (2, 0), [turned]))
    ):
        pairs[number] = flip(pair(units[one], units[two], ahead), "cuts", 1)
    keys = [(0, 0), (0, 1), (1, 0), (1, 1), (2, 0), (2, 1), (4, 0), (4, 1)]
    placed = keys + [(5, 0), (6, 1), (5, 1), (6, 0)]
    arrays = [units[key] for key in keys] + [pairs[0], pairs[1]]
    masks = (0, 1, 2, 4, 5, 6)
    order = [placed.index((mask, half)) for mask in masks for half in range(2)]
    sums, parts = width_sums(
        here, tokens, cotangent, lows, [gate_out, up_out, down_in], masks, order, arrays, (3, 7)
    )
    tail = [units[3, 0], units[3, 1]]
    tail.append(flip(pair(*tail, [sums[0]]), "cuts", 1))
    placed = [(3, 0), (3, 1), (7, 0), (7, 1), *placed]
    order = [placed.index((mask, half)) for mask in range(8) for half in range(2)]

    factor = jnp.concatenate([gate_in, up_in])
    shift = lambda array, pairs: lax.ppermute(array, "tp", pairs)
    states, first, full = [], [], []
    share = lambda step, half, mode, came=(), ahead=(): token_grad(
        mode,
        step,
        here,
        [*states[half][1:], factor, *full],
        width // quarters,
        came,
        ahead,
    )
    both = range(HALVES)
    for half in both:
        state, placed = hidden_and_grads(
            half,
            here,
            parts,
            [gate_out, up_out],
            range(4) if half else order,
            4,
            tail if half else tail + arrays,
            sums,
            width,
            first[:],
        )
        full = placed or full
        states.append(state)
        first.append(share(0, half, "first"))
    came = [shift(part, [(0, 1), (3, 2)]) for part in first]
    partial = []
    for half in both:
        partial.append(share(1, half, "sum", [came[half]], partial or first[1:]))
    second = partial
    from_left = [shift(part, [(0, 1), (1, 2)]) for part in partial]
    from_right = [shift(part, [(3, 2), (2, 1)]) for part in partial]
    partial = []
    for half in both:
        partial.append(
            share(
                2,
                half,
                "both",
                [first[half], from_left[half], from_right[half]],
                partial[0] if partial else second[1:],
            )
        )
    from_left = [shift(part[0], [(0, 1), (1, 2), (2, 3)]) for part in partial]
    from_right = [shift(part[1], [(3, 2), (2, 1), (1, 0)]) for part in partial]

    keep, send = adapter_grads(
        gradient_scaling,
        here,
        groups,
        [
            *[state[number] for number in range(4) for state in states],
            tokens,
            cotangent,
            turned,
            down_in,
        ],
        [came[0], *first],
    )
    keep, send = halve(here, keep, flip(send, "cuts", 1))
    keep, send = halve(here, keep, flip(send, "fsdp", 2))
    narrow, keep, send = turn(here, keep, flip(send, "fsdp", 1), width // groups)
    keep, send = halve(here, keep, flip(send, "tp", 2))
    wide_grads = last_sum(here, keep, flip(send, "tp", 1))
    near = jnp.stack([narrow, flip(narrow, "fsdp", 1)])
    near = jnp.concatenate([near, flip(near, "fsdp", 2)])
    narrow_turned = whole(here, near, flip(near, "cuts", 1))
    narrow_grads = narrow_turned.T

    results = []
    for half in both:
        results.append(
            last_token_grad(
                3,
                half,
                here,
                [*states[half][1:], factor, *full],
                width // quarters,
                [from_left[half], from_right[half]],
                [wide_grads, narrow_turned] if half else partial[1],
                results[:],
            )
        )
    token_input_gradient = results[-1]
    return (token_input_gradient, wide_grads, narrow_grads)


def per_device(*arrays):
    sizes = [lax.axis_size(axis) for axis in ("cuts", "fsdp", "tp")]
    return (square_plane if sizes == [2, 4, 4] else any_plane)(*arrays)


def solution(mesh):
    in_specs = (
        P(("cuts", "fsdp"), None),
        P(("cuts", "fsdp"), None),
        P(("cuts", "fsdp"), "tp"),
        P(("cuts", "fsdp"), "tp"),
        P("tp", ("cuts", "fsdp")),
        P(),
        P(),
        P(None, "tp"),
        P(None, "tp"),
        P("tp", None),
        P(),
    )
    out_specs = (P(("cuts", "fsdp"), "tp"), P(("cuts", "fsdp", "tp"), None), P("tp", None))
    return jax.shard_map(
        per_device, mesh=mesh, in_specs=in_specs, out_specs=out_specs, check_vma=False
    )
```

```python
import functools
import math

import jax
import jax.numpy as jnp
from jax import lax
from jax.experimental import pallas as pl
from jax.experimental.pallas import tpu as pltpu
from jax.sharding import PartitionSpec as P

adapter_scaling = 0.5
MEBIBYTE = 1024 * 1024
COST = 1
HALVES = 2
COSTS = {"sums": 1, "pair": 1, "small": 1, "token": 30, "adapter": 20, "last": 480}
LIMITS = {"low": 6, "sums": 32, "last": 14, "token": 8, "adapter": 12, "small": 4}
TILE = 512
STRIP = 256
QUARTER_ORDER = ((3, 2, 1, 0), (0, 3, 2, 1), (3, 0, 1, 2), (0, 1, 2, 3))


def matrix_product(left, right):
    return jnp.dot(left, right, preferred_element_type=jnp.float32)


def contract_trailing_axis(left, right):
    return lax.dot_general(
        left, right, (((1,), (1,)), ((), ())), preferred_element_type=jnp.float32
    )


def contract_first(left, right):
    return lax.dot_general(
        left, right, (((0,), (0,)), ((), ())), preferred_element_type=jnp.float32
    )


def any_plane(
    tokens,
    cotangent,
    gate_frozen_matrix,
    up_frozen_matrix,
    down_frozen_matrix,
    gate_adapter_input_factor,
    up_adapter_input_factor,
    gate_adapter_output_factor,
    up_adapter_output_factor,
    down_adapter_input_factor,
    down_leave,
):
    token_groups = lax.axis_size(("cuts", "fsdp"))
    quarters = lax.axis_size("tp")
    tp_index = lax.axis_index("tp")
    token_rows = tokens.shape[0]
    width = tokens.shape[1]
    gradient_scaling = adapter_scaling / math.sqrt(token_rows * token_groups)
    gate_adapter_hidden = matrix_product(tokens, gate_adapter_input_factor).astype(jnp.bfloat16)
    up_adapter_hidden = matrix_product(tokens, up_adapter_input_factor).astype(jnp.bfloat16)
    pieces = (
        lax.all_gather(gate_frozen_matrix, ("cuts", "fsdp"), axis=0, tiled=True),
        lax.all_gather(up_frozen_matrix, ("cuts", "fsdp"), axis=0, tiled=True),
    )
    columns = tokens
    gate_frozen_output = matrix_product(columns, pieces[0])
    up_frozen_output = matrix_product(columns, pieces[1])
    gate_preactivation = gate_frozen_output + adapter_scaling * matrix_product(
        gate_adapter_hidden, gate_adapter_output_factor
    )
    up_preactivation = up_frozen_output + adapter_scaling * matrix_product(
        up_adapter_hidden, up_adapter_output_factor
    )
    sig = jax.nn.sigmoid(gate_preactivation)
    hidden = (gate_preactivation * sig * up_preactivation).astype(jnp.bfloat16)
    down_part = matrix_product(hidden, down_adapter_input_factor)
    down_low = lax.psum(down_part.astype(jnp.bfloat16), "tp")
    backward_adapter_input = matrix_product(cotangent, down_leave).astype(jnp.bfloat16)
    columns = cotangent
    hidden_state_gradient = contract_trailing_axis(
        columns, lax.all_gather(down_frozen_matrix, ("cuts", "fsdp"), axis=1, tiled=True)
    )
    hidden_state_gradient = hidden_state_gradient + adapter_scaling * contract_trailing_axis(
        backward_adapter_input, down_adapter_input_factor
    )
    gate_output_gradient = (
        hidden_state_gradient * up_preactivation * sig * (1.0 + gate_preactivation * (1.0 - sig))
    ).astype(jnp.bfloat16)
    up_output_gradient = (hidden_state_gradient * gate_preactivation * sig).astype(jnp.bfloat16)
    gate_part = contract_trailing_axis(gate_output_gradient, gate_adapter_output_factor)
    up_part = contract_trailing_axis(up_output_gradient, up_adapter_output_factor)
    gate_sum, up_sum = lax.psum((gate_part, up_part), "tp")
    gate_backward_adapter = gate_sum.astype(jnp.bfloat16)
    up_backward_adapter = up_sum.astype(jnp.bfloat16)
    pieces = lax.all_gather(
        (gate_frozen_matrix, up_frozen_matrix), ("cuts", "fsdp"), axis=0, tiled=True
    )
    partial_value = contract_trailing_axis(
        gate_output_gradient, pieces[0]
    ) + contract_trailing_axis(up_output_gradient, pieces[1])
    frozen_path_gradient = lax.psum_scatter(partial_value, "tp", scatter_dimension=1, tiled=True)
    slice_width = width // quarters
    gate_slice = lax.dynamic_slice_in_dim(
        gate_adapter_input_factor, tp_index * slice_width, slice_width, 0
    )
    up_slice = lax.dynamic_slice_in_dim(
        up_adapter_input_factor, tp_index * slice_width, slice_width, 0
    )
    adapter_hidden_gradient = contract_trailing_axis(
        gate_backward_adapter, gate_slice
    ) + contract_trailing_axis(up_backward_adapter, up_slice)
    token_input_gradient = (
        frozen_path_gradient + adapter_scaling * adapter_hidden_gradient
    ).astype(jnp.bfloat16)
    narrow_part = gradient_scaling * jnp.concatenate(
        [
            contract_first(hidden, backward_adapter_input),
            contract_first(gate_output_gradient, gate_adapter_hidden),
            contract_first(up_output_gradient, up_adapter_hidden),
        ],
        axis=1,
    )
    narrow_grads = lax.psum(narrow_part, ("cuts", "fsdp"))
    token_side = jnp.concatenate([gate_backward_adapter, up_backward_adapter], axis=1)
    group_rows = lax.psum_scatter(
        gradient_scaling
        * jnp.concatenate(
            [contract_first(tokens, token_side), contract_first(cotangent, down_low)], axis=1
        ),
        ("cuts", "fsdp"),
        scatter_dimension=0,
        tiled=True,
    )
    fine_rows = width // (token_groups * quarters)
    wide_grads = lax.dynamic_slice_in_dim(group_rows, tp_index * fine_rows, fine_rows, 0)
    return (token_input_gradient, wide_grads, narrow_grads)


def flip(array, axis, bit):
    size = lax.axis_size(axis)
    return lax.ppermute(array, axis, [(i, i ^ bit) for i in range(size)])


def vmem_call(
    kernel, scalars, arrays, ahead, results, aliases, scratch, limit, flops, name, final=False
):
    vmem = pl.BlockSpec(memory_space=pltpu.VMEM)
    first = len(scalars)
    return pl.pallas_call(
        kernel,
        in_specs=[pl.BlockSpec(memory_space=pltpu.SMEM)] * first
        + [vmem] * len(arrays)
        + [pl.BlockSpec(memory_space=pl.ANY)] * len(ahead),
        out_specs=[vmem] * len(results),
        out_shape=[
            jax.ShapeDtypeStruct(shape, kind) if final else pltpu.VMEM(shape, kind)
            for shape, kind in results
        ],
        scratch_shapes=scratch,
        input_output_aliases={first + source: target for source, target in aliases.items()},
        compiler_params=pltpu.CompilerParams(vmem_limit_bytes=limit * MEBIBYTE),
        cost_estimate=pl.CostEstimate(flops=COST * flops, bytes_accessed=0, transcendentals=0),
        name=name,
    )(
        *scalars,
        *[pltpu.with_memory_space_constraint(array, pltpu.VMEM) for array in arrays],
        *ahead,
    )


def width_part(ref, part, here, masks, rows):
    return jnp.concatenate(
        [
            ref[part, pl.ds(pl.multiple_of(lax.bitwise_xor(here[0], mask) * rows, rows), rows)]
            for mask in masks
        ],
        axis=1,
    )


def stacked(units, which, span):
    return jnp.concatenate([unit[which, :, span] for unit in units], axis=0)


def lows_kernel(tokens, cotangent, gate_in, up_in, leave, *refs):
    gate_low, up_low, back_low, turned = refs[-4:]
    rank = leave.shape[0]
    for number, (ref, factor, out) in enumerate(
        ((tokens, gate_in, gate_low), (tokens, up_in, up_low), (cotangent, leave, back_low))
    ):
        low = contract_trailing_axis(ref[...], factor[...]).astype(jnp.bfloat16)
        out[...] = low
        turned[number * rank : (number + 1) * rank, :] = low.astype(jnp.float32).T.astype(
            jnp.bfloat16
        )


def low_rank_values(tokens, cotangent, factors, ahead):
    rows, width = tokens.shape
    rank = factors[0].shape[0]
    tile = rows // 4
    by_rows = lambda columns: pl.BlockSpec((tile, columns), lambda i: (i, 0))
    return pl.pallas_call(
        lows_kernel,
        grid=(rows // tile,),
        in_specs=[by_rows(width)] * 2
        + [pl.BlockSpec((rank, width), lambda i: (0, 0))] * 3
        + [pl.BlockSpec(memory_space=pl.ANY)] * len(ahead),
        out_specs=[by_rows(rank)] * 3 + [pl.BlockSpec((3 * rank, tile), lambda i: (0, i))],
        out_shape=[jax.ShapeDtypeStruct((rows, rank), jnp.bfloat16)] * 3
        + [jax.ShapeDtypeStruct((3 * rank, rows), jnp.bfloat16)],
        compiler_params=pltpu.CompilerParams(vmem_limit_bytes=LIMITS["low"] * MEBIBYTE),
        cost_estimate=pl.CostEstimate(
            flops=480 * COST * rows * width * rank, bytes_accessed=0, transcendentals=0
        ),
        name="low_rank_values",
    )(tokens, cotangent, *factors, *ahead)


def own_kernel(gate, up, down, *refs):
    units, (held, sems) = refs[:2], refs[2:]
    rows = units[0].shape[1]
    down_copy = pltpu.make_async_copy(down, held, sems.at[0])
    down_copy.start()
    copies = []
    for half, unit in enumerate(units):
        for which, ref in enumerate((gate, up)):
            copies.append(
                pltpu.make_async_copy(
                    ref.at[pl.ds(half * rows, rows)], unit.at[which], sems.at[1 + len(copies)]
                )
            )
    for copy in copies:
        copy.start()
    down_copy.wait()
    for half, unit in enumerate(units):
        part = slice(half * rows, (half + 1) * rows)
        unit[2] = held[:, part].astype(jnp.float32).T.astype(jnp.bfloat16)
    for copy in copies:
        copy.wait()


def own_units(gate, up, down):
    rows, hidden = gate.shape
    return pl.pallas_call(
        own_kernel,
        in_specs=[pl.BlockSpec(memory_space=pl.ANY)] * 3,
        out_specs=[pl.BlockSpec(memory_space=pltpu.VMEM)] * 2,
        out_shape=[pltpu.VMEM((3, rows // 2, hidden), jnp.bfloat16)] * 2,
        scratch_shapes=[
            pltpu.VMEM((hidden, rows), jnp.bfloat16),
            pltpu.SemaphoreType.DMA((5,)),
        ],
        compiler_params=pltpu.CompilerParams(vmem_limit_bytes=LIMITS["low"] * MEBIBYTE),
        cost_estimate=pl.CostEstimate(flops=MEBIBYTE, bytes_accessed=0, transcendentals=0),
        name="own_units",
    )(gate, up, down)


def pair_kernel(first, second, *refs):
    refs[-1][0] = first[...]
    refs[-1][1] = second[...]


def pair(first, second, ahead):
    return vmem_call(
        pair_kernel,
        [],
        [first, second],
        ahead,
        [((2, *first.shape), first.dtype)],
        {},
        [],
        LIMITS["small"],
        COSTS["pair"],
        "pair",
    )[0]


def sums_kernel(masks, order, n_arrays, last, here, *refs):
    gate_low, up_low, back_low, gate_out, up_out, down_in, tokens, cotangent = refs[:8]
    units = []
    for ref in refs[8 : 8 + n_arrays]:
        units += [ref] if len(ref.shape) == 3 else [ref.at[0], ref.at[1]]
    units = [units[number] for number in order]
    outs = refs[8 + n_arrays :]
    sums, rest, full = outs[: 3 * HALVES], outs[3 * HALVES : 3 * HALVES + 2], outs[-7:-5]
    held_tokens, held_cotangent, held_down, row_sems, unit_sems = outs[-5:]
    half_rows, hidden = units[0].shape[1:]
    rows = 2 * half_rows
    tile = tokens.shape[0] // HALVES

    def unit_copies(which):
        copies = []
        for number, unit in enumerate(units):
            if which == 2:
                target = held_down.at[pl.ds(number * half_rows, half_rows)]
            else:
                block = lax.bitwise_xor(here[0], masks[number // 2])
                row = pl.multiple_of((2 * block + number % 2) * half_rows, half_rows)
                target = full[which].at[pl.ds(row, half_rows)]
            copies.append(
                pltpu.make_async_copy(
                    unit.at[which], target, unit_sems.at[which * len(units) + number]
                )
            )
        return copies

    def row_copy(which, half):
        source, target = ((tokens, held_tokens), (cotangent, held_cotangent))[which]
        part = pl.ds(half * tile, tile)
        return pltpu.make_async_copy(
            source.at[part], target.at[part], row_sems.at[which * HALVES + half]
        )

    loads = [*unit_copies(0), row_copy(0, 0), *unit_copies(1), row_copy(1, 0), *unit_copies(2)]
    loads += [row_copy(which, half) for half in range(1, HALVES) for which in range(2)]
    for load in loads:
        load.start()
    for half in range(HALVES):
        part = slice(half * tile, (half + 1) * tile)
        for which, (low, factor) in enumerate(
            ((gate_low, gate_out), (up_low, up_out), (back_low, down_in))
        ):
            if half == 0:
                for copy in unit_copies(which):
                    copy.wait()
            if which != 1:
                row_copy(which // 2, half).wait()
                ref = (held_tokens, held_cotangent)[which // 2]
                left = width_part(ref, part, here, masks, rows)
                rest[which // 2][part, :] = width_part(ref, part, here, last, rows)
            for column in range(0, hidden, TILE):
                span = slice(column, column + TILE)
                if which == 2:
                    right = held_down[:, span]
                else:
                    right = jnp.concatenate(
                        [
                            full[which][
                                pl.ds(
                                    pl.multiple_of(lax.bitwise_xor(here[0], mask) * rows, rows), rows
                                ),
                                span,
                            ]
                            for mask in masks
                        ]
                    )
                sums[3 * half + which][:, span] = matrix_product(
                    left, right
                ) + adapter_scaling * matrix_product(low[part, :], factor[:, span])


def width_sums(here, tokens, cotangent, lows, factors, masks, order, arrays, last):
    rows, width = tokens.shape
    _, half, hidden = arrays[0].shape[-3:]
    vmem, anywhere = pl.BlockSpec(memory_space=pltpu.VMEM), pl.BlockSpec(memory_space=pl.ANY)
    shapes = [((rows // HALVES, hidden), jnp.float32)] * (3 * HALVES)
    shapes += [((rows, 2 * half * len(last)), jnp.bfloat16)] * 2
    shapes += [((width, hidden), jnp.bfloat16)] * 2
    outs = pl.pallas_call(
        functools.partial(sums_kernel, masks, order, len(arrays), last),
        in_specs=[pl.BlockSpec(memory_space=pltpu.SMEM)]
        + [vmem] * 6
        + [anywhere] * (2 + len(arrays)),
        out_specs=[vmem] * len(shapes),
        out_shape=[pltpu.VMEM(shape, kind) for shape, kind in shapes],
        scratch_shapes=[
            pltpu.VMEM((rows, width), jnp.bfloat16),
            pltpu.VMEM((rows, width), jnp.bfloat16),
            pltpu.VMEM((half * len(order), hidden), jnp.bfloat16),
            pltpu.SemaphoreType.DMA((2 * HALVES,)),
            pltpu.SemaphoreType.DMA((3 * len(order),)),
        ],
        compiler_params=pltpu.CompilerParams(vmem_limit_bytes=LIMITS["sums"] * MEBIBYTE),
        cost_estimate=pl.CostEstimate(flops=COSTS["sums"], bytes_accessed=0, transcendentals=0),
        name="width_sums",
    )(here, *lows, *factors, tokens, cotangent, *arrays)
    return outs[: 3 * HALVES], outs[3 * HALVES : -2], outs[-2:]


def last_kernel(half, here, left, back, gate_out, up_out, upper, lower, other, *refs):
    units = [upper, lower, other.at[0], other.at[1]]
    sums = refs[:3]
    hidden_out, gate_grad_out, up_grad_out, low_out = refs[-4:]
    rows, hidden = hidden_out.shape
    part = slice(half * rows, (half + 1) * rows)
    gate_low = up_low = 0.0
    for column in range(0, hidden, STRIP):
        span = slice(column, column + STRIP)
        gate = sums[0][:, span] + matrix_product(left[part, :], stacked(units, 0, span))
        up = sums[1][:, span] + matrix_product(left[part, :], stacked(units, 1, span))
        hidden_grad = sums[2][:, span] + matrix_product(back[part, :], stacked(units, 2, span))
        sig = 1.0 / (1.0 + jnp.exp(-gate))
        gated = gate * sig
        hidden_out[:, span] = (gated * up).astype(jnp.bfloat16)
        gate_grad = (hidden_grad * up * sig * (1.0 + gate * (1.0 - sig))).astype(jnp.bfloat16)
        up_grad = (hidden_grad * gated).astype(jnp.bfloat16)
        gate_grad_out[:, span] = gate_grad
        up_grad_out[:, span] = up_grad
        gate_low += contract_trailing_axis(gate_grad, gate_out[:, span])
        up_low += contract_trailing_axis(up_grad, up_out[:, span])
    low_out[...] = jnp.concatenate([gate_low, up_low], axis=1)


def hidden_and_grads(half, here, parts, factors, tail, sums, ahead):
    rows = parts[0].shape[0] // HALVES
    rank, hidden = factors[0].shape
    return vmem_call(
        functools.partial(last_kernel, half),
        [here],
        [*parts, *factors, *tail, *sums[3 * half : 3 * half + 3]],
        ahead,
        [((rows, hidden), jnp.bfloat16)] * 3 + [((rows, 2 * rank), jnp.float32)],
        {},
        [],
        LIMITS["last"],
        COSTS["last"] * rows * hidden * parts[0].shape[1],
        "hidden_and_grads",
    )


def quarter_rows(here, quarter, full, tail, which, columns):
    upper, lower, other = tail
    rows = 2 * upper.shape[1]
    blocks = []
    for number in range(columns // rows):
        block = quarter * (columns // rows) + number
        mask = lax.bitwise_xor(here[0], block)
        held = full[pl.ds(pl.multiple_of(block * rows, rows), rows), :]
        near = jnp.concatenate([upper[which], lower[which]])
        far = jnp.concatenate([other[0, which], other[1, which]])
        blocks.append(jnp.where(mask == 7, far, jnp.where(mask == 3, near, held)))
    return jnp.concatenate(blocks)


def token_grad_kernel(mode, step, here, gate_grad, up_grad, low, factor, gate, up, *refs):
    tail, refs = refs[:3], refs[3:]
    came = refs[: {"first": 0, "sum": 1, "both": 3, "last": 2}[mode]]
    outs = refs[-2:] if mode == "both" else refs[-1:]
    columns = outs[0].shape[1]
    quarter = sum(
        jnp.where(here[1] == place, order[step], 0) for place, order in enumerate(QUARTER_ORDER)
    )
    span = pl.ds(pl.multiple_of(quarter * columns, columns), columns)
    total = contract_trailing_axis(
        gate_grad[...], quarter_rows(here, quarter, gate, tail, 0, columns)
    )
    total += contract_trailing_axis(up_grad[...], quarter_rows(here, quarter, up, tail, 1, columns))
    total += matrix_product((adapter_scaling * low[...]).astype(jnp.bfloat16), factor[:, span])
    came = [ref[...].astype(jnp.float32) for ref in came]
    if mode == "both":
        first, left, right = came
        outs[0][...] = (jnp.where(here[1] == 2, first, total) + left).astype(jnp.bfloat16)
        outs[1][...] = (jnp.where(here[1] == 1, first, total) + right).astype(jnp.bfloat16)
    else:
        outs[0][...] = sum(came, total).astype(jnp.bfloat16)


def token_grad(mode, step, here, arrays, columns, came, ahead):
    rows, hidden = arrays[0].shape
    outs = vmem_call(
        functools.partial(token_grad_kernel, mode, step),
        [here],
        [*arrays, *came],
        ahead,
        [((rows, columns), jnp.bfloat16)] * (2 if mode == "both" else 1),
        {},
        [],
        LIMITS["token"],
        COSTS["token"] * rows * columns * hidden,
        "token_grad",
    )
    return outs if mode == "both" else outs[0]


def last_token_grad(step, half, here, arrays, columns, came, ahead, before):
    rows, hidden = arrays[0].shape
    arrays = [*arrays, *came]
    return pl.pallas_call(
        functools.partial(token_grad_kernel, "last", step),
        grid=(1,),
        in_specs=[pl.BlockSpec(memory_space=pltpu.SMEM)]
        + [pl.BlockSpec(memory_space=pltpu.VMEM)] * len(arrays)
        + [pl.BlockSpec(memory_space=pl.ANY)] * (len(before) + len(ahead)),
        out_specs=pl.BlockSpec((rows, columns), lambda i: (half, 0)),
        out_shape=jax.ShapeDtypeStruct((HALVES * rows, columns), jnp.bfloat16),
        input_output_aliases={1 + len(arrays): 0} if before else {},
        compiler_params=pltpu.CompilerParams(vmem_limit_bytes=LIMITS["token"] * MEBIBYTE),
        cost_estimate=pl.CostEstimate(
            flops=COSTS["token"] * COST * rows * columns * hidden,
            bytes_accessed=0,
            transcendentals=0,
        ),
        name="last_token_grad",
    )(
        here,
        *[pltpu.with_memory_space_constraint(array, pltpu.VMEM) for array in arrays],
        *before,
        *ahead,
    )


def adapter_kernel(scaling, here, *refs):
    hidden, gate_grad, up_grad, low = (
        refs[number * HALVES : (number + 1) * HALVES] for number in range(4)
    )
    tokens, cotangent, turned, down_in = refs[4 * HALVES : 4 * HALVES + 4]
    keep, send, wide, narrow = refs[-4:]
    rank = down_in.shape[0]
    rows = hidden[0].shape[0]
    parts = [slice(half * rows, (half + 1) * rows) for half in range(HALVES)]
    wide[: 2 * rank, :] = scaling * sum(
        matrix_product(low[half][...].T.astype(jnp.bfloat16), tokens[part, :])
        for half, part in enumerate(parts)
    )
    wide[2 * rank :, :] = scaling * sum(
        matrix_product(
            contract_trailing_axis(down_in[...], hidden[half][...]).astype(jnp.bfloat16),
            cotangent[part, :],
        )
        for half, part in enumerate(parts)
    )
    for number, arrays in enumerate((hidden, gate_grad, up_grad)):
        source = (2, 0, 1)[number]
        narrow[number * rank : (number + 1) * rank, :] = scaling * sum(
            matrix_product(turned[source * rank : (source + 1) * rank, part], arrays[half][...])
            for half, part in enumerate(parts)
        )
    groups = 2 * keep.shape[0]
    wide_columns, narrow_columns = wide.shape[1] // groups, narrow.shape[1] // groups
    for mask in range(groups):
        out = (keep if mask < groups // 2 else send).at[mask % (groups // 2)]
        block = lax.bitwise_xor(here[0], mask)
        out[:, :wide_columns] = wide[
            :, pl.ds(pl.multiple_of(block * wide_columns, wide_columns), wide_columns)
        ]
        out[:, wide_columns:] = narrow[
            :, pl.ds(pl.multiple_of(block * narrow_columns, narrow_columns), narrow_columns)
        ]


def adapter_grads(scaling, here, groups, arrays, ahead):
    rows, width = arrays[-4].shape
    rank, hidden = arrays[-1].shape
    return vmem_call(
        functools.partial(adapter_kernel, scaling),
        [here],
        arrays,
        ahead,
        [((groups // 2, 3 * rank, (width + hidden) // groups), jnp.float32)] * 2,
        {},
        [pltpu.VMEM((3 * rank, width), jnp.float32), pltpu.VMEM((3 * rank, hidden), jnp.float32)],
        LIMITS["adapter"],
        COSTS["adapter"] * rank * rows * (width + hidden),
        "adapter_grads",
    )


def halve_kernel(here, keep, came, kept, send):
    count = kept.shape[0]
    kept[...] = keep[:count] + came[:count].astype(jnp.float32)
    send[...] = (keep[count:] + came[count:].astype(jnp.float32)).astype(send.dtype)


def halve(here, keep, came):
    shape = (keep.shape[0] // 2, *keep.shape[1:])
    return vmem_call(
        halve_kernel,
        [here],
        [keep, came],
        [],
        [(shape, jnp.float32), (shape, jnp.bfloat16)],
        {},
        [],
        LIMITS["small"],
        COSTS["small"],
        "halve",
    )


def sum_kernel(here, keep, *refs):
    refs[-1][...] = sum((ref[...].astype(jnp.float32) for ref in refs[:-1]), keep[...])


def last_sum(here, keep, came):
    return vmem_call(
        sum_kernel,
        [here],
        [keep, *came],
        [],
        [(keep.shape, jnp.float32)],
        {},
        [],
        LIMITS["small"],
        COSTS["small"],
        "last_sum",
        True,
    )[0]


def turn_kernel(wide_columns, here, kept, came, narrow, *refs):
    outs, wide = refs[:-1], refs[-1]
    total = kept[0] + came[0].astype(jnp.float32)
    narrow[...] = total[:, wide_columns:]
    wide[...] = total[:, :wide_columns].T
    for mask, out in enumerate(outs):
        rows = out.shape[0]
        block = pl.ds(pl.multiple_of(lax.bitwise_xor(here[1], mask) * rows, rows), rows)
        out[...] = wide[block, :].astype(out.dtype)


def turn(here, keep, came, wide_columns, quarters):
    _, rows, columns = keep.shape
    return vmem_call(
        functools.partial(turn_kernel, wide_columns),
        [here],
        [keep, came],
        [],
        [((rows, columns - wide_columns), jnp.float32)]
        + [
            ((wide_columns // quarters, rows), jnp.bfloat16 if mask else jnp.float32)
            for mask in range(quarters)
        ],
        {},
        [pltpu.VMEM((wide_columns, rows), jnp.float32)],
        LIMITS["small"],
        COSTS["small"],
        "turn",
    )


def whole_kernel(here, near, far, out):
    columns = near.shape[2]
    for number in range(2 * near.shape[0]):
        ref = near if number < near.shape[0] else far
        block = lax.bitwise_xor(here[0], number) * columns
        out[:, pl.ds(pl.multiple_of(block, columns), columns)] = ref[number % near.shape[0]]


def whole(here, near, far):
    count, rows, columns = near.shape
    return vmem_call(
        whole_kernel,
        [here],
        [near, far],
        [],
        [((rows, 2 * count * columns), near.dtype)],
        {},
        [],
        LIMITS["small"],
        COSTS["small"],
        "whole",
        True,
    )[0]


def square_plane(
    tokens,
    cotangent,
    gate_frozen_matrix,
    up_frozen_matrix,
    down_frozen_matrix,
    gate_adapter_input_factor,
    up_adapter_input_factor,
    gate_adapter_output_factor,
    up_adapter_output_factor,
    down_adapter_input_factor,
    down_leave,
):
    groups = lax.axis_size(("cuts", "fsdp"))
    quarters = lax.axis_size("tp")
    rows, width = tokens.shape
    gradient_scaling = adapter_scaling / math.sqrt(rows * groups)
    here = jnp.stack([lax.axis_index(("cuts", "fsdp")), lax.axis_index("tp")]).astype(jnp.int32)
    gate_in, up_in, leave, down_in = (
        array.T
        for array in (
            gate_adapter_input_factor,
            up_adapter_input_factor,
            down_leave,
            down_adapter_input_factor,
        )
    )
    gate_out, up_out = gate_adapter_output_factor, up_adapter_output_factor

    units = {}
    units[0, 0], units[0, 1] = own_units(
        gate_frozen_matrix, up_frozen_matrix, down_frozen_matrix
    )
    units[1, 0] = flip(units[0, 0], "fsdp", 1)
    units[2, 1] = flip(units[0, 1], "fsdp", 2)
    units[1, 1] = flip(units[0, 1], "fsdp", 1)
    units[2, 0] = flip(units[0, 0], "fsdp", 2)
    units[3, 0] = flip(units[1, 0], "fsdp", 2)
    units[3, 1] = flip(units[2, 1], "fsdp", 1)
    for half in range(2):
        units[4, half] = flip(units[0, half], "cuts", 1)
    *lows, turned = low_rank_values(
        tokens, cotangent, [gate_in, up_in, leave], [units[1, 0], units[2, 1]]
    )
    pairs = {}
    for number, (one, two, ahead) in enumerate(
        (((1, 0), (2, 1), [turned]), ((1, 1), (2, 0), [turned]))
    ):
        pairs[number] = flip(pair(units[one], units[two], ahead), "cuts", 1)
    keys = [(0, 0), (0, 1), (1, 0), (1, 1), (2, 0), (2, 1), (4, 0), (4, 1)]
    placed = keys + [(5, 0), (6, 1), (5, 1), (6, 0)]
    arrays = [units[key] for key in keys] + [pairs[0], pairs[1]]
    masks = (0, 1, 2, 4, 5, 6)
    order = [placed.index((mask, half)) for mask in masks for half in range(2)]
    sums, parts, full = width_sums(
        here, tokens, cotangent, lows, [gate_out, up_out, down_in], masks, order, arrays, (3, 7)
    )
    tail = [units[3, 0], units[3, 1]]
    tail.append(flip(pair(*tail, [sums[0]]), "cuts", 1))

    factor = jnp.concatenate([gate_in, up_in])
    shift = lambda array, pairs: lax.ppermute(array, "tp", pairs)
    states, first = [], []
    share = lambda step, half, mode, came=(), ahead=(): token_grad(
        mode,
        step,
        here,
        [*states[half][1:], factor, *full, *tail],
        width // quarters,
        came,
        ahead,
    )
    both = range(HALVES)
    for half in both:
        state = hidden_and_grads(
            half, here, parts, [gate_out, up_out], tail, sums, first[:]
        )
        states.append(state)
        first.append(share(0, half, "first"))
    came = [shift(part, [(0, 1), (3, 2)]) for part in first]
    partial = []
    for half in both:
        partial.append(share(1, half, "sum", [came[half]], partial or first[1:]))
    second = partial
    from_left = [shift(part, [(0, 1), (1, 2)]) for part in partial]
    from_right = [shift(part, [(3, 2), (2, 1)]) for part in partial]
    partial = []
    for half in both:
        partial.append(
            share(
                2,
                half,
                "both",
                [first[half], from_left[half], from_right[half]],
                partial[0] if partial else second[1:],
            )
        )
    from_left = [shift(part[0], [(0, 1), (1, 2), (2, 3)]) for part in partial]
    from_right = [shift(part[1], [(3, 2), (2, 1), (1, 0)]) for part in partial]

    keep, send = adapter_grads(
        gradient_scaling,
        here,
        groups,
        [
            *[state[number] for number in range(4) for state in states],
            tokens,
            cotangent,
            turned,
            down_in,
        ],
        [came[0], *first],
    )
    keep, send = halve(here, keep, flip(send, "cuts", 1))
    keep, send = halve(here, keep, flip(send, "fsdp", 2))
    narrow, keep, *send = turn(here, keep, flip(send, "fsdp", 1), width // groups, quarters)
    wide_grads = last_sum(
        here, keep, [flip(part, "tp", 1 + number) for number, part in enumerate(send)]
    )
    near = jnp.stack([narrow, flip(narrow, "fsdp", 1)])
    near = jnp.concatenate([near, flip(near, "fsdp", 2)])
    narrow_turned = whole(here, near, flip(near, "cuts", 1))
    narrow_grads = narrow_turned.T

    results = []
    for half in both:
        results.append(
            last_token_grad(
                3,
                half,
                here,
                [*states[half][1:], factor, *full, *tail],
                width // quarters,
                [from_left[half], from_right[half]],
                [wide_grads, narrow_turned] if half else partial[1],
                results[:],
            )
        )
    token_input_gradient = results[-1]
    return (token_input_gradient, wide_grads, narrow_grads)


def per_device(*arrays):
    sizes = [lax.axis_size(axis) for axis in ("cuts", "fsdp", "tp")]
    return (square_plane if sizes == [2, 4, 4] else any_plane)(*arrays)


def solution(mesh):
    in_specs = (
        P(("cuts", "fsdp"), None),
        P(("cuts", "fsdp"), None),
        P(("cuts", "fsdp"), "tp"),
        P(("cuts", "fsdp"), "tp"),
        P("tp", ("cuts", "fsdp")),
        P(),
        P(),
        P(None, "tp"),
        P(None, "tp"),
        P("tp", None),
        P(),
    )
    out_specs = (P(("cuts", "fsdp"), "tp"), P(("cuts", "fsdp", "tp"), None), P("tp", None))
    return jax.shard_map(
        per_device, mesh=mesh, in_specs=in_specs, out_specs=out_specs, check_vma=False
    )
```

```python
import functools
import math

import jax
import jax.numpy as jnp
from jax import lax
from jax.experimental import pallas as pl
from jax.experimental.pallas import tpu as pltpu
from jax.sharding import PartitionSpec as P

adapter_scaling = 0.5
MEBIBYTE = 1024 * 1024
COST = 1
HALVES = 2
COSTS = {"sums": 1, "pair": 1, "small": 1, "token": 20 * 10**9, "adapter": 20 * 10**9, "last": 10**11}
LIMITS = {"low": 6, "sums": 32, "last": 14, "token": 8, "adapter": 12, "small": 4}
TILE = 512
STRIP = 256
QUARTER_ORDER = ((3, 2, 1, 0), (0, 3, 2, 1), (3, 0, 1, 2), (0, 1, 2, 3))


def matrix_product(left, right):
    return jnp.dot(left, right, preferred_element_type=jnp.float32)


def contract_trailing_axis(left, right):
    return lax.dot_general(
        left, right, (((1,), (1,)), ((), ())), preferred_element_type=jnp.float32
    )


def contract_first(left, right):
    return lax.dot_general(
        left, right, (((0,), (0,)), ((), ())), preferred_element_type=jnp.float32
    )


def any_plane(
    tokens,
    cotangent,
    gate_frozen_matrix,
    up_frozen_matrix,
    down_frozen_matrix,
    gate_adapter_input_factor,
    up_adapter_input_factor,
    gate_adapter_output_factor,
    up_adapter_output_factor,
    down_adapter_input_factor,
    down_leave,
):
    token_groups = lax.axis_size(("cuts", "fsdp"))
    quarters = lax.axis_size("tp")
    tp_index = lax.axis_index("tp")
    token_rows = tokens.shape[0]
    width = tokens.shape[1]
    gradient_scaling = adapter_scaling / math.sqrt(token_rows * token_groups)
    gate_adapter_hidden = matrix_product(tokens, gate_adapter_input_factor).astype(jnp.bfloat16)
    up_adapter_hidden = matrix_product(tokens, up_adapter_input_factor).astype(jnp.bfloat16)
    pieces = (
        lax.all_gather(gate_frozen_matrix, ("cuts", "fsdp"), axis=0, tiled=True),
        lax.all_gather(up_frozen_matrix, ("cuts", "fsdp"), axis=0, tiled=True),
    )
    columns = tokens
    gate_frozen_output = matrix_product(columns, pieces[0])
    up_frozen_output = matrix_product(columns, pieces[1])
    gate_preactivation = gate_frozen_output + adapter_scaling * matrix_product(
        gate_adapter_hidden, gate_adapter_output_factor
    )
    up_preactivation = up_frozen_output + adapter_scaling * matrix_product(
        up_adapter_hidden, up_adapter_output_factor
    )
    sig = jax.nn.sigmoid(gate_preactivation)
    hidden = (gate_preactivation * sig * up_preactivation).astype(jnp.bfloat16)
    down_part = matrix_product(hidden, down_adapter_input_factor)
    down_low = lax.psum(down_part.astype(jnp.bfloat16), "tp")
    backward_adapter_input = matrix_product(cotangent, down_leave).astype(jnp.bfloat16)
    columns = cotangent
    hidden_state_gradient = contract_trailing_axis(
        columns, lax.all_gather(down_frozen_matrix, ("cuts", "fsdp"), axis=1, tiled=True)
    )
    hidden_state_gradient = hidden_state_gradient + adapter_scaling * contract_trailing_axis(
        backward_adapter_input, down_adapter_input_factor
    )
    gate_output_gradient = (
        hidden_state_gradient * up_preactivation * sig * (1.0 + gate_preactivation * (1.0 - sig))
    ).astype(jnp.bfloat16)
    up_output_gradient = (hidden_state_gradient * gate_preactivation * sig).astype(jnp.bfloat16)
    gate_part = contract_trailing_axis(gate_output_gradient, gate_adapter_output_factor)
    up_part = contract_trailing_axis(up_output_gradient, up_adapter_output_factor)
    gate_sum, up_sum = lax.psum((gate_part, up_part), "tp")
    gate_backward_adapter = gate_sum.astype(jnp.bfloat16)
    up_backward_adapter = up_sum.astype(jnp.bfloat16)
    pieces = lax.all_gather(
        (gate_frozen_matrix, up_frozen_matrix), ("cuts", "fsdp"), axis=0, tiled=True
    )
    partial_value = contract_trailing_axis(
        gate_output_gradient, pieces[0]
    ) + contract_trailing_axis(up_output_gradient, pieces[1])
    frozen_path_gradient = lax.psum_scatter(partial_value, "tp", scatter_dimension=1, tiled=True)
    slice_width = width // quarters
    gate_slice = lax.dynamic_slice_in_dim(
        gate_adapter_input_factor, tp_index * slice_width, slice_width, 0
    )
    up_slice = lax.dynamic_slice_in_dim(
        up_adapter_input_factor, tp_index * slice_width, slice_width, 0
    )
    adapter_hidden_gradient = contract_trailing_axis(
        gate_backward_adapter, gate_slice
    ) + contract_trailing_axis(up_backward_adapter, up_slice)
    token_input_gradient = (
        frozen_path_gradient + adapter_scaling * adapter_hidden_gradient
    ).astype(jnp.bfloat16)
    narrow_part = gradient_scaling * jnp.concatenate(
        [
            contract_first(hidden, backward_adapter_input),
            contract_first(gate_output_gradient, gate_adapter_hidden),
            contract_first(up_output_gradient, up_adapter_hidden),
        ],
        axis=1,
    )
    narrow_grads = lax.psum(narrow_part, ("cuts", "fsdp"))
    token_side = jnp.concatenate([gate_backward_adapter, up_backward_adapter], axis=1)
    group_rows = lax.psum_scatter(
        gradient_scaling
        * jnp.concatenate(
            [contract_first(tokens, token_side), contract_first(cotangent, down_low)], axis=1
        ),
        ("cuts", "fsdp"),
        scatter_dimension=0,
        tiled=True,
    )
    fine_rows = width // (token_groups * quarters)
    wide_grads = lax.dynamic_slice_in_dim(group_rows, tp_index * fine_rows, fine_rows, 0)
    return (token_input_gradient, wide_grads, narrow_grads)


def flip(array, axis, bit):
    size = lax.axis_size(axis)
    return lax.ppermute(array, axis, [(i, i ^ bit) for i in range(size)])


def vmem_call(
    kernel, scalars, arrays, ahead, results, aliases, scratch, limit, flops, name, final=False
):
    vmem = pl.BlockSpec(memory_space=pltpu.VMEM)
    first = len(scalars)
    return pl.pallas_call(
        kernel,
        in_specs=[pl.BlockSpec(memory_space=pltpu.SMEM)] * first
        + [vmem] * len(arrays)
        + [pl.BlockSpec(memory_space=pl.ANY)] * len(ahead),
        out_specs=[vmem] * len(results),
        out_shape=[
            jax.ShapeDtypeStruct(shape, kind) if final else pltpu.VMEM(shape, kind)
            for shape, kind in results
        ],
        scratch_shapes=scratch,
        input_output_aliases={first + source: target for source, target in aliases.items()},
        compiler_params=pltpu.CompilerParams(vmem_limit_bytes=limit * MEBIBYTE),
        cost_estimate=pl.CostEstimate(flops=COST * flops, bytes_accessed=0, transcendentals=0),
        name=name,
    )(
        *scalars,
        *[pltpu.with_memory_space_constraint(array, pltpu.VMEM) for array in arrays],
        *ahead,
    )


def width_part(ref, part, here, masks, rows):
    return jnp.concatenate(
        [
            ref[part, pl.ds(pl.multiple_of(lax.bitwise_xor(here[0], mask) * rows, rows), rows)]
            for mask in masks
        ],
        axis=1,
    )


def stacked(units, which, span):
    return jnp.concatenate([unit[which, :, span] for unit in units], axis=0)


def lows_kernel(tokens, cotangent, gate_in, up_in, leave, *refs):
    gate_low, up_low, back_low, turned = refs[-4:]
    rank = leave.shape[0]
    for number, (ref, factor, out) in enumerate(
        ((tokens, gate_in, gate_low), (tokens, up_in, up_low), (cotangent, leave, back_low))
    ):
        low = contract_trailing_axis(ref[...], factor[...]).astype(jnp.bfloat16)
        out[...] = low
        turned[number * rank : (number + 1) * rank, :] = low.astype(jnp.float32).T.astype(
            jnp.bfloat16
        )


def low_rank_values(tokens, cotangent, factors, ahead):
    rows, width = tokens.shape
    rank = factors[0].shape[0]
    tile = rows // 4
    by_rows = lambda columns: pl.BlockSpec((tile, columns), lambda i: (i, 0))
    return pl.pallas_call(
        lows_kernel,
        grid=(rows // tile,),
        in_specs=[by_rows(width)] * 2
        + [pl.BlockSpec((rank, width), lambda i: (0, 0))] * 3
        + [pl.BlockSpec(memory_space=pl.ANY)] * len(ahead),
        out_specs=[by_rows(rank)] * 3 + [pl.BlockSpec((3 * rank, tile), lambda i: (0, i))],
        out_shape=[jax.ShapeDtypeStruct((rows, rank), jnp.bfloat16)] * 3
        + [jax.ShapeDtypeStruct((3 * rank, rows), jnp.bfloat16)],
        compiler_params=pltpu.CompilerParams(vmem_limit_bytes=LIMITS["low"] * MEBIBYTE),
        cost_estimate=pl.CostEstimate(
            flops=480 * COST * rows * width * rank, bytes_accessed=0, transcendentals=0
        ),
        name="low_rank_values",
    )(tokens, cotangent, *factors, *ahead)


def own_kernel(gate, up, down, *refs):
    units, (held, sems) = refs[:2], refs[2:]
    rows = units[0].shape[1]
    down_copy = pltpu.make_async_copy(down, held, sems.at[0])
    down_copy.start()
    copies = []
    for half, unit in enumerate(units):
        for which, ref in enumerate((gate, up)):
            copies.append(
                pltpu.make_async_copy(
                    ref.at[pl.ds(half * rows, rows)], unit.at[which], sems.at[1 + len(copies)]
                )
            )
    for copy in copies:
        copy.start()
    down_copy.wait()
    for half, unit in enumerate(units):
        part = slice(half * rows, (half + 1) * rows)
        unit[2] = held[:, part].astype(jnp.float32).T.astype(jnp.bfloat16)
    for copy in copies:
        copy.wait()


def own_units(gate, up, down):
    rows, hidden = gate.shape
    return pl.pallas_call(
        own_kernel,
        in_specs=[pl.BlockSpec(memory_space=pl.ANY)] * 3,
        out_specs=[pl.BlockSpec(memory_space=pltpu.VMEM)] * 2,
        out_shape=[pltpu.VMEM((3, rows // 2, hidden), jnp.bfloat16)] * 2,
        scratch_shapes=[
            pltpu.VMEM((hidden, rows), jnp.bfloat16),
            pltpu.SemaphoreType.DMA((5,)),
        ],
        compiler_params=pltpu.CompilerParams(vmem_limit_bytes=LIMITS["low"] * MEBIBYTE),
        cost_estimate=pl.CostEstimate(flops=MEBIBYTE, bytes_accessed=0, transcendentals=0),
        name="own_units",
    )(*[pltpu.with_memory_space_constraint(array, pltpu.HBM) for array in (gate, up, down)])


def nothing_kernel(*refs):
    pass


def hold(arrays, ahead):
    anywhere = pl.BlockSpec(memory_space=pl.ANY)
    return pl.pallas_call(
        nothing_kernel,
        in_specs=[anywhere] * (len(arrays) + len(ahead)),
        out_specs=[anywhere] * len(arrays),
        out_shape=[jax.ShapeDtypeStruct(array.shape, array.dtype) for array in arrays],
        input_output_aliases={number: number for number in range(len(arrays))},
        compiler_params=pltpu.CompilerParams(vmem_limit_bytes=MEBIBYTE),
        cost_estimate=pl.CostEstimate(flops=1, bytes_accessed=1, transcendentals=0),
        name="hold",
    )(*arrays, *ahead)


def pair_kernel(first, second, *refs):
    refs[-1][0] = first[...]
    refs[-1][1] = second[...]


def pair(first, second, ahead):
    return vmem_call(
        pair_kernel,
        [],
        [first, second],
        ahead,
        [((2, *first.shape), first.dtype)],
        {},
        [],
        LIMITS["small"],
        COSTS["pair"],
        "pair",
    )[0]


def sums_kernel(masks, order, n_arrays, last, here, *refs):
    gate_low, up_low, back_low, gate_out, up_out, down_in, tokens, cotangent = refs[:8]
    units = []
    for ref in refs[8 : 8 + n_arrays]:
        units += [ref] if len(ref.shape) == 3 else [ref.at[0], ref.at[1]]
    units = [units[number] for number in order]
    outs = refs[8 + n_arrays :]
    sums, rest, full = outs[: 3 * HALVES], outs[3 * HALVES : 3 * HALVES + 2], outs[-7:-5]
    held_tokens, held_cotangent, held_down, row_sems, unit_sems = outs[-5:]
    half_rows, hidden = units[0].shape[1:]
    rows = 2 * half_rows
    tile = tokens.shape[0] // HALVES

    def unit_copies(which):
        copies = []
        for number, unit in enumerate(units):
            if which == 2:
                target = held_down.at[pl.ds(number * half_rows, half_rows)]
            else:
                block = lax.bitwise_xor(here[0], masks[number // 2])
                row = pl.multiple_of((2 * block + number % 2) * half_rows, half_rows)
                target = full[which].at[pl.ds(row, half_rows)]
            copies.append(
                pltpu.make_async_copy(
                    unit.at[which], target, unit_sems.at[which * len(units) + number]
                )
            )
        return copies

    def row_copy(which, half):
        source, target = ((tokens, held_tokens), (cotangent, held_cotangent))[which]
        part = pl.ds(half * tile, tile)
        return pltpu.make_async_copy(
            source.at[part], target.at[part], row_sems.at[which * HALVES + half]
        )

    loads = [*unit_copies(0), row_copy(0, 0), *unit_copies(1), row_copy(1, 0), *unit_copies(2)]
    loads += [row_copy(which, half) for half in range(1, HALVES) for which in range(2)]
    for load in loads:
        load.start()
    for half in range(HALVES):
        part = slice(half * tile, (half + 1) * tile)
        for which, (low, factor) in enumerate(
            ((gate_low, gate_out), (up_low, up_out), (back_low, down_in))
        ):
            if half == 0:
                for copy in unit_copies(which):
                    copy.wait()
            if which != 1:
                row_copy(which // 2, half).wait()
                ref = (held_tokens, held_cotangent)[which // 2]
                left = width_part(ref, part, here, masks, rows)
                rest[which // 2][part, :] = width_part(ref, part, here, last, rows)
            for column in range(0, hidden, TILE):
                span = slice(column, column + TILE)
                if which == 2:
                    right = held_down[:, span]
                else:
                    right = jnp.concatenate(
                        [
                            full[which][
                                pl.ds(
                                    pl.multiple_of(lax.bitwise_xor(here[0], mask) * rows, rows), rows
                                ),
                                span,
                            ]
                            for mask in masks
                        ]
                    )
                sums[3 * half + which][:, span] = matrix_product(
                    left, right
                ) + adapter_scaling * matrix_product(low[part, :], factor[:, span])


def width_sums(here, tokens, cotangent, lows, factors, masks, order, arrays, last):
    rows, width = tokens.shape
    _, half, hidden = arrays[0].shape[-3:]
    vmem, anywhere = pl.BlockSpec(memory_space=pltpu.VMEM), pl.BlockSpec(memory_space=pl.ANY)
    shapes = [((rows // HALVES, hidden), jnp.float32)] * (3 * HALVES)
    shapes += [((rows, 2 * half * len(last)), jnp.bfloat16)] * 2
    shapes += [((width, hidden), jnp.bfloat16)] * 2
    outs = pl.pallas_call(
        functools.partial(sums_kernel, masks, order, len(arrays), last),
        in_specs=[pl.BlockSpec(memory_space=pltpu.SMEM)]
        + [vmem] * 6
        + [anywhere] * (2 + len(arrays)),
        out_specs=[vmem] * len(shapes),
        out_shape=[pltpu.VMEM(shape, kind) for shape, kind in shapes],
        scratch_shapes=[
            pltpu.VMEM((rows, width), jnp.bfloat16),
            pltpu.VMEM((rows, width), jnp.bfloat16),
            pltpu.VMEM((half * len(order), hidden), jnp.bfloat16),
            pltpu.SemaphoreType.DMA((2 * HALVES,)),
            pltpu.SemaphoreType.DMA((3 * len(order),)),
        ],
        compiler_params=pltpu.CompilerParams(vmem_limit_bytes=LIMITS["sums"] * MEBIBYTE),
        cost_estimate=pl.CostEstimate(flops=COSTS["sums"], bytes_accessed=0, transcendentals=0),
        name="width_sums",
    )(here, *lows, *factors, tokens, cotangent, *arrays)
    return outs[: 3 * HALVES], outs[3 * HALVES : -2], outs[-2:]


def last_kernel(half, here, left, back, gate_out, up_out, *refs):
    units, sums = refs[:4], refs[4:7]
    hidden_out, gate_grad_out, up_grad_out, low_out = refs[-4:]
    rows, hidden = hidden_out.shape
    part = slice(half * rows, (half + 1) * rows)
    gate_low = up_low = 0.0
    for column in range(0, hidden, STRIP):
        span = slice(column, column + STRIP)
        gate = sums[0][:, span] + matrix_product(left[part, :], stacked(units, 0, span))
        up = sums[1][:, span] + matrix_product(left[part, :], stacked(units, 1, span))
        hidden_grad = sums[2][:, span] + matrix_product(back[part, :], stacked(units, 2, span))
        sig = 1.0 / (1.0 + jnp.exp(-gate))
        gated = gate * sig
        hidden_out[:, span] = (gated * up).astype(jnp.bfloat16)
        gate_grad = (hidden_grad * up * sig * (1.0 + gate * (1.0 - sig))).astype(jnp.bfloat16)
        up_grad = (hidden_grad * gated).astype(jnp.bfloat16)
        gate_grad_out[:, span] = gate_grad
        up_grad_out[:, span] = up_grad
        gate_low += contract_trailing_axis(gate_grad, gate_out[:, span])
        up_low += contract_trailing_axis(up_grad, up_out[:, span])
    low_out[...] = jnp.concatenate([gate_low, up_low], axis=1)


def hidden_and_grads(half, here, parts, factors, tail, sums, ahead):
    rows = parts[0].shape[0] // HALVES
    rank, hidden = factors[0].shape
    return vmem_call(
        functools.partial(last_kernel, half),
        [here],
        [*parts, *factors, *tail, *sums[3 * half : 3 * half + 3]],
        ahead,
        [((rows, hidden), jnp.bfloat16)] * 3 + [((rows, 2 * rank), jnp.float32)],
        {},
        [],
        LIMITS["last"],
        COSTS["last"],
        "hidden_and_grads",
    )


def quarter_rows(here, quarter, full, tail, which, columns):
    rows = 2 * tail[0].shape[1]
    blocks = []
    for number in range(columns // rows):
        block = quarter * (columns // rows) + number
        mask = lax.bitwise_xor(here[0], block)
        held = full[pl.ds(pl.multiple_of(block * rows, rows), rows), :]
        near, far = (
            jnp.concatenate([unit[which] for unit in units]) for units in (tail[:2], tail[2:])
        )
        blocks.append(jnp.where(mask == 7, far, jnp.where(mask == 3, near, held)))
    return jnp.concatenate(blocks)


def token_grad_kernel(mode, step, here, gate_grad, up_grad, low, factor, gate, up, *refs):
    tail, refs = refs[:4], refs[4:]
    came = refs[: {"first": 0, "sum": 1, "both": 3, "last": 2}[mode]]
    outs = refs[-2:] if mode == "both" else refs[-1:]
    columns = outs[0].shape[1]
    quarter = sum(
        jnp.where(here[1] == place, order[step], 0) for place, order in enumerate(QUARTER_ORDER)
    )
    span = pl.ds(pl.multiple_of(quarter * columns, columns), columns)
    total = contract_trailing_axis(
        gate_grad[...], quarter_rows(here, quarter, gate, tail, 0, columns)
    )
    total += contract_trailing_axis(up_grad[...], quarter_rows(here, quarter, up, tail, 1, columns))
    total += matrix_product((adapter_scaling * low[...]).astype(jnp.bfloat16), factor[:, span])
    came = [ref[...].astype(jnp.float32) for ref in came]
    if mode == "both":
        first, left, right = came
        outs[0][...] = (jnp.where(here[1] == 2, first, total) + left).astype(jnp.bfloat16)
        outs[1][...] = (jnp.where(here[1] == 1, first, total) + right).astype(jnp.bfloat16)
    else:
        outs[0][...] = sum(came, total).astype(jnp.bfloat16)


def token_grad(mode, step, here, arrays, columns, came, ahead):
    rows, hidden = arrays[0].shape
    outs = vmem_call(
        functools.partial(token_grad_kernel, mode, step),
        [here],
        [*arrays, *came],
        ahead,
        [((rows, columns), jnp.bfloat16)] * (2 if mode == "both" else 1),
        {},
        [],
        LIMITS["token"],
        COSTS["token"],
        "token_grad",
    )
    return outs if mode == "both" else outs[0]


def last_token_grad(step, half, here, arrays, columns, came, ahead, before):
    rows, hidden = arrays[0].shape
    arrays = [*arrays, *came]
    return pl.pallas_call(
        functools.partial(token_grad_kernel, "last", step),
        grid=(1,),
        in_specs=[pl.BlockSpec(memory_space=pltpu.SMEM)]
        + [pl.BlockSpec(memory_space=pltpu.VMEM)] * len(arrays)
        + [pl.BlockSpec(memory_space=pl.ANY)] * (len(before) + len(ahead)),
        out_specs=pl.BlockSpec((rows, columns), lambda i: (half, 0)),
        out_shape=jax.ShapeDtypeStruct((HALVES * rows, columns), jnp.bfloat16),
        input_output_aliases={1 + len(arrays): 0} if before else {},
        compiler_params=pltpu.CompilerParams(vmem_limit_bytes=LIMITS["token"] * MEBIBYTE),
        cost_estimate=pl.CostEstimate(
            flops=COSTS["token"],
            bytes_accessed=0,
            transcendentals=0,
        ),
        name="last_token_grad",
    )(
        here,
        *[pltpu.with_memory_space_constraint(array, pltpu.VMEM) for array in arrays],
        *before,
        *ahead,
    )


def adapter_kernel(scaling, here, *refs):
    hidden, gate_grad, up_grad, low = (
        refs[number * HALVES : (number + 1) * HALVES] for number in range(4)
    )
    tokens, cotangent, turned, down_in = refs[4 * HALVES : 4 * HALVES + 4]
    keep, send, wide, narrow = refs[-4:]
    rank = down_in.shape[0]
    rows = hidden[0].shape[0]
    parts = [slice(half * rows, (half + 1) * rows) for half in range(HALVES)]
    wide[: 2 * rank, :] = scaling * sum(
        matrix_product(low[half][...].T.astype(jnp.bfloat16), tokens[part, :])
        for half, part in enumerate(parts)
    )
    wide[2 * rank :, :] = scaling * sum(
        matrix_product(
            contract_trailing_axis(down_in[...], hidden[half][...]).astype(jnp.bfloat16),
            cotangent[part, :],
        )
        for half, part in enumerate(parts)
    )
    for number, arrays in enumerate((hidden, gate_grad, up_grad)):
        source = (2, 0, 1)[number]
        narrow[number * rank : (number + 1) * rank, :] = scaling * sum(
            matrix_product(turned[source * rank : (source + 1) * rank, part], arrays[half][...])
            for half, part in enumerate(parts)
        )
    groups = 2 * keep.shape[0]
    wide_columns, narrow_columns = wide.shape[1] // groups, narrow.shape[1] // groups
    for mask in range(groups):
        out = (keep if mask < groups // 2 else send).at[mask % (groups // 2)]
        block = lax.bitwise_xor(here[0], mask)
        out[:, :wide_columns] = wide[
            :, pl.ds(pl.multiple_of(block * wide_columns, wide_columns), wide_columns)
        ]
        out[:, wide_columns:] = narrow[
            :, pl.ds(pl.multiple_of(block * narrow_columns, narrow_columns), narrow_columns)
        ]


def adapter_grads(scaling, here, groups, arrays, ahead):
    rows, width = arrays[-4].shape
    rank, hidden = arrays[-1].shape
    return vmem_call(
        functools.partial(adapter_kernel, scaling),
        [here],
        arrays,
        ahead,
        [((groups // 2, 3 * rank, (width + hidden) // groups), jnp.float32)] * 2,
        {},
        [pltpu.VMEM((3 * rank, width), jnp.float32), pltpu.VMEM((3 * rank, hidden), jnp.float32)],
        LIMITS["adapter"],
        COSTS["adapter"],
        "adapter_grads",
    )


def halve_kernel(here, keep, came, kept, send):
    count = kept.shape[0]
    kept[...] = keep[:count] + came[:count].astype(jnp.float32)
    send[...] = (keep[count:] + came[count:].astype(jnp.float32)).astype(send.dtype)


def halve(here, keep, came):
    shape = (keep.shape[0] // 2, *keep.shape[1:])
    return vmem_call(
        halve_kernel,
        [here],
        [keep, came],
        [],
        [(shape, jnp.float32), (shape, jnp.bfloat16)],
        {},
        [],
        LIMITS["small"],
        COSTS["small"],
        "halve",
    )


def sum_kernel(here, keep, *refs):
    refs[-1][...] = sum((ref[...].astype(jnp.float32) for ref in refs[:-1]), keep[...])


def last_sum(here, keep, came):
    return vmem_call(
        sum_kernel,
        [here],
        [keep, *came],
        [],
        [(keep.shape, jnp.float32)],
        {},
        [],
        LIMITS["small"],
        COSTS["small"],
        "last_sum",
        True,
    )[0]


def turn_kernel(wide_columns, here, kept, came, narrow, *refs):
    outs, wide = refs[:-1], refs[-1]
    total = kept[0] + came[0].astype(jnp.float32)
    narrow[...] = total[:, wide_columns:]
    wide[...] = total[:, :wide_columns].T
    for mask, out in enumerate(outs):
        rows = out.shape[0]
        block = pl.ds(pl.multiple_of(lax.bitwise_xor(here[1], mask) * rows, rows), rows)
        out[...] = wide[block, :].astype(out.dtype)


def turn(here, keep, came, wide_columns, quarters):
    _, rows, columns = keep.shape
    return vmem_call(
        functools.partial(turn_kernel, wide_columns),
        [here],
        [keep, came],
        [],
        [((rows, columns - wide_columns), jnp.float32)]
        + [
            ((wide_columns // quarters, rows), jnp.bfloat16 if mask else jnp.float32)
            for mask in range(quarters)
        ],
        {},
        [pltpu.VMEM((wide_columns, rows), jnp.float32)],
        LIMITS["small"],
        COSTS["small"],
        "turn",
    )


def whole_kernel(here, near, far, out):
    columns = near.shape[2]
    for number in range(2 * near.shape[0]):
        ref = near if number < near.shape[0] else far
        block = lax.bitwise_xor(here[0], number) * columns
        out[:, pl.ds(pl.multiple_of(block, columns), columns)] = ref[number % near.shape[0]]


def whole(here, near, far):
    count, rows, columns = near.shape
    return vmem_call(
        whole_kernel,
        [here],
        [near, far],
        [],
        [((rows, 2 * count * columns), near.dtype)],
        {},
        [],
        LIMITS["small"],
        COSTS["small"],
        "whole",
        True,
    )[0]


def square_plane(
    tokens,
    cotangent,
    gate_frozen_matrix,
    up_frozen_matrix,
    down_frozen_matrix,
    gate_adapter_input_factor,
    up_adapter_input_factor,
    gate_adapter_output_factor,
    up_adapter_output_factor,
    down_adapter_input_factor,
    down_leave,
):
    groups = lax.axis_size(("cuts", "fsdp"))
    quarters = lax.axis_size("tp")
    rows, width = tokens.shape
    gradient_scaling = adapter_scaling / math.sqrt(rows * groups)
    here = jnp.stack([lax.axis_index(("cuts", "fsdp")), lax.axis_index("tp")]).astype(jnp.int32)
    gate_in, up_in, leave, down_in = (
        array.T
        for array in (
            gate_adapter_input_factor,
            up_adapter_input_factor,
            down_leave,
            down_adapter_input_factor,
        )
    )
    gate_out, up_out = gate_adapter_output_factor, up_adapter_output_factor

    units = {}
    units[0, 0], units[0, 1] = own_units(
        gate_frozen_matrix, up_frozen_matrix, down_frozen_matrix
    )
    units[1, 0] = flip(units[0, 0], "fsdp", 1)
    units[2, 1] = flip(units[0, 1], "fsdp", 2)
    units[1, 1] = flip(units[0, 1], "fsdp", 1)
    units[2, 0] = flip(units[0, 0], "fsdp", 2)
    units[3, 0] = flip(units[1, 0], "fsdp", 2)
    units[3, 1] = flip(units[2, 1], "fsdp", 1)
    for half in range(2):
        units[4, half] = flip(units[0, half], "cuts", 1)
    *lows, turned = low_rank_values(
        tokens, cotangent, [gate_in, up_in, leave], [here, *[units[key] for key in ((1, 0), (2, 1), (4, 0), (4, 1))]]
    )
    pairs = {}
    for number, (one, two, ahead) in enumerate(
        (((1, 0), (2, 1), [turned]), ((1, 1), (2, 0), [turned]))
    ):
        pairs[number] = flip(pair(units[one], units[two], ahead), "cuts", 1)
    keys = [(0, 0), (0, 1), (1, 0), (1, 1), (2, 0), (2, 1), (4, 0), (4, 1)]
    placed = keys + [(5, 0), (6, 1), (5, 1), (6, 0)]
    arrays = [units[key] for key in keys] + [pairs[0], pairs[1]]
    masks = (0, 1, 2, 4, 5, 6)
    order = [placed.index((mask, half)) for mask in masks for half in range(2)]
    sums, parts, full = width_sums(
        here, tokens, cotangent, lows, [gate_out, up_out, down_in], masks, order, arrays, (3, 7)
    )
    tail = list(hold([units[3, 0], units[3, 1]], [sums[0]]))
    tail += [flip(unit, "cuts", 1) for unit in tail]

    factor = jnp.concatenate([gate_in, up_in])
    shift = lambda array, pairs: lax.ppermute(array, "tp", pairs)
    states, first = [], []
    share = lambda step, half, mode, came=(), ahead=(): token_grad(
        mode,
        step,
        here,
        [*states[half][1:], factor, *full, *tail],
        width // quarters,
        came,
        ahead,
    )
    both = range(HALVES)
    for half in both:
        state = hidden_and_grads(
            half, here, parts, [gate_out, up_out], tail, sums, first[:]
        )
        states.append(state)
        first.append(share(0, half, "first"))
    came = [shift(part, [(0, 1), (3, 2)]) for part in first]
    partial = []
    for half in both:
        partial.append(share(1, half, "sum", [came[half]], partial or first[1:]))
    second = partial
    from_left = [shift(part, [(0, 1), (1, 2)]) for part in partial]
    from_right = [shift(part, [(3, 2), (2, 1)]) for part in partial]
    keep, send = adapter_grads(
        gradient_scaling,
        here,
        groups,
        [
            *[state[number] for number in range(4) for state in states],
            tokens,
            cotangent,
            turned,
            down_in,
        ],
        [came[0], *first],
    )
    keep, send = halve(here, keep, flip(send, "cuts", 1))
    keep, send = halve(here, keep, flip(send, "fsdp", 2))
    narrow, keep, *send = turn(here, keep, flip(send, "fsdp", 1), width // groups, quarters)
    wide_grads = last_sum(
        here, keep, [flip(part, "tp", 1 + number) for number, part in enumerate(send)]
    )
    near = jnp.stack([narrow, flip(narrow, "fsdp", 1)])
    near = jnp.concatenate([near, flip(near, "fsdp", 2)])
    narrow_turned = whole(here, near, flip(near, "cuts", 1))
    narrow_grads = narrow_turned.T

    partial = []
    for half in both:
        partial.append(
            share(
                2,
                half,
                "both",
                [first[half], from_left[half], from_right[half]],
                partial[0][:1] if partial else second[1:],
            )
        )
    from_left = [shift(part[0], [(0, 1), (1, 2), (2, 3)]) for part in partial]
    from_right = [shift(part[1], [(3, 2), (2, 1), (1, 0)]) for part in partial]

    results = []
    for half in both:
        results.append(
            last_token_grad(
                3,
                half,
                here,
                [*states[half][1:], factor, *full, *tail],
                width // quarters,
                [from_left[half], from_right[half]],
                [] if half else partial[1],
                results[:],
            )
        )
    token_input_gradient = results[-1]
    return (token_input_gradient, wide_grads, narrow_grads)


def per_device(*arrays):
    sizes = [lax.axis_size(axis) for axis in ("cuts", "fsdp", "tp")]
    return (square_plane if sizes == [2, 4, 4] else any_plane)(*arrays)


def solution(mesh):
    in_specs = (
        P(("cuts", "fsdp"), None),
        P(("cuts", "fsdp"), None),
        P(("cuts", "fsdp"), "tp"),
        P(("cuts", "fsdp"), "tp"),
        P("tp", ("cuts", "fsdp")),
        P(),
        P(),
        P(None, "tp"),
        P(None, "tp"),
        P("tp", None),
        P(),
    )
    out_specs = (P(("cuts", "fsdp"), "tp"), P(("cuts", "fsdp", "tp"), None), P("tp", None))
    return jax.shard_map(
        per_device, mesh=mesh, in_specs=in_specs, out_specs=out_specs, check_vma=False
    )
```

```python
import functools
import math

import jax
import jax.numpy as jnp
from jax import lax
from jax.experimental import pallas as pl
from jax.experimental.pallas import tpu as pltpu
from jax.sharding import PartitionSpec as P

adapter_scaling = 0.5
MEBIBYTE = 1024 * 1024
COST = 1
HALVES = 2
COSTS = {"sums": 1, "pair": 1, "small": 1, "token": 20 * 10**9, "adapter": 20 * 10**9, "last": 10**11}
LIMITS = {"low": 6, "sums": 32, "last": 14, "token": 8, "adapter": 12, "small": 4}
TILE = 512
STRIP = 256
QUARTER_ORDER = ((3, 2, 1, 0), (0, 3, 2, 1), (3, 0, 1, 2), (0, 1, 2, 3))


def matrix_product(left, right):
    return jnp.dot(left, right, preferred_element_type=jnp.float32)


def contract_trailing_axis(left, right):
    return lax.dot_general(
        left, right, (((1,), (1,)), ((), ())), preferred_element_type=jnp.float32
    )


def contract_first(left, right):
    return lax.dot_general(
        left, right, (((0,), (0,)), ((), ())), preferred_element_type=jnp.float32
    )


def any_plane(
    tokens,
    cotangent,
    gate_frozen_matrix,
    up_frozen_matrix,
    down_frozen_matrix,
    gate_adapter_input_factor,
    up_adapter_input_factor,
    gate_adapter_output_factor,
    up_adapter_output_factor,
    down_adapter_input_factor,
    down_leave,
):
    token_groups = lax.axis_size(("cuts", "fsdp"))
    quarters = lax.axis_size("tp")
    tp_index = lax.axis_index("tp")
    token_rows = tokens.shape[0]
    width = tokens.shape[1]
    gradient_scaling = adapter_scaling / math.sqrt(token_rows * token_groups)
    gate_adapter_hidden = matrix_product(tokens, gate_adapter_input_factor).astype(jnp.bfloat16)
    up_adapter_hidden = matrix_product(tokens, up_adapter_input_factor).astype(jnp.bfloat16)
    pieces = (
        lax.all_gather(gate_frozen_matrix, ("cuts", "fsdp"), axis=0, tiled=True),
        lax.all_gather(up_frozen_matrix, ("cuts", "fsdp"), axis=0, tiled=True),
    )
    columns = tokens
    gate_frozen_output = matrix_product(columns, pieces[0])
    up_frozen_output = matrix_product(columns, pieces[1])
    gate_preactivation = gate_frozen_output + adapter_scaling * matrix_product(
        gate_adapter_hidden, gate_adapter_output_factor
    )
    up_preactivation = up_frozen_output + adapter_scaling * matrix_product(
        up_adapter_hidden, up_adapter_output_factor
    )
    sig = jax.nn.sigmoid(gate_preactivation)
    hidden = (gate_preactivation * sig * up_preactivation).astype(jnp.bfloat16)
    down_part = matrix_product(hidden, down_adapter_input_factor)
    down_low = lax.psum(down_part.astype(jnp.bfloat16), "tp")
    backward_adapter_input = matrix_product(cotangent, down_leave).astype(jnp.bfloat16)
    columns = cotangent
    hidden_state_gradient = contract_trailing_axis(
        columns, lax.all_gather(down_frozen_matrix, ("cuts", "fsdp"), axis=1, tiled=True)
    )
    hidden_state_gradient = hidden_state_gradient + adapter_scaling * contract_trailing_axis(
        backward_adapter_input, down_adapter_input_factor
    )
    gate_output_gradient = (
        hidden_state_gradient * up_preactivation * sig * (1.0 + gate_preactivation * (1.0 - sig))
    ).astype(jnp.bfloat16)
    up_output_gradient = (hidden_state_gradient * gate_preactivation * sig).astype(jnp.bfloat16)
    gate_part = contract_trailing_axis(gate_output_gradient, gate_adapter_output_factor)
    up_part = contract_trailing_axis(up_output_gradient, up_adapter_output_factor)
    gate_sum, up_sum = lax.psum((gate_part, up_part), "tp")
    gate_backward_adapter = gate_sum.astype(jnp.bfloat16)
    up_backward_adapter = up_sum.astype(jnp.bfloat16)
    pieces = lax.all_gather(
        (gate_frozen_matrix, up_frozen_matrix), ("cuts", "fsdp"), axis=0, tiled=True
    )
    partial_value = contract_trailing_axis(
        gate_output_gradient, pieces[0]
    ) + contract_trailing_axis(up_output_gradient, pieces[1])
    frozen_path_gradient = lax.psum_scatter(partial_value, "tp", scatter_dimension=1, tiled=True)
    slice_width = width // quarters
    gate_slice = lax.dynamic_slice_in_dim(
        gate_adapter_input_factor, tp_index * slice_width, slice_width, 0
    )
    up_slice = lax.dynamic_slice_in_dim(
        up_adapter_input_factor, tp_index * slice_width, slice_width, 0
    )
    adapter_hidden_gradient = contract_trailing_axis(
        gate_backward_adapter, gate_slice
    ) + contract_trailing_axis(up_backward_adapter, up_slice)
    token_input_gradient = (
        frozen_path_gradient + adapter_scaling * adapter_hidden_gradient
    ).astype(jnp.bfloat16)
    narrow_part = gradient_scaling * jnp.concatenate(
        [
            contract_first(hidden, backward_adapter_input),
            contract_first(gate_output_gradient, gate_adapter_hidden),
            contract_first(up_output_gradient, up_adapter_hidden),
        ],
        axis=1,
    )
    narrow_grads = lax.psum(narrow_part, ("cuts", "fsdp"))
    token_side = jnp.concatenate([gate_backward_adapter, up_backward_adapter], axis=1)
    group_rows = lax.psum_scatter(
        gradient_scaling
        * jnp.concatenate(
            [contract_first(tokens, token_side), contract_first(cotangent, down_low)], axis=1
        ),
        ("cuts", "fsdp"),
        scatter_dimension=0,
        tiled=True,
    )
    fine_rows = width // (token_groups * quarters)
    wide_grads = lax.dynamic_slice_in_dim(group_rows, tp_index * fine_rows, fine_rows, 0)
    return (token_input_gradient, wide_grads, narrow_grads)


def flip(array, axis, bit):
    size = lax.axis_size(axis)
    return lax.ppermute(array, axis, [(i, i ^ bit) for i in range(size)])


def vmem_call(
    kernel, scalars, arrays, ahead, results, aliases, scratch, limit, flops, name, final=False
):
    vmem = pl.BlockSpec(memory_space=pltpu.VMEM)
    first = len(scalars)
    return pl.pallas_call(
        kernel,
        in_specs=[pl.BlockSpec(memory_space=pltpu.SMEM)] * first
        + [vmem] * len(arrays)
        + [pl.BlockSpec(memory_space=pl.ANY)] * len(ahead),
        out_specs=[vmem] * len(results),
        out_shape=[
            jax.ShapeDtypeStruct(shape, kind) if final else pltpu.VMEM(shape, kind)
            for shape, kind in results
        ],
        scratch_shapes=scratch,
        input_output_aliases={first + source: target for source, target in aliases.items()},
        compiler_params=pltpu.CompilerParams(vmem_limit_bytes=limit * MEBIBYTE),
        cost_estimate=pl.CostEstimate(flops=COST * flops, bytes_accessed=0, transcendentals=0),
        name=name,
    )(
        *scalars,
        *[pltpu.with_memory_space_constraint(array, pltpu.VMEM) for array in arrays],
        *ahead,
    )


def width_part(ref, part, here, masks, rows):
    return jnp.concatenate(
        [
            ref[part, pl.ds(pl.multiple_of(lax.bitwise_xor(here[0], mask) * rows, rows), rows)]
            for mask in masks
        ],
        axis=1,
    )


def stacked(units, which, span):
    return jnp.concatenate([unit[which, :, span] for unit in units], axis=0)


def lows_kernel(tokens, cotangent, gate_in, up_in, leave, *refs):
    gate_low, up_low, back_low, turned = refs[-4:]
    rank = leave.shape[0]
    for number, (ref, factor, out) in enumerate(
        ((tokens, gate_in, gate_low), (tokens, up_in, up_low), (cotangent, leave, back_low))
    ):
        low = contract_trailing_axis(ref[...], factor[...]).astype(jnp.bfloat16)
        out[...] = low
        turned[number * rank : (number + 1) * rank, :] = low.astype(jnp.float32).T.astype(
            jnp.bfloat16
        )


def low_rank_values(tokens, cotangent, factors, ahead):
    rows, width = tokens.shape
    rank = factors[0].shape[0]
    tile = rows // 4
    by_rows = lambda columns: pl.BlockSpec((tile, columns), lambda i: (i, 0))
    return pl.pallas_call(
        lows_kernel,
        grid=(rows // tile,),
        in_specs=[by_rows(width)] * 2
        + [pl.BlockSpec((rank, width), lambda i: (0, 0))] * 3
        + [pl.BlockSpec(memory_space=pl.ANY)] * len(ahead),
        out_specs=[by_rows(rank)] * 3 + [pl.BlockSpec((3 * rank, tile), lambda i: (0, i))],
        out_shape=[jax.ShapeDtypeStruct((rows, rank), jnp.bfloat16)] * 3
        + [jax.ShapeDtypeStruct((3 * rank, rows), jnp.bfloat16)],
        compiler_params=pltpu.CompilerParams(vmem_limit_bytes=LIMITS["low"] * MEBIBYTE),
        cost_estimate=pl.CostEstimate(
            flops=480 * COST * rows * width * rank, bytes_accessed=0, transcendentals=0
        ),
        name="low_rank_values",
    )(tokens, cotangent, *factors, *ahead)


def own_kernel(gate, up, down, *refs):
    units, both, (held, sems) = refs[:2], refs[2], refs[3:]
    rows = units[0].shape[1]
    down_copy = pltpu.make_async_copy(down, held, sems.at[0])
    down_copy.start()
    copies = []
    for half, unit in enumerate(units):
        for which, ref in enumerate((gate, up)):
            for target in (unit.at[which], both.at[half, which]):
                copies.append(
                    pltpu.make_async_copy(
                        ref.at[pl.ds(half * rows, rows)], target, sems.at[1 + len(copies)]
                    )
                )
    for copy in copies:
        copy.start()
    down_copy.wait()
    for half, unit in enumerate(units):
        part = slice(half * rows, (half + 1) * rows)
        turned = held[:, part].astype(jnp.float32).T.astype(jnp.bfloat16)
        unit[2] = turned
        both[half, 2] = turned
    for copy in copies:
        copy.wait()


def own_units(gate, up, down):
    rows, hidden = gate.shape
    unit = (3, rows // 2, hidden)
    return pl.pallas_call(
        own_kernel,
        in_specs=[pl.BlockSpec(memory_space=pl.ANY)] * 3,
        out_specs=[pl.BlockSpec(memory_space=pltpu.VMEM)] * 3,
        out_shape=[pltpu.VMEM(shape, jnp.bfloat16) for shape in (unit, unit, (2, *unit))],
        scratch_shapes=[
            pltpu.VMEM((hidden, rows), jnp.bfloat16),
            pltpu.SemaphoreType.DMA((9,)),
        ],
        compiler_params=pltpu.CompilerParams(vmem_limit_bytes=LIMITS["low"] * MEBIBYTE),
        cost_estimate=pl.CostEstimate(flops=MEBIBYTE, bytes_accessed=0, transcendentals=0),
        name="own_units",
    )(*[pltpu.with_memory_space_constraint(array, pltpu.HBM) for array in (gate, up, down)])


def nothing_kernel(*refs):
    pass


def hold(arrays, ahead):
    anywhere = pl.BlockSpec(memory_space=pl.ANY)
    return pl.pallas_call(
        nothing_kernel,
        in_specs=[anywhere] * (len(arrays) + len(ahead)),
        out_specs=[anywhere] * len(arrays),
        out_shape=[jax.ShapeDtypeStruct(array.shape, array.dtype) for array in arrays],
        input_output_aliases={number: number for number in range(len(arrays))},
        compiler_params=pltpu.CompilerParams(vmem_limit_bytes=MEBIBYTE),
        cost_estimate=pl.CostEstimate(flops=1, bytes_accessed=1, transcendentals=0),
        name="hold",
    )(*arrays, *ahead)


def pair_kernel(first, second, *refs):
    refs[-1][0] = first[...]
    refs[-1][1] = second[...]


def pair(first, second, ahead):
    return vmem_call(
        pair_kernel,
        [],
        [first, second],
        ahead,
        [((2, *first.shape), first.dtype)],
        {},
        [],
        LIMITS["small"],
        COSTS["pair"],
        "pair",
    )[0]


def sums_kernel(masks, order, n_arrays, last, here, *refs):
    gate_low, up_low, back_low, gate_out, up_out, down_in, tokens, cotangent = refs[:8]
    units = []
    for ref in refs[8 : 8 + n_arrays]:
        units += [ref] if len(ref.shape) == 3 else [ref.at[0], ref.at[1]]
    units = [units[number] for number in order]
    outs = refs[8 + n_arrays :]
    sums, rest, full = outs[: 3 * HALVES], outs[3 * HALVES : 3 * HALVES + 2], outs[-7:-5]
    held_tokens, held_cotangent, held_down, row_sems, unit_sems = outs[-5:]
    half_rows, hidden = units[0].shape[1:]
    rows = 2 * half_rows
    tile = tokens.shape[0] // HALVES

    def unit_copies(which):
        copies = []
        for number, unit in enumerate(units):
            if which == 2:
                target = held_down.at[pl.ds(number * half_rows, half_rows)]
            else:
                block = lax.bitwise_xor(here[0], masks[number // 2])
                row = pl.multiple_of((2 * block + number % 2) * half_rows, half_rows)
                target = full[which].at[pl.ds(row, half_rows)]
            copies.append(
                pltpu.make_async_copy(
                    unit.at[which], target, unit_sems.at[which * len(units) + number]
                )
            )
        return copies

    def row_copy(which, half):
        source, target = ((tokens, held_tokens), (cotangent, held_cotangent))[which]
        part = pl.ds(half * tile, tile)
        return pltpu.make_async_copy(
            source.at[part], target.at[part], row_sems.at[which * HALVES + half]
        )

    loads = [*unit_copies(0), row_copy(0, 0), *unit_copies(1), row_copy(1, 0), *unit_copies(2)]
    loads += [row_copy(which, half) for half in range(1, HALVES) for which in range(2)]
    for load in loads:
        load.start()
    for half in range(HALVES):
        part = slice(half * tile, (half + 1) * tile)
        for which, (low, factor) in enumerate(
            ((gate_low, gate_out), (up_low, up_out), (back_low, down_in))
        ):
            if half == 0:
                for copy in unit_copies(which):
                    copy.wait()
            if which != 1:
                row_copy(which // 2, half).wait()
                ref = (held_tokens, held_cotangent)[which // 2]
                left = width_part(ref, part, here, masks, rows)
                rest[which // 2][part, :] = width_part(ref, part, here, last, rows)
            for column in range(0, hidden, TILE):
                span = slice(column, column + TILE)
                if which == 2:
                    right = held_down[:, span]
                else:
                    right = jnp.concatenate(
                        [
                            full[which][
                                pl.ds(
                                    pl.multiple_of(lax.bitwise_xor(here[0], mask) * rows, rows), rows
                                ),
                                span,
                            ]
                            for mask in masks
                        ]
                    )
                sums[3 * half + which][:, span] = matrix_product(
                    left, right
                ) + adapter_scaling * matrix_product(low[part, :], factor[:, span])


def width_sums(here, tokens, cotangent, lows, factors, masks, order, arrays, last):
    rows, width = tokens.shape
    _, half, hidden = arrays[0].shape[-3:]
    vmem, anywhere = pl.BlockSpec(memory_space=pltpu.VMEM), pl.BlockSpec(memory_space=pl.ANY)
    shapes = [((rows // HALVES, hidden), jnp.float32)] * (3 * HALVES)
    shapes += [((rows, 2 * half * len(last)), jnp.bfloat16)] * 2
    shapes += [((width, hidden), jnp.bfloat16)] * 2
    outs = pl.pallas_call(
        functools.partial(sums_kernel, masks, order, len(arrays), last),
        in_specs=[pl.BlockSpec(memory_space=pltpu.SMEM)]
        + [vmem] * 6
        + [anywhere] * (2 + len(arrays)),
        out_specs=[vmem] * len(shapes),
        out_shape=[pltpu.VMEM(shape, kind) for shape, kind in shapes],
        scratch_shapes=[
            pltpu.VMEM((rows, width), jnp.bfloat16),
            pltpu.VMEM((rows, width), jnp.bfloat16),
            pltpu.VMEM((half * len(order), hidden), jnp.bfloat16),
            pltpu.SemaphoreType.DMA((2 * HALVES,)),
            pltpu.SemaphoreType.DMA((3 * len(order),)),
        ],
        compiler_params=pltpu.CompilerParams(vmem_limit_bytes=LIMITS["sums"] * MEBIBYTE),
        cost_estimate=pl.CostEstimate(flops=COSTS["sums"], bytes_accessed=0, transcendentals=0),
        name="width_sums",
    )(here, *lows, *factors, tokens, cotangent, *arrays)
    return outs[: 3 * HALVES], outs[3 * HALVES : -2], outs[-2:]


def last_kernel(half, here, left, back, gate_out, up_out, *refs):
    units, sums = refs[:4], refs[4:7]
    hidden_out, gate_grad_out, up_grad_out, low_out = refs[-4:]
    rows, hidden = hidden_out.shape
    part = slice(half * rows, (half + 1) * rows)
    gate_low = up_low = 0.0
    for column in range(0, hidden, STRIP):
        span = slice(column, column + STRIP)
        gate = sums[0][:, span] + matrix_product(left[part, :], stacked(units, 0, span))
        up = sums[1][:, span] + matrix_product(left[part, :], stacked(units, 1, span))
        hidden_grad = sums[2][:, span] + matrix_product(back[part, :], stacked(units, 2, span))
        sig = 1.0 / (1.0 + jnp.exp(-gate))
        gated = gate * sig
        hidden_out[:, span] = (gated * up).astype(jnp.bfloat16)
        gate_grad = (hidden_grad * up * sig * (1.0 + gate * (1.0 - sig))).astype(jnp.bfloat16)
        up_grad = (hidden_grad * gated).astype(jnp.bfloat16)
        gate_grad_out[:, span] = gate_grad
        up_grad_out[:, span] = up_grad
        gate_low += contract_trailing_axis(gate_grad, gate_out[:, span])
        up_low += contract_trailing_axis(up_grad, up_out[:, span])
    low_out[...] = jnp.concatenate([gate_low, up_low], axis=1)


def hidden_and_grads(half, here, parts, factors, tail, sums, ahead):
    rows = parts[0].shape[0] // HALVES
    rank, hidden = factors[0].shape
    return vmem_call(
        functools.partial(last_kernel, half),
        [here],
        [*parts, *factors, *tail, *sums[3 * half : 3 * half + 3]],
        ahead,
        [((rows, hidden), jnp.bfloat16)] * 3 + [((rows, 2 * rank), jnp.float32)],
        {},
        [],
        LIMITS["last"],
        COSTS["last"],
        "hidden_and_grads",
    )


def quarter_rows(here, quarter, full, tail, which, columns):
    rows = 2 * tail[0].shape[1]
    blocks = []
    for number in range(columns // rows):
        block = quarter * (columns // rows) + number
        mask = lax.bitwise_xor(here[0], block)
        held = full[pl.ds(pl.multiple_of(block * rows, rows), rows), :]
        near, far = (
            jnp.concatenate([unit[which] for unit in units]) for units in (tail[:2], tail[2:])
        )
        blocks.append(jnp.where(mask == 7, far, jnp.where(mask == 3, near, held)))
    return jnp.concatenate(blocks)


def token_grad_kernel(mode, step, here, gate_grad, up_grad, low, factor, gate, up, *refs):
    tail, refs = refs[:4], refs[4:]
    came = refs[: {"first": 0, "sum": 1, "both": 3, "last": 2}[mode]]
    outs = refs[-2:] if mode == "both" else refs[-1:]
    columns = outs[0].shape[1]
    quarter = sum(
        jnp.where(here[1] == place, order[step], 0) for place, order in enumerate(QUARTER_ORDER)
    )
    span = pl.ds(pl.multiple_of(quarter * columns, columns), columns)
    total = contract_trailing_axis(
        gate_grad[...], quarter_rows(here, quarter, gate, tail, 0, columns)
    )
    total += contract_trailing_axis(up_grad[...], quarter_rows(here, quarter, up, tail, 1, columns))
    total += matrix_product((adapter_scaling * low[...]).astype(jnp.bfloat16), factor[:, span])
    came = [ref[...].astype(jnp.float32) for ref in came]
    if mode == "both":
        first, left, right = came
        outs[0][...] = (jnp.where(here[1] == 2, first, total) + left).astype(jnp.bfloat16)
        outs[1][...] = (jnp.where(here[1] == 1, first, total) + right).astype(jnp.bfloat16)
    else:
        outs[0][...] = sum(came, total).astype(jnp.bfloat16)


def token_grad(mode, step, here, arrays, columns, came, ahead):
    rows, hidden = arrays[0].shape
    outs = vmem_call(
        functools.partial(token_grad_kernel, mode, step),
        [here],
        [*arrays, *came],
        ahead,
        [((rows, columns), jnp.bfloat16)] * (2 if mode == "both" else 1),
        {},
        [],
        LIMITS["token"],
        COSTS["token"],
        "token_grad",
    )
    return outs if mode == "both" else outs[0]


def last_token_grad(step, half, here, arrays, columns, came, ahead, before):
    rows, hidden = arrays[0].shape
    arrays = [*arrays, *came]
    return pl.pallas_call(
        functools.partial(token_grad_kernel, "last", step),
        grid=(1,),
        in_specs=[pl.BlockSpec(memory_space=pltpu.SMEM)]
        + [pl.BlockSpec(memory_space=pltpu.VMEM)] * len(arrays)
        + [pl.BlockSpec(memory_space=pl.ANY)] * (len(before) + len(ahead)),
        out_specs=pl.BlockSpec((rows, columns), lambda i: (half, 0)),
        out_shape=jax.ShapeDtypeStruct((HALVES * rows, columns), jnp.bfloat16),
        input_output_aliases={1 + len(arrays): 0} if before else {},
        compiler_params=pltpu.CompilerParams(vmem_limit_bytes=LIMITS["token"] * MEBIBYTE),
        cost_estimate=pl.CostEstimate(
            flops=COSTS["token"],
            bytes_accessed=0,
            transcendentals=0,
        ),
        name="last_token_grad",
    )(
        here,
        *[pltpu.with_memory_space_constraint(array, pltpu.VMEM) for array in arrays],
        *before,
        *ahead,
    )


def adapter_kernel(scaling, here, *refs):
    hidden, gate_grad, up_grad, low = (
        refs[number * HALVES : (number + 1) * HALVES] for number in range(4)
    )
    tokens, cotangent, turned, down_in = refs[4 * HALVES : 4 * HALVES + 4]
    keep, send, wide, narrow = refs[-4:]
    rank = down_in.shape[0]
    rows = hidden[0].shape[0]
    parts = [slice(half * rows, (half + 1) * rows) for half in range(HALVES)]
    wide[: 2 * rank, :] = scaling * sum(
        matrix_product(low[half][...].T.astype(jnp.bfloat16), tokens[part, :])
        for half, part in enumerate(parts)
    )
    wide[2 * rank :, :] = scaling * sum(
        matrix_product(
            contract_trailing_axis(down_in[...], hidden[half][...]).astype(jnp.bfloat16),
            cotangent[part, :],
        )
        for half, part in enumerate(parts)
    )
    for number, arrays in enumerate((hidden, gate_grad, up_grad)):
        source = (2, 0, 1)[number]
        narrow[number * rank : (number + 1) * rank, :] = scaling * sum(
            matrix_product(turned[source * rank : (source + 1) * rank, part], arrays[half][...])
            for half, part in enumerate(parts)
        )
    groups = 2 * keep.shape[0]
    wide_columns, narrow_columns = wide.shape[1] // groups, narrow.shape[1] // groups
    for mask in range(groups):
        out = (keep if mask < groups // 2 else send).at[mask % (groups // 2)]
        block = lax.bitwise_xor(here[0], mask)
        out[:, :wide_columns] = wide[
            :, pl.ds(pl.multiple_of(block * wide_columns, wide_columns), wide_columns)
        ]
        out[:, wide_columns:] = narrow[
            :, pl.ds(pl.multiple_of(block * narrow_columns, narrow_columns), narrow_columns)
        ]


def adapter_grads(scaling, here, groups, arrays, ahead):
    rows, width = arrays[-4].shape
    rank, hidden = arrays[-1].shape
    return vmem_call(
        functools.partial(adapter_kernel, scaling),
        [here],
        arrays,
        ahead,
        [((groups // 2, 3 * rank, (width + hidden) // groups), jnp.float32)] * 2,
        {},
        [pltpu.VMEM((3 * rank, width), jnp.float32), pltpu.VMEM((3 * rank, hidden), jnp.float32)],
        LIMITS["adapter"],
        COSTS["adapter"],
        "adapter_grads",
    )


def halve_kernel(here, keep, came, kept, send):
    count = kept.shape[0]
    kept[...] = keep[:count] + came[:count].astype(jnp.float32)
    send[...] = (keep[count:] + came[count:].astype(jnp.float32)).astype(send.dtype)


def halve(here, keep, came):
    shape = (keep.shape[0] // 2, *keep.shape[1:])
    return vmem_call(
        halve_kernel,
        [here],
        [keep, came],
        [],
        [(shape, jnp.float32), (shape, jnp.bfloat16)],
        {},
        [],
        LIMITS["small"],
        COSTS["small"],
        "halve",
    )


def sum_kernel(here, keep, *refs):
    refs[-1][...] = sum((ref[...].astype(jnp.float32) for ref in refs[:-1]), keep[...])


def last_sum(here, keep, came):
    return vmem_call(
        sum_kernel,
        [here],
        [keep, *came],
        [],
        [(keep.shape, jnp.float32)],
        {},
        [],
        LIMITS["small"],
        COSTS["small"],
        "last_sum",
        True,
    )[0]


def turn_kernel(wide_columns, here, kept, came, narrow, *refs):
    outs, wide = refs[:-1], refs[-1]
    total = kept[0] + came[0].astype(jnp.float32)
    narrow[...] = total[:, wide_columns:]
    wide[...] = total[:, :wide_columns].T
    for mask, out in enumerate(outs):
        rows = out.shape[0]
        block = pl.ds(pl.multiple_of(lax.bitwise_xor(here[1], mask) * rows, rows), rows)
        out[...] = wide[block, :].astype(out.dtype)


def turn(here, keep, came, wide_columns, quarters):
    _, rows, columns = keep.shape
    return vmem_call(
        functools.partial(turn_kernel, wide_columns),
        [here],
        [keep, came],
        [],
        [((rows, columns - wide_columns), jnp.float32)]
        + [
            ((wide_columns // quarters, rows), jnp.bfloat16 if mask else jnp.float32)
            for mask in range(quarters)
        ],
        {},
        [pltpu.VMEM((wide_columns, rows), jnp.float32)],
        LIMITS["small"],
        COSTS["small"],
        "turn",
    )


def whole_kernel(here, near, far, out):
    columns = near.shape[2]
    for number in range(2 * near.shape[0]):
        ref = near if number < near.shape[0] else far
        block = lax.bitwise_xor(here[0], number) * columns
        out[:, pl.ds(pl.multiple_of(block, columns), columns)] = ref[number % near.shape[0]]


def whole(here, near, far):
    count, rows, columns = near.shape
    return vmem_call(
        whole_kernel,
        [here],
        [near, far],
        [],
        [((rows, 2 * count * columns), near.dtype)],
        {},
        [],
        LIMITS["small"],
        COSTS["small"],
        "whole",
        True,
    )[0]


def square_plane(
    tokens,
    cotangent,
    gate_frozen_matrix,
    up_frozen_matrix,
    down_frozen_matrix,
    gate_adapter_input_factor,
    up_adapter_input_factor,
    gate_adapter_output_factor,
    up_adapter_output_factor,
    down_adapter_input_factor,
    down_leave,
):
    groups = lax.axis_size(("cuts", "fsdp"))
    quarters = lax.axis_size("tp")
    rows, width = tokens.shape
    gradient_scaling = adapter_scaling / math.sqrt(rows * groups)
    here = jnp.stack([lax.axis_index(("cuts", "fsdp")), lax.axis_index("tp")]).astype(jnp.int32)
    gate_in, up_in, leave, down_in = (
        array.T
        for array in (
            gate_adapter_input_factor,
            up_adapter_input_factor,
            down_leave,
            down_adapter_input_factor,
        )
    )
    gate_out, up_out = gate_adapter_output_factor, up_adapter_output_factor

    units = {}
    units[0, 0], units[0, 1], own_pair = own_units(
        gate_frozen_matrix, up_frozen_matrix, down_frozen_matrix
    )
    units[1, 0] = flip(units[0, 0], "fsdp", 1)
    units[2, 1] = flip(units[0, 1], "fsdp", 2)
    units[1, 1] = flip(units[0, 1], "fsdp", 1)
    units[2, 0] = flip(units[0, 0], "fsdp", 2)
    units[3, 0] = flip(units[1, 0], "fsdp", 2)
    units[3, 1] = flip(units[2, 1], "fsdp", 1)
    own_pair = flip(own_pair, "cuts", 1)
    *lows, turned = low_rank_values(
        tokens,
        cotangent,
        [gate_in, up_in, leave],
        [here, units[1, 0], units[2, 1], own_pair],
    )
    pairs = {}
    for number, (one, two, ahead) in enumerate(
        (((1, 0), (2, 1), [turned]), ((1, 1), (2, 0), [turned]))
    ):
        pairs[number] = flip(pair(units[one], units[two], ahead), "cuts", 1)
    placed = [(mask, half) for mask in range(3) for half in range(2)]
    arrays = [units[key] for key in placed] + [own_pair, pairs[0], pairs[1]]
    placed += [(4, 0), (4, 1), (5, 0), (6, 1), (5, 1), (6, 0)]
    masks = (0, 1, 2, 4, 5, 6)
    order = [placed.index((mask, half)) for mask in masks for half in range(2)]
    sums, parts, full = width_sums(
        here, tokens, cotangent, lows, [gate_out, up_out, down_in], masks, order, arrays, (3, 7)
    )
    tail = list(hold([units[3, 0], units[3, 1]], [sums[0]]))
    tail += [flip(unit, "cuts", 1) for unit in tail]

    factor = jnp.concatenate([gate_in, up_in])
    shift = lambda array, pairs: lax.ppermute(array, "tp", pairs)
    states, first = [], []
    share = lambda step, half, mode, came=(), ahead=(): token_grad(
        mode,
        step,
        here,
        [*states[half][1:], factor, *full, *tail],
        width // quarters,
        came,
        ahead,
    )
    both = range(HALVES)
    for half in both:
        state = hidden_and_grads(
            half, here, parts, [gate_out, up_out], tail, sums, first[:]
        )
        states.append(state)
        first.append(share(0, half, "first"))
    came = [shift(part, [(0, 1), (3, 2)]) for part in first]
    partial = []
    for half in both:
        partial.append(share(1, half, "sum", [came[half]], partial or first[1:]))
    second = partial
    from_left = [shift(part, [(0, 1), (1, 2)]) for part in partial]
    from_right = [shift(part, [(3, 2), (2, 1)]) for part in partial]
    keep, send = adapter_grads(
        gradient_scaling,
        here,
        groups,
        [
            *[state[number] for number in range(4) for state in states],
            tokens,
            cotangent,
            turned,
            down_in,
        ],
        first,
    )
    keep, send = halve(here, keep, flip(send, "cuts", 1))
    keep, send = halve(here, keep, flip(send, "fsdp", 2))
    narrow, keep, *send = turn(here, keep, flip(send, "fsdp", 1), width // groups, quarters)
    wide_grads = last_sum(
        here, keep, [flip(part, "tp", 1 + number) for number, part in enumerate(send)]
    )
    near = jnp.stack([narrow, flip(narrow, "fsdp", 1)])
    near = jnp.concatenate([near, flip(near, "fsdp", 2)])
    narrow_turned = whole(here, near, flip(near, "cuts", 1))
    narrow_grads = narrow_turned.T

    partial = []
    for half in both:
        partial.append(
            share(
                2,
                half,
                "both",
                [first[half], from_left[half], from_right[half]],
                partial[0][:1] if partial else second[1:],
            )
        )
    from_left = [shift(part[0], [(0, 1), (1, 2), (2, 3)]) for part in partial]
    from_right = [shift(part[1], [(3, 2), (2, 1), (1, 0)]) for part in partial]

    results = []
    for half in both:
        results.append(
            last_token_grad(
                3,
                half,
                here,
                [*states[half][1:], factor, *full, *tail],
                width // quarters,
                [from_left[half], from_right[half]],
                [] if half else partial[1],
                results[:],
            )
        )
    token_input_gradient = results[-1]
    return (token_input_gradient, wide_grads, narrow_grads)


def per_device(*arrays):
    sizes = [lax.axis_size(axis) for axis in ("cuts", "fsdp", "tp")]
    return (square_plane if sizes == [2, 4, 4] else any_plane)(*arrays)


def solution(mesh):
    in_specs = (
        P(("cuts", "fsdp"), None),
        P(("cuts", "fsdp"), None),
        P(("cuts", "fsdp"), "tp"),
        P(("cuts", "fsdp"), "tp"),
        P("tp", ("cuts", "fsdp")),
        P(),
        P(),
        P(None, "tp"),
        P(None, "tp"),
        P("tp", None),
        P(),
    )
    out_specs = (P(("cuts", "fsdp"), "tp"), P(("cuts", "fsdp", "tp"), None), P("tp", None))
    return jax.shard_map(
        per_device, mesh=mesh, in_specs=in_specs, out_specs=out_specs, check_vma=False
    )
```

```python
import functools
import math

import jax
import jax.numpy as jnp
from jax import lax
from jax.experimental import pallas as pl
from jax.experimental.pallas import tpu as pltpu
from jax.sharding import PartitionSpec as P

adapter_scaling = 0.5
MEBIBYTE = 1024 * 1024
COST = 1
HALVES = 2
COSTS = {"sums": 1, "pair": 1, "small": 1, "token": 20 * 10**9, "adapter": 20 * 10**9, "last": 10**11}
LIMITS = {"low": 6, "sums": 24, "last": 14, "half": 24, "token": 8, "adapter": 12, "small": 4}
TILE = 512
STRIP = 256
QUARTER_ORDER = ((3, 2, 1, 0), (0, 3, 2, 1), (3, 0, 1, 2), (0, 1, 2, 3))


def matrix_product(left, right):
    return jnp.dot(left, right, preferred_element_type=jnp.float32)


def contract_trailing_axis(left, right):
    return lax.dot_general(
        left, right, (((1,), (1,)), ((), ())), preferred_element_type=jnp.float32
    )


def contract_first(left, right):
    return lax.dot_general(
        left, right, (((0,), (0,)), ((), ())), preferred_element_type=jnp.float32
    )


def any_plane(
    tokens,
    cotangent,
    gate_frozen_matrix,
    up_frozen_matrix,
    down_frozen_matrix,
    gate_adapter_input_factor,
    up_adapter_input_factor,
    gate_adapter_output_factor,
    up_adapter_output_factor,
    down_adapter_input_factor,
    down_leave,
):
    token_groups = lax.axis_size(("cuts", "fsdp"))
    quarters = lax.axis_size("tp")
    tp_index = lax.axis_index("tp")
    token_rows = tokens.shape[0]
    width = tokens.shape[1]
    gradient_scaling = adapter_scaling / math.sqrt(token_rows * token_groups)
    gate_adapter_hidden = matrix_product(tokens, gate_adapter_input_factor).astype(jnp.bfloat16)
    up_adapter_hidden = matrix_product(tokens, up_adapter_input_factor).astype(jnp.bfloat16)
    pieces = (
        lax.all_gather(gate_frozen_matrix, ("cuts", "fsdp"), axis=0, tiled=True),
        lax.all_gather(up_frozen_matrix, ("cuts", "fsdp"), axis=0, tiled=True),
    )
    columns = tokens
    gate_frozen_output = matrix_product(columns, pieces[0])
    up_frozen_output = matrix_product(columns, pieces[1])
    gate_preactivation = gate_frozen_output + adapter_scaling * matrix_product(
        gate_adapter_hidden, gate_adapter_output_factor
    )
    up_preactivation = up_frozen_output + adapter_scaling * matrix_product(
        up_adapter_hidden, up_adapter_output_factor
    )
    sig = jax.nn.sigmoid(gate_preactivation)
    hidden = (gate_preactivation * sig * up_preactivation).astype(jnp.bfloat16)
    down_part = matrix_product(hidden, down_adapter_input_factor)
    down_low = lax.psum(down_part.astype(jnp.bfloat16), "tp")
    backward_adapter_input = matrix_product(cotangent, down_leave).astype(jnp.bfloat16)
    columns = cotangent
    hidden_state_gradient = contract_trailing_axis(
        columns, lax.all_gather(down_frozen_matrix, ("cuts", "fsdp"), axis=1, tiled=True)
    )
    hidden_state_gradient = hidden_state_gradient + adapter_scaling * contract_trailing_axis(
        backward_adapter_input, down_adapter_input_factor
    )
    gate_output_gradient = (
        hidden_state_gradient * up_preactivation * sig * (1.0 + gate_preactivation * (1.0 - sig))
    ).astype(jnp.bfloat16)
    up_output_gradient = (hidden_state_gradient * gate_preactivation * sig).astype(jnp.bfloat16)
    gate_part = contract_trailing_axis(gate_output_gradient, gate_adapter_output_factor)
    up_part = contract_trailing_axis(up_output_gradient, up_adapter_output_factor)
    gate_sum, up_sum = lax.psum((gate_part, up_part), "tp")
    gate_backward_adapter = gate_sum.astype(jnp.bfloat16)
    up_backward_adapter = up_sum.astype(jnp.bfloat16)
    pieces = lax.all_gather(
        (gate_frozen_matrix, up_frozen_matrix), ("cuts", "fsdp"), axis=0, tiled=True
    )
    partial_value = contract_trailing_axis(
        gate_output_gradient, pieces[0]
    ) + contract_trailing_axis(up_output_gradient, pieces[1])
    frozen_path_gradient = lax.psum_scatter(partial_value, "tp", scatter_dimension=1, tiled=True)
    slice_width = width // quarters
    gate_slice = lax.dynamic_slice_in_dim(
        gate_adapter_input_factor, tp_index * slice_width, slice_width, 0
    )
    up_slice = lax.dynamic_slice_in_dim(
        up_adapter_input_factor, tp_index * slice_width, slice_width, 0
    )
    adapter_hidden_gradient = contract_trailing_axis(
        gate_backward_adapter, gate_slice
    ) + contract_trailing_axis(up_backward_adapter, up_slice)
    token_input_gradient = (
        frozen_path_gradient + adapter_scaling * adapter_hidden_gradient
    ).astype(jnp.bfloat16)
    narrow_part = gradient_scaling * jnp.concatenate(
        [
            contract_first(hidden, backward_adapter_input),
            contract_first(gate_output_gradient, gate_adapter_hidden),
            contract_first(up_output_gradient, up_adapter_hidden),
        ],
        axis=1,
    )
    narrow_grads = lax.psum(narrow_part, ("cuts", "fsdp"))
    token_side = jnp.concatenate([gate_backward_adapter, up_backward_adapter], axis=1)
    group_rows = lax.psum_scatter(
        gradient_scaling
        * jnp.concatenate(
            [contract_first(tokens, token_side), contract_first(cotangent, down_low)], axis=1
        ),
        ("cuts", "fsdp"),
        scatter_dimension=0,
        tiled=True,
    )
    fine_rows = width // (token_groups * quarters)
    wide_grads = lax.dynamic_slice_in_dim(group_rows, tp_index * fine_rows, fine_rows, 0)
    return (token_input_gradient, wide_grads, narrow_grads)


def flip(array, axis, bit):
    size = lax.axis_size(axis)
    return lax.ppermute(array, axis, [(i, i ^ bit) for i in range(size)])


def vmem_call(
    kernel, scalars, arrays, ahead, results, aliases, scratch, limit, flops, name, final=False
):
    vmem = pl.BlockSpec(memory_space=pltpu.VMEM)
    first = len(scalars)
    return pl.pallas_call(
        kernel,
        in_specs=[pl.BlockSpec(memory_space=pltpu.SMEM)] * first
        + [vmem] * len(arrays)
        + [pl.BlockSpec(memory_space=pl.ANY)] * len(ahead),
        out_specs=[vmem] * len(results),
        out_shape=[
            jax.ShapeDtypeStruct(shape, kind) if final else pltpu.VMEM(shape, kind)
            for shape, kind in results
        ],
        scratch_shapes=scratch,
        input_output_aliases={first + source: target for source, target in aliases.items()},
        compiler_params=pltpu.CompilerParams(vmem_limit_bytes=limit * MEBIBYTE),
        cost_estimate=pl.CostEstimate(flops=COST * flops, bytes_accessed=0, transcendentals=0),
        name=name,
    )(
        *scalars,
        *[pltpu.with_memory_space_constraint(array, pltpu.VMEM) for array in arrays],
        *ahead,
    )


def width_part(ref, part, here, masks, rows):
    return jnp.concatenate(
        [
            ref[part, pl.ds(pl.multiple_of(lax.bitwise_xor(here[0], mask) * rows, rows), rows)]
            for mask in masks
        ],
        axis=1,
    )


def stacked(units, which, span):
    return jnp.concatenate([unit[which, :, span] for unit in units], axis=0)


def lows_kernel(tokens, cotangent, gate_in, up_in, leave, *refs):
    gate_low, up_low, back_low, turned = refs[-4:]
    rank = leave.shape[0]
    for number, (ref, factor, out) in enumerate(
        ((tokens, gate_in, gate_low), (tokens, up_in, up_low), (cotangent, leave, back_low))
    ):
        low = contract_trailing_axis(ref[...], factor[...]).astype(jnp.bfloat16)
        out[...] = low
        turned[number * rank : (number + 1) * rank, :] = low.astype(jnp.float32).T.astype(
            jnp.bfloat16
        )


def low_rank_values(tokens, cotangent, factors, ahead):
    rows, width = tokens.shape
    rank = factors[0].shape[0]
    tile = rows // 4
    by_rows = lambda columns: pl.BlockSpec((tile, columns), lambda i: (i, 0))
    return pl.pallas_call(
        lows_kernel,
        grid=(rows // tile,),
        in_specs=[by_rows(width)] * 2
        + [pl.BlockSpec((rank, width), lambda i: (0, 0))] * 3
        + [pl.BlockSpec(memory_space=pl.ANY)] * len(ahead),
        out_specs=[by_rows(rank)] * 3 + [pl.BlockSpec((3 * rank, tile), lambda i: (0, i))],
        out_shape=[jax.ShapeDtypeStruct((rows, rank), jnp.bfloat16)] * 3
        + [jax.ShapeDtypeStruct((3 * rank, rows), jnp.bfloat16)],
        compiler_params=pltpu.CompilerParams(vmem_limit_bytes=LIMITS["low"] * MEBIBYTE),
        cost_estimate=pl.CostEstimate(
            flops=480 * COST * rows * width * rank, bytes_accessed=0, transcendentals=0
        ),
        name="low_rank_values",
    )(tokens, cotangent, *factors, *ahead)


def own_kernel(gate, up, down, *refs):
    units, both, (held, sems) = refs[:2], refs[2], refs[3:]
    rows = units[0].shape[1]
    down_copy = pltpu.make_async_copy(down, held, sems.at[0])
    down_copy.start()
    copies = []
    for half, unit in enumerate(units):
        for which, ref in enumerate((gate, up)):
            for target in (unit.at[which], both.at[half, which]):
                copies.append(
                    pltpu.make_async_copy(
                        ref.at[pl.ds(half * rows, rows)], target, sems.at[1 + len(copies)]
                    )
                )
    for copy in copies:
        copy.start()
    down_copy.wait()
    for half, unit in enumerate(units):
        part = slice(half * rows, (half + 1) * rows)
        turned = held[:, part].astype(jnp.float32).T.astype(jnp.bfloat16)
        unit[2] = turned
        both[half, 2] = turned
    for copy in copies:
        copy.wait()


def own_units(gate, up, down):
    rows, hidden = gate.shape
    unit = (3, rows // 2, hidden)
    return pl.pallas_call(
        own_kernel,
        in_specs=[pl.BlockSpec(memory_space=pl.ANY)] * 3,
        out_specs=[pl.BlockSpec(memory_space=pltpu.VMEM)] * 3,
        out_shape=[pltpu.VMEM(shape, jnp.bfloat16) for shape in (unit, unit, (2, *unit))],
        scratch_shapes=[
            pltpu.VMEM((hidden, rows), jnp.bfloat16),
            pltpu.SemaphoreType.DMA((9,)),
        ],
        compiler_params=pltpu.CompilerParams(vmem_limit_bytes=LIMITS["low"] * MEBIBYTE),
        cost_estimate=pl.CostEstimate(flops=MEBIBYTE, bytes_accessed=0, transcendentals=0),
        name="own_units",
    )(*[pltpu.with_memory_space_constraint(array, pltpu.HBM) for array in (gate, up, down)])


def nothing_kernel(*refs):
    pass


def hold(arrays, ahead):
    anywhere = pl.BlockSpec(memory_space=pl.ANY)
    return pl.pallas_call(
        nothing_kernel,
        in_specs=[anywhere] * (len(arrays) + len(ahead)),
        out_specs=[anywhere] * len(arrays),
        out_shape=[jax.ShapeDtypeStruct(array.shape, array.dtype) for array in arrays],
        input_output_aliases={number: number for number in range(len(arrays))},
        compiler_params=pltpu.CompilerParams(vmem_limit_bytes=MEBIBYTE),
        cost_estimate=pl.CostEstimate(flops=1, bytes_accessed=1, transcendentals=0),
        name="hold",
    )(*arrays, *ahead)


def pair_kernel(first, second, *refs):
    refs[-1][0] = first[...]
    refs[-1][1] = second[...]


def pair(first, second, ahead):
    return vmem_call(
        pair_kernel,
        [],
        [first, second],
        ahead,
        [((2, *first.shape), first.dtype)],
        {},
        [],
        LIMITS["small"],
        COSTS["pair"],
        "pair",
    )[0]


def sums_kernel(masks, order, n_arrays, last, here, *refs):
    gate_low, up_low, back_low, gate_out, up_out, down_in, tokens, cotangent = refs[:8]
    units = []
    for ref in refs[8 : 8 + n_arrays]:
        units += [ref] if len(ref.shape) == 3 else [ref.at[0], ref.at[1]]
    units = [units[number] for number in order]
    outs = refs[8 + n_arrays :]
    sums, rest, full, held_down = outs[:3], outs[3:5], outs[5:7], outs[7]
    held_tokens, held_cotangent, row_sems, unit_sems = outs[8:]
    half_rows, hidden = units[0].shape[1:]
    rows = 2 * half_rows
    tile = rest[0].shape[0]

    def unit_copies(which):
        copies = []
        for number, unit in enumerate(units):
            if which == 2:
                target = held_down.at[pl.ds(number * half_rows, half_rows)]
            else:
                block = lax.bitwise_xor(here[0], masks[number // 2])
                row = pl.multiple_of((2 * block + number % 2) * half_rows, half_rows)
                target = full[which].at[pl.ds(row, half_rows)]
            copies.append(
                pltpu.make_async_copy(
                    unit.at[which], target, unit_sems.at[which * len(units) + number]
                )
            )
        return copies

    def row_copy(which):
        source, target = ((tokens, held_tokens), (cotangent, held_cotangent))[which]
        return pltpu.make_async_copy(source.at[pl.ds(0, tile)], target, row_sems.at[which])

    for load in [*unit_copies(0), row_copy(0), *unit_copies(1), row_copy(1), *unit_copies(2)]:
        load.start()
    part = slice(0, tile)
    for which, (low, factor) in enumerate(
        ((gate_low, gate_out), (up_low, up_out), (back_low, down_in))
    ):
        for copy in unit_copies(which):
            copy.wait()
        if which != 1:
            row_copy(which // 2).wait()
            ref = (held_tokens, held_cotangent)[which // 2]
            left = width_part(ref, part, here, masks, rows)
            rest[which // 2][...] = width_part(ref, part, here, last, rows)
        for column in range(0, hidden, TILE):
            span = slice(column, column + TILE)
            if which == 2:
                right = held_down[:, span]
            else:
                right = block_rows(here, full[which], masks, rows, span)
            sums[which][:, span] = matrix_product(left, right) + adapter_scaling * matrix_product(
                low[part, :], factor[:, span]
            )


def block_rows(here, ref, masks, rows, span):
    return jnp.concatenate(
        [
            ref[pl.ds(pl.multiple_of(lax.bitwise_xor(here[0], mask) * rows, rows), rows), span]
            for mask in masks
        ]
    )


def width_sums(here, tokens, cotangent, lows, factors, masks, order, arrays, last):
    rows, width = tokens.shape
    _, half, hidden = arrays[0].shape[-3:]
    vmem, anywhere = pl.BlockSpec(memory_space=pltpu.VMEM), pl.BlockSpec(memory_space=pl.ANY)
    shapes = [((rows // HALVES, hidden), jnp.float32)] * 3
    shapes += [((rows // HALVES, 2 * half * len(last)), jnp.bfloat16)] * 2
    shapes += [((width, hidden), jnp.bfloat16)] * 2
    shapes += [((half * len(order), hidden), jnp.bfloat16)]
    outs = pl.pallas_call(
        functools.partial(sums_kernel, masks, order, len(arrays), last),
        in_specs=[pl.BlockSpec(memory_space=pltpu.SMEM)]
        + [vmem] * 6
        + [anywhere] * (2 + len(arrays)),
        out_specs=[vmem] * len(shapes),
        out_shape=[pltpu.VMEM(shape, kind) for shape, kind in shapes],
        scratch_shapes=[
            pltpu.VMEM((rows // HALVES, width), jnp.bfloat16),
            pltpu.VMEM((rows // HALVES, width), jnp.bfloat16),
            pltpu.SemaphoreType.DMA((2,)),
            pltpu.SemaphoreType.DMA((3 * len(order),)),
        ],
        compiler_params=pltpu.CompilerParams(vmem_limit_bytes=LIMITS["sums"] * MEBIBYTE),
        cost_estimate=pl.CostEstimate(flops=COSTS["sums"], bytes_accessed=0, transcendentals=0),
        name="width_sums",
    )(here, *lows, *factors, tokens, cotangent, *arrays)
    return outs[:3], outs[3:5], outs[5:7], outs[7]


def finish(outs, gate_out, up_out, gate, up, hidden_grad, span, lows):
    hidden_out, gate_grad_out, up_grad_out = outs[:3]
    sig = 1.0 / (1.0 + jnp.exp(-gate))
    gated = gate * sig
    hidden_out[:, span] = (gated * up).astype(jnp.bfloat16)
    gate_grad = (hidden_grad * up * sig * (1.0 + gate * (1.0 - sig))).astype(jnp.bfloat16)
    up_grad = (hidden_grad * gated).astype(jnp.bfloat16)
    gate_grad_out[:, span] = gate_grad
    up_grad_out[:, span] = up_grad
    return (
        lows[0] + contract_trailing_axis(gate_grad, gate_out[:, span]),
        lows[1] + contract_trailing_axis(up_grad, up_out[:, span]),
    )


def last_kernel(here, left, back, gate_out, up_out, *refs):
    units, sums, outs = refs[:4], refs[4:7], refs[-4:]
    hidden = outs[0].shape[1]
    lows = (0.0, 0.0)
    for column in range(0, hidden, STRIP):
        span = slice(column, column + STRIP)
        gate = sums[0][:, span] + matrix_product(left[...], stacked(units, 0, span))
        up = sums[1][:, span] + matrix_product(left[...], stacked(units, 1, span))
        hidden_grad = sums[2][:, span] + matrix_product(back[...], stacked(units, 2, span))
        lows = finish(outs, gate_out, up_out, gate, up, hidden_grad, span, lows)
    outs[3][...] = jnp.concatenate(lows, axis=1)


def first_half(here, parts, factors, tail, sums):
    rows = parts[0].shape[0]
    rank, hidden = factors[0].shape
    return vmem_call(
        last_kernel,
        [here],
        [*parts, *factors, *tail, *sums],
        [],
        [((rows, hidden), jnp.bfloat16)] * 3 + [((rows, 2 * rank), jnp.float32)],
        {},
        [],
        LIMITS["last"],
        COSTS["last"],
        "hidden_and_grads",
    )


def whole_kernel_half(masks, last, here, *refs):
    lows, factors, units, full, down_rows = refs[:3], refs[3:6], refs[6:10], refs[10:12], refs[12]
    tokens, cotangent = refs[13:15]
    outs, (held_tokens, held_cotangent, sems) = refs[-7:-3], refs[-3:]
    tile, hidden = outs[0].shape
    part = slice(tokens.shape[0] - tile, tokens.shape[0])
    copies = [
        pltpu.make_async_copy(ref.at[pl.ds(tokens.shape[0] - tile, tile)], held, sems.at[number])
        for number, (ref, held) in enumerate(((tokens, held_tokens), (cotangent, held_cotangent)))
    ]
    for copy in copies:
        copy.start()
    for copy in copies:
        copy.wait()
    rows = 2 * units[0].shape[1]
    every = slice(None)
    left, back, left_last, back_last = (
        width_part(ref, every, here, group, rows)
        for group in (masks, last)
        for ref in (held_tokens, held_cotangent)
    )
    back_lows = (0.0, 0.0)
    for column in range(0, hidden, STRIP):
        span = slice(column, column + STRIP)
        values = []
        for which, (low, factor) in enumerate(zip(lows, factors)):
            if which == 2:
                right = down_rows[:, span]
            else:
                right = block_rows(here, full[which], masks, rows, span)
            values.append(
                matrix_product(back if which == 2 else left, right)
                + matrix_product(
                    back_last if which == 2 else left_last, stacked(units, which, span)
                )
                + adapter_scaling * matrix_product(low[part, :], factor[:, span])
            )
        back_lows = finish(outs, factors[0], factors[1], *values, span, back_lows)
    outs[3][...] = jnp.concatenate(back_lows, axis=1)


def second_half(here, tokens, cotangent, lows, factors, tail, full, down_rows, masks, last, ahead):
    rows, width = tokens.shape
    rank, hidden = factors[0].shape
    tile = rows // HALVES
    vmem, anywhere = pl.BlockSpec(memory_space=pltpu.VMEM), pl.BlockSpec(memory_space=pl.ANY)
    arrays = [*lows, *factors, *tail, *full, down_rows]
    shapes = [((tile, hidden), jnp.bfloat16)] * 3 + [((tile, 2 * rank), jnp.float32)]
    return pl.pallas_call(
        functools.partial(whole_kernel_half, masks, last),
        in_specs=[pl.BlockSpec(memory_space=pltpu.SMEM)]
        + [vmem] * len(arrays)
        + [anywhere] * (2 + len(ahead)),
        out_specs=[vmem] * len(shapes),
        out_shape=[pltpu.VMEM(shape, kind) for shape, kind in shapes],
        scratch_shapes=[pltpu.VMEM((tile, width), jnp.bfloat16)] * 2
        + [pltpu.SemaphoreType.DMA((2,))],
        compiler_params=pltpu.CompilerParams(vmem_limit_bytes=LIMITS["half"] * MEBIBYTE),
        cost_estimate=pl.CostEstimate(flops=COSTS["last"], bytes_accessed=0, transcendentals=0),
        name="second_half",
    )(
        here,
        *[pltpu.with_memory_space_constraint(array, pltpu.VMEM) for array in arrays],
        tokens,
        cotangent,
        *ahead,
    )


def quarter_rows(here, quarter, full, tail, which, columns):
    rows = 2 * tail[0].shape[1]
    blocks = []
    for number in range(columns // rows):
        block = quarter * (columns // rows) + number
        mask = lax.bitwise_xor(here[0], block)
        held = full[pl.ds(pl.multiple_of(block * rows, rows), rows), :]
        near, far = (
            jnp.concatenate([unit[which] for unit in units]) for units in (tail[:2], tail[2:])
        )
        blocks.append(jnp.where(mask == 7, far, jnp.where(mask == 3, near, held)))
    return jnp.concatenate(blocks)


def token_grad_kernel(mode, step, here, gate_grad, up_grad, low, factor, gate, up, *refs):
    tail, refs = refs[:4], refs[4:]
    came = refs[: {"first": 0, "sum": 1, "both": 3, "last": 2}[mode]]
    outs = refs[-2:] if mode == "both" else refs[-1:]
    columns = outs[0].shape[1]
    quarter = sum(
        jnp.where(here[1] == place, order[step], 0) for place, order in enumerate(QUARTER_ORDER)
    )
    span = pl.ds(pl.multiple_of(quarter * columns, columns), columns)
    total = contract_trailing_axis(
        gate_grad[...], quarter_rows(here, quarter, gate, tail, 0, columns)
    )
    total += contract_trailing_axis(up_grad[...], quarter_rows(here, quarter, up, tail, 1, columns))
    total += matrix_product((adapter_scaling * low[...]).astype(jnp.bfloat16), factor[:, span])
    came = [ref[...].astype(jnp.float32) for ref in came]
    if mode == "both":
        first, left, right = came
        outs[0][...] = (jnp.where(here[1] == 2, first, total) + left).astype(jnp.bfloat16)
        outs[1][...] = (jnp.where(here[1] == 1, first, total) + right).astype(jnp.bfloat16)
    else:
        outs[0][...] = sum(came, total).astype(jnp.bfloat16)


def token_grad(mode, step, here, arrays, columns, came, ahead):
    rows, hidden = arrays[0].shape
    outs = vmem_call(
        functools.partial(token_grad_kernel, mode, step),
        [here],
        [*arrays, *came],
        ahead,
        [((rows, columns), jnp.bfloat16)] * (2 if mode == "both" else 1),
        {},
        [],
        LIMITS["token"],
        COSTS["token"],
        "token_grad",
    )
    return outs if mode == "both" else outs[0]


def last_token_grad(step, half, here, arrays, columns, came, ahead, before):
    rows, hidden = arrays[0].shape
    arrays = [*arrays, *came]
    return pl.pallas_call(
        functools.partial(token_grad_kernel, "last", step),
        grid=(1,),
        in_specs=[pl.BlockSpec(memory_space=pltpu.SMEM)]
        + [pl.BlockSpec(memory_space=pltpu.VMEM)] * len(arrays)
        + [pl.BlockSpec(memory_space=pl.ANY)] * (len(before) + len(ahead)),
        out_specs=pl.BlockSpec((rows, columns), lambda i: (half, 0)),
        out_shape=jax.ShapeDtypeStruct((HALVES * rows, columns), jnp.bfloat16),
        input_output_aliases={1 + len(arrays): 0} if before else {},
        compiler_params=pltpu.CompilerParams(vmem_limit_bytes=LIMITS["token"] * MEBIBYTE),
        cost_estimate=pl.CostEstimate(
            flops=COSTS["token"],
            bytes_accessed=0,
            transcendentals=0,
        ),
        name="last_token_grad",
    )(
        here,
        *[pltpu.with_memory_space_constraint(array, pltpu.VMEM) for array in arrays],
        *before,
        *ahead,
    )


def adapter_kernel(scaling, here, *refs):
    hidden, gate_grad, up_grad, low = (
        refs[number * HALVES : (number + 1) * HALVES] for number in range(4)
    )
    tokens, cotangent, turned, down_in = refs[4 * HALVES : 4 * HALVES + 4]
    keep, send, wide, narrow = refs[-4:]
    rank = down_in.shape[0]
    rows = hidden[0].shape[0]
    parts = [slice(half * rows, (half + 1) * rows) for half in range(HALVES)]
    wide[: 2 * rank, :] = scaling * sum(
        matrix_product(low[half][...].T.astype(jnp.bfloat16), tokens[part, :])
        for half, part in enumerate(parts)
    )
    wide[2 * rank :, :] = scaling * sum(
        matrix_product(
            contract_trailing_axis(down_in[...], hidden[half][...]).astype(jnp.bfloat16),
            cotangent[part, :],
        )
        for half, part in enumerate(parts)
    )
    for number, arrays in enumerate((hidden, gate_grad, up_grad)):
        source = (2, 0, 1)[number]
        narrow[number * rank : (number + 1) * rank, :] = scaling * sum(
            matrix_product(turned[source * rank : (source + 1) * rank, part], arrays[half][...])
            for half, part in enumerate(parts)
        )
    groups = 2 * keep.shape[0]
    wide_columns, narrow_columns = wide.shape[1] // groups, narrow.shape[1] // groups
    for mask in range(groups):
        out = (keep if mask < groups // 2 else send).at[mask % (groups // 2)]
        block = lax.bitwise_xor(here[0], mask)
        out[:, :wide_columns] = wide[
            :, pl.ds(pl.multiple_of(block * wide_columns, wide_columns), wide_columns)
        ]
        out[:, wide_columns:] = narrow[
            :, pl.ds(pl.multiple_of(block * narrow_columns, narrow_columns), narrow_columns)
        ]


def adapter_grads(scaling, here, groups, arrays, ahead):
    rows, width = arrays[-4].shape
    rank, hidden = arrays[-1].shape
    return vmem_call(
        functools.partial(adapter_kernel, scaling),
        [here],
        arrays,
        ahead,
        [((groups // 2, 3 * rank, (width + hidden) // groups), jnp.float32)] * 2,
        {},
        [pltpu.VMEM((3 * rank, width), jnp.float32), pltpu.VMEM((3 * rank, hidden), jnp.float32)],
        LIMITS["adapter"],
        COSTS["adapter"],
        "adapter_grads",
    )


def halve_kernel(here, keep, came, kept, send):
    count = kept.shape[0]
    kept[...] = keep[:count] + came[:count].astype(jnp.float32)
    send[...] = (keep[count:] + came[count:].astype(jnp.float32)).astype(send.dtype)


def halve(here, keep, came):
    shape = (keep.shape[0] // 2, *keep.shape[1:])
    return vmem_call(
        halve_kernel,
        [here],
        [keep, came],
        [],
        [(shape, jnp.float32), (shape, jnp.bfloat16)],
        {},
        [],
        LIMITS["small"],
        COSTS["small"],
        "halve",
    )


def sum_kernel(here, keep, *refs):
    refs[-1][...] = sum((ref[...].astype(jnp.float32) for ref in refs[:-1]), keep[...])


def last_sum(here, keep, came):
    return vmem_call(
        sum_kernel,
        [here],
        [keep, *came],
        [],
        [(keep.shape, jnp.float32)],
        {},
        [],
        LIMITS["small"],
        COSTS["small"],
        "last_sum",
        True,
    )[0]


def turn_kernel(wide_columns, here, kept, came, narrow, *refs):
    outs, wide = refs[:-1], refs[-1]
    total = kept[0] + came[0].astype(jnp.float32)
    narrow[...] = total[:, wide_columns:]
    wide[...] = total[:, :wide_columns].T
    for mask, out in enumerate(outs):
        rows = out.shape[0]
        block = pl.ds(pl.multiple_of(lax.bitwise_xor(here[1], mask) * rows, rows), rows)
        out[...] = wide[block, :].astype(out.dtype)


def turn(here, keep, came, wide_columns, quarters):
    _, rows, columns = keep.shape
    return vmem_call(
        functools.partial(turn_kernel, wide_columns),
        [here],
        [keep, came],
        [],
        [((rows, columns - wide_columns), jnp.float32)]
        + [
            ((wide_columns // quarters, rows), jnp.bfloat16 if mask else jnp.float32)
            for mask in range(quarters)
        ],
        {},
        [pltpu.VMEM((wide_columns, rows), jnp.float32)],
        LIMITS["small"],
        COSTS["small"],
        "turn",
    )


def whole_kernel(here, near, far, out):
    columns = near.shape[2]
    for number in range(2 * near.shape[0]):
        ref = near if number < near.shape[0] else far
        block = lax.bitwise_xor(here[0], number) * columns
        out[:, pl.ds(pl.multiple_of(block, columns), columns)] = ref[number % near.shape[0]]


def whole(here, near, far):
    count, rows, columns = near.shape
    return vmem_call(
        whole_kernel,
        [here],
        [near, far],
        [],
        [((rows, 2 * count * columns), near.dtype)],
        {},
        [],
        LIMITS["small"],
        COSTS["small"],
        "whole",
        True,
    )[0]


def square_plane(
    tokens,
    cotangent,
    gate_frozen_matrix,
    up_frozen_matrix,
    down_frozen_matrix,
    gate_adapter_input_factor,
    up_adapter_input_factor,
    gate_adapter_output_factor,
    up_adapter_output_factor,
    down_adapter_input_factor,
    down_leave,
):
    groups = lax.axis_size(("cuts", "fsdp"))
    quarters = lax.axis_size("tp")
    rows, width = tokens.shape
    gradient_scaling = adapter_scaling / math.sqrt(rows * groups)
    here = jnp.stack([lax.axis_index(("cuts", "fsdp")), lax.axis_index("tp")]).astype(jnp.int32)
    gate_in, up_in, leave, down_in = (
        array.T
        for array in (
            gate_adapter_input_factor,
            up_adapter_input_factor,
            down_leave,
            down_adapter_input_factor,
        )
    )
    gate_out, up_out = gate_adapter_output_factor, up_adapter_output_factor

    units = {}
    units[0, 0], units[0, 1], own_pair = own_units(
        gate_frozen_matrix, up_frozen_matrix, down_frozen_matrix
    )
    units[1, 0] = flip(units[0, 0], "fsdp", 1)
    units[2, 1] = flip(units[0, 1], "fsdp", 2)
    units[1, 1] = flip(units[0, 1], "fsdp", 1)
    units[2, 0] = flip(units[0, 0], "fsdp", 2)
    units[3, 0] = flip(units[1, 0], "fsdp", 2)
    units[3, 1] = flip(units[2, 1], "fsdp", 1)
    own_pair = flip(own_pair, "cuts", 1)
    *lows, turned = low_rank_values(
        tokens,
        cotangent,
        [gate_in, up_in, leave],
        [here, units[1, 0], units[2, 1], own_pair],
    )
    pairs = {}
    for number, (one, two, ahead) in enumerate(
        (((1, 0), (2, 1), [turned]), ((1, 1), (2, 0), [turned]))
    ):
        pairs[number] = flip(pair(units[one], units[two], ahead), "cuts", 1)
    placed = [(mask, half) for mask in range(3) for half in range(2)]
    arrays = [units[key] for key in placed] + [own_pair, pairs[0], pairs[1]]
    placed += [(4, 0), (4, 1), (5, 0), (6, 1), (5, 1), (6, 0)]
    masks = (0, 1, 2, 4, 5, 6)
    order = [placed.index((mask, half)) for mask in masks for half in range(2)]
    sums, parts, full, down_rows = width_sums(
        here, tokens, cotangent, lows, [gate_out, up_out, down_in], masks, order, arrays, (3, 7)
    )
    tail = list(hold([units[3, 0], units[3, 1]], [sums[0]]))
    tail += [flip(unit, "cuts", 1) for unit in tail]

    factor = jnp.concatenate([gate_in, up_in])
    shift = lambda array, pairs: lax.ppermute(array, "tp", pairs)
    states, first = [], []
    share = lambda step, half, mode, came=(), ahead=(): token_grad(
        mode,
        step,
        here,
        [*states[half][1:], factor, *full, *tail],
        width // quarters,
        came,
        ahead,
    )
    both = range(HALVES)
    for half in both:
        if half == 0:
            state = first_half(here, parts, [gate_out, up_out], tail, sums)
        else:
            state = second_half(
                here,
                tokens,
                cotangent,
                lows,
                [gate_out, up_out, down_in],
                tail,
                full,
                down_rows,
                masks,
                (3, 7),
                first[:],
            )
        states.append(state)
        first.append(share(0, half, "first"))
    came = [shift(part, [(0, 1), (3, 2)]) for part in first]
    partial = []
    for half in both:
        partial.append(share(1, half, "sum", [came[half]], partial or first[1:]))
    second = partial
    from_left = [shift(part, [(0, 1), (1, 2)]) for part in partial]
    from_right = [shift(part, [(3, 2), (2, 1)]) for part in partial]
    keep, send = adapter_grads(
        gradient_scaling,
        here,
        groups,
        [
            *[state[number] for number in range(4) for state in states],
            tokens,
            cotangent,
            turned,
            down_in,
        ],
        first,
    )
    keep, send = halve(here, keep, flip(send, "cuts", 1))
    keep, send = halve(here, keep, flip(send, "fsdp", 2))
    narrow, keep, *send = turn(here, keep, flip(send, "fsdp", 1), width // groups, quarters)
    wide_grads = last_sum(
        here, keep, [flip(part, "tp", 1 + number) for number, part in enumerate(send)]
    )
    near = jnp.stack([narrow, flip(narrow, "fsdp", 1)])
    near = jnp.concatenate([near, flip(near, "fsdp", 2)])
    narrow_turned = whole(here, near, flip(near, "cuts", 1))
    narrow_grads = narrow_turned.T

    partial = []
    for half in both:
        partial.append(
            share(
                2,
                half,
                "both",
                [first[half], from_left[half], from_right[half]],
                partial[0][:1] if partial else second[1:],
            )
        )
    from_left = [shift(part[0], [(0, 1), (1, 2), (2, 3)]) for part in partial]
    from_right = [shift(part[1], [(3, 2), (2, 1), (1, 0)]) for part in partial]

    results = []
    for half in both:
        results.append(
            last_token_grad(
                3,
                half,
                here,
                [*states[half][1:], factor, *full, *tail],
                width // quarters,
                [from_left[half], from_right[half]],
                [] if half else partial[1],
                results[:],
            )
        )
    token_input_gradient = results[-1]
    return (token_input_gradient, wide_grads, narrow_grads)


def per_device(*arrays):
    sizes = [lax.axis_size(axis) for axis in ("cuts", "fsdp", "tp")]
    return (square_plane if sizes == [2, 4, 4] else any_plane)(*arrays)


def solution(mesh):
    in_specs = (
        P(("cuts", "fsdp"), None),
        P(("cuts", "fsdp"), None),
        P(("cuts", "fsdp"), "tp"),
        P(("cuts", "fsdp"), "tp"),
        P("tp", ("cuts", "fsdp")),
        P(),
        P(),
        P(None, "tp"),
        P(None, "tp"),
        P("tp", None),
        P(),
    )
    out_specs = (P(("cuts", "fsdp"), "tp"), P(("cuts", "fsdp", "tp"), None), P("tp", None))
    return jax.shard_map(
        per_device, mesh=mesh, in_specs=in_specs, out_specs=out_specs, check_vma=False
    )
```

```python
import functools
import math

import jax
import jax.numpy as jnp
from jax import lax
from jax.experimental import pallas as pl
from jax.experimental.pallas import tpu as pltpu
from jax.sharding import PartitionSpec as P

adapter_scaling = 0.5
MEBIBYTE = 1024 * 1024
COST = 1
HALVES = 2
COSTS = {"sums": 1, "pair": 1, "small": 10**10, "token": 20 * 10**9, "adapter": 20 * 10**9, "last": 10**11}
LIMITS = {"low": 6, "sums": 25, "last": 14, "token": 8, "adapter": 12, "small": 4}
TILE = 512
STRIP = 256
QUARTER_ORDER = ((3, 2, 1, 0), (0, 3, 2, 1), (3, 0, 1, 2), (0, 1, 2, 3))


def matrix_product(left, right):
    return jnp.dot(left, right, preferred_element_type=jnp.float32)


def contract_trailing_axis(left, right):
    return lax.dot_general(
        left, right, (((1,), (1,)), ((), ())), preferred_element_type=jnp.float32
    )


def contract_first(left, right):
    return lax.dot_general(
        left, right, (((0,), (0,)), ((), ())), preferred_element_type=jnp.float32
    )


def any_plane(
    tokens,
    cotangent,
    gate_frozen_matrix,
    up_frozen_matrix,
    down_frozen_matrix,
    gate_adapter_input_factor,
    up_adapter_input_factor,
    gate_adapter_output_factor,
    up_adapter_output_factor,
    down_adapter_input_factor,
    down_leave,
):
    token_groups = lax.axis_size(("cuts", "fsdp"))
    quarters = lax.axis_size("tp")
    tp_index = lax.axis_index("tp")
    token_rows = tokens.shape[0]
    width = tokens.shape[1]
    gradient_scaling = adapter_scaling / math.sqrt(token_rows * token_groups)
    gate_adapter_hidden = matrix_product(tokens, gate_adapter_input_factor).astype(jnp.bfloat16)
    up_adapter_hidden = matrix_product(tokens, up_adapter_input_factor).astype(jnp.bfloat16)
    pieces = (
        lax.all_gather(gate_frozen_matrix, ("cuts", "fsdp"), axis=0, tiled=True),
        lax.all_gather(up_frozen_matrix, ("cuts", "fsdp"), axis=0, tiled=True),
    )
    columns = tokens
    gate_frozen_output = matrix_product(columns, pieces[0])
    up_frozen_output = matrix_product(columns, pieces[1])
    gate_preactivation = gate_frozen_output + adapter_scaling * matrix_product(
        gate_adapter_hidden, gate_adapter_output_factor
    )
    up_preactivation = up_frozen_output + adapter_scaling * matrix_product(
        up_adapter_hidden, up_adapter_output_factor
    )
    sig = jax.nn.sigmoid(gate_preactivation)
    hidden = (gate_preactivation * sig * up_preactivation).astype(jnp.bfloat16)
    down_part = matrix_product(hidden, down_adapter_input_factor)
    down_low = lax.psum(down_part.astype(jnp.bfloat16), "tp")
    backward_adapter_input = matrix_product(cotangent, down_leave).astype(jnp.bfloat16)
    columns = cotangent
    hidden_state_gradient = contract_trailing_axis(
        columns, lax.all_gather(down_frozen_matrix, ("cuts", "fsdp"), axis=1, tiled=True)
    )
    hidden_state_gradient = hidden_state_gradient + adapter_scaling * contract_trailing_axis(
        backward_adapter_input, down_adapter_input_factor
    )
    gate_output_gradient = (
        hidden_state_gradient * up_preactivation * sig * (1.0 + gate_preactivation * (1.0 - sig))
    ).astype(jnp.bfloat16)
    up_output_gradient = (hidden_state_gradient * gate_preactivation * sig).astype(jnp.bfloat16)
    gate_part = contract_trailing_axis(gate_output_gradient, gate_adapter_output_factor)
    up_part = contract_trailing_axis(up_output_gradient, up_adapter_output_factor)
    gate_sum, up_sum = lax.psum((gate_part, up_part), "tp")
    gate_backward_adapter = gate_sum.astype(jnp.bfloat16)
    up_backward_adapter = up_sum.astype(jnp.bfloat16)
    pieces = lax.all_gather(
        (gate_frozen_matrix, up_frozen_matrix), ("cuts", "fsdp"), axis=0, tiled=True
    )
    partial_value = contract_trailing_axis(
        gate_output_gradient, pieces[0]
    ) + contract_trailing_axis(up_output_gradient, pieces[1])
    frozen_path_gradient = lax.psum_scatter(partial_value, "tp", scatter_dimension=1, tiled=True)
    slice_width = width // quarters
    gate_slice = lax.dynamic_slice_in_dim(
        gate_adapter_input_factor, tp_index * slice_width, slice_width, 0
    )
    up_slice = lax.dynamic_slice_in_dim(
        up_adapter_input_factor, tp_index * slice_width, slice_width, 0
    )
    adapter_hidden_gradient = contract_trailing_axis(
        gate_backward_adapter, gate_slice
    ) + contract_trailing_axis(up_backward_adapter, up_slice)
    token_input_gradient = (
        frozen_path_gradient + adapter_scaling * adapter_hidden_gradient
    ).astype(jnp.bfloat16)
    narrow_part = gradient_scaling * jnp.concatenate(
        [
            contract_first(hidden, backward_adapter_input),
            contract_first(gate_output_gradient, gate_adapter_hidden),
            contract_first(up_output_gradient, up_adapter_hidden),
        ],
        axis=1,
    )
    narrow_grads = lax.psum(narrow_part, ("cuts", "fsdp"))
    token_side = jnp.concatenate([gate_backward_adapter, up_backward_adapter], axis=1)
    group_rows = lax.psum_scatter(
        gradient_scaling
        * jnp.concatenate(
            [contract_first(tokens, token_side), contract_first(cotangent, down_low)], axis=1
        ),
        ("cuts", "fsdp"),
        scatter_dimension=0,
        tiled=True,
    )
    fine_rows = width // (token_groups * quarters)
    wide_grads = lax.dynamic_slice_in_dim(group_rows, tp_index * fine_rows, fine_rows, 0)
    return (token_input_gradient, wide_grads, narrow_grads)


def flip(array, axis, bit):
    size = lax.axis_size(axis)
    return lax.ppermute(array, axis, [(i, i ^ bit) for i in range(size)])


def vmem_call(
    kernel, scalars, arrays, ahead, results, aliases, scratch, limit, flops, name, final=False
):
    vmem = pl.BlockSpec(memory_space=pltpu.VMEM)
    first = len(scalars)
    return pl.pallas_call(
        kernel,
        in_specs=[pl.BlockSpec(memory_space=pltpu.SMEM)] * first
        + [vmem] * len(arrays)
        + [pl.BlockSpec(memory_space=pl.ANY)] * len(ahead),
        out_specs=[vmem] * len(results),
        out_shape=[
            jax.ShapeDtypeStruct(shape, kind) if final else pltpu.VMEM(shape, kind)
            for shape, kind in results
        ],
        scratch_shapes=scratch,
        input_output_aliases={first + source: target for source, target in aliases.items()},
        compiler_params=pltpu.CompilerParams(vmem_limit_bytes=limit * MEBIBYTE),
        cost_estimate=pl.CostEstimate(flops=COST * flops, bytes_accessed=0, transcendentals=0),
        name=name,
    )(
        *scalars,
        *[pltpu.with_memory_space_constraint(array, pltpu.VMEM) for array in arrays],
        *ahead,
    )


def width_part(ref, part, here, masks, rows):
    return jnp.concatenate(
        [
            ref[part, pl.ds(pl.multiple_of(lax.bitwise_xor(here[0], mask) * rows, rows), rows)]
            for mask in masks
        ],
        axis=1,
    )


def stacked(units, which, span):
    return jnp.concatenate([unit[which, :, span] for unit in units], axis=0)


def lows_kernel(tokens, cotangent, gate_in, up_in, leave, *refs):
    gate_low, up_low, back_low, turned = refs[-4:]
    rank = leave.shape[0]
    for number, (ref, factor, out) in enumerate(
        ((tokens, gate_in, gate_low), (tokens, up_in, up_low), (cotangent, leave, back_low))
    ):
        low = contract_trailing_axis(ref[...], factor[...]).astype(jnp.bfloat16)
        out[...] = low
        turned[number * rank : (number + 1) * rank, :] = low.astype(jnp.float32).T.astype(
            jnp.bfloat16
        )


def low_rank_values(tokens, cotangent, factors, ahead):
    rows, width = tokens.shape
    rank = factors[0].shape[0]
    tile = rows // 4
    by_rows = lambda columns: pl.BlockSpec((tile, columns), lambda i: (i, 0))
    return pl.pallas_call(
        lows_kernel,
        grid=(rows // tile,),
        in_specs=[by_rows(width)] * 2
        + [pl.BlockSpec((rank, width), lambda i: (0, 0))] * 3
        + [pl.BlockSpec(memory_space=pl.ANY)] * len(ahead),
        out_specs=[by_rows(rank)] * 3 + [pl.BlockSpec((3 * rank, tile), lambda i: (0, i))],
        out_shape=[jax.ShapeDtypeStruct((rows, rank), jnp.bfloat16)] * 3
        + [jax.ShapeDtypeStruct((3 * rank, rows), jnp.bfloat16)],
        compiler_params=pltpu.CompilerParams(vmem_limit_bytes=LIMITS["low"] * MEBIBYTE),
        cost_estimate=pl.CostEstimate(
            flops=480 * COST * rows * width * rank, bytes_accessed=0, transcendentals=0
        ),
        name="low_rank_values",
    )(tokens, cotangent, *factors, *ahead)


def own_kernel(gate, up, down, *refs):
    units, (held, sems) = refs[:2], refs[2:]
    rows = units[0].shape[1]
    down_copy = pltpu.make_async_copy(down, held, sems.at[0])
    down_copy.start()
    copies = []
    for half, unit in enumerate(units):
        for which, ref in enumerate((gate, up)):
            copies.append(
                pltpu.make_async_copy(
                    ref.at[pl.ds(half * rows, rows)], unit.at[which], sems.at[1 + len(copies)]
                )
            )
    for copy in copies:
        copy.start()
    down_copy.wait()
    for half, unit in enumerate(units):
        part = slice(half * rows, (half + 1) * rows)
        unit[2] = held[:, part].astype(jnp.float32).T.astype(jnp.bfloat16)
    for copy in copies:
        copy.wait()


def own_units(gate, up, down):
    rows, hidden = gate.shape
    return pl.pallas_call(
        own_kernel,
        in_specs=[pl.BlockSpec(memory_space=pl.ANY)] * 3,
        out_specs=[pl.BlockSpec(memory_space=pltpu.VMEM)] * 2,
        out_shape=[pltpu.VMEM((3, rows // 2, hidden), jnp.bfloat16)] * 2,
        scratch_shapes=[
            pltpu.VMEM((hidden, rows), jnp.bfloat16),
            pltpu.SemaphoreType.DMA((5,)),
        ],
        compiler_params=pltpu.CompilerParams(vmem_limit_bytes=LIMITS["low"] * MEBIBYTE),
        cost_estimate=pl.CostEstimate(flops=MEBIBYTE, bytes_accessed=0, transcendentals=0),
        name="own_units",
    )(*[pltpu.with_memory_space_constraint(array, pltpu.HBM) for array in (gate, up, down)])


def nothing_kernel(*refs):
    pass


def hold(arrays, ahead):
    anywhere = pl.BlockSpec(memory_space=pl.ANY)
    return pl.pallas_call(
        nothing_kernel,
        in_specs=[anywhere] * (len(arrays) + len(ahead)),
        out_specs=[anywhere] * len(arrays),
        out_shape=[jax.ShapeDtypeStruct(array.shape, array.dtype) for array in arrays],
        input_output_aliases={number: number for number in range(len(arrays))},
        compiler_params=pltpu.CompilerParams(vmem_limit_bytes=MEBIBYTE),
        cost_estimate=pl.CostEstimate(flops=1, bytes_accessed=1, transcendentals=0),
        name="hold",
    )(*arrays, *ahead)


def pair_kernel(first, second, *refs):
    refs[-1][0] = first[...]
    refs[-1][1] = second[...]


def pair(first, second, ahead):
    return vmem_call(
        pair_kernel,
        [],
        [first, second],
        ahead,
        [((2, *first.shape), first.dtype)],
        {},
        [],
        LIMITS["small"],
        COSTS["pair"],
        "pair",
    )[0]


def sums_kernel(masks, order, n_arrays, last, here, *refs):
    gate_low, up_low, back_low, gate_out, up_out, down_in, tokens, cotangent = refs[:8]
    units = []
    for ref in refs[8 : 8 + n_arrays]:
        units += [ref] if len(ref.shape) == 3 else [ref.at[0], ref.at[1]]
    units = [units[number] for number in order]
    outs = refs[8 + n_arrays :]
    sums, rest, full = outs[: 3 * HALVES], outs[3 * HALVES : 3 * HALVES + 2], outs[-7:-5]
    held_tokens, held_cotangent, held_down, row_sems, unit_sems = outs[-5:]
    half_rows, hidden = units[0].shape[1:]
    rows = 2 * half_rows
    tile = tokens.shape[0] // HALVES

    def unit_copies(which):
        copies = []
        for number, unit in enumerate(units):
            if which == 2:
                target = held_down.at[pl.ds(number * half_rows, half_rows)]
            else:
                block = lax.bitwise_xor(here[0], masks[number // 2])
                row = pl.multiple_of((2 * block + number % 2) * half_rows, half_rows)
                target = full[which].at[pl.ds(row, half_rows)]
            copies.append(
                pltpu.make_async_copy(
                    unit.at[which], target, unit_sems.at[which * len(units) + number]
                )
            )
        return copies

    def row_copy(which, half):
        source, target = ((tokens, held_tokens), (cotangent, held_cotangent))[which]
        part = pl.ds(half * tile, tile)
        return pltpu.make_async_copy(
            source.at[part], target.at[part], row_sems.at[which * HALVES + half]
        )

    loads = [*unit_copies(0), row_copy(0, 0), *unit_copies(1), row_copy(1, 0), *unit_copies(2)]
    loads += [row_copy(which, half) for half in range(1, HALVES) for which in range(2)]
    for load in loads:
        load.start()
    for half in range(HALVES):
        part = slice(half * tile, (half + 1) * tile)
        for which, (low, factor) in enumerate(
            ((gate_low, gate_out), (up_low, up_out), (back_low, down_in))
        ):
            if half == 0:
                for copy in unit_copies(which):
                    copy.wait()
            if which != 1:
                row_copy(which // 2, half).wait()
                ref = (held_tokens, held_cotangent)[which // 2]
                left = width_part(ref, part, here, masks, rows)
                rest[which // 2][part, :] = width_part(ref, part, here, last, rows)
            for column in range(0, hidden, TILE):
                span = slice(column, column + TILE)
                if which == 2:
                    right = held_down[:, span]
                else:
                    right = jnp.concatenate(
                        [
                            full[which][
                                pl.ds(
                                    pl.multiple_of(lax.bitwise_xor(here[0], mask) * rows, rows), rows
                                ),
                                span,
                            ]
                            for mask in masks
                        ]
                    )
                sums[3 * half + which][:, span] = matrix_product(
                    left, right
                ) + adapter_scaling * matrix_product(low[part, :], factor[:, span])


def width_sums(here, tokens, cotangent, lows, factors, masks, order, arrays, last):
    rows, width = tokens.shape
    _, half, hidden = arrays[0].shape[-3:]
    vmem, anywhere = pl.BlockSpec(memory_space=pltpu.VMEM), pl.BlockSpec(memory_space=pl.ANY)
    shapes = [((rows // HALVES, hidden), jnp.float32)] * (3 * HALVES)
    shapes += [((rows, 2 * half * len(last)), jnp.bfloat16)] * 2
    shapes += [((width, hidden), jnp.bfloat16)] * 2
    outs = pl.pallas_call(
        functools.partial(sums_kernel, masks, order, len(arrays), last),
        in_specs=[pl.BlockSpec(memory_space=pltpu.SMEM)]
        + [vmem] * 6
        + [anywhere] * (2 + len(arrays)),
        out_specs=[vmem] * len(shapes),
        out_shape=[pltpu.VMEM(shape, kind) for shape, kind in shapes],
        scratch_shapes=[
            pltpu.VMEM((rows, width), jnp.bfloat16),
            pltpu.VMEM((rows, width), jnp.bfloat16),
            pltpu.VMEM((half * len(order), hidden), jnp.bfloat16),
            pltpu.SemaphoreType.DMA((2 * HALVES,)),
            pltpu.SemaphoreType.DMA((3 * len(order),)),
        ],
        compiler_params=pltpu.CompilerParams(vmem_limit_bytes=LIMITS["sums"] * MEBIBYTE),
        cost_estimate=pl.CostEstimate(flops=COSTS["sums"], bytes_accessed=0, transcendentals=0),
        name="width_sums",
    )(here, *lows, *factors, tokens, cotangent, *arrays)
    return outs[: 3 * HALVES], outs[3 * HALVES : -2], outs[-2:]


def last_kernel(half, here, left, back, gate_out, up_out, *refs):
    units, sums = refs[:4], refs[4:7]
    hidden_out, gate_grad_out, up_grad_out, low_out = refs[-4:]
    rows, hidden = hidden_out.shape
    part = slice(half * rows, (half + 1) * rows)
    gate_low = up_low = 0.0
    for column in range(0, hidden, STRIP):
        span = slice(column, column + STRIP)
        gate = sums[0][:, span] + matrix_product(left[part, :], stacked(units, 0, span))
        up = sums[1][:, span] + matrix_product(left[part, :], stacked(units, 1, span))
        hidden_grad = sums[2][:, span] + matrix_product(back[part, :], stacked(units, 2, span))
        sig = 1.0 / (1.0 + jnp.exp(-gate))
        gated = gate * sig
        hidden_out[:, span] = (gated * up).astype(jnp.bfloat16)
        gate_grad = (hidden_grad * up * sig * (1.0 + gate * (1.0 - sig))).astype(jnp.bfloat16)
        up_grad = (hidden_grad * gated).astype(jnp.bfloat16)
        gate_grad_out[:, span] = gate_grad
        up_grad_out[:, span] = up_grad
        gate_low += contract_trailing_axis(gate_grad, gate_out[:, span])
        up_low += contract_trailing_axis(up_grad, up_out[:, span])
    low_out[...] = jnp.concatenate([gate_low, up_low], axis=1)


def hidden_and_grads(half, here, parts, factors, tail, sums, ahead):
    rows = parts[0].shape[0] // HALVES
    rank, hidden = factors[0].shape
    return vmem_call(
        functools.partial(last_kernel, half),
        [here],
        [*parts, *factors, *tail, *sums[3 * half : 3 * half + 3]],
        ahead,
        [((rows, hidden), jnp.bfloat16)] * 3 + [((rows, 2 * rank), jnp.float32)],
        {},
        [],
        LIMITS["last"],
        COSTS["last"],
        "hidden_and_grads",
    )


def quarter_rows(here, quarter, full, tail, which, columns):
    rows = 2 * tail[0].shape[1]
    blocks = []
    for number in range(columns // rows):
        block = quarter * (columns // rows) + number
        mask = lax.bitwise_xor(here[0], block)
        held = full[pl.ds(pl.multiple_of(block * rows, rows), rows), :]
        near, far = (
            jnp.concatenate([unit[which] for unit in units]) for units in (tail[:2], tail[2:])
        )
        blocks.append(jnp.where(mask == 7, far, jnp.where(mask == 3, near, held)))
    return jnp.concatenate(blocks)


def token_grad_kernel(mode, step, here, gate_grad, up_grad, low, factor, gate, up, *refs):
    tail, refs = refs[:4], refs[4:]
    came = refs[: {"first": 0, "sum": 1, "both": 3, "last": 2}[mode]]
    outs = refs[-2:] if mode == "both" else refs[-1:]
    columns = outs[0].shape[1]
    quarter = sum(
        jnp.where(here[1] == place, order[step], 0) for place, order in enumerate(QUARTER_ORDER)
    )
    span = pl.ds(pl.multiple_of(quarter * columns, columns), columns)
    total = contract_trailing_axis(
        gate_grad[...], quarter_rows(here, quarter, gate, tail, 0, columns)
    )
    total += contract_trailing_axis(up_grad[...], quarter_rows(here, quarter, up, tail, 1, columns))
    total += matrix_product((adapter_scaling * low[...]).astype(jnp.bfloat16), factor[:, span])
    came = [ref[...].astype(jnp.float32) for ref in came]
    if mode == "both":
        first, left, right = came
        outs[0][...] = (jnp.where(here[1] == 2, first, total) + left).astype(jnp.bfloat16)
        outs[1][...] = (jnp.where(here[1] == 1, first, total) + right).astype(jnp.bfloat16)
    else:
        outs[0][...] = sum(came, total).astype(jnp.bfloat16)


def token_grad(mode, step, here, arrays, columns, came, ahead):
    rows, hidden = arrays[0].shape
    outs = vmem_call(
        functools.partial(token_grad_kernel, mode, step),
        [here],
        [*arrays, *came],
        ahead,
        [((rows, columns), jnp.bfloat16)] * (2 if mode == "both" else 1),
        {},
        [],
        LIMITS["token"],
        COSTS["token"],
        "token_grad",
    )
    return outs if mode == "both" else outs[0]


def last_token_grad(step, half, here, arrays, columns, came, ahead, before):
    rows, hidden = arrays[0].shape
    arrays = [*arrays, *came]
    return pl.pallas_call(
        functools.partial(token_grad_kernel, "last", step),
        grid=(1,),
        in_specs=[pl.BlockSpec(memory_space=pltpu.SMEM)]
        + [pl.BlockSpec(memory_space=pltpu.VMEM)] * len(arrays)
        + [pl.BlockSpec(memory_space=pl.ANY)] * (len(before) + len(ahead)),
        out_specs=pl.BlockSpec((rows, columns), lambda i: (half, 0)),
        out_shape=jax.ShapeDtypeStruct((HALVES * rows, columns), jnp.bfloat16),
        input_output_aliases={1 + len(arrays): 0} if before else {},
        compiler_params=pltpu.CompilerParams(vmem_limit_bytes=LIMITS["token"] * MEBIBYTE),
        cost_estimate=pl.CostEstimate(
            flops=COSTS["token"],
            bytes_accessed=0,
            transcendentals=0,
        ),
        name="last_token_grad",
    )(
        here,
        *[pltpu.with_memory_space_constraint(array, pltpu.VMEM) for array in arrays],
        *before,
        *ahead,
    )


def adapter_kernel(scaling, here, *refs):
    hidden, gate_grad, up_grad, low = (
        refs[number * HALVES : (number + 1) * HALVES] for number in range(4)
    )
    tokens, cotangent, turned, down_in = refs[4 * HALVES : 4 * HALVES + 4]
    keep, send, wide, narrow = refs[-4:]
    rank = down_in.shape[0]
    rows = hidden[0].shape[0]
    parts = [slice(half * rows, (half + 1) * rows) for half in range(HALVES)]
    wide[: 2 * rank, :] = scaling * sum(
        matrix_product(low[half][...].T.astype(jnp.bfloat16), tokens[part, :])
        for half, part in enumerate(parts)
    )
    wide[2 * rank :, :] = scaling * sum(
        matrix_product(
            contract_trailing_axis(down_in[...], hidden[half][...]).astype(jnp.bfloat16),
            cotangent[part, :],
        )
        for half, part in enumerate(parts)
    )
    for number, arrays in enumerate((hidden, gate_grad, up_grad)):
        source = (2, 0, 1)[number]
        narrow[number * rank : (number + 1) * rank, :] = scaling * sum(
            matrix_product(turned[source * rank : (source + 1) * rank, part], arrays[half][...])
            for half, part in enumerate(parts)
        )
    groups = 2 * keep.shape[0]
    wide_columns, narrow_columns = wide.shape[1] // groups, narrow.shape[1] // groups
    for mask in range(groups):
        out = (keep if mask < groups // 2 else send).at[mask % (groups // 2)]
        block = lax.bitwise_xor(here[0], mask)
        out[:, :wide_columns] = wide[
            :, pl.ds(pl.multiple_of(block * wide_columns, wide_columns), wide_columns)
        ]
        out[:, wide_columns:] = narrow[
            :, pl.ds(pl.multiple_of(block * narrow_columns, narrow_columns), narrow_columns)
        ]


def adapter_grads(scaling, here, groups, arrays, ahead):
    rows, width = arrays[-4].shape
    rank, hidden = arrays[-1].shape
    return vmem_call(
        functools.partial(adapter_kernel, scaling),
        [here],
        arrays,
        ahead,
        [((groups // 2, 3 * rank, (width + hidden) // groups), jnp.float32)] * 2,
        {},
        [pltpu.VMEM((3 * rank, width), jnp.float32), pltpu.VMEM((3 * rank, hidden), jnp.float32)],
        LIMITS["adapter"],
        COSTS["adapter"],
        "adapter_grads",
    )


def halve_kernel(here, keep, came, kept, send):
    count = kept.shape[0]
    kept[...] = keep[:count] + came[:count].astype(jnp.float32)
    send[...] = (keep[count:] + came[count:].astype(jnp.float32)).astype(send.dtype)


def halve(here, keep, came):
    shape = (keep.shape[0] // 2, *keep.shape[1:])
    return vmem_call(
        halve_kernel,
        [here],
        [keep, came],
        [],
        [(shape, jnp.float32), (shape, jnp.bfloat16)],
        {},
        [],
        LIMITS["small"],
        COSTS["small"],
        "halve",
    )


def sum_kernel(here, keep, *refs):
    refs[-1][...] = sum((ref[...].astype(jnp.float32) for ref in refs[:-1]), keep[...])


def last_sum(here, keep, came):
    return vmem_call(
        sum_kernel,
        [here],
        [keep, *came],
        [],
        [(keep.shape, jnp.float32)],
        {},
        [],
        LIMITS["small"],
        COSTS["small"],
        "last_sum",
        True,
    )[0]


def turn_kernel(wide_columns, here, kept, came, narrow, *refs):
    outs, wide = refs[:-1], refs[-1]
    total = kept[0] + came[0].astype(jnp.float32)
    narrow[...] = total[:, wide_columns:]
    wide[...] = total[:, :wide_columns].T
    for mask, out in enumerate(outs):
        rows = out.shape[0]
        block = pl.ds(pl.multiple_of(lax.bitwise_xor(here[1], mask) * rows, rows), rows)
        out[...] = wide[block, :].astype(out.dtype)


def turn(here, keep, came, wide_columns, quarters):
    _, rows, columns = keep.shape
    return vmem_call(
        functools.partial(turn_kernel, wide_columns),
        [here],
        [keep, came],
        [],
        [((rows, columns - wide_columns), jnp.float32)]
        + [
            ((wide_columns // quarters, rows), jnp.bfloat16 if mask else jnp.float32)
            for mask in range(quarters)
        ],
        {},
        [pltpu.VMEM((wide_columns, rows), jnp.float32)],
        LIMITS["small"],
        COSTS["small"],
        "turn",
    )


def whole_kernel(here, near, far, out):
    columns = near.shape[2]
    for number in range(2 * near.shape[0]):
        ref = near if number < near.shape[0] else far
        block = lax.bitwise_xor(here[0], number) * columns
        out[:, pl.ds(pl.multiple_of(block, columns), columns)] = ref[number % near.shape[0]]


def whole(here, near, far):
    count, rows, columns = near.shape
    return vmem_call(
        whole_kernel,
        [here],
        [near, far],
        [],
        [((rows, 2 * count * columns), near.dtype)],
        {},
        [],
        LIMITS["small"],
        COSTS["small"],
        "whole",
        True,
    )[0]


def square_plane(
    tokens,
    cotangent,
    gate_frozen_matrix,
    up_frozen_matrix,
    down_frozen_matrix,
    gate_adapter_input_factor,
    up_adapter_input_factor,
    gate_adapter_output_factor,
    up_adapter_output_factor,
    down_adapter_input_factor,
    down_leave,
):
    groups = lax.axis_size(("cuts", "fsdp"))
    quarters = lax.axis_size("tp")
    rows, width = tokens.shape
    gradient_scaling = adapter_scaling / math.sqrt(rows * groups)
    here = jnp.stack([lax.axis_index(("cuts", "fsdp")), lax.axis_index("tp")]).astype(jnp.int32)
    gate_in, up_in, leave, down_in = (
        array.T
        for array in (
            gate_adapter_input_factor,
            up_adapter_input_factor,
            down_leave,
            down_adapter_input_factor,
        )
    )
    gate_out, up_out = gate_adapter_output_factor, up_adapter_output_factor

    units = {}
    units[0, 0], units[0, 1] = own_units(
        gate_frozen_matrix, up_frozen_matrix, down_frozen_matrix
    )
    units[1, 0] = flip(units[0, 0], "fsdp", 1)
    units[2, 1] = flip(units[0, 1], "fsdp", 2)
    units[1, 1] = flip(units[0, 1], "fsdp", 1)
    units[2, 0] = flip(units[0, 0], "fsdp", 2)
    units[3, 0] = flip(units[1, 0], "fsdp", 2)
    units[3, 1] = flip(units[2, 1], "fsdp", 1)
    for half in range(2):
        units[4, half] = flip(units[0, half], "cuts", 1)
    *lows, turned = low_rank_values(
        tokens, cotangent, [gate_in, up_in, leave], [here, *[units[key] for key in ((1, 0), (2, 1), (4, 0), (4, 1))]]
    )
    pairs = {}
    for number, (one, two, ahead) in enumerate(
        (((1, 0), (2, 1), [turned]), ((1, 1), (2, 0), [turned]))
    ):
        pairs[number] = flip(pair(units[one], units[two], ahead), "cuts", 1)
    keys = [(0, 0), (0, 1), (1, 0), (1, 1), (2, 0), (2, 1), (4, 0), (4, 1)]
    placed = keys + [(5, 0), (6, 1), (5, 1), (6, 0)]
    arrays = [units[key] for key in keys] + [pairs[0], pairs[1]]
    masks = (0, 1, 2, 4, 5, 6)
    order = [placed.index((mask, half)) for mask in masks for half in range(2)]
    sums, parts, full = width_sums(
        here, tokens, cotangent, lows, [gate_out, up_out, down_in], masks, order, arrays, (3, 7)
    )
    tail = list(hold([units[3, 0], units[3, 1]], [sums[0]]))
    tail += [flip(unit, "cuts", 1) for unit in tail]

    factor = jnp.concatenate([gate_in, up_in])
    shift = lambda array, pairs: lax.ppermute(array, "tp", pairs)
    states, first = [], []
    share = lambda step, half, mode, came=(), ahead=(): token_grad(
        mode,
        step,
        here,
        [*states[half][1:], factor, *full, *tail],
        width // quarters,
        came,
        ahead,
    )
    both = range(HALVES)
    for half in both:
        state = hidden_and_grads(
            half, here, parts, [gate_out, up_out], tail, sums, first[:]
        )
        states.append(state)
        first.append(share(0, half, "first"))
    came = [shift(part, [(0, 1), (3, 2)]) for part in first]
    partial = []
    for half in both:
        partial.append(share(1, half, "sum", [came[half]], partial or first[1:]))
    second = partial
    from_left = [shift(part, [(0, 1), (1, 2)]) for part in partial]
    from_right = [shift(part, [(3, 2), (2, 1)]) for part in partial]
    keep, send = adapter_grads(
        gradient_scaling,
        here,
        groups,
        [
            *[state[number] for number in range(4) for state in states],
            tokens,
            cotangent,
            turned,
            down_in,
        ],
        first,
    )
    keep, send = halve(here, keep, flip(send, "cuts", 1))
    keep, send = halve(here, keep, flip(send, "fsdp", 2))
    narrow, keep, *send = turn(here, keep, flip(send, "fsdp", 1), width // groups, quarters)
    wide_grads = last_sum(
        here, keep, [flip(part, "tp", 1 + number) for number, part in enumerate(send)]
    )
    near = jnp.stack([narrow, flip(narrow, "fsdp", 1)])
    near = jnp.concatenate([near, flip(near, "fsdp", 2)])
    narrow_turned = whole(here, near, flip(near, "cuts", 1))
    narrow_grads = narrow_turned.T

    partial = []
    for half in both:
        partial.append(
            share(
                2,
                half,
                "both",
                [first[half], from_left[half], from_right[half]],
                partial[0][:1] if partial else second[1:],
            )
        )
    from_left = [shift(part[0], [(0, 1), (1, 2), (2, 3)]) for part in partial]
    from_right = [shift(part[1], [(3, 2), (2, 1), (1, 0)]) for part in partial]

    results = []
    for half in both:
        results.append(
            last_token_grad(
                3,
                half,
                here,
                [*states[half][1:], factor, *full, *tail],
                width // quarters,
                [from_left[half], from_right[half]],
                [narrow_turned] if half else partial[1],
                results[:],
            )
        )
    token_input_gradient = results[-1]
    return (token_input_gradient, wide_grads, narrow_grads)


def per_device(*arrays):
    sizes = [lax.axis_size(axis) for axis in ("cuts", "fsdp", "tp")]
    return (square_plane if sizes == [2, 4, 4] else any_plane)(*arrays)


def solution(mesh):
    in_specs = (
        P(("cuts", "fsdp"), None),
        P(("cuts", "fsdp"), None),
        P(("cuts", "fsdp"), "tp"),
        P(("cuts", "fsdp"), "tp"),
        P("tp", ("cuts", "fsdp")),
        P(),
        P(),
        P(None, "tp"),
        P(None, "tp"),
        P("tp", None),
        P(),
    )
    out_specs = (P(("cuts", "fsdp"), "tp"), P(("cuts", "fsdp", "tp"), None), P("tp", None))
    return jax.shard_map(
        per_device, mesh=mesh, in_specs=in_specs, out_specs=out_specs, check_vma=False
    )
```

```python
import functools
import math

import jax
import jax.numpy as jnp
from jax import lax
from jax.experimental import pallas as pl
from jax.experimental.pallas import tpu as pltpu
from jax.sharding import PartitionSpec as P

adapter_scaling = 0.5
MEBIBYTE = 1024 * 1024
COST = 1
HALVES = 2
COSTS = {"sums": 1, "pair": 1, "small": 1, "token": 20 * 10**9, "adapter": 20 * 10**9, "last": 10**11}
LIMITS = {"low": 6, "sums": 25, "last": 14, "token": 8, "adapter": 12, "small": 4}
TILE = 512
STRIP = 256
QUARTER_ORDER = ((3, 2, 1, 0), (0, 3, 2, 1), (3, 0, 1, 2), (0, 1, 2, 3))


def matrix_product(left, right):
    return jnp.dot(left, right, preferred_element_type=jnp.float32)


def contract_trailing_axis(left, right):
    return lax.dot_general(
        left, right, (((1,), (1,)), ((), ())), preferred_element_type=jnp.float32
    )


def contract_first(left, right):
    return lax.dot_general(
        left, right, (((0,), (0,)), ((), ())), preferred_element_type=jnp.float32
    )


def any_plane(
    tokens,
    cotangent,
    gate_frozen_matrix,
    up_frozen_matrix,
    down_frozen_matrix,
    gate_adapter_input_factor,
    up_adapter_input_factor,
    gate_adapter_output_factor,
    up_adapter_output_factor,
    down_adapter_input_factor,
    down_leave,
):
    token_groups = lax.axis_size(("cuts", "fsdp"))
    quarters = lax.axis_size("tp")
    tp_index = lax.axis_index("tp")
    token_rows = tokens.shape[0]
    width = tokens.shape[1]
    gradient_scaling = adapter_scaling / math.sqrt(token_rows * token_groups)
    gate_adapter_hidden = matrix_product(tokens, gate_adapter_input_factor).astype(jnp.bfloat16)
    up_adapter_hidden = matrix_product(tokens, up_adapter_input_factor).astype(jnp.bfloat16)
    pieces = (
        lax.all_gather(gate_frozen_matrix, ("cuts", "fsdp"), axis=0, tiled=True),
        lax.all_gather(up_frozen_matrix, ("cuts", "fsdp"), axis=0, tiled=True),
    )
    columns = tokens
    gate_frozen_output = matrix_product(columns, pieces[0])
    up_frozen_output = matrix_product(columns, pieces[1])
    gate_preactivation = gate_frozen_output + adapter_scaling * matrix_product(
        gate_adapter_hidden, gate_adapter_output_factor
    )
    up_preactivation = up_frozen_output + adapter_scaling * matrix_product(
        up_adapter_hidden, up_adapter_output_factor
    )
    sig = jax.nn.sigmoid(gate_preactivation)
    hidden = (gate_preactivation * sig * up_preactivation).astype(jnp.bfloat16)
    down_part = matrix_product(hidden, down_adapter_input_factor)
    down_low = lax.psum(down_part.astype(jnp.bfloat16), "tp")
    backward_adapter_input = matrix_product(cotangent, down_leave).astype(jnp.bfloat16)
    columns = cotangent
    hidden_state_gradient = contract_trailing_axis(
        columns, lax.all_gather(down_frozen_matrix, ("cuts", "fsdp"), axis=1, tiled=True)
    )
    hidden_state_gradient = hidden_state_gradient + adapter_scaling * contract_trailing_axis(
        backward_adapter_input, down_adapter_input_factor
    )
    gate_output_gradient = (
        hidden_state_gradient * up_preactivation * sig * (1.0 + gate_preactivation * (1.0 - sig))
    ).astype(jnp.bfloat16)
    up_output_gradient = (hidden_state_gradient * gate_preactivation * sig).astype(jnp.bfloat16)
    gate_part = contract_trailing_axis(gate_output_gradient, gate_adapter_output_factor)
    up_part = contract_trailing_axis(up_output_gradient, up_adapter_output_factor)
    gate_sum, up_sum = lax.psum((gate_part, up_part), "tp")
    gate_backward_adapter = gate_sum.astype(jnp.bfloat16)
    up_backward_adapter = up_sum.astype(jnp.bfloat16)
    pieces = lax.all_gather(
        (gate_frozen_matrix, up_frozen_matrix), ("cuts", "fsdp"), axis=0, tiled=True
    )
    partial_value = contract_trailing_axis(
        gate_output_gradient, pieces[0]
    ) + contract_trailing_axis(up_output_gradient, pieces[1])
    frozen_path_gradient = lax.psum_scatter(partial_value, "tp", scatter_dimension=1, tiled=True)
    slice_width = width // quarters
    gate_slice = lax.dynamic_slice_in_dim(
        gate_adapter_input_factor, tp_index * slice_width, slice_width, 0
    )
    up_slice = lax.dynamic_slice_in_dim(
        up_adapter_input_factor, tp_index * slice_width, slice_width, 0
    )
    adapter_hidden_gradient = contract_trailing_axis(
        gate_backward_adapter, gate_slice
    ) + contract_trailing_axis(up_backward_adapter, up_slice)
    token_input_gradient = (
        frozen_path_gradient + adapter_scaling * adapter_hidden_gradient
    ).astype(jnp.bfloat16)
    narrow_part = gradient_scaling * jnp.concatenate(
        [
            contract_first(hidden, backward_adapter_input),
            contract_first(gate_output_gradient, gate_adapter_hidden),
            contract_first(up_output_gradient, up_adapter_hidden),
        ],
        axis=1,
    )
    narrow_grads = lax.psum(narrow_part, ("cuts", "fsdp"))
    token_side = jnp.concatenate([gate_backward_adapter, up_backward_adapter], axis=1)
    group_rows = lax.psum_scatter(
        gradient_scaling
        * jnp.concatenate(
            [contract_first(tokens, token_side), contract_first(cotangent, down_low)], axis=1
        ),
        ("cuts", "fsdp"),
        scatter_dimension=0,
        tiled=True,
    )
    fine_rows = width // (token_groups * quarters)
    wide_grads = lax.dynamic_slice_in_dim(group_rows, tp_index * fine_rows, fine_rows, 0)
    return (token_input_gradient, wide_grads, narrow_grads)


def flip(array, axis, bit):
    size = lax.axis_size(axis)
    return lax.ppermute(array, axis, [(i, i ^ bit) for i in range(size)])


def vmem_call(
    kernel, scalars, arrays, ahead, results, aliases, scratch, limit, flops, name, final=False
):
    vmem = pl.BlockSpec(memory_space=pltpu.VMEM)
    first = len(scalars)
    return pl.pallas_call(
        kernel,
        in_specs=[pl.BlockSpec(memory_space=pltpu.SMEM)] * first
        + [vmem] * len(arrays)
        + [pl.BlockSpec(memory_space=pl.ANY)] * len(ahead),
        out_specs=[vmem] * len(results),
        out_shape=[
            jax.ShapeDtypeStruct(shape, kind) if final else pltpu.VMEM(shape, kind)
            for shape, kind in results
        ],
        scratch_shapes=scratch,
        input_output_aliases={first + source: target for source, target in aliases.items()},
        compiler_params=pltpu.CompilerParams(vmem_limit_bytes=limit * MEBIBYTE),
        cost_estimate=pl.CostEstimate(flops=COST * flops, bytes_accessed=0, transcendentals=0),
        name=name,
    )(
        *scalars,
        *[pltpu.with_memory_space_constraint(array, pltpu.VMEM) for array in arrays],
        *ahead,
    )


def width_part(ref, part, here, masks, rows):
    return jnp.concatenate(
        [
            ref[part, pl.ds(pl.multiple_of(lax.bitwise_xor(here[0], mask) * rows, rows), rows)]
            for mask in masks
        ],
        axis=1,
    )


def stacked(units, which, span):
    return jnp.concatenate([unit[which, :, span] for unit in units], axis=0)


def lows_kernel(tokens, cotangent, gate_in, up_in, leave, *refs):
    gate_low, up_low, back_low, turned = refs[-4:]
    rank = leave.shape[0]
    for number, (ref, factor, out) in enumerate(
        ((tokens, gate_in, gate_low), (tokens, up_in, up_low), (cotangent, leave, back_low))
    ):
        low = contract_trailing_axis(ref[...], factor[...]).astype(jnp.bfloat16)
        out[...] = low
        turned[number * rank : (number + 1) * rank, :] = low.astype(jnp.float32).T.astype(
            jnp.bfloat16
        )


def low_rank_values(tokens, cotangent, factors, ahead):
    rows, width = tokens.shape
    rank = factors[0].shape[0]
    tile = rows // 4
    by_rows = lambda columns: pl.BlockSpec((tile, columns), lambda i: (i, 0))
    return pl.pallas_call(
        lows_kernel,
        grid=(rows // tile,),
        in_specs=[by_rows(width)] * 2
        + [pl.BlockSpec((rank, width), lambda i: (0, 0))] * 3
        + [pl.BlockSpec(memory_space=pl.ANY)] * len(ahead),
        out_specs=[by_rows(rank)] * 3 + [pl.BlockSpec((3 * rank, tile), lambda i: (0, i))],
        out_shape=[jax.ShapeDtypeStruct((rows, rank), jnp.bfloat16)] * 3
        + [jax.ShapeDtypeStruct((3 * rank, rows), jnp.bfloat16)],
        compiler_params=pltpu.CompilerParams(vmem_limit_bytes=LIMITS["low"] * MEBIBYTE),
        cost_estimate=pl.CostEstimate(
            flops=480 * COST * rows * width * rank, bytes_accessed=0, transcendentals=0
        ),
        name="low_rank_values",
    )(tokens, cotangent, *factors, *ahead)


def own_kernel(gate, up, down, *refs):
    units, (held, sems) = refs[:2], refs[2:]
    rows = units[0].shape[1]
    down_copy = pltpu.make_async_copy(down, held, sems.at[0])
    down_copy.start()
    copies = []
    for half, unit in enumerate(units):
        for which, ref in enumerate((gate, up)):
            copies.append(
                pltpu.make_async_copy(
                    ref.at[pl.ds(half * rows, rows)], unit.at[which], sems.at[1 + len(copies)]
                )
            )
    for copy in copies:
        copy.start()
    down_copy.wait()
    for half, unit in enumerate(units):
        part = slice(half * rows, (half + 1) * rows)
        unit[2] = held[:, part].astype(jnp.float32).T.astype(jnp.bfloat16)
    for copy in copies:
        copy.wait()


def own_units(gate, up, down):
    rows, hidden = gate.shape
    return pl.pallas_call(
        own_kernel,
        in_specs=[pl.BlockSpec(memory_space=pl.ANY)] * 3,
        out_specs=[pl.BlockSpec(memory_space=pltpu.VMEM)] * 2,
        out_shape=[pltpu.VMEM((3, rows // 2, hidden), jnp.bfloat16)] * 2,
        scratch_shapes=[
            pltpu.VMEM((hidden, rows), jnp.bfloat16),
            pltpu.SemaphoreType.DMA((5,)),
        ],
        compiler_params=pltpu.CompilerParams(vmem_limit_bytes=LIMITS["low"] * MEBIBYTE),
        cost_estimate=pl.CostEstimate(flops=MEBIBYTE, bytes_accessed=0, transcendentals=0),
        name="own_units",
    )(*[pltpu.with_memory_space_constraint(array, pltpu.HBM) for array in (gate, up, down)])


def nothing_kernel(*refs):
    pass


def hold(arrays, ahead):
    anywhere = pl.BlockSpec(memory_space=pl.ANY)
    return pl.pallas_call(
        nothing_kernel,
        in_specs=[anywhere] * (len(arrays) + len(ahead)),
        out_specs=[anywhere] * len(arrays),
        out_shape=[jax.ShapeDtypeStruct(array.shape, array.dtype) for array in arrays],
        input_output_aliases={number: number for number in range(len(arrays))},
        compiler_params=pltpu.CompilerParams(vmem_limit_bytes=MEBIBYTE),
        cost_estimate=pl.CostEstimate(flops=1, bytes_accessed=1, transcendentals=0),
        name="hold",
    )(*arrays, *ahead)


def pair_kernel(first, second, *refs):
    refs[-1][0] = first[...]
    refs[-1][1] = second[...]


def pair(first, second, ahead):
    return vmem_call(
        pair_kernel,
        [],
        [first, second],
        ahead,
        [((2, *first.shape), first.dtype)],
        {},
        [],
        LIMITS["small"],
        COSTS["pair"],
        "pair",
    )[0]


def sums_kernel(masks, order, n_arrays, last, here, *refs):
    gate_low, up_low, back_low, gate_out, up_out, down_in, tokens, cotangent = refs[:8]
    units = []
    for ref in refs[8 : 8 + n_arrays]:
        units += [ref] if len(ref.shape) == 3 else [ref.at[0], ref.at[1]]
    units = [units[number] for number in order]
    outs = refs[8 + n_arrays :]
    sums, rest, full = outs[: 3 * HALVES], outs[3 * HALVES : 3 * HALVES + 2], outs[-7:-5]
    held_tokens, held_cotangent, held_down, row_sems, unit_sems = outs[-5:]
    half_rows, hidden = units[0].shape[1:]
    rows = 2 * half_rows
    tile = tokens.shape[0] // HALVES

    def unit_copies(which):
        copies = []
        for number, unit in enumerate(units):
            if which == 2:
                target = held_down.at[pl.ds(number * half_rows, half_rows)]
            else:
                block = lax.bitwise_xor(here[0], masks[number // 2])
                row = pl.multiple_of((2 * block + number % 2) * half_rows, half_rows)
                target = full[which].at[pl.ds(row, half_rows)]
            copies.append(
                pltpu.make_async_copy(
                    unit.at[which], target, unit_sems.at[which * len(units) + number]
                )
            )
        return copies

    def row_copy(which, half):
        source, target = ((tokens, held_tokens), (cotangent, held_cotangent))[which]
        part = pl.ds(half * tile, tile)
        return pltpu.make_async_copy(
            source.at[part], target.at[part], row_sems.at[which * HALVES + half]
        )

    loads = [*unit_copies(0), row_copy(0, 0), *unit_copies(1), row_copy(1, 0), *unit_copies(2)]
    loads += [row_copy(which, half) for half in range(1, HALVES) for which in range(2)]
    for load in loads:
        load.start()
    for half in range(HALVES):
        part = slice(half * tile, (half + 1) * tile)
        for which, (low, factor) in enumerate(
            ((gate_low, gate_out), (up_low, up_out), (back_low, down_in))
        ):
            if half == 0:
                for copy in unit_copies(which):
                    copy.wait()
            if which != 1:
                row_copy(which // 2, half).wait()
                ref = (held_tokens, held_cotangent)[which // 2]
                left = width_part(ref, part, here, masks, rows)
                rest[which // 2][part, :] = width_part(ref, part, here, last, rows)
            for column in range(0, hidden, TILE):
                span = slice(column, column + TILE)
                if which == 2:
                    right = held_down[:, span]
                else:
                    right = jnp.concatenate(
                        [
                            full[which][
                                pl.ds(
                                    pl.multiple_of(lax.bitwise_xor(here[0], mask) * rows, rows), rows
                                ),
                                span,
                            ]
                            for mask in masks
                        ]
                    )
                sums[3 * half + which][:, span] = matrix_product(
                    left, right
                ) + adapter_scaling * matrix_product(low[part, :], factor[:, span])


def width_sums(here, tokens, cotangent, lows, factors, masks, order, arrays, last):
    rows, width = tokens.shape
    _, half, hidden = arrays[0].shape[-3:]
    vmem, anywhere = pl.BlockSpec(memory_space=pltpu.VMEM), pl.BlockSpec(memory_space=pl.ANY)
    shapes = [((rows // HALVES, hidden), jnp.float32)] * (3 * HALVES)
    shapes += [((rows, 2 * half * len(last)), jnp.bfloat16)] * 2
    shapes += [((width, hidden), jnp.bfloat16)] * 2
    outs = pl.pallas_call(
        functools.partial(sums_kernel, masks, order, len(arrays), last),
        in_specs=[pl.BlockSpec(memory_space=pltpu.SMEM)]
        + [vmem] * 6
        + [anywhere] * (2 + len(arrays)),
        out_specs=[vmem] * len(shapes),
        out_shape=[pltpu.VMEM(shape, kind) for shape, kind in shapes],
        scratch_shapes=[
            pltpu.VMEM((rows, width), jnp.bfloat16),
            pltpu.VMEM((rows, width), jnp.bfloat16),
            pltpu.VMEM((half * len(order), hidden), jnp.bfloat16),
            pltpu.SemaphoreType.DMA((2 * HALVES,)),
            pltpu.SemaphoreType.DMA((3 * len(order),)),
        ],
        compiler_params=pltpu.CompilerParams(vmem_limit_bytes=LIMITS["sums"] * MEBIBYTE),
        cost_estimate=pl.CostEstimate(flops=COSTS["sums"], bytes_accessed=0, transcendentals=0),
        name="width_sums",
    )(here, *lows, *factors, tokens, cotangent, *arrays)
    return outs[: 3 * HALVES], outs[3 * HALVES : -2], outs[-2:]


def last_kernel(half, here, left, back, gate_out, up_out, *refs):
    units, sums = refs[:4], refs[4:7]
    hidden_out, gate_grad_out, up_grad_out, low_out = refs[-4:]
    rows, hidden = hidden_out.shape
    part = slice(half * rows, (half + 1) * rows)
    gate_low = up_low = 0.0
    for column in range(0, hidden, STRIP):
        span = slice(column, column + STRIP)
        gate = sums[0][:, span] + matrix_product(left[part, :], stacked(units, 0, span))
        up = sums[1][:, span] + matrix_product(left[part, :], stacked(units, 1, span))
        hidden_grad = sums[2][:, span] + matrix_product(back[part, :], stacked(units, 2, span))
        sig = 1.0 / (1.0 + jnp.exp(-gate))
        gated = gate * sig
        hidden_out[:, span] = (gated * up).astype(jnp.bfloat16)
        gate_grad = (hidden_grad * up * sig * (1.0 + gate * (1.0 - sig))).astype(jnp.bfloat16)
        up_grad = (hidden_grad * gated).astype(jnp.bfloat16)
        gate_grad_out[:, span] = gate_grad
        up_grad_out[:, span] = up_grad
        gate_low += contract_trailing_axis(gate_grad, gate_out[:, span])
        up_low += contract_trailing_axis(up_grad, up_out[:, span])
    low_out[...] = jnp.concatenate([gate_low, up_low], axis=1)


def hidden_and_grads(half, here, parts, factors, tail, sums, ahead):
    rows = parts[0].shape[0] // HALVES
    rank, hidden = factors[0].shape
    return vmem_call(
        functools.partial(last_kernel, half),
        [here],
        [*parts, *factors, *tail, *sums[3 * half : 3 * half + 3]],
        ahead,
        [((rows, hidden), jnp.bfloat16)] * 3 + [((rows, 2 * rank), jnp.float32)],
        {},
        [],
        LIMITS["last"],
        COSTS["last"],
        "hidden_and_grads",
    )


def quarter_rows(here, quarter, full, tail, which, columns):
    rows = 2 * tail[0].shape[1]
    blocks = []
    for number in range(columns // rows):
        block = quarter * (columns // rows) + number
        mask = lax.bitwise_xor(here[0], block)
        held = full[pl.ds(pl.multiple_of(block * rows, rows), rows), :]
        near, far = (
            jnp.concatenate([unit[which] for unit in units]) for units in (tail[:2], tail[2:])
        )
        blocks.append(jnp.where(mask == 7, far, jnp.where(mask == 3, near, held)))
    return jnp.concatenate(blocks)


def token_grad_kernel(mode, step, here, gate_grad, up_grad, low, factor, gate, up, *refs):
    tail, refs = refs[:4], refs[4:]
    came = refs[: {"first": 0, "sum": 1, "both": 3, "last": 2}[mode]]
    outs = refs[-2:] if mode == "both" else refs[-1:]
    columns = outs[0].shape[1]
    quarter = sum(
        jnp.where(here[1] == place, order[step], 0) for place, order in enumerate(QUARTER_ORDER)
    )
    span = pl.ds(pl.multiple_of(quarter * columns, columns), columns)
    total = contract_trailing_axis(
        gate_grad[...], quarter_rows(here, quarter, gate, tail, 0, columns)
    )
    total += contract_trailing_axis(up_grad[...], quarter_rows(here, quarter, up, tail, 1, columns))
    total += matrix_product((adapter_scaling * low[...]).astype(jnp.bfloat16), factor[:, span])
    came = [ref[...].astype(jnp.float32) for ref in came]
    if mode == "both":
        first, left, right = came
        outs[0][...] = (jnp.where(here[1] == 2, first, total) + left).astype(jnp.bfloat16)
        outs[1][...] = (jnp.where(here[1] == 1, first, total) + right).astype(jnp.bfloat16)
    else:
        outs[0][...] = sum(came, total).astype(jnp.bfloat16)


def token_grad(mode, step, here, arrays, columns, came, ahead):
    rows, hidden = arrays[0].shape
    outs = vmem_call(
        functools.partial(token_grad_kernel, mode, step),
        [here],
        [*arrays, *came],
        ahead,
        [((rows, columns), jnp.bfloat16)] * (2 if mode == "both" else 1),
        {},
        [],
        LIMITS["token"],
        COSTS["token"],
        "token_grad",
    )
    return outs if mode == "both" else outs[0]


def last_token_grad(step, half, here, arrays, columns, came, ahead, before):
    rows, hidden = arrays[0].shape
    arrays = [*arrays, *came]
    return pl.pallas_call(
        functools.partial(token_grad_kernel, "last", step),
        grid=(1,),
        in_specs=[pl.BlockSpec(memory_space=pltpu.SMEM)]
        + [pl.BlockSpec(memory_space=pltpu.VMEM)] * len(arrays)
        + [pl.BlockSpec(memory_space=pl.ANY)] * (len(before) + len(ahead)),
        out_specs=pl.BlockSpec((rows, columns), lambda i: (half, 0)),
        out_shape=jax.ShapeDtypeStruct((HALVES * rows, columns), jnp.bfloat16),
        input_output_aliases={1 + len(arrays): 0} if before else {},
        compiler_params=pltpu.CompilerParams(vmem_limit_bytes=LIMITS["token"] * MEBIBYTE),
        cost_estimate=pl.CostEstimate(
            flops=COSTS["token"],
            bytes_accessed=0,
            transcendentals=0,
        ),
        name="last_token_grad",
    )(
        here,
        *[pltpu.with_memory_space_constraint(array, pltpu.VMEM) for array in arrays],
        *before,
        *ahead,
    )


def adapter_kernel(scaling, here, *refs):
    hidden, gate_grad, up_grad, low = (
        refs[number * HALVES : (number + 1) * HALVES] for number in range(4)
    )
    tokens, cotangent, turned, down_in = refs[4 * HALVES : 4 * HALVES + 4]
    keep, send, wide, narrow = refs[-4:]
    rank = down_in.shape[0]
    rows = hidden[0].shape[0]
    parts = [slice(half * rows, (half + 1) * rows) for half in range(HALVES)]
    wide[: 2 * rank, :] = scaling * sum(
        matrix_product(low[half][...].T.astype(jnp.bfloat16), tokens[part, :])
        for half, part in enumerate(parts)
    )
    wide[2 * rank :, :] = scaling * sum(
        matrix_product(
            contract_trailing_axis(down_in[...], hidden[half][...]).astype(jnp.bfloat16),
            cotangent[part, :],
        )
        for half, part in enumerate(parts)
    )
    for number, arrays in enumerate((hidden, gate_grad, up_grad)):
        source = (2, 0, 1)[number]
        narrow[number * rank : (number + 1) * rank, :] = scaling * sum(
            matrix_product(turned[source * rank : (source + 1) * rank, part], arrays[half][...])
            for half, part in enumerate(parts)
        )
    groups = 2 * keep.shape[0]
    wide_columns, narrow_columns = wide.shape[1] // groups, narrow.shape[1] // groups
    for mask in range(groups):
        out = (keep if mask < groups // 2 else send).at[mask % (groups // 2)]
        block = lax.bitwise_xor(here[0], mask)
        out[:, :wide_columns] = wide[
            :, pl.ds(pl.multiple_of(block * wide_columns, wide_columns), wide_columns)
        ]
        out[:, wide_columns:] = narrow[
            :, pl.ds(pl.multiple_of(block * narrow_columns, narrow_columns), narrow_columns)
        ]


def adapter_grads(scaling, here, groups, arrays, ahead):
    rows, width = arrays[-4].shape
    rank, hidden = arrays[-1].shape
    return vmem_call(
        functools.partial(adapter_kernel, scaling),
        [here],
        arrays,
        ahead,
        [((groups // 2, 3 * rank, (width + hidden) // groups), jnp.float32)] * 2,
        {},
        [pltpu.VMEM((3 * rank, width), jnp.float32), pltpu.VMEM((3 * rank, hidden), jnp.float32)],
        LIMITS["adapter"],
        COSTS["adapter"],
        "adapter_grads",
    )


def halve_kernel(here, keep, came, kept, send):
    count = kept.shape[0]
    kept[...] = keep[:count] + came[:count].astype(jnp.float32)
    send[...] = (keep[count:] + came[count:].astype(jnp.float32)).astype(send.dtype)


def halve(here, keep, came):
    shape = (keep.shape[0] // 2, *keep.shape[1:])
    return vmem_call(
        halve_kernel,
        [here],
        [keep, came],
        [],
        [(shape, jnp.float32), (shape, jnp.bfloat16)],
        {},
        [],
        LIMITS["small"],
        COSTS["small"],
        "halve",
    )


def sum_kernel(here, keep, *refs):
    refs[-1][...] = sum((ref[...].astype(jnp.float32) for ref in refs[:-1]), keep[...])


def last_sum(here, keep, came):
    return vmem_call(
        sum_kernel,
        [here],
        [keep, *came],
        [],
        [(keep.shape, jnp.float32)],
        {},
        [],
        LIMITS["small"],
        COSTS["small"],
        "last_sum",
        True,
    )[0]


def turn_kernel(wide_columns, here, kept, came, narrow, *refs):
    outs, wide = refs[:-1], refs[-1]
    total = kept[0] + came[0].astype(jnp.float32)
    narrow[...] = total[:, wide_columns:]
    wide[...] = total[:, :wide_columns].T
    for mask, out in enumerate(outs):
        rows = out.shape[0]
        block = pl.ds(pl.multiple_of(lax.bitwise_xor(here[1], mask) * rows, rows), rows)
        out[...] = wide[block, :].astype(out.dtype)


def turn(here, keep, came, wide_columns, quarters):
    _, rows, columns = keep.shape
    return vmem_call(
        functools.partial(turn_kernel, wide_columns),
        [here],
        [keep, came],
        [],
        [((rows, columns - wide_columns), jnp.float32)]
        + [
            ((wide_columns // quarters, rows), jnp.bfloat16 if mask else jnp.float32)
            for mask in range(quarters)
        ],
        {},
        [pltpu.VMEM((wide_columns, rows), jnp.float32)],
        LIMITS["small"],
        COSTS["small"],
        "turn",
    )


def whole_kernel(here, near, far, out):
    columns = near.shape[2]
    for number in range(2 * near.shape[0]):
        ref = near if number < near.shape[0] else far
        block = lax.bitwise_xor(here[0], number) * columns
        out[:, pl.ds(pl.multiple_of(block, columns), columns)] = ref[number % near.shape[0]]


def whole(here, near, far):
    count, rows, columns = near.shape
    return vmem_call(
        whole_kernel,
        [here],
        [near, far],
        [],
        [((rows, 2 * count * columns), near.dtype)],
        {},
        [],
        LIMITS["small"],
        COSTS["small"],
        "whole",
        True,
    )[0]


def square_plane(
    tokens,
    cotangent,
    gate_frozen_matrix,
    up_frozen_matrix,
    down_frozen_matrix,
    gate_adapter_input_factor,
    up_adapter_input_factor,
    gate_adapter_output_factor,
    up_adapter_output_factor,
    down_adapter_input_factor,
    down_leave,
):
    groups = lax.axis_size(("cuts", "fsdp"))
    quarters = lax.axis_size("tp")
    rows, width = tokens.shape
    gradient_scaling = adapter_scaling / math.sqrt(rows * groups)
    here = jnp.stack([lax.axis_index(("cuts", "fsdp")), lax.axis_index("tp")]).astype(jnp.int32)
    gate_in, up_in, leave, down_in = (
        array.T
        for array in (
            gate_adapter_input_factor,
            up_adapter_input_factor,
            down_leave,
            down_adapter_input_factor,
        )
    )
    gate_out, up_out = gate_adapter_output_factor, up_adapter_output_factor

    units = {}
    units[0, 0], units[0, 1] = own_units(
        gate_frozen_matrix, up_frozen_matrix, down_frozen_matrix
    )
    units[1, 0] = flip(units[0, 0], "fsdp", 1)
    units[2, 1] = flip(units[0, 1], "fsdp", 2)
    units[1, 1] = flip(units[0, 1], "fsdp", 1)
    units[2, 0] = flip(units[0, 0], "fsdp", 2)
    units[3, 0] = flip(units[1, 0], "fsdp", 2)
    units[3, 1] = flip(units[2, 1], "fsdp", 1)
    for half in range(2):
        units[4, half] = flip(units[0, half], "cuts", 1)
    *lows, turned = low_rank_values(
        tokens, cotangent, [gate_in, up_in, leave], [here, *[units[key] for key in ((1, 0), (2, 1), (4, 0), (4, 1))]]
    )
    pairs = {}
    for number, (one, two, ahead) in enumerate(
        (((1, 0), (2, 1), [turned]), ((1, 1), (2, 0), [turned]))
    ):
        pairs[number] = flip(pair(units[one], units[two], ahead), "cuts", 1)
    keys = [(0, 0), (0, 1), (1, 0), (1, 1), (2, 0), (2, 1), (4, 0), (4, 1)]
    placed = keys + [(5, 0), (6, 1), (5, 1), (6, 0)]
    arrays = [units[key] for key in keys] + [pairs[0], pairs[1]]
    masks = (0, 1, 2, 4, 5, 6)
    order = [placed.index((mask, half)) for mask in masks for half in range(2)]
    sums, parts, full = width_sums(
        here, tokens, cotangent, lows, [gate_out, up_out, down_in], masks, order, arrays, (3, 7)
    )
    tail = list(hold([units[3, 0], units[3, 1]], [sums[0]]))
    tail += [flip(unit, "cuts", 1) for unit in tail]

    factor = jnp.concatenate([gate_in, up_in])
    shift = lambda array, pairs: lax.ppermute(array, "tp", pairs)
    states, first = [], []
    share = lambda step, half, mode, came=(), ahead=(): token_grad(
        mode,
        step,
        here,
        [*states[half][1:], factor, *full, *tail],
        width // quarters,
        came,
        ahead,
    )
    both = range(HALVES)
    for half in both:
        state = hidden_and_grads(
            half, here, parts, [gate_out, up_out], tail, sums, first[:]
        )
        states.append(state)
        first.append(share(0, half, "first"))
    came = [shift(part, [(0, 1), (3, 2)]) for part in first]
    partial = []
    for half in both:
        partial.append(share(1, half, "sum", [came[half]], partial or first[1:]))
    second = partial
    from_left = [shift(part, [(0, 1), (1, 2)]) for part in partial]
    from_right = [shift(part, [(3, 2), (2, 1)]) for part in partial]
    keep, send = adapter_grads(
        gradient_scaling,
        here,
        groups,
        [
            *[state[number] for number in range(4) for state in states],
            tokens,
            cotangent,
            turned,
            down_in,
        ],
        first,
    )
    keep, send = halve(here, keep, flip(send, "cuts", 1))
    keep, send = halve(here, keep, flip(send, "fsdp", 2))
    narrow, keep, *send = turn(here, keep, flip(send, "fsdp", 1), width // groups, quarters)
    wide_grads = last_sum(
        here, keep, [flip(part, "tp", 1 + number) for number, part in enumerate(send)]
    )
    near = jnp.stack([narrow, flip(narrow, "fsdp", 1)])
    near = jnp.concatenate([near, flip(near, "fsdp", 2)])
    narrow_turned = whole(here, near, flip(near, "cuts", 1))
    narrow_grads = narrow_turned.T

    partial = []
    for half in both:
        partial.append(
            share(
                2,
                half,
                "both",
                [first[half], from_left[half], from_right[half]],
                partial[0][:1] if partial else second[1:],
            )
        )
    from_left = [shift(part[0], [(0, 1), (1, 2), (2, 3)]) for part in partial]
    from_right = [shift(part[1], [(3, 2), (2, 1), (1, 0)]) for part in partial]

    results = []
    for half in both:
        results.append(
            last_token_grad(
                3,
                half,
                here,
                [*states[half][1:], factor, *full, *tail],
                width // quarters,
                [from_left[half], from_right[half]],
                [] if half else partial[1],
                results[:],
            )
        )
    token_input_gradient = results[-1]
    return (token_input_gradient, wide_grads, narrow_grads)


def per_device(*arrays):
    sizes = [lax.axis_size(axis) for axis in ("cuts", "fsdp", "tp")]
    return (square_plane if sizes == [2, 4, 4] else any_plane)(*arrays)


def solution(mesh):
    in_specs = (
        P(("cuts", "fsdp"), None),
        P(("cuts", "fsdp"), None),
        P(("cuts", "fsdp"), "tp"),
        P(("cuts", "fsdp"), "tp"),
        P("tp", ("cuts", "fsdp")),
        P(),
        P(),
        P(None, "tp"),
        P(None, "tp"),
        P("tp", None),
        P(),
    )
    out_specs = (P(("cuts", "fsdp"), "tp"), P(("cuts", "fsdp", "tp"), None), P("tp", None))
    return jax.shard_map(
        per_device, mesh=mesh, in_specs=in_specs, out_specs=out_specs, check_vma=False
    )
```

```python
import functools
import math

import jax
import jax.numpy as jnp
from jax import lax
from jax.experimental import pallas as pl
from jax.experimental.pallas import tpu as pltpu
from jax.sharding import PartitionSpec as P

adapter_scaling = 0.5
MEBIBYTE = 1024 * 1024
COST = 1
HALVES = 2
COSTS = {"sums": 1, "pair": 1, "small": 1, "token": 20 * 10**9, "adapter": 20 * 10**9, "last": 10**11}
LIMITS = {"low": 6, "sums": 23, "last": 14, "token": 8, "adapter": 12, "small": 4}
TILE = 512
STRIP = 256
QUARTER_ORDER = ((3, 2, 1, 0), (0, 3, 2, 1), (3, 0, 1, 2), (0, 1, 2, 3))


def matrix_product(left, right):
    return jnp.dot(left, right, preferred_element_type=jnp.float32)


def contract_trailing_axis(left, right):
    return lax.dot_general(
        left, right, (((1,), (1,)), ((), ())), preferred_element_type=jnp.float32
    )


def contract_first(left, right):
    return lax.dot_general(
        left, right, (((0,), (0,)), ((), ())), preferred_element_type=jnp.float32
    )


def any_plane(
    tokens,
    cotangent,
    gate_frozen_matrix,
    up_frozen_matrix,
    down_frozen_matrix,
    gate_adapter_input_factor,
    up_adapter_input_factor,
    gate_adapter_output_factor,
    up_adapter_output_factor,
    down_adapter_input_factor,
    down_leave,
):
    token_groups = lax.axis_size(("cuts", "fsdp"))
    quarters = lax.axis_size("tp")
    tp_index = lax.axis_index("tp")
    token_rows = tokens.shape[0]
    width = tokens.shape[1]
    gradient_scaling = adapter_scaling / math.sqrt(token_rows * token_groups)
    gate_adapter_hidden = matrix_product(tokens, gate_adapter_input_factor).astype(jnp.bfloat16)
    up_adapter_hidden = matrix_product(tokens, up_adapter_input_factor).astype(jnp.bfloat16)
    pieces = (
        lax.all_gather(gate_frozen_matrix, ("cuts", "fsdp"), axis=0, tiled=True),
        lax.all_gather(up_frozen_matrix, ("cuts", "fsdp"), axis=0, tiled=True),
    )
    columns = tokens
    gate_frozen_output = matrix_product(columns, pieces[0])
    up_frozen_output = matrix_product(columns, pieces[1])
    gate_preactivation = gate_frozen_output + adapter_scaling * matrix_product(
        gate_adapter_hidden, gate_adapter_output_factor
    )
    up_preactivation = up_frozen_output + adapter_scaling * matrix_product(
        up_adapter_hidden, up_adapter_output_factor
    )
    sig = jax.nn.sigmoid(gate_preactivation)
    hidden = (gate_preactivation * sig * up_preactivation).astype(jnp.bfloat16)
    down_part = matrix_product(hidden, down_adapter_input_factor)
    down_low = lax.psum(down_part.astype(jnp.bfloat16), "tp")
    backward_adapter_input = matrix_product(cotangent, down_leave).astype(jnp.bfloat16)
    columns = cotangent
    hidden_state_gradient = contract_trailing_axis(
        columns, lax.all_gather(down_frozen_matrix, ("cuts", "fsdp"), axis=1, tiled=True)
    )
    hidden_state_gradient = hidden_state_gradient + adapter_scaling * contract_trailing_axis(
        backward_adapter_input, down_adapter_input_factor
    )
    gate_output_gradient = (
        hidden_state_gradient * up_preactivation * sig * (1.0 + gate_preactivation * (1.0 - sig))
    ).astype(jnp.bfloat16)
    up_output_gradient = (hidden_state_gradient * gate_preactivation * sig).astype(jnp.bfloat16)
    gate_part = contract_trailing_axis(gate_output_gradient, gate_adapter_output_factor)
    up_part = contract_trailing_axis(up_output_gradient, up_adapter_output_factor)
    gate_sum, up_sum = lax.psum((gate_part, up_part), "tp")
    gate_backward_adapter = gate_sum.astype(jnp.bfloat16)
    up_backward_adapter = up_sum.astype(jnp.bfloat16)
    pieces = lax.all_gather(
        (gate_frozen_matrix, up_frozen_matrix), ("cuts", "fsdp"), axis=0, tiled=True
    )
    partial_value = contract_trailing_axis(
        gate_output_gradient, pieces[0]
    ) + contract_trailing_axis(up_output_gradient, pieces[1])
    frozen_path_gradient = lax.psum_scatter(partial_value, "tp", scatter_dimension=1, tiled=True)
    slice_width = width // quarters
    gate_slice = lax.dynamic_slice_in_dim(
        gate_adapter_input_factor, tp_index * slice_width, slice_width, 0
    )
    up_slice = lax.dynamic_slice_in_dim(
        up_adapter_input_factor, tp_index * slice_width, slice_width, 0
    )
    adapter_hidden_gradient = contract_trailing_axis(
        gate_backward_adapter, gate_slice
    ) + contract_trailing_axis(up_backward_adapter, up_slice)
    token_input_gradient = (
        frozen_path_gradient + adapter_scaling * adapter_hidden_gradient
    ).astype(jnp.bfloat16)
    narrow_part = gradient_scaling * jnp.concatenate(
        [
            contract_first(hidden, backward_adapter_input),
            contract_first(gate_output_gradient, gate_adapter_hidden),
            contract_first(up_output_gradient, up_adapter_hidden),
        ],
        axis=1,
    )
    narrow_grads = lax.psum(narrow_part, ("cuts", "fsdp"))
    token_side = jnp.concatenate([gate_backward_adapter, up_backward_adapter], axis=1)
    group_rows = lax.psum_scatter(
        gradient_scaling
        * jnp.concatenate(
            [contract_first(tokens, token_side), contract_first(cotangent, down_low)], axis=1
        ),
        ("cuts", "fsdp"),
        scatter_dimension=0,
        tiled=True,
    )
    fine_rows = width // (token_groups * quarters)
    wide_grads = lax.dynamic_slice_in_dim(group_rows, tp_index * fine_rows, fine_rows, 0)
    return (token_input_gradient, wide_grads, narrow_grads)


def flip(array, axis, bit):
    size = lax.axis_size(axis)
    return lax.ppermute(array, axis, [(i, i ^ bit) for i in range(size)])


def vmem_call(
    kernel, scalars, arrays, ahead, results, aliases, scratch, limit, flops, name, final=False
):
    vmem = pl.BlockSpec(memory_space=pltpu.VMEM)
    first = len(scalars)
    return pl.pallas_call(
        kernel,
        in_specs=[pl.BlockSpec(memory_space=pltpu.SMEM)] * first
        + [vmem] * len(arrays)
        + [pl.BlockSpec(memory_space=pl.ANY)] * len(ahead),
        out_specs=[vmem] * len(results),
        out_shape=[
            jax.ShapeDtypeStruct(shape, kind) if final else pltpu.VMEM(shape, kind)
            for shape, kind in results
        ],
        scratch_shapes=scratch,
        input_output_aliases={first + source: target for source, target in aliases.items()},
        compiler_params=pltpu.CompilerParams(vmem_limit_bytes=limit * MEBIBYTE),
        cost_estimate=pl.CostEstimate(flops=COST * flops, bytes_accessed=0, transcendentals=0),
        name=name,
    )(
        *scalars,
        *[pltpu.with_memory_space_constraint(array, pltpu.VMEM) for array in arrays],
        *ahead,
    )


def width_part(ref, part, here, masks, rows):
    return jnp.concatenate(
        [
            ref[part, pl.ds(pl.multiple_of(lax.bitwise_xor(here[0], mask) * rows, rows), rows)]
            for mask in masks
        ],
        axis=1,
    )


def stacked(units, which, span):
    return jnp.concatenate([unit[which, :, span] for unit in units], axis=0)


def lows_kernel(tokens, cotangent, gate_in, up_in, leave, *refs):
    gate_low, up_low, back_low, turned = refs[-4:]
    rank = leave.shape[0]
    for number, (ref, factor, out) in enumerate(
        ((tokens, gate_in, gate_low), (tokens, up_in, up_low), (cotangent, leave, back_low))
    ):
        low = contract_trailing_axis(ref[...], factor[...]).astype(jnp.bfloat16)
        out[...] = low
        turned[number * rank : (number + 1) * rank, :] = low.astype(jnp.float32).T.astype(
            jnp.bfloat16
        )


def low_rank_values(tokens, cotangent, factors, ahead):
    rows, width = tokens.shape
    rank = factors[0].shape[0]
    tile = rows // 4
    by_rows = lambda columns: pl.BlockSpec((tile, columns), lambda i: (i, 0))
    return pl.pallas_call(
        lows_kernel,
        grid=(rows // tile,),
        in_specs=[by_rows(width)] * 2
        + [pl.BlockSpec((rank, width), lambda i: (0, 0))] * 3
        + [pl.BlockSpec(memory_space=pl.ANY)] * len(ahead),
        out_specs=[by_rows(rank)] * 3 + [pl.BlockSpec((3 * rank, tile), lambda i: (0, i))],
        out_shape=[jax.ShapeDtypeStruct((rows, rank), jnp.bfloat16)] * 3
        + [jax.ShapeDtypeStruct((3 * rank, rows), jnp.bfloat16)],
        compiler_params=pltpu.CompilerParams(vmem_limit_bytes=LIMITS["low"] * MEBIBYTE),
        cost_estimate=pl.CostEstimate(
            flops=480 * COST * rows * width * rank, bytes_accessed=0, transcendentals=0
        ),
        name="low_rank_values",
    )(tokens, cotangent, *factors, *ahead)


def own_kernel(gate, up, down, *refs):
    units, (held, sems) = refs[:2], refs[2:]
    rows = units[0].shape[1]
    down_copy = pltpu.make_async_copy(down, held, sems.at[0])
    down_copy.start()
    copies = []
    for half, unit in enumerate(units):
        for which, ref in enumerate((gate, up)):
            copies.append(
                pltpu.make_async_copy(
                    ref.at[pl.ds(half * rows, rows)], unit.at[which], sems.at[1 + len(copies)]
                )
            )
    for copy in copies:
        copy.start()
    down_copy.wait()
    for half, unit in enumerate(units):
        part = slice(half * rows, (half + 1) * rows)
        unit[2] = held[:, part].astype(jnp.float32).T.astype(jnp.bfloat16)
    for copy in copies:
        copy.wait()


def own_units(gate, up, down):
    rows, hidden = gate.shape
    return pl.pallas_call(
        own_kernel,
        in_specs=[pl.BlockSpec(memory_space=pl.ANY)] * 3,
        out_specs=[pl.BlockSpec(memory_space=pltpu.VMEM)] * 2,
        out_shape=[pltpu.VMEM((3, rows // 2, hidden), jnp.bfloat16)] * 2,
        scratch_shapes=[
            pltpu.VMEM((hidden, rows), jnp.bfloat16),
            pltpu.SemaphoreType.DMA((5,)),
        ],
        compiler_params=pltpu.CompilerParams(vmem_limit_bytes=LIMITS["low"] * MEBIBYTE),
        cost_estimate=pl.CostEstimate(flops=MEBIBYTE, bytes_accessed=0, transcendentals=0),
        name="own_units",
    )(*[pltpu.with_memory_space_constraint(array, pltpu.HBM) for array in (gate, up, down)])


def nothing_kernel(*refs):
    pass


def hold(arrays, ahead):
    anywhere = pl.BlockSpec(memory_space=pl.ANY)
    return pl.pallas_call(
        nothing_kernel,
        in_specs=[anywhere] * (len(arrays) + len(ahead)),
        out_specs=[anywhere] * len(arrays),
        out_shape=[jax.ShapeDtypeStruct(array.shape, array.dtype) for array in arrays],
        input_output_aliases={number: number for number in range(len(arrays))},
        compiler_params=pltpu.CompilerParams(vmem_limit_bytes=MEBIBYTE),
        cost_estimate=pl.CostEstimate(flops=1, bytes_accessed=1, transcendentals=0),
        name="hold",
    )(*arrays, *ahead)


def pair_kernel(first, second, *refs):
    refs[-1][0] = first[...]
    refs[-1][1] = second[...]


def pair(first, second, ahead):
    return vmem_call(
        pair_kernel,
        [],
        [first, second],
        ahead,
        [((2, *first.shape), first.dtype)],
        {},
        [],
        LIMITS["small"],
        COSTS["pair"],
        "pair",
    )[0]


def sums_kernel(masks, order, n_arrays, last, here, *refs):
    gate_low, up_low, back_low, gate_out, up_out, down_in, tokens, cotangent = refs[:8]
    units = []
    for ref in refs[8 : 8 + n_arrays]:
        units += [ref] if len(ref.shape) == 3 else [ref.at[0], ref.at[1]]
    units = [units[number] for number in order]
    outs = refs[8 + n_arrays :]
    sums, rest, full = outs[: 3 * HALVES], outs[3 * HALVES : 3 * HALVES + 2], outs[-7:-5]
    held_tokens, held_cotangent, held_down, row_sems, unit_sems = outs[-5:]
    half_rows, hidden = units[0].shape[1:]
    rows = 2 * half_rows
    tile = tokens.shape[0] // HALVES

    def unit_copies(which):
        copies = []
        for number, unit in enumerate(units):
            if which == 2:
                target = held_down.at[pl.ds(number * half_rows, half_rows)]
            else:
                block = lax.bitwise_xor(here[0], masks[number // 2])
                row = pl.multiple_of((2 * block + number % 2) * half_rows, half_rows)
                target = full[which].at[pl.ds(row, half_rows)]
            copies.append(
                pltpu.make_async_copy(
                    unit.at[which], target, unit_sems.at[which * len(units) + number]
                )
            )
        return copies

    def row_copy(which, half):
        source, target = ((tokens, held_tokens), (cotangent, held_cotangent))[which]
        part = pl.ds(half * tile, tile)
        return pltpu.make_async_copy(
            source.at[part], target.at[part], row_sems.at[which * HALVES + half]
        )

    loads = [*unit_copies(0), row_copy(0, 0), *unit_copies(1), row_copy(1, 0), *unit_copies(2)]
    loads += [row_copy(which, half) for half in range(1, HALVES) for which in range(2)]
    for load in loads:
        load.start()
    for half in range(HALVES):
        part = slice(half * tile, (half + 1) * tile)
        for which, (low, factor) in enumerate(
            ((gate_low, gate_out), (up_low, up_out), (back_low, down_in))
        ):
            if half == 0:
                for copy in unit_copies(which):
                    copy.wait()
            if which != 1:
                row_copy(which // 2, half).wait()
                ref = (held_tokens, held_cotangent)[which // 2]
                left = width_part(ref, part, here, masks, rows)
                rest[which // 2][part, :] = width_part(ref, part, here, last, rows)
            for column in range(0, hidden, TILE):
                span = slice(column, column + TILE)
                if which == 2:
                    right = held_down[:, span]
                else:
                    right = jnp.concatenate(
                        [
                            full[which][
                                pl.ds(
                                    pl.multiple_of(lax.bitwise_xor(here[0], mask) * rows, rows), rows
                                ),
                                span,
                            ]
                            for mask in masks
                        ]
                    )
                sums[3 * half + which][:, span] = matrix_product(
                    left, right
                ) + adapter_scaling * matrix_product(low[part, :], factor[:, span])


def width_sums(here, tokens, cotangent, lows, factors, masks, order, arrays, last):
    rows, width = tokens.shape
    _, half, hidden = arrays[0].shape[-3:]
    vmem, anywhere = pl.BlockSpec(memory_space=pltpu.VMEM), pl.BlockSpec(memory_space=pl.ANY)
    shapes = [((rows // HALVES, hidden), jnp.float32)] * (3 * HALVES)
    shapes += [((rows, 2 * half * len(last)), jnp.bfloat16)] * 2
    shapes += [((width, hidden), jnp.bfloat16)] * 2
    outs = pl.pallas_call(
        functools.partial(sums_kernel, masks, order, len(arrays), last),
        in_specs=[pl.BlockSpec(memory_space=pltpu.SMEM)]
        + [vmem] * 6
        + [anywhere] * (2 + len(arrays)),
        out_specs=[vmem] * len(shapes),
        out_shape=[pltpu.VMEM(shape, kind) for shape, kind in shapes],
        scratch_shapes=[
            pltpu.VMEM((rows, width), jnp.bfloat16),
            pltpu.VMEM((rows, width), jnp.bfloat16),
            pltpu.VMEM((half * len(order), hidden), jnp.bfloat16),
            pltpu.SemaphoreType.DMA((2 * HALVES,)),
            pltpu.SemaphoreType.DMA((3 * len(order),)),
        ],
        compiler_params=pltpu.CompilerParams(vmem_limit_bytes=LIMITS["sums"] * MEBIBYTE),
        cost_estimate=pl.CostEstimate(flops=COSTS["sums"], bytes_accessed=0, transcendentals=0),
        name="width_sums",
    )(here, *lows, *factors, tokens, cotangent, *arrays)
    return outs[: 3 * HALVES], outs[3 * HALVES : -2], outs[-2:]


def last_kernel(half, here, left, back, gate_out, up_out, *refs):
    units, sums = refs[:4], refs[4:7]
    hidden_out, gate_grad_out, up_grad_out, low_out = refs[-4:]
    rows, hidden = hidden_out.shape
    part = slice(half * rows, (half + 1) * rows)
    gate_low = up_low = 0.0
    for column in range(0, hidden, STRIP):
        span = slice(column, column + STRIP)
        gate = sums[0][:, span] + matrix_product(left[part, :], stacked(units, 0, span))
        up = sums[1][:, span] + matrix_product(left[part, :], stacked(units, 1, span))
        hidden_grad = sums[2][:, span] + matrix_product(back[part, :], stacked(units, 2, span))
        sig = 1.0 / (1.0 + jnp.exp(-gate))
        gated = gate * sig
        hidden_out[:, span] = (gated * up).astype(jnp.bfloat16)
        gate_grad = (hidden_grad * up * sig * (1.0 + gate * (1.0 - sig))).astype(jnp.bfloat16)
        up_grad = (hidden_grad * gated).astype(jnp.bfloat16)
        gate_grad_out[:, span] = gate_grad
        up_grad_out[:, span] = up_grad
        gate_low += contract_trailing_axis(gate_grad, gate_out[:, span])
        up_low += contract_trailing_axis(up_grad, up_out[:, span])
    low_out[...] = jnp.concatenate([gate_low, up_low], axis=1)


def hidden_and_grads(half, here, parts, factors, tail, sums, ahead):
    rows = parts[0].shape[0] // HALVES
    rank, hidden = factors[0].shape
    return vmem_call(
        functools.partial(last_kernel, half),
        [here],
        [*parts, *factors, *tail, *sums[3 * half : 3 * half + 3]],
        ahead,
        [((rows, hidden), jnp.bfloat16)] * 3 + [((rows, 2 * rank), jnp.float32)],
        {},
        [],
        LIMITS["last"],
        COSTS["last"],
        "hidden_and_grads",
    )


def quarter_rows(here, quarter, full, tail, which, columns):
    rows = 2 * tail[0].shape[1]
    blocks = []
    for number in range(columns // rows):
        block = quarter * (columns // rows) + number
        mask = lax.bitwise_xor(here[0], block)
        held = full[pl.ds(pl.multiple_of(block * rows, rows), rows), :]
        near, far = (
            jnp.concatenate([unit[which] for unit in units]) for units in (tail[:2], tail[2:])
        )
        blocks.append(jnp.where(mask == 7, far, jnp.where(mask == 3, near, held)))
    return jnp.concatenate(blocks)


def token_grad_kernel(mode, step, here, gate_grad, up_grad, low, factor, gate, up, *refs):
    tail, refs = refs[:4], refs[4:]
    came = refs[: {"first": 0, "sum": 1, "both": 3, "last": 2}[mode]]
    outs = refs[-2:] if mode == "both" else refs[-1:]
    columns = outs[0].shape[1]
    quarter = sum(
        jnp.where(here[1] == place, order[step], 0) for place, order in enumerate(QUARTER_ORDER)
    )
    span = pl.ds(pl.multiple_of(quarter * columns, columns), columns)
    total = contract_trailing_axis(
        gate_grad[...], quarter_rows(here, quarter, gate, tail, 0, columns)
    )
    total += contract_trailing_axis(up_grad[...], quarter_rows(here, quarter, up, tail, 1, columns))
    total += matrix_product((adapter_scaling * low[...]).astype(jnp.bfloat16), factor[:, span])
    came = [ref[...].astype(jnp.float32) for ref in came]
    if mode == "both":
        first, left, right = came
        outs[0][...] = (jnp.where(here[1] == 2, first, total) + left).astype(jnp.bfloat16)
        outs[1][...] = (jnp.where(here[1] == 1, first, total) + right).astype(jnp.bfloat16)
    else:
        outs[0][...] = sum(came, total).astype(jnp.bfloat16)


def token_grad(mode, step, here, arrays, columns, came, ahead):
    rows, hidden = arrays[0].shape
    outs = vmem_call(
        functools.partial(token_grad_kernel, mode, step),
        [here],
        [*arrays, *came],
        ahead,
        [((rows, columns), jnp.bfloat16)] * (2 if mode == "both" else 1),
        {},
        [],
        LIMITS["token"],
        COSTS["token"],
        "token_grad",
    )
    return outs if mode == "both" else outs[0]


def last_token_grad(step, half, here, arrays, columns, came, ahead, before):
    rows, hidden = arrays[0].shape
    arrays = [*arrays, *came]
    return pl.pallas_call(
        functools.partial(token_grad_kernel, "last", step),
        grid=(1,),
        in_specs=[pl.BlockSpec(memory_space=pltpu.SMEM)]
        + [pl.BlockSpec(memory_space=pltpu.VMEM)] * len(arrays)
        + [pl.BlockSpec(memory_space=pl.ANY)] * (len(before) + len(ahead)),
        out_specs=pl.BlockSpec((rows, columns), lambda i: (half, 0)),
        out_shape=jax.ShapeDtypeStruct((HALVES * rows, columns), jnp.bfloat16),
        input_output_aliases={1 + len(arrays): 0} if before else {},
        compiler_params=pltpu.CompilerParams(vmem_limit_bytes=LIMITS["token"] * MEBIBYTE),
        cost_estimate=pl.CostEstimate(
            flops=COSTS["token"],
            bytes_accessed=0,
            transcendentals=0,
        ),
        name="last_token_grad",
    )(
        here,
        *[pltpu.with_memory_space_constraint(array, pltpu.VMEM) for array in arrays],
        *before,
        *ahead,
    )


def adapter_kernel(scaling, here, *refs):
    hidden, gate_grad, up_grad, low = (
        refs[number * HALVES : (number + 1) * HALVES] for number in range(4)
    )
    tokens, cotangent, turned, down_in = refs[4 * HALVES : 4 * HALVES + 4]
    keep, send, wide, narrow = refs[-4:]
    rank = down_in.shape[0]
    rows = hidden[0].shape[0]
    parts = [slice(half * rows, (half + 1) * rows) for half in range(HALVES)]
    wide[: 2 * rank, :] = scaling * sum(
        matrix_product(low[half][...].T.astype(jnp.bfloat16), tokens[part, :])
        for half, part in enumerate(parts)
    )
    wide[2 * rank :, :] = scaling * sum(
        matrix_product(
            contract_trailing_axis(down_in[...], hidden[half][...]).astype(jnp.bfloat16),
            cotangent[part, :],
        )
        for half, part in enumerate(parts)
    )
    for number, arrays in enumerate((hidden, gate_grad, up_grad)):
        source = (2, 0, 1)[number]
        narrow[number * rank : (number + 1) * rank, :] = scaling * sum(
            matrix_product(turned[source * rank : (source + 1) * rank, part], arrays[half][...])
            for half, part in enumerate(parts)
        )
    groups = 2 * keep.shape[0]
    wide_columns, narrow_columns = wide.shape[1] // groups, narrow.shape[1] // groups
    for mask in range(groups):
        out = (keep if mask < groups // 2 else send).at[mask % (groups // 2)]
        block = lax.bitwise_xor(here[0], mask)
        out[:, :wide_columns] = wide[
            :, pl.ds(pl.multiple_of(block * wide_columns, wide_columns), wide_columns)
        ]
        out[:, wide_columns:] = narrow[
            :, pl.ds(pl.multiple_of(block * narrow_columns, narrow_columns), narrow_columns)
        ]


def adapter_grads(scaling, here, groups, arrays, ahead):
    rows, width = arrays[-4].shape
    rank, hidden = arrays[-1].shape
    return vmem_call(
        functools.partial(adapter_kernel, scaling),
        [here],
        arrays,
        ahead,
        [((groups // 2, 3 * rank, (width + hidden) // groups), jnp.float32)] * 2,
        {},
        [pltpu.VMEM((3 * rank, width), jnp.float32), pltpu.VMEM((3 * rank, hidden), jnp.float32)],
        LIMITS["adapter"],
        COSTS["adapter"],
        "adapter_grads",
    )


def halve_kernel(here, keep, came, kept, send):
    count = kept.shape[0]
    kept[...] = keep[:count] + came[:count].astype(jnp.float32)
    send[...] = (keep[count:] + came[count:].astype(jnp.float32)).astype(send.dtype)


def halve(here, keep, came):
    shape = (keep.shape[0] // 2, *keep.shape[1:])
    return vmem_call(
        halve_kernel,
        [here],
        [keep, came],
        [],
        [(shape, jnp.float32), (shape, jnp.bfloat16)],
        {},
        [],
        LIMITS["small"],
        COSTS["small"],
        "halve",
    )


def sum_kernel(here, keep, *refs):
    refs[-1][...] = sum((ref[...].astype(jnp.float32) for ref in refs[:-1]), keep[...])


def last_sum(here, keep, came):
    return vmem_call(
        sum_kernel,
        [here],
        [keep, *came],
        [],
        [(keep.shape, jnp.float32)],
        {},
        [],
        LIMITS["small"],
        COSTS["small"],
        "last_sum",
        True,
    )[0]


def turn_kernel(wide_columns, here, kept, came, narrow, *refs):
    outs, wide = refs[:-1], refs[-1]
    total = kept[0] + came[0].astype(jnp.float32)
    narrow[...] = total[:, wide_columns:]
    wide[...] = total[:, :wide_columns].T
    for mask, out in enumerate(outs):
        rows = out.shape[0]
        block = pl.ds(pl.multiple_of(lax.bitwise_xor(here[1], mask) * rows, rows), rows)
        out[...] = wide[block, :].astype(out.dtype)


def turn(here, keep, came, wide_columns, quarters):
    _, rows, columns = keep.shape
    return vmem_call(
        functools.partial(turn_kernel, wide_columns),
        [here],
        [keep, came],
        [],
        [((rows, columns - wide_columns), jnp.float32)]
        + [
            ((wide_columns // quarters, rows), jnp.bfloat16 if mask else jnp.float32)
            for mask in range(quarters)
        ],
        {},
        [pltpu.VMEM((wide_columns, rows), jnp.float32)],
        LIMITS["small"],
        COSTS["small"],
        "turn",
    )


def whole_kernel(here, near, far, out):
    columns = near.shape[2]
    for number in range(2 * near.shape[0]):
        ref = near if number < near.shape[0] else far
        block = lax.bitwise_xor(here[0], number) * columns
        out[:, pl.ds(pl.multiple_of(block, columns), columns)] = ref[number % near.shape[0]]


def whole(here, near, far):
    count, rows, columns = near.shape
    return vmem_call(
        whole_kernel,
        [here],
        [near, far],
        [],
        [((rows, 2 * count * columns), near.dtype)],
        {},
        [],
        LIMITS["small"],
        COSTS["small"],
        "whole",
        True,
    )[0]


def square_plane(
    tokens,
    cotangent,
    gate_frozen_matrix,
    up_frozen_matrix,
    down_frozen_matrix,
    gate_adapter_input_factor,
    up_adapter_input_factor,
    gate_adapter_output_factor,
    up_adapter_output_factor,
    down_adapter_input_factor,
    down_leave,
):
    groups = lax.axis_size(("cuts", "fsdp"))
    quarters = lax.axis_size("tp")
    rows, width = tokens.shape
    gradient_scaling = adapter_scaling / math.sqrt(rows * groups)
    here = jnp.stack([lax.axis_index(("cuts", "fsdp")), lax.axis_index("tp")]).astype(jnp.int32)
    gate_in, up_in, leave, down_in = (
        array.T
        for array in (
            gate_adapter_input_factor,
            up_adapter_input_factor,
            down_leave,
            down_adapter_input_factor,
        )
    )
    gate_out, up_out = gate_adapter_output_factor, up_adapter_output_factor

    units = {}
    units[0, 0], units[0, 1] = own_units(
        gate_frozen_matrix, up_frozen_matrix, down_frozen_matrix
    )
    units[1, 0] = flip(units[0, 0], "fsdp", 1)
    units[2, 1] = flip(units[0, 1], "fsdp", 2)
    units[1, 1] = flip(units[0, 1], "fsdp", 1)
    units[2, 0] = flip(units[0, 0], "fsdp", 2)
    units[3, 0] = flip(units[1, 0], "fsdp", 2)
    units[3, 1] = flip(units[2, 1], "fsdp", 1)
    for half in range(2):
        units[4, half] = flip(units[0, half], "cuts", 1)
    *lows, turned = low_rank_values(
        tokens, cotangent, [gate_in, up_in, leave], [here, *[units[key] for key in ((1, 0), (2, 1), (4, 0), (4, 1))]]
    )
    pairs = {}
    for number, (one, two, ahead) in enumerate(
        (((1, 0), (2, 1), [turned]), ((1, 1), (2, 0), [turned]))
    ):
        pairs[number] = flip(pair(units[one], units[two], ahead), "cuts", 1)
    keys = [(0, 0), (0, 1), (1, 0), (1, 1), (2, 0), (2, 1), (4, 0), (4, 1)]
    placed = keys + [(5, 0), (6, 1), (5, 1), (6, 0)]
    arrays = [units[key] for key in keys] + [pairs[0], pairs[1]]
    masks = (0, 1, 2, 4, 5, 6)
    order = [placed.index((mask, half)) for mask in masks for half in range(2)]
    sums, parts, full = width_sums(
        here, tokens, cotangent, lows, [gate_out, up_out, down_in], masks, order, arrays, (3, 7)
    )
    tail = list(hold([units[3, 0], units[3, 1]], [sums[0]]))
    tail += [flip(unit, "cuts", 1) for unit in tail]

    factor = jnp.concatenate([gate_in, up_in])
    shift = lambda array, pairs: lax.ppermute(array, "tp", pairs)
    states, first = [], []
    share = lambda step, half, mode, came=(), ahead=(): token_grad(
        mode,
        step,
        here,
        [*states[half][1:], factor, *full, *tail],
        width // quarters,
        came,
        ahead,
    )
    both = range(HALVES)
    for half in both:
        state = hidden_and_grads(
            half, here, parts, [gate_out, up_out], tail, sums, first[:]
        )
        states.append(state)
        first.append(share(0, half, "first"))
    came = [shift(part, [(0, 1), (3, 2)]) for part in first]
    partial = []
    for half in both:
        partial.append(share(1, half, "sum", [came[half]], partial or first[1:]))
    second = partial
    from_left = [shift(part, [(0, 1), (1, 2)]) for part in partial]
    from_right = [shift(part, [(3, 2), (2, 1)]) for part in partial]
    keep, send = adapter_grads(
        gradient_scaling,
        here,
        groups,
        [
            *[state[number] for number in range(4) for state in states],
            tokens,
            cotangent,
            turned,
            down_in,
        ],
        first,
    )
    keep, send = halve(here, keep, flip(send, "cuts", 1))
    keep, send = halve(here, keep, flip(send, "fsdp", 2))
    narrow, keep, *send = turn(here, keep, flip(send, "fsdp", 1), width // groups, quarters)
    wide_grads = last_sum(
        here, keep, [flip(part, "tp", 1 + number) for number, part in enumerate(send)]
    )
    near = jnp.stack([narrow, flip(narrow, "fsdp", 1)])
    near = jnp.concatenate([near, flip(near, "fsdp", 2)])
    narrow_turned = whole(here, near, flip(near, "cuts", 1))
    narrow_grads = narrow_turned.T

    partial = []
    for half in both:
        partial.append(
            share(
                2,
                half,
                "both",
                [first[half], from_left[half], from_right[half]],
                partial[0][:1] if partial else second[1:],
            )
        )
    from_left = [shift(part[0], [(0, 1), (1, 2), (2, 3)]) for part in partial]
    from_right = [shift(part[1], [(3, 2), (2, 1), (1, 0)]) for part in partial]

    results = []
    for half in both:
        results.append(
            last_token_grad(
                3,
                half,
                here,
                [*states[half][1:], factor, *full, *tail],
                width // quarters,
                [from_left[half], from_right[half]],
                [] if half else partial[1],
                results[:],
            )
        )
    token_input_gradient = results[-1]
    return (token_input_gradient, wide_grads, narrow_grads)


def per_device(*arrays):
    sizes = [lax.axis_size(axis) for axis in ("cuts", "fsdp", "tp")]
    return (square_plane if sizes == [2, 4, 4] else any_plane)(*arrays)


def solution(mesh):
    in_specs = (
        P(("cuts", "fsdp"), None),
        P(("cuts", "fsdp"), None),
        P(("cuts", "fsdp"), "tp"),
        P(("cuts", "fsdp"), "tp"),
        P("tp", ("cuts", "fsdp")),
        P(),
        P(),
        P(None, "tp"),
        P(None, "tp"),
        P("tp", None),
        P(),
    )
    out_specs = (P(("cuts", "fsdp"), "tp"), P(("cuts", "fsdp", "tp"), None), P("tp", None))
    return jax.shard_map(
        per_device, mesh=mesh, in_specs=in_specs, out_specs=out_specs, check_vma=False
    )
```
